32 devices in a mesh: col: 4 (over x, core), row: 8 (over z, y).
Axes of the slice: x: 2, y: 2, z: 4, core: 2. Of those that a mesh axis runs over, the one named last changes fastest.
Arguments:
- drive: float32 [8192], P(('col', 'row')), may hold values from -6 to 6
- resist: float32 [8192], P(('col', 'row')), may hold values from 1 to 4
- centers: float32 [3, 8192], P(None, 'col'), may hold values from 0 to 1
- tangents: float32 [3, 8192], P(None, 'col'), may hold values from -5 to 5
- iron_points: float32 [3, 65536], P(None, ('col', 'row')), may hold values from 0 to 1
- owner: int32 [65536, 1], P(('col', 'row')), may hold values from 0 to 7; in each aligned block of 2048 rows (0 to 2047, 2048 to 4095, ...) at most 512 rows name the same one
- range_len: int32 [8], replicated, may hold values from 256 to 1024, as said below
Outputs:
- currents: float32 [8192], P(('col', 'row'))
- iron_field: float32 [3, 65536], P(None, ('col', 'row'))
The draws below stay inside these ranges and needn't reach their ends.
Inputs may be any that keep to these rules, and one draw needn't show every extreme that they name: `owner`: the 2048 points of one device name each block at most 512 times, and in every draw some device names some block exactly 512 times. `range_len`: some block has all 1024 segments active.
All inputs are finite; a program needn't handle non-finite values.
Results may differ from the reference program's by a relative error of at most 0.0003.
Values sent between devices are 32-bit elements; how exact they have to be, the bound alone decides.
No kernel may reach another device: no remote copies, remote signals or barrier semaphores. Data moves between devices by JAX's collectives and lax.ppermute only.
A program may use at most 64 MiB of HBM per device.

```python
import math
import jax
import jax.numpy as jnp
import numpy as np
from jax import lax

SEG_DEV = 256
P_DEV = 2048
KRYLOV = 2
SEGMENTS = 8192
BLOCKSEG = 1024
IRON = 65536
CAP = 512
N_COL = 4
N_ROW = 8


def draw_range_len(key, part):
    key = jax.random.fold_in(key, 5)
    key_lengths, key_choice = jax.random.split(key)
    lengths = jax.random.randint(key_lengths, (N_ROW,), BLOCKSEG // 4, BLOCKSEG + 1)
    chosen = jax.random.randint(key_choice, (), 0, N_ROW)
    return jnp.where(jnp.arange(N_ROW) == chosen, BLOCKSEG, lengths).astype(jnp.int32)


def draw_drive(key, part):
    key = jax.random.fold_in(key, 11)
    ramp = 1.0 + 0.75 * (jnp.arange(SEGMENTS).astype(jnp.float32) / SEGMENTS)
    noise = 0.35 * jnp.clip(jax.random.normal(key, (SEGMENTS,), jnp.float32), -3.0, 3.0)
    level = 1.0
    return (ramp * (level + noise)).astype(jnp.float32)


def draw_tangents(key, part):
    key = jax.random.fold_in(key, 13)
    key_dir, key_noise = jax.random.split(key)
    angles = jax.random.uniform(key_dir, (2,), jnp.float32, -3.1, 3.1)
    common = jnp.stack([jnp.cos(angles[0]) * jnp.cos(angles[1]), jnp.cos(angles[0]) * jnp.sin(angles[1]), jnp.sin(angles[0])])
    strength = 7.5 * float(SEGMENTS) ** (-0.25)
    noise = 0.4 * jnp.clip(jax.random.normal(key_noise, (3, SEGMENTS), jnp.float32), -3.0, 3.0)
    return (strength * (common[:, None] + noise)).astype(jnp.float32)


def draw_centers(key, part):
    key = jax.random.fold_in(key, 17)
    key_slab, key_depth, key_plane = jax.random.split(key, 3)
    plane = jax.random.uniform(key_plane, (2, SEGMENTS), jnp.float32, 0.0, 1.0)
    slab = jax.random.randint(key_slab, (SEGMENTS,), 0, 4).astype(jnp.float32)
    depth = 0.1 + 0.2667 * slab + jax.random.uniform(key_depth, (SEGMENTS,), jnp.float32, -0.02, 0.02)
    return jnp.stack([depth, plane[0], plane[1]]).astype(jnp.float32)


def level_of(stream_key, extent, cuts, low, top_value):
    loudness, own = 1.0, jax.random.fold_in(stream_key, 6)
    for position, parts in cuts:
        steps = jnp.exp(jax.random.uniform(jax.random.fold_in(own, position), (parts,), jnp.float32, low / len(cuts), top_value / len(cuts)))
        loudness = loudness * jnp.repeat(steps, extent[position] // parts).reshape([-1 if axis == position else 1 for axis in range(len(extent))])
    return loudness


def assign_block(own_key, own, number, rows, amount, top, bound, lean):
    ranking = jax.random.permutation(own_key, amount)
    packed, usual = shares(amount, rows * top, bound, lean, True), shares(amount, rows * top, bound, lean, False)
    places = jnp.arange(amount)

    def named(tallies, rotation):
        used = int((tallies > 0).sum())
        fixed = max(1, used // 4)
        shifted = fixed + (places - fixed + rotation * (used - fixed)) % max(1, amount - fixed)
        return jnp.zeros((amount,), jnp.int32).at[ranking[jnp.where(places < fixed, places, shifted)]].set(jnp.asarray(tallies, jnp.int32))

    tallies = jnp.where(number % 4 == 0, named(packed, number // 4), named(usual, number - number // 4 - 1))
    mixed = jax.random.permutation(jax.random.fold_in(own, 3), amount)
    giver, receiver = mixed[0:amount // 2 * 2:2], mixed[1:amount // 2 * 2:2]
    margin = jnp.minimum(tallies[giver] - 1, bound - tallies[receiver]) // 2
    margin = jnp.where((giver == ranking[0]) | (receiver == ranking[0]) | (tallies[receiver] == 0), 0, jnp.maximum(margin, 0))
    shifted = jax.random.randint(jax.random.fold_in(own, 4), (amount // 2,), 0, 1 << 20) % (margin + 1)
    tallies = tallies.at[giver].add(-shifted).at[receiver].add(shifted)
    labels = jnp.searchsorted(jnp.cumsum(tallies), jnp.arange(rows * top), side="right").astype(jnp.int32)
    table = labels.reshape(top, rows).T
    table = table[jax.random.permutation(jax.random.fold_in(own, 1), rows)]
    rotation = jax.random.randint(jax.random.fold_in(own, 2), (rows, 1), 0, top)
    return jnp.take_along_axis(table, (jnp.arange(top)[None, :] + rotation) % top, axis=1)


def shares(number_of, total, limit, slope, full):
    weights = [(1 << 20) // math.isqrt(standing ** slope) + 1 for standing in range(1, number_of + 1)]
    largest = limit if full else min(limit, max(-(-total // number_of), total * weights[0] // sum(weights)))
    least = 1 if total - largest >= number_of - 1 else 0
    holding, surplus = [largest] + [least] * (number_of - 1), total - largest - least * (number_of - 1)
    while surplus > 0:
        movable = [i for i in range(1, number_of) if holding[i] < largest] or [i for i in range(1, number_of) if holding[i] < limit]
        whole, left = sum([weights[i] for i in movable]), surplus
        for i in movable:
            addition = min(limit - holding[i], max(1, left * weights[i] // whole), surplus)
            holding[i] = holding[i] + addition
            surplus = surplus - addition
    return np.array(holding)


def setup_inputs(seed: int = 0) -> dict:
    seeds = jax.random.split(jax.random.key(seed), 8)
    drive = draw_drive(jax.random.fold_in(seeds[7], 71), 0)
    resist = jnp.clip(jnp.exp(math.log(4.0) - 1.3862944 * jax.random.uniform(seeds[1], (SEGMENTS,), jnp.float32) ** level_of(seeds[1], (SEGMENTS,), ((0, 32),), -0.2, 0.2)), 1.0, 4.0)
    centers = draw_centers(jax.random.fold_in(seeds[7], 71), 0)
    tangents = draw_tangents(jax.random.fold_in(seeds[7], 71), 0)
    iron_points = jnp.clip(1.0 * jax.random.uniform(seeds[4], (3, IRON), jnp.float32) ** level_of(seeds[4], (3, IRON), ((1, 32),), -0.2, 0.2), 0.0, 1.0)
    owner_keys = jax.random.split(jax.random.fold_in(seeds[5], 1), IRON // P_DEV)
    owner_turns = jax.random.permutation(jax.random.fold_in(seeds[5], 3), IRON // P_DEV)
    owner = jax.vmap(lambda own, number: assign_block(jax.random.fold_in(seeds[5], 2), own, number, P_DEV, N_ROW, 1, CAP, 2))(owner_keys, owner_turns).reshape((IRON, 1))
    range_len = draw_range_len(jax.random.fold_in(seeds[7], 71), 0)
    return dict(drive=drive, resist=resist, centers=centers, tangents=tangents, iron_points=iron_points, owner=owner, range_len=range_len)


EPS_SEG = 0.0004
EPS_FIELD = 0.0025

def tile_product(row_geo, col_geo, vector):
    diff_x = row_geo[0][:, None] - col_geo[0][None, :]
    diff_y = row_geo[1][:, None] - col_geo[1][None, :]
    diff_z = row_geo[2][:, None] - col_geo[2][None, :]
    inverse = lax.rsqrt(diff_x * diff_x + diff_y * diff_y + diff_z * diff_z + EPS_SEG)
    along = row_geo[3][:, None] * col_geo[3][None, :] + row_geo[4][:, None] * col_geo[4][None, :] + row_geo[5][:, None] * col_geo[5][None, :]
    return jnp.dot(along * inverse, vector, precision=lax.Precision.HIGHEST)

def point_field(points, blocks, masks):
    diff_x = points[0][:, None] - blocks[:, 1, :]
    diff_y = points[1][:, None] - blocks[:, 2, :]
    diff_z = points[2][:, None] - blocks[:, 3, :]
    radius_sq = diff_x * diff_x + diff_y * diff_y + diff_z * diff_z + EPS_FIELD
    weight = blocks[:, 0, :] * masks * lax.rsqrt(radius_sq) / radius_sq
    field_x = lax.optimization_barrier(jnp.sum(weight * (blocks[:, 5, :] * diff_z - blocks[:, 6, :] * diff_y), axis=1))
    field_y = lax.optimization_barrier(jnp.sum(weight * (blocks[:, 6, :] * diff_x - blocks[:, 4, :] * diff_z), axis=1))
    field_z = lax.optimization_barrier(jnp.sum(weight * (blocks[:, 4, :] * diff_y - blocks[:, 5, :] * diff_x), axis=1))
    return jnp.stack([field_x, field_y, field_z])

def reference(drive, resist, centers, tangents, iron_points, owner, range_len):
    geometry = jnp.concatenate([centers, tangents], axis=0)
    coupling = 0.5 / math.sqrt(SEGMENTS)
    row_part = math.gcd(SEGMENTS, 512)
    row_blocks = geometry.reshape(6, SEGMENTS // row_part, row_part).transpose(1, 0, 2)

    def apply(vector):
        image = lax.map(lambda row_geo: tile_product(row_geo, geometry, vector), row_blocks).reshape(SEGMENTS)
        return resist * vector + coupling * image
    initial_norm = jnp.sqrt(jnp.sum(drive * drive))
    basis = [drive / initial_norm]
    columns = []
    for krylov_step in range(KRYLOV):
        image = apply(basis[krylov_step])
        coeffs = [jnp.sum(image * vector) for vector in basis]
        rest = image
        for projected, vector in zip(coeffs, basis):
            rest = rest - projected * vector
        length = jnp.sqrt(jnp.sum(rest * rest))
        columns.append((coeffs, length))
        basis.append(rest / length)
    hessen_a = columns[0][0][0]
    hessen_b = columns[0][1]
    hessen_c = columns[1][0][0]
    hessen_d = columns[1][0][1]
    hessen_e = columns[1][1]
    normal_first = hessen_a * hessen_a + hessen_b * hessen_b
    normal_cross = hessen_a * hessen_c + hessen_b * hessen_d
    normal_second = hessen_c * hessen_c + hessen_d * hessen_d + hessen_e * hessen_e
    target_first = initial_norm * hessen_a
    target_second = initial_norm * hessen_c
    determinant = normal_first * normal_second - normal_cross * normal_cross
    weight_first = (normal_second * target_first - normal_cross * target_second) / determinant
    weight_second = (normal_first * target_second - normal_cross * target_first) / determinant
    currents = weight_first * basis[0] + weight_second * basis[1]
    blocks = jnp.concatenate([currents[None, :], geometry], axis=0)
    blocks = blocks.reshape(7, N_COL, N_ROW, SEG_DEV).transpose(2, 0, 1, 3).reshape(N_ROW, 7, BLOCKSEG)
    masks = (jnp.arange(BLOCKSEG)[None, :] < range_len[:, None]).astype(jnp.float32)
    owners = owner[:, 0]
    batch_size = math.gcd(IRON, 256)
    point_batches = iron_points.reshape(3, IRON // batch_size, batch_size).transpose(1, 0, 2)
    owner_batches = owners.reshape(IRON // batch_size, batch_size)

    def evaluate(pair):
        return point_field(pair[0], blocks[pair[1]], masks[pair[1]])
    fields = lax.map(evaluate, (point_batches, owner_batches))
    iron_field = fields.transpose(1, 0, 2).reshape(3, IRON) * (1.0 / math.sqrt(BLOCKSEG))
    return (currents, iron_field)
```

```python
import functools
import math

import jax
import jax.numpy as jnp
from jax import lax
from jax.experimental import pallas as pl
from jax.experimental.pallas import tpu as pltpu
from jax.sharding import PartitionSpec as P

EPS_SEG = 0.0004
EPS_FIELD = 0.0025
AXES = ("col", "row")
CHUNK = 128
VMEM_LIMIT = 48 * 1024 * 1024


def split3(x):
    high = x.astype(jnp.bfloat16).astype(jnp.float32)
    rest = x - high
    middle = rest.astype(jnp.bfloat16).astype(jnp.float32)
    low = (rest - middle).astype(jnp.bfloat16).astype(jnp.float32)
    return high, middle, low


def left_parts(x):
    high, middle, low = split3(x)
    return jnp.concatenate([high, high, middle, middle, high, low], axis=0).astype(jnp.bfloat16)


def right_parts(x):
    high, middle, low = split3(x)
    return jnp.concatenate([high, middle, high, middle, low, high], axis=0).astype(jnp.bfloat16)


def rows8(*rows):
    width = rows[0].shape[1]
    count = sum(r.shape[0] for r in rows)
    if count < 8:
        rows = rows + (jnp.zeros((8 - count, width), jnp.float32),)
    return jnp.concatenate(rows, axis=0)


def moving_center(c):
    square = jnp.sum(c * c, axis=0, keepdims=True)
    return rows8(-2.0 * c, jnp.ones_like(square), square)


def fixed_center(c, eps):
    square = jnp.sum(c * c, axis=0, keepdims=True) + eps
    return rows8(c, square, jnp.ones_like(square))


def dot(a, b):
    return jnp.dot(a, b, preferred_element_type=jnp.float32)


def dot_nt(a, b):
    return lax.dot_general(a, b, (((1,), (1,)), ((), ())), preferred_element_type=jnp.float32)


def couple(own_ref, geo_ref, vec_ref, acc_ref, tile):
    own = own_ref[...]
    count = geo_ref.shape[1] // tile
    lc = transposed(left_parts_f32(moving_center(own[0:3] - 0.5)))
    lt = transposed(left_parts_f32(rows8(own[3:6])))
    acc_ref[...] = jnp.zeros_like(acc_ref)

    def step(k, carry):
        at = pl.ds(pl.multiple_of(k * tile, tile), tile)
        geo = geo_ref[:, at]
        vec = vec_ref[:, at]
        rc = right_parts(fixed_center(geo[0:3] - 0.5, EPS_SEG))
        rt = right_parts(rows8(geo[3:6] * vec))
        pair = dot(lt, rt) * lax.rsqrt(dot(lc, rc))
        total = pair[:, 0:128]
        for piece in range(1, tile // 128):
            total = total + pair[:, piece * 128:(piece + 1) * 128]
        acc_ref[...] += total
        return carry

    lax.fori_loop(0, count, step, 0)
    return jnp.sum(acc_ref[...].T, axis=0, keepdims=True)


def left_parts_f32(x):
    high, middle, low = split3(x)
    return jnp.concatenate([high, high, middle, middle, high, low], axis=0)


def transposed(x):
    return x.T.astype(jnp.bfloat16)


def first_kernel(coupling, own_ref, geo_ref, drive_ref, drive_own_ref, resist_ref, image_ref, vec_ref, acc_ref, *, tile):
    drive = drive_ref[...]
    scale = 1.0 / jnp.sqrt(jnp.sum(drive * drive, keepdims=True))
    vec_ref[...] = drive * scale
    product = couple(own_ref, geo_ref, vec_ref, acc_ref, tile)
    image_ref[...] = resist_ref[...] * (drive_own_ref[...] * scale) + coupling * product


def second_kernel(
    coupling, own_ref, geo_ref, drive_ref, image_ref, drive_own_ref, image_own_ref, resist_ref,
    basis_ref, basis_own_ref, stats_ref, vec_ref, acc_ref, *, tile
):
    drive = drive_ref[...]
    norm_sq = jnp.sum(drive * drive, keepdims=True)
    norm = jnp.sqrt(norm_sq)
    scale = 1.0 / norm
    basis_a = drive * scale
    image = image_ref[...]
    hessen_a = jnp.sum(image * basis_a, keepdims=True)
    rest = image - hessen_a * basis_a
    hessen_b = jnp.sqrt(jnp.sum(rest * rest, keepdims=True))
    inverse = 1.0 / hessen_b
    basis_b = rest * inverse
    vec_ref[...] = basis_b
    basis_ref[0:1, :] = basis_a
    basis_ref[1:2, :] = basis_b
    own_a = drive_own_ref[...] * scale
    own_b = (image_own_ref[...] - hessen_a * own_a) * inverse
    basis_own_ref[0:1, :] = own_a
    basis_own_ref[1:2, :] = own_b
    product = couple(own_ref, geo_ref, vec_ref, acc_ref, tile)
    second = resist_ref[...] * own_b + coupling * product
    lane = lax.broadcasted_iota(jnp.int32, (1, 128), 1)
    part_c = jnp.sum(second * own_a, keepdims=True)
    part_d = jnp.sum(second * own_b, keepdims=True)
    part_s = jnp.sum(second * second, keepdims=True)
    stats_ref[0:1, :] = jnp.where(lane == 0, part_c, jnp.where(lane == 1, part_d, jnp.where(lane == 2, part_s, 0.0)))
    stats_ref[1:2, :] = jnp.where(lane == 0, norm, jnp.where(lane == 1, hessen_a, jnp.where(lane == 2, hessen_b, 0.0)))


def field_kernel(counts_ref, length_ref, points_ref, geo_ref, basis_ref, out_ref, rc_ref, table_ref, *, n_col, n_row, seg_dev, capacity):
    width = n_col * seg_dev
    quarter = width // 4
    scale = 1.0 / math.sqrt(width)
    lane = lax.broadcasted_iota(jnp.int32, (1, seg_dev), 1)

    def block_step(block, carry):
        length = length_ref[block]
        for col in range(n_col):
            at = pl.ds(pl.multiple_of((col * n_row + block) * seg_dev, seg_dev), seg_dev)
            to = pl.ds(col * seg_dev, seg_dev)
            geo = geo_ref[:, at]
            center = geo[0:3] - 0.5
            tangent = geo[3:6]
            rc_ref[:, to] = right_parts(fixed_center(center, EPS_FIELD))
            cross = jnp.concatenate([
                tangent[1:2] * center[2:3] - tangent[2:3] * center[1:2],
                tangent[2:3] * center[0:1] - tangent[0:1] * center[2:3],
                tangent[0:1] * center[1:2] - tangent[1:2] * center[0:1],
            ], axis=0)
            both = rows8(tangent, cross)
            active = jnp.where(lane + col * seg_dev < length, scale, 0.0)
            first = both * (basis_ref[0:1, at] * active)
            second = both * (basis_ref[1:2, at] * active)
            parts = jnp.concatenate([first, second], axis=0)
            high = parts.astype(jnp.bfloat16).astype(jnp.float32)
            table_ref[:, to] = jnp.concatenate([high, parts - high], axis=0).astype(jnp.bfloat16)
        chunks = (counts_ref[block] + CHUNK - 1) // CHUNK
        tiles = (length + quarter - 1) // quarter

        def chunk_step(chunk, carry):
            at = pl.ds(pl.multiple_of(block * capacity + chunk * CHUNK, CHUNK), CHUNK)
            left = transposed(left_parts_f32(moving_center(points_ref[:, at] - 0.5)))
            for size in range(1, 5):
                @pl.when(tiles == size)
                def _():
                    used = size * quarter
                    inverse = lax.rsqrt(dot(left, rc_ref[:, 0:used]))
                    cube = inverse * inverse * inverse
                    high = cube.astype(jnp.bfloat16)
                    low = (cube - high.astype(jnp.float32)).astype(jnp.bfloat16)
                    table = table_ref[:, 0:used]
                    total = dot_nt(high, table) + dot_nt(low, table)
                    total = total.T
                    out_ref[:, at] = total[0:16] + total[16:32]
            return carry

        lax.fori_loop(0, chunks, chunk_step, 0)
        return carry

    lax.fori_loop(0, n_row, block_step, 0)


def shift_sum(x, axis):
    size = lax.axis_size(axis)
    total = x
    for shift in range(1, size):
        total = total + lax.ppermute(x, axis, [(i, (i + shift) % size) for i in range(size)])
    return total


def shards(drive, resist, centers, tangents, iron_points, owner, range_len):
    seg_dev = drive.shape[0]
    n_col = lax.axis_size("col")
    n_row = lax.axis_size("row")
    n_dev = n_col * n_row
    segments = seg_dev * n_dev
    coupling = 0.5 / math.sqrt(segments)
    geometry = jnp.concatenate([centers, tangents], axis=0)
    row_index = lax.axis_index("row")
    own = lax.dynamic_slice_in_dim(geometry, row_index * seg_dev, seg_dev, 1)
    params = pltpu.CompilerParams(vmem_limit_bytes=VMEM_LIMIT)
    tile = 512
    drive_own = drive[None, :]
    resist_own = resist[None, :]
    drive_all = lax.all_gather(drive, AXES, axis=0, tiled=True)[None, :]
    geo_all = lax.all_gather(geometry, "col", axis=1, tiled=True)
    scratch = [pltpu.VMEM((1, segments), jnp.float32), pltpu.VMEM((seg_dev, 128), jnp.float32)]
    image_own = pl.pallas_call(
        functools.partial(first_kernel, coupling, tile=tile),
        out_shape=jax.ShapeDtypeStruct((1, seg_dev), jnp.float32),
        scratch_shapes=scratch,
        compiler_params=params,
        name="first_image",
    )(own, geo_all, drive_all, drive_own, resist_own)
    spread = jnp.broadcast_to(image_own, (n_dev, seg_dev))
    image_all = lax.all_to_all(spread, AXES, 0, 0, tiled=True).reshape(1, segments)
    basis, basis_own, stats = pl.pallas_call(
        functools.partial(second_kernel, coupling, tile=tile),
        out_shape=(
            jax.ShapeDtypeStruct((2, segments), jnp.float32),
            jax.ShapeDtypeStruct((2, seg_dev), jnp.float32),
            jax.ShapeDtypeStruct((2, 128), jnp.float32),
        ),
        scratch_shapes=scratch,
        compiler_params=params,
        name="second_image",
    )(own, geo_all, drive_all, image_all, drive_own, image_own, resist_own)
    sums = shift_sum(shift_sum(stats[0:1], "col"), "row")

    points_count = iron_points.shape[1]
    owners = owner[:, 0]
    capacity = 2 * points_count // n_row
    marks = (owners[:, None] == jnp.arange(n_row)[None, :]).astype(jnp.int32)
    ranks = jnp.sum((jnp.cumsum(marks, axis=0) - 1) * marks, axis=1)
    counts = jnp.sum(marks, axis=0)
    slots = owners * capacity + ranks
    grouped = jnp.zeros((3, n_row * capacity), jnp.float32).at[:, slots].set(iron_points)
    smem = pl.BlockSpec(memory_space=pltpu.SMEM)
    vmem = pl.BlockSpec(memory_space=pltpu.VMEM)
    field = pl.pallas_call(
        functools.partial(field_kernel, n_col=n_col, n_row=n_row, seg_dev=seg_dev, capacity=capacity),
        out_shape=jax.ShapeDtypeStruct((16, n_row * capacity), jnp.float32),
        in_specs=[smem, smem, vmem, vmem, vmem],
        scratch_shapes=[
            pltpu.VMEM((48, n_col * seg_dev), jnp.bfloat16),
            pltpu.VMEM((32, n_col * seg_dev), jnp.bfloat16),
        ],
        compiler_params=params,
        name="block_field",
    )(counts, range_len, grouped, geo_all, basis)

    initial_norm = stats[1, 0]
    hessen_a = stats[1, 1]
    hessen_b = stats[1, 2]
    hessen_c = sums[0, 0]
    hessen_d = sums[0, 1]
    normal_first = hessen_a * hessen_a + hessen_b * hessen_b
    normal_cross = hessen_a * hessen_c + hessen_b * hessen_d
    normal_second = sums[0, 2]
    target_first = initial_norm * hessen_a
    target_second = initial_norm * hessen_c
    determinant = normal_first * normal_second - normal_cross * normal_cross
    weight_first = (normal_second * target_first - normal_cross * target_second) / determinant
    weight_second = (normal_first * target_second - normal_cross * target_first) / determinant
    currents = weight_first * basis_own[0] + weight_second * basis_own[1]
    moments = (weight_first * field[0:6] + weight_second * field[8:14])[:, slots]
    px, py, pz = iron_points[0] - 0.5, iron_points[1] - 0.5, iron_points[2] - 0.5
    iron_field = jnp.stack([
        pz * moments[1] - py * moments[2] - moments[3],
        px * moments[2] - pz * moments[0] - moments[4],
        py * moments[0] - px * moments[1] - moments[5],
    ])
    return (currents, iron_field)


def solution(mesh):
    return jax.shard_map(
        shards,
        mesh=mesh,
        in_specs=(
            P(AXES),
            P(AXES),
            P(None, "col"),
            P(None, "col"),
            P(None, AXES),
            P(AXES, None),
            P(),
        ),
        out_specs=(P(AXES), P(None, AXES)),
        check_vma=False,
    )
```

```python
import functools
import math

import jax
import jax.numpy as jnp
from jax import lax
from jax.experimental import pallas as pl
from jax.experimental.pallas import tpu as pltpu
from jax.sharding import PartitionSpec as P

EPS_SEG = 0.0004
EPS_FIELD = 0.0025
AXES = ("col", "row")
CHUNK = 128
PAIR = 2 * CHUNK
KEEP_BYTES = 16 * 1024 * 1024
VMEM_LIMIT = 32 * 1024 * 1024


def split3(x):
    high = x.astype(jnp.bfloat16).astype(jnp.float32)
    rest = x - high
    middle = rest.astype(jnp.bfloat16).astype(jnp.float32)
    low = (rest - middle).astype(jnp.bfloat16).astype(jnp.float32)
    return high, middle, low


def left_parts(x):
    high, middle, low = split3(x)
    return jnp.concatenate([high, high, middle, middle, high, low], axis=0)


def right_parts(x):
    high, middle, low = split3(x)
    return jnp.concatenate([high, middle, high, middle, low, high], axis=0).astype(jnp.bfloat16)


def rows8(*rows):
    width = rows[0].shape[1]
    count = sum(r.shape[0] for r in rows)
    if count < 8:
        rows = rows + (jnp.zeros((8 - count, width), jnp.float32),)
    return jnp.concatenate(rows, axis=0)


def moving_center(c):
    square = jnp.sum(c * c, axis=0, keepdims=True)
    return rows8(-2.0 * c, jnp.ones_like(square), square)


def fixed_center(c, eps):
    square = jnp.sum(c * c, axis=0, keepdims=True) + eps
    return rows8(c, square, jnp.ones_like(square))


def dot(a, b):
    return jnp.dot(a, b, preferred_element_type=jnp.float32)


def dot_nt(a, b):
    return lax.dot_general(a, b, (((1,), (1,)), ((), ())), preferred_element_type=jnp.float32)


def transposed(x):
    return x.T.astype(jnp.bfloat16)


def fold_lanes(x):
    total = x[:, 0:128]
    for piece in range(1, x.shape[1] // 128):
        total = total + x[:, piece * 128:(piece + 1) * 128]
    return total


def couple(geo_ref, vec_ref, acc_ref, kept_ref, tile):
    seg_dev = acc_ref.shape[0]
    n_col, _, length = geo_ref.shape
    column = lax.axis_index("col")
    at = pl.ds(pl.multiple_of(lax.axis_index("row") * seg_dev, seg_dev), seg_dev)
    own = geo_ref[column, :, at]
    lc = transposed(left_parts(moving_center(own[0:3] - 0.5)))
    lt = transposed(left_parts(rows8(own[3:6])))
    acc_ref[...] = jnp.zeros_like(acc_ref)
    per_col = length // tile

    def step(k, carry):
        at = pl.ds(pl.multiple_of((k % per_col) * tile, tile), tile)
        to = pl.ds(pl.multiple_of(k * tile, tile), tile)
        geo = geo_ref[k // per_col, :, at]
        rc = right_parts(fixed_center(geo[0:3] - 0.5, EPS_SEG))
        rt = right_parts(rows8(geo[3:6]))
        pair = dot(lt, rt) * lax.rsqrt(dot(lc, rc))
        if kept_ref is not None:
            kept_ref[:, to] = pair
        acc_ref[...] += fold_lanes(pair * vec_ref[:, to])
        return carry

    lax.fori_loop(0, n_col * per_col, step, 0)
    return jnp.sum(acc_ref[...].T, axis=0, keepdims=True)


def couple_kept(kept_ref, vec_ref, acc_ref, tile):
    acc_ref[...] = jnp.zeros_like(acc_ref)

    def step(k, carry):
        to = pl.ds(pl.multiple_of(k * tile, tile), tile)
        acc_ref[...] += fold_lanes(kept_ref[:, to] * vec_ref[:, to])
        return carry

    lax.fori_loop(0, vec_ref.shape[1] // tile, step, 0)
    return jnp.sum(acc_ref[...].T, axis=0, keepdims=True)


def spread_rows(ref, row):
    for k in range(ref.shape[0]):
        ref[k] = row


def spread_kernel(row_ref, out_ref):
    spread_rows(out_ref, row_ref[...])


def pack_kernel(centers_ref, tangents_ref, out_ref):
    for k in range(out_ref.shape[0]):
        out_ref[k, 0:3] = centers_ref[...]
        out_ref[k, 3:6] = tangents_ref[...]


def first_kernel(coupling, tile, keep, geo_ref, drive_ref, drive_own_ref, resist_ref, *refs):
    image_ref, spread_ref = refs[0:2]
    kept_ref = refs[2] if keep else None
    vec_ref, acc_ref = refs[-2:]
    drive = drive_ref[...]
    scale = 1.0 / jnp.sqrt(jnp.sum(drive * drive, keepdims=True))
    vec_ref[...] = drive * scale
    product = couple(geo_ref, vec_ref, acc_ref, kept_ref, tile)
    image = resist_ref[...] * (drive_own_ref[...] * scale) + coupling * product
    image_ref[...] = image
    spread_rows(spread_ref, image)


def second_kernel(coupling, tile, matrix_ref, drive_ref, image_ref, drive_own_ref, image_own_ref, resist_ref,
                  basis_ref, basis_own_ref, stats_ref, known_ref, vec_ref, acc_ref):
    drive = drive_ref[...]
    norm = jnp.sqrt(jnp.sum(drive * drive, keepdims=True))
    scale = 1.0 / norm
    basis_a = drive * scale
    image = image_ref[...]
    hessen_a = jnp.sum(image * basis_a, keepdims=True)
    rest = image - hessen_a * basis_a
    hessen_b = jnp.sqrt(jnp.sum(rest * rest, keepdims=True))
    inverse = 1.0 / hessen_b
    basis_b = rest * inverse
    vec_ref[...] = basis_b
    basis_ref[0:1, :] = basis_a
    basis_ref[1:2, :] = basis_b
    own_a = drive_own_ref[...] * scale
    own_b = (image_own_ref[...] - hessen_a * own_a) * inverse
    basis_own_ref[0:1, :] = own_a
    basis_own_ref[1:2, :] = own_b
    if len(matrix_ref.shape) == 3:
        product = couple(matrix_ref, vec_ref, acc_ref, None, tile)
    else:
        product = couple_kept(matrix_ref, vec_ref, acc_ref, tile)
    second = resist_ref[...] * own_b + coupling * product
    lane = lax.broadcasted_iota(jnp.int32, (1, 128), 1)

    def three(a, b, c):
        return jnp.where(lane == 0, a, jnp.where(lane == 1, b, jnp.where(lane == 2, c, 0.0)))

    spread_rows(stats_ref, three(
        jnp.sum(second * own_a, keepdims=True),
        jnp.sum(second * own_b, keepdims=True),
        jnp.sum(second * second, keepdims=True),
    ))
    known_ref[...] = three(norm, hessen_a, hessen_b)


def one_hot(slot, base):
    near = jnp.clip(slot - base, -1, PAIR).astype(jnp.bfloat16)
    row = lax.broadcasted_iota(jnp.int32, (PAIR, slot.shape[1]), 0).astype(jnp.bfloat16)
    return jnp.where(row == near, jnp.ones((), jnp.bfloat16), jnp.zeros((), jnp.bfloat16))


def group_kernel(owner_ref, points_ref, slot_ref, table_ref, left_ref, *, n_row, pairs):
    points = owner_ref.shape[1]
    owner = owner_ref[...]
    rows = max(8, n_row)
    names = lax.broadcasted_iota(jnp.int32, (rows, points), 0)
    marks = jnp.where(names == owner, 1.0, 0.0)
    tile = 256
    upper = jnp.where(
        lax.broadcasted_iota(jnp.int32, (tile, tile), 0) <= lax.broadcasted_iota(jnp.int32, (tile, tile), 1), 1.0, 0.0
    ).astype(jnp.bfloat16)
    before = jnp.zeros((rows, 1), jnp.float32)
    ranks = []
    for piece in range(points // tile):
        part = dot(marks[:, piece * tile:(piece + 1) * tile].astype(jnp.bfloat16), upper)
        ranks.append(part + before - 1.0)
        before = before + part[:, tile - 1:tile]
    ranks = jnp.concatenate(ranks, axis=1)
    chunks = jnp.floor((before + (CHUNK - 1)) * (1.0 / CHUNK))
    start = jnp.zeros((1, 1), jnp.float32)
    starts = []
    for name in range(rows):
        starts.append(start)
        start = start + chunks[name:name + 1]
    starts = jnp.concatenate(starts, axis=0)
    slot = jnp.sum(marks * (ranks + starts * CHUNK), axis=0, keepdims=True).astype(jnp.int32)
    slot_ref[...] = slot
    lane = lax.broadcasted_iota(jnp.int32, (rows, 128), 1)
    table_ref[...] = jnp.where(lane == 0, before, jnp.where(lane == 1, starts, start)).astype(jnp.int32)
    parts = left_parts(moving_center(points_ref[...] - 0.5)).astype(jnp.bfloat16)

    def step(pair, carry):
        at = pl.ds(pl.multiple_of(pair * PAIR, PAIR), PAIR)
        left_ref[at, :] = dot_nt(one_hot(slot, pair * PAIR), parts).astype(jnp.bfloat16)
        return carry

    lax.fori_loop(0, pairs, step, 0)


def field_kernel(table_in_ref, length_ref, slot_ref, left_ref, geo_ref, basis_ref, out_ref, rc_ref, table_ref, sums_ref, acc_ref,
                 *, n_row, seg_dev):
    n_col = geo_ref.shape[0]
    width = n_col * seg_dev
    quarter = width // 4
    scale = 1.0 / math.sqrt(width)
    lane = lax.broadcasted_iota(jnp.int32, (1, seg_dev), 1)
    chunk_lane = lax.broadcasted_iota(jnp.int32, (1, CHUNK), 1)
    sums_ref[...] = jnp.zeros_like(sums_ref)

    def block_step(block, carry):
        length = length_ref[block]
        count = table_in_ref[block, 0]
        first_chunk = table_in_ref[block, 1]
        for col in range(n_col):
            at = pl.ds(pl.multiple_of(block * seg_dev, seg_dev), seg_dev)
            vec_at = pl.ds(pl.multiple_of((col * n_row + block) * seg_dev, seg_dev), seg_dev)
            to = pl.ds(col * seg_dev, seg_dev)
            geo = geo_ref[col, :, at]
            center = geo[0:3] - 0.5
            tangent = geo[3:6]
            rc_ref[:, to] = right_parts(fixed_center(center, EPS_FIELD))
            cross = jnp.concatenate([
                tangent[1:2] * center[2:3] - tangent[2:3] * center[1:2],
                tangent[2:3] * center[0:1] - tangent[0:1] * center[2:3],
                tangent[0:1] * center[1:2] - tangent[1:2] * center[0:1],
            ], axis=0)
            both = rows8(tangent, cross)
            active = jnp.where(lane + col * seg_dev < length, scale, 0.0)
            first = both * (basis_ref[0:1, vec_at] * active)
            second = both * (basis_ref[1:2, vec_at] * active)
            parts = jnp.concatenate([first, second], axis=0)
            high = parts.astype(jnp.bfloat16).astype(jnp.float32)
            table_ref[:, to] = jnp.concatenate([high, parts - high], axis=0).astype(jnp.bfloat16)
        tiles = (length + quarter - 1) // quarter

        def chunk_step(chunk, carry):
            at = pl.ds(pl.multiple_of((first_chunk + chunk) * CHUNK, CHUNK), CHUNK)
            left = left_ref[at, :]
            for size in range(1, 5):
                @pl.when(tiles == size)
                def _():
                    used = size * quarter
                    inverse = lax.rsqrt(dot(left, rc_ref[:, 0:used]))
                    cube = inverse * inverse * inverse
                    high = cube.astype(jnp.bfloat16)
                    low = (cube - high.astype(jnp.float32)).astype(jnp.bfloat16)
                    table = table_ref[:, 0:used]
                    total = (dot_nt(high, table) + dot_nt(low, table)).T
                    total = jnp.where(chunk_lane < count - chunk * CHUNK, total[0:16] + total[16:32], 0.0)
                    sums_ref[:, at] = jnp.concatenate(split3(total), axis=0).astype(jnp.bfloat16)
            return carry

        lax.fori_loop(0, (count + CHUNK - 1) // CHUNK, chunk_step, 0)
        return carry

    lax.fori_loop(0, n_row, block_step, 0)
    acc_ref[...] = jnp.zeros_like(acc_ref)
    slot = slot_ref[...]

    def back_step(pair, carry):
        at = pl.ds(pl.multiple_of(pair * PAIR, PAIR), PAIR)
        acc_ref[...] += dot(sums_ref[:, at], one_hot(slot, pair * PAIR))
        return carry

    lax.fori_loop(0, (table_in_ref[0, 2] + 1) // 2, back_step, 0)
    out_ref[...] = acc_ref[0:16] + acc_ref[16:32] + acc_ref[32:48]


def final_kernel(stats_ref, known_ref, basis_own_ref, field_ref, points_ref, currents_ref, iron_ref):
    stats = jnp.sum(stats_ref[...], axis=0)
    known = known_ref[...]
    initial_norm, hessen_a, hessen_b = known[:, 0:1], known[:, 1:2], known[:, 2:3]
    hessen_c, hessen_d, normal_second = stats[:, 0:1], stats[:, 1:2], stats[:, 2:3]
    normal_first = hessen_a * hessen_a + hessen_b * hessen_b
    normal_cross = hessen_a * hessen_c + hessen_b * hessen_d
    target_first = initial_norm * hessen_a
    target_second = initial_norm * hessen_c
    determinant = normal_first * normal_second - normal_cross * normal_cross
    weight_first = (normal_second * target_first - normal_cross * target_second) / determinant
    weight_second = (normal_first * target_second - normal_cross * target_first) / determinant
    currents_ref[...] = weight_first * basis_own_ref[0:1, :] + weight_second * basis_own_ref[1:2, :]
    moments = weight_first * field_ref[0:8, :] + weight_second * field_ref[8:16, :]
    points = points_ref[...] - 0.5
    px, py, pz = points[0:1], points[1:2], points[2:3]
    iron_ref[0:1, :] = pz * moments[1:2] - py * moments[2:3] - moments[3:4]
    iron_ref[1:2, :] = px * moments[2:3] - pz * moments[0:1] - moments[4:5]
    iron_ref[2:3, :] = py * moments[0:1] - px * moments[1:2] - moments[5:6]


def shape(*sizes, dtype=jnp.float32):
    return jax.ShapeDtypeStruct(sizes, dtype)


def shards(drive, resist, centers, tangents, iron_points, owner, range_len):
    seg_dev = drive.shape[0]
    col_len = centers.shape[1]
    n_col = lax.axis_size("col")
    n_row = lax.axis_size("row")
    n_dev = n_col * n_row
    segments = seg_dev * n_dev
    points_count = iron_points.shape[1]
    coupling = 0.5 / math.sqrt(segments)
    keep = seg_dev * segments * 4 <= KEEP_BYTES
    tile = 512
    params = pltpu.CompilerParams(vmem_limit_bytes=VMEM_LIMIT)
    call = functools.partial(pl.pallas_call, compiler_params=params)
    scratch = [pltpu.VMEM((1, segments), jnp.float32), pltpu.VMEM((seg_dev, 128), jnp.float32)]
    drive_own = drive[None, :]
    resist_own = resist[None, :]

    def exchange(x, axes):
        return lax.all_to_all(x, axes, 0, 0, tiled=True)

    drive_all = exchange(call(spread_kernel, out_shape=shape(n_dev, 1, seg_dev), name="spread")(drive_own), AXES)
    drive_all = drive_all.reshape(1, segments)
    geo_all = exchange(call(pack_kernel, out_shape=shape(n_col, 6, col_len), name="pack")(centers, tangents), "col")

    pairs = (points_count // CHUNK + n_row * (CHUNK - 1) // CHUNK + 1) // 2
    slot, group_table, left = call(
        functools.partial(group_kernel, n_row=n_row, pairs=pairs),
        out_shape=(
            shape(1, points_count, dtype=jnp.int32),
            shape(max(8, n_row), 128, dtype=jnp.int32),
            shape(pairs * PAIR, 48, dtype=jnp.bfloat16),
        ),
        name="group_points",
    )(owner.reshape(1, points_count), iron_points)

    first = call(
        functools.partial(first_kernel, coupling, tile, keep),
        out_shape=(shape(1, seg_dev), shape(n_dev, 1, seg_dev)) + ((shape(seg_dev, segments),) if keep else ()),
        scratch_shapes=scratch,
        name="first_image",
    )(geo_all, drive_all, drive_own, resist_own)
    image_own = first[0]
    image_all = exchange(first[1], AXES).reshape(1, segments)
    basis, basis_own, stats, known = call(
        functools.partial(second_kernel, coupling, tile),
        out_shape=(shape(2, segments), shape(2, seg_dev), shape(n_dev, 1, 128), shape(1, 128)),
        scratch_shapes=scratch,
        name="second_image",
    )(first[2] if keep else geo_all, drive_all, image_all, drive_own, image_own, resist_own)
    stats_all = exchange(stats, AXES)

    smem = pl.BlockSpec(memory_space=pltpu.SMEM)
    vmem = pl.BlockSpec(memory_space=pltpu.VMEM)
    width = n_col * seg_dev
    field = call(
        functools.partial(field_kernel, n_row=n_row, seg_dev=seg_dev),
        out_shape=shape(16, points_count),
        in_specs=[smem, smem, vmem, vmem, vmem, vmem],
        scratch_shapes=[
            pltpu.VMEM((48, width), jnp.bfloat16),
            pltpu.VMEM((32, width), jnp.bfloat16),
            pltpu.VMEM((48, pairs * PAIR), jnp.bfloat16),
            pltpu.VMEM((48, points_count), jnp.float32),
        ],
        name="block_field",
    )(group_table, range_len, slot, left, geo_all, basis)
    currents, iron_field = call(
        final_kernel,
        out_shape=(shape(1, seg_dev), shape(3, points_count)),
        name="combine",
    )(stats_all, known, basis_own, field, iron_points)
    return (currents[0], iron_field)


def solution(mesh):
    return jax.shard_map(
        shards,
        mesh=mesh,
        in_specs=(
            P(AXES),
            P(AXES),
            P(None, "col"),
            P(None, "col"),
            P(None, AXES),
            P(AXES, None),
            P(),
        ),
        out_specs=(P(AXES), P(None, AXES)),
        check_vma=False,
    )
```

```python
import functools
import math

import jax
import jax.numpy as jnp
from jax import lax
from jax.experimental import pallas as pl
from jax.experimental.pallas import tpu as pltpu
from jax.sharding import PartitionSpec as P

EPS_SEG = 0.0004
EPS_FIELD = 0.0025
AXES = ("col", "row")
CHUNK = 128
PAIR = 2 * CHUNK
KEEP_BYTES = 16 * 1024 * 1024
VMEM_LIMIT = 32 * 1024 * 1024


def split3(x):
    high = x.astype(jnp.bfloat16).astype(jnp.float32)
    rest = x - high
    middle = rest.astype(jnp.bfloat16).astype(jnp.float32)
    low = (rest - middle).astype(jnp.bfloat16).astype(jnp.float32)
    return high, middle, low


def left_parts(x):
    high, middle, low = split3(x)
    return jnp.concatenate([high, high, middle, middle, high, low], axis=0)


def right_parts(x):
    high, middle, low = split3(x)
    return jnp.concatenate([high, middle, high, middle, low, high], axis=0).astype(jnp.bfloat16)


def rows8(*rows):
    width = rows[0].shape[1]
    count = sum(r.shape[0] for r in rows)
    if count < 8:
        rows = rows + (jnp.zeros((8 - count, width), jnp.float32),)
    return jnp.concatenate(rows, axis=0)


def left_center(c, eps):
    square = jnp.sum(c * c, axis=0, keepdims=True)
    return rows8(-2.0 * c, jnp.ones_like(square), square + eps)


def right_center(c):
    square = jnp.sum(c * c, axis=0, keepdims=True)
    return rows8(c, square, jnp.ones_like(square))


def dot(a, b):
    return jnp.dot(a, b, preferred_element_type=jnp.float32)


def dot_nt(a, b):
    return lax.dot_general(a, b, (((1,), (1,)), ((), ())), preferred_element_type=jnp.float32)


def transposed(x):
    return x.T.astype(jnp.bfloat16)


def fold_lanes(x):
    total = x[:, 0:128]
    for piece in range(1, x.shape[1] // 128):
        total = total + x[:, piece * 128:(piece + 1) * 128]
    return total


def couple(geo_ref, vec_ref, acc_ref, kept_ref, right_ref, moment_ref, tile):
    seg_dev = acc_ref.shape[0]
    n_col, _, length = geo_ref.shape
    column = lax.axis_index("col")
    at = pl.ds(pl.multiple_of(lax.axis_index("row") * seg_dev, seg_dev), seg_dev)
    own = geo_ref[column, :, at]
    lc = transposed(left_parts(left_center(own[0:3] - 0.5, EPS_SEG)))
    lt = transposed(left_parts(rows8(own[3:6])))
    acc_ref[...] = jnp.zeros_like(acc_ref)
    per_col = length // tile

    def step(k, carry):
        col = k // per_col
        at = pl.ds(pl.multiple_of((k % per_col) * tile, tile), tile)
        to = pl.ds(pl.multiple_of(k * tile, tile), tile)
        geo = geo_ref[col, :, at]
        center, tangent = geo[0:3] - 0.5, geo[3:6]
        rc = right_parts(right_center(center))
        rt = right_parts(rows8(tangent))
        pair = dot(lt, rt) * lax.rsqrt(dot(lc, rc))
        if kept_ref is not None:
            kept_ref[:, to] = pair
        if right_ref is not None:
            cross = jnp.concatenate([
                tangent[1:2] * center[2:3] - tangent[2:3] * center[1:2],
                tangent[2:3] * center[0:1] - tangent[0:1] * center[2:3],
                tangent[0:1] * center[1:2] - tangent[1:2] * center[0:1],
            ], axis=0)
            both = rows8(tangent, cross)
            for part in range(tile // seg_dev):
                row = (k % per_col) * (tile // seg_dev) + part
                block_at = pl.ds(pl.multiple_of((row * n_col + col) * seg_dev, seg_dev), seg_dev)
                right_ref[:, block_at] = rc[:, part * seg_dev:(part + 1) * seg_dev]
                moment_ref[:, block_at] = both[:, part * seg_dev:(part + 1) * seg_dev]
        acc_ref[...] += fold_lanes(pair * vec_ref[:, to])
        return carry

    lax.fori_loop(0, n_col * per_col, step, 0, unroll=2)
    return jnp.sum(acc_ref[...].T, axis=0, keepdims=True)


def couple_kept(kept_ref, vec_ref, acc_ref, tile):
    acc_ref[...] = jnp.zeros_like(acc_ref)

    def step(k, carry):
        to = pl.ds(pl.multiple_of(k * tile, tile), tile)
        acc_ref[...] += fold_lanes(kept_ref[:, to] * vec_ref[:, to])
        return carry

    lax.fori_loop(0, vec_ref.shape[1] // tile, step, 0)
    return jnp.sum(acc_ref[...].T, axis=0, keepdims=True)


def spread_rows(ref, row):
    for k in range(ref.shape[0]):
        ref[k] = row


def entry_kernel(drive_hbm, resist_hbm, centers_hbm, tangents_hbm, drive_ref, resist_ref, spread_ref, geo_ref, centers, tangents, sems):
    copies = [
        pltpu.make_async_copy(source, target, sems.at[k])
        for k, (source, target) in enumerate([
            (drive_hbm, drive_ref), (resist_hbm, resist_ref), (centers_hbm, centers), (tangents_hbm, tangents),
        ])
    ]
    for copy in copies:
        copy.start()
    for copy in copies:
        copy.wait()
    spread_rows(spread_ref, drive_ref[...])
    for k in range(geo_ref.shape[0]):
        geo_ref[k, 0:3] = centers[...]
        geo_ref[k, 3:6] = tangents[...]


def first_kernel(coupling, tile, keep, geo_ref, drive_ref, drive_own_ref, resist_ref, after_ref, *refs):
    image_ref, spread_ref, right_ref, moment_ref = refs[0:4]
    kept_ref = refs[4] if keep else None
    vec_ref, acc_ref = refs[-2:]
    drive = drive_ref[...]
    scale = 1.0 / jnp.sqrt(jnp.sum(drive * drive, keepdims=True))
    vec_ref[...] = drive * scale
    product = couple(geo_ref, vec_ref, acc_ref, kept_ref, right_ref, moment_ref, tile)
    image = resist_ref[...] * (drive_own_ref[...] * scale) + coupling * product
    image_ref[...] = image
    spread_rows(spread_ref, image)


def second_kernel(coupling, tile, matrix_ref, drive_ref, image_ref, drive_own_ref, image_own_ref, resist_ref, after_ref,
                  basis_ref, basis_own_ref, stats_ref, known_ref, vec_ref, acc_ref):
    drive = drive_ref[...]
    norm = jnp.sqrt(jnp.sum(drive * drive, keepdims=True))
    scale = 1.0 / norm
    basis_a = drive * scale
    image = image_ref[...]
    hessen_a = jnp.sum(image * basis_a, keepdims=True)
    rest = image - hessen_a * basis_a
    hessen_b = jnp.sqrt(jnp.sum(rest * rest, keepdims=True))
    inverse = 1.0 / hessen_b
    basis_b = rest * inverse
    vec_ref[...] = basis_b
    basis_ref[0:1, :] = basis_a
    basis_ref[1:2, :] = basis_b
    own_a = drive_own_ref[...] * scale
    own_b = (image_own_ref[...] - hessen_a * own_a) * inverse
    basis_own_ref[0:1, :] = own_a
    basis_own_ref[1:2, :] = own_b
    if len(matrix_ref.shape) == 3:
        product = couple(matrix_ref, vec_ref, acc_ref, None, None, None, tile)
    else:
        product = couple_kept(matrix_ref, vec_ref, acc_ref, tile)
    second = resist_ref[...] * own_b + coupling * product
    lane = lax.broadcasted_iota(jnp.int32, (1, 128), 1)

    def three(a, b, c):
        return jnp.where(lane == 0, a, jnp.where(lane == 1, b, jnp.where(lane == 2, c, 0.0)))

    spread_rows(stats_ref, three(
        jnp.sum(second * own_a, keepdims=True),
        jnp.sum(second * own_b, keepdims=True),
        jnp.sum(second * second, keepdims=True),
    ))
    known_ref[...] = three(norm, hessen_a, hessen_b)


def one_hot(slot, base):
    near = jnp.clip(slot - base, -1, PAIR).astype(jnp.bfloat16)
    row = lax.broadcasted_iota(jnp.int32, (PAIR, slot.shape[1]), 0).astype(jnp.bfloat16)
    return jnp.where(row == near, jnp.ones((), jnp.bfloat16), jnp.zeros((), jnp.bfloat16))


def group_kernel(owner_ref, points_ref, slot_ref, table_ref, left_ref, *, n_row, pairs):
    points = owner_ref.shape[1]
    owner = owner_ref[...]
    rows = max(8, n_row)
    names = lax.broadcasted_iota(jnp.int32, (rows, points), 0)
    marks = jnp.where(names == owner, 1.0, 0.0)
    tile = 256
    upper = jnp.where(
        lax.broadcasted_iota(jnp.int32, (tile, tile), 0) <= lax.broadcasted_iota(jnp.int32, (tile, tile), 1), 1.0, 0.0
    ).astype(jnp.bfloat16)
    before = jnp.zeros((rows, 1), jnp.float32)
    ranks = []
    for piece in range(points // tile):
        part = dot(marks[:, piece * tile:(piece + 1) * tile].astype(jnp.bfloat16), upper)
        ranks.append(part + before - 1.0)
        before = before + part[:, tile - 1:tile]
    ranks = jnp.concatenate(ranks, axis=1)
    chunks = jnp.floor((before + (CHUNK - 1)) * (1.0 / CHUNK))
    start = jnp.zeros((1, 1), jnp.float32)
    starts = []
    for name in range(rows):
        starts.append(start)
        start = start + chunks[name:name + 1]
    starts = jnp.concatenate(starts, axis=0)
    slot = jnp.sum(marks * (ranks + starts * CHUNK), axis=0, keepdims=True).astype(jnp.int32)
    slot_ref[...] = slot
    lane = lax.broadcasted_iota(jnp.int32, (rows, 128), 1)
    ended = jnp.sum(jnp.where(starts + chunks <= lane.astype(jnp.float32), 1.0, 0.0), axis=0, keepdims=True)
    info = jnp.where(lane == 0, before, jnp.where(lane == 1, starts, start))
    table_ref[...] = jnp.concatenate([info, jnp.broadcast_to(ended, (8, 128))], axis=0).astype(jnp.int32)
    parts = left_parts(left_center(points_ref[...] - 0.5, EPS_FIELD)).astype(jnp.bfloat16)

    def step(pair, carry):
        at = pl.ds(pl.multiple_of(pair * PAIR, PAIR), PAIR)
        left_ref[at, :] = dot_nt(one_hot(slot, pair * PAIR), parts).astype(jnp.bfloat16)
        return carry

    lax.fori_loop(0, pairs, step, 0)


def cube_halves(left, right):
    inverse = lax.rsqrt(dot(left, right))
    cube = inverse * inverse * inverse
    high = cube.astype(jnp.bfloat16)
    return high, (cube - high.astype(jnp.float32)).astype(jnp.bfloat16)


def weigh_kernel(group_ref, left_ref, right_ref, high_ref, low_ref, done_ref, *, n_row):
    width = right_ref.shape[1] // n_row
    names = group_ref.shape[0] - 8
    done_ref[...] = jnp.zeros_like(done_ref)

    def step(pair, carry):
        for half in range(2):
            chunk = pair * 2 + half
            block = jnp.minimum(group_ref[names, chunk], n_row - 1)
            at = pl.ds(pl.multiple_of(chunk * CHUNK, CHUNK), CHUNK)
            block_at = pl.ds(pl.multiple_of(block * width, width), width)
            high_ref[at, :], low_ref[at, :] = cube_halves(left_ref[at, :], right_ref[:, block_at])
        return carry

    lax.fori_loop(0, (group_ref[0, 2] + 1) // 2, step, 0)


def field_kernel(group_ref, length_ref, slot_ref, moment_ref, basis_ref, *refs, n_row, n_col, kept):
    if kept:
        high_ref, low_ref = refs[0:2]
    else:
        left_ref, right_ref = refs[0:2]
    out_ref, table_ref, sums_ref, acc_ref = refs[2:]
    segments = moment_ref.shape[1]
    width = segments // n_row
    seg_dev = width // n_col
    quarter = width // 4
    scale = 1.0 / math.sqrt(width)
    lane = lax.broadcasted_iota(jnp.int32, (1, seg_dev), 1)
    chunk_lane = lax.broadcasted_iota(jnp.int32, (1, CHUNK), 1)
    names = group_ref.shape[0] - 8
    sums_ref[...] = jnp.zeros_like(sums_ref)

    def table_step(block, carry):
        length = length_ref[block]
        for col in range(n_col):
            vec_at = pl.ds(pl.multiple_of((col * n_row + block) * seg_dev, seg_dev), seg_dev)
            block_at = pl.ds(pl.multiple_of((block * n_col + col) * seg_dev, seg_dev), seg_dev)
            both = moment_ref[:, block_at]
            active = jnp.where(lane + col * seg_dev < length, scale, 0.0)
            first = both * (basis_ref[0:1, vec_at] * active)
            second = both * (basis_ref[1:2, vec_at] * active)
            parts = jnp.concatenate([first, second], axis=0)
            high = parts.astype(jnp.bfloat16).astype(jnp.float32)
            table_ref[:, block_at] = jnp.concatenate([high, parts - high], axis=0).astype(jnp.bfloat16)
        return carry

    lax.fori_loop(0, n_row, table_step, 0)

    def chunk_step(chunk, carry):
        block = jnp.minimum(group_ref[names, chunk], n_row - 1)
        left_over = group_ref[block, 0] - (chunk - group_ref[block, 1]) * CHUNK
        tiles = (length_ref[block] + quarter - 1) // quarter
        at = pl.ds(pl.multiple_of(chunk * CHUNK, CHUNK), CHUNK)
        for size in range(1, 5):
            @pl.when(tiles == size)
            def _():
                used = size * quarter
                block_at = pl.ds(pl.multiple_of(block * width, width), used)
                if kept:
                    high, low = high_ref[at, 0:used], low_ref[at, 0:used]
                else:
                    high, low = cube_halves(left_ref[at, :], right_ref[:, block_at])
                table = table_ref[:, block_at]
                total = (dot_nt(high, table) + dot_nt(low, table)).T
                total = jnp.where(chunk_lane < left_over, total[0:16] + total[16:32], 0.0)
                sums_ref[:, at] = jnp.concatenate(split3(total), axis=0).astype(jnp.bfloat16)
        return carry

    lax.fori_loop(0, group_ref[0, 2], chunk_step, 0)
    acc_ref[...] = jnp.zeros_like(acc_ref)
    slot = slot_ref[...]

    def back_step(pair, carry):
        at = pl.ds(pl.multiple_of(pair * PAIR, PAIR), PAIR)
        acc_ref[...] += dot(sums_ref[:, at], one_hot(slot, pair * PAIR))
        return carry

    lax.fori_loop(0, (group_ref[0, 2] + 1) // 2, back_step, 0)
    out_ref[...] = acc_ref[0:16] + acc_ref[16:32] + acc_ref[32:48]


def final_kernel(stats_ref, known_ref, basis_own_ref, field_ref, points_ref, currents_ref, iron_ref):
    stats = jnp.sum(stats_ref[...], axis=0)
    known = known_ref[...]
    initial_norm, hessen_a, hessen_b = known[:, 0:1], known[:, 1:2], known[:, 2:3]
    hessen_c, hessen_d, normal_second = stats[:, 0:1], stats[:, 1:2], stats[:, 2:3]
    normal_first = hessen_a * hessen_a + hessen_b * hessen_b
    normal_cross = hessen_a * hessen_c + hessen_b * hessen_d
    target_first = initial_norm * hessen_a
    target_second = initial_norm * hessen_c
    determinant = normal_first * normal_second - normal_cross * normal_cross
    weight_first = (normal_second * target_first - normal_cross * target_second) / determinant
    weight_second = (normal_first * target_second - normal_cross * target_first) / determinant
    currents_ref[...] = weight_first * basis_own_ref[0:1, :] + weight_second * basis_own_ref[1:2, :]
    moments = weight_first * field_ref[0:8, :] + weight_second * field_ref[8:16, :]
    points = points_ref[...] - 0.5
    px, py, pz = points[0:1], points[1:2], points[2:3]
    iron_ref[0:1, :] = pz * moments[1:2] - py * moments[2:3] - moments[3:4]
    iron_ref[1:2, :] = px * moments[2:3] - pz * moments[0:1] - moments[4:5]
    iron_ref[2:3, :] = py * moments[0:1] - px * moments[1:2] - moments[5:6]


def shape(*sizes, dtype=jnp.float32):
    return jax.ShapeDtypeStruct(sizes, dtype)


def shards(drive, resist, centers, tangents, iron_points, owner, range_len):
    seg_dev = drive.shape[0]
    col_len = centers.shape[1]
    n_col = lax.axis_size("col")
    n_row = lax.axis_size("row")
    n_dev = n_col * n_row
    segments = seg_dev * n_dev
    points_count = iron_points.shape[1]
    coupling = 0.5 / math.sqrt(segments)
    keep = seg_dev * segments * 4 <= KEEP_BYTES
    tile = 512
    params = pltpu.CompilerParams(vmem_limit_bytes=VMEM_LIMIT)
    call = functools.partial(pl.pallas_call, compiler_params=params)
    scratch = [pltpu.VMEM((1, segments), jnp.float32), pltpu.VMEM((seg_dev, 128), jnp.float32)]
    hbm = pl.BlockSpec(memory_space=pltpu.HBM)
    smem = pl.BlockSpec(memory_space=pltpu.SMEM)
    vmem = pl.BlockSpec(memory_space=pltpu.VMEM)

    def work(microseconds):
        return pl.CostEstimate(flops=int(microseconds * 1e9), bytes_accessed=0, transcendentals=0)

    def exchange(x, axes):
        return lax.all_to_all(x, axes, 0, 0, tiled=True)

    drive_own, resist_own, spread, packed = call(
        entry_kernel,
        out_shape=(shape(1, seg_dev), shape(1, seg_dev), shape(n_dev, 1, seg_dev), shape(n_col, 6, col_len)),
        in_specs=[hbm] * 4,
        scratch_shapes=[
            pltpu.VMEM((3, col_len), jnp.float32),
            pltpu.VMEM((3, col_len), jnp.float32),
            pltpu.SemaphoreType.DMA((4,)),
        ],
        name="entry",
    )(drive[None, :], resist[None, :], centers, tangents)
    drive_all = exchange(spread, AXES).reshape(1, segments)
    geo_all = exchange(packed, "col")

    pairs = (points_count // CHUNK + n_row * (CHUNK - 1) // CHUNK + 1) // 2
    slot, group_table, left = call(
        functools.partial(group_kernel, n_row=n_row, pairs=pairs),
        out_shape=(
            shape(1, points_count, dtype=jnp.int32),
            shape(max(8, n_row) + 8, 128, dtype=jnp.int32),
            shape(pairs * PAIR, 48, dtype=jnp.bfloat16),
        ),
        cost_estimate=work(5),
        name="group_points",
    )(owner.reshape(1, points_count), iron_points)

    first = call(
        functools.partial(first_kernel, coupling, tile, keep),
        out_shape=(
            shape(1, seg_dev), shape(n_dev, 1, seg_dev), shape(48, segments, dtype=jnp.bfloat16), shape(8, segments),
        ) + ((shape(seg_dev, segments),) if keep else ()),
        scratch_shapes=scratch,
        cost_estimate=work(5),
        name="first_image",
    )(geo_all, drive_all, drive_own, resist_own, group_table)
    image_own, image_spread, right, moment = first[0:4]
    image_all = exchange(image_spread, AXES).reshape(1, segments)
    width = n_col * seg_dev
    if keep:
        high, low, after = call(
            functools.partial(weigh_kernel, n_row=n_row),
            out_shape=(
                shape(pairs * PAIR, width, dtype=jnp.bfloat16),
                shape(pairs * PAIR, width, dtype=jnp.bfloat16),
                shape(8, 128),
            ),
            in_specs=[smem, vmem, vmem],
            cost_estimate=work(6),
            name="weigh",
        )(group_table, left, right)
    else:
        high, low, after = left, right, group_table
    basis, basis_own, stats, known = call(
        functools.partial(second_kernel, coupling, tile),
        out_shape=(shape(2, segments), shape(2, seg_dev), shape(n_dev, 1, 128), shape(1, 128)),
        scratch_shapes=scratch,
        cost_estimate=work(2),
        name="second_image",
    )(first[4] if keep else geo_all, drive_all, image_all, drive_own, image_own, resist_own, after)
    stats_all = exchange(stats, AXES)

    field = call(
        functools.partial(field_kernel, n_row=n_row, n_col=n_col, kept=keep),
        out_shape=shape(16, points_count),
        in_specs=[smem, smem, vmem, vmem, vmem, vmem, vmem],
        scratch_shapes=[
            pltpu.VMEM((32, segments), jnp.bfloat16),
            pltpu.VMEM((48, pairs * PAIR), jnp.bfloat16),
            pltpu.VMEM((48, points_count), jnp.float32),
        ],
        cost_estimate=work(6),
        name="block_field",
    )(group_table, range_len, slot, moment, basis, high, low)
    currents, iron_field = call(
        final_kernel,
        out_shape=(shape(1, seg_dev), shape(3, points_count)),
        name="combine",
    )(stats_all, known, basis_own, field, iron_points)
    return (currents[0], iron_field)


def solution(mesh):
    return jax.shard_map(
        shards,
        mesh=mesh,
        in_specs=(
            P(AXES),
            P(AXES),
            P(None, "col"),
            P(None, "col"),
            P(None, AXES),
            P(AXES, None),
            P(),
        ),
        out_specs=(P(AXES), P(None, AXES)),
        check_vma=False,
    )
```

```python
import functools
import math

import jax
import jax.numpy as jnp
from jax import lax
from jax.experimental import pallas as pl
from jax.experimental.pallas import tpu as pltpu
from jax.sharding import PartitionSpec as P

EPS_SEG = 0.0004
EPS_FIELD = 0.0025
AXES = ("col", "row")
CHUNK = 128
GROUP = 4
TILE = 512
KEEP_BYTES = 16 * 1024 * 1024
VMEM_LIMIT = 32 * 1024 * 1024
ENTRY_LIMIT = 60 * 1024 * 1024


def split3(x):
    high = x.astype(jnp.bfloat16).astype(jnp.float32)
    rest = x - high
    middle = rest.astype(jnp.bfloat16).astype(jnp.float32)
    low = (rest - middle).astype(jnp.bfloat16).astype(jnp.float32)
    return high, middle, low


def left_parts(x):
    high, middle, low = split3(x)
    return jnp.concatenate([high, high, middle, middle, high, low], axis=0)


def right_parts(x):
    high, middle, low = split3(x)
    return jnp.concatenate([high, middle, high, middle, low, high], axis=0).astype(jnp.bfloat16)


def rows8(*rows):
    width = rows[0].shape[1]
    count = sum(r.shape[0] for r in rows)
    if count < 8:
        rows = rows + (jnp.zeros((8 - count, width), jnp.float32),)
    return jnp.concatenate(rows, axis=0)


def left_center(c, eps):
    square = jnp.sum(c * c, axis=0, keepdims=True)
    return rows8(-2.0 * c, jnp.ones_like(square), square + eps)


def right_center(c):
    square = jnp.sum(c * c, axis=0, keepdims=True)
    return rows8(c, square, jnp.ones_like(square))


def dot(a, b):
    return jnp.dot(a, b, preferred_element_type=jnp.float32)


def dot_nt(a, b):
    return lax.dot_general(a, b, (((1,), (1,)), ((), ())), preferred_element_type=jnp.float32)


def transposed(x):
    return x.T.astype(jnp.bfloat16)


def fold_lanes(x):
    total = x[:, 0:128]
    for piece in range(1, x.shape[1] // 128):
        total = total + x[:, piece * 128:(piece + 1) * 128]
    return total


def iota(shape, axis):
    return lax.broadcasted_iota(jnp.int32, shape, axis)


def aligned(start, size):
    return pl.ds(pl.multiple_of(start, size), size)


def piece_column(shift, n_col):
    return lax.rem(lax.axis_index("col") + n_col - shift, n_col)


def couple(pieces, vec_ref, acc_ref, kept=None, right_ref=None, moment_ref=None):
    seg_dev = acc_ref.shape[0]
    n_col = len(pieces)
    length = pieces[0].shape[1]
    own = pieces[0][:, aligned(lax.axis_index("row") * seg_dev, seg_dev)]
    lc = transposed(left_parts(left_center(own[0:3] - 0.5, EPS_SEG)))
    lt = transposed(left_parts(rows8(own[3:6])))
    acc_ref[...] = jnp.zeros_like(acc_ref)
    count = length // TILE
    for shift, piece in enumerate(pieces):
        col = piece_column(shift, n_col)

        def step(k, carry):
            geo = piece[:, aligned(k * TILE, TILE)]
            vec_at = pl.ds(pl.multiple_of(col * length + k * TILE, TILE), TILE)
            center, tangent = geo[0:3] - 0.5, geo[3:6]
            rc = right_parts(right_center(center))
            rt = right_parts(rows8(tangent))
            pair = dot(lt, rt) * lax.rsqrt(dot(lc, rc))
            if kept is not None:
                kept[0][shift * count + k] = pair
                kept_copy(kept, shift * count + k, out=True).start()
            if right_ref is not None:
                cross = jnp.concatenate([
                    tangent[1:2] * center[2:3] - tangent[2:3] * center[1:2],
                    tangent[2:3] * center[0:1] - tangent[0:1] * center[2:3],
                    tangent[0:1] * center[1:2] - tangent[1:2] * center[0:1],
                ], axis=0)
                both = rows8(tangent, cross)
                for part in range(TILE // seg_dev):
                    row = k * (TILE // seg_dev) + part
                    block_at = aligned((row * n_col + col) * seg_dev, seg_dev)
                    right_ref[:, block_at] = rc[:, part * seg_dev:(part + 1) * seg_dev]
                    moment_ref[:, block_at] = both[:, part * seg_dev:(part + 1) * seg_dev]
            acc_ref[...] += fold_lanes(pair * vec_ref[:, vec_at])
            return carry

        lax.fori_loop(0, count, step, 0, unroll=4)
    return jnp.sum(acc_ref[...].T, axis=0, keepdims=True)


def kept_copy(kept, index, out):
    local, remote, sems = kept
    if out:
        return pltpu.make_async_copy(local.at[index], remote.at[index], sems.at[index])
    return pltpu.make_async_copy(remote.at[index], local.at[index], sems.at[index])


def couple_kept(kept, vec_ref, acc_ref, n_col):
    acc_ref[...] = jnp.zeros_like(acc_ref)
    length = vec_ref.shape[1] // n_col
    count = length // TILE
    for shift in range(n_col):
        col = piece_column(shift, n_col)

        def step(k, carry):
            kept_copy(kept, shift * count + k, out=False).wait()
            vec_at = pl.ds(pl.multiple_of(col * length + k * TILE, TILE), TILE)
            acc_ref[...] += fold_lanes(kept[0][shift * count + k] * vec_ref[:, vec_at])
            return carry

        lax.fori_loop(0, count, step, 0, unroll=2)
    return jnp.sum(acc_ref[...].T, axis=0, keepdims=True)


def spread_rows(ref, row):
    for k in range(ref.shape[0]):
        ref[k] = row


def entry_kernel(*refs):
    sources = refs[0:6]
    drive_ref, resist_ref, owner_ref, points_ref, spread_ref, geo_ref, centers, tangents, sems = refs[6:]
    targets = (drive_ref, resist_ref, centers, tangents, owner_ref, points_ref)
    copies = [pltpu.make_async_copy(sources[k], targets[k], sems.at[k]) for k in range(6)]
    for copy in copies:
        copy.start()
    for copy in copies:
        copy.wait()
    spread_rows(spread_ref, drive_ref[...])
    geo_ref[0:3] = centers[...]
    geo_ref[3:6] = tangents[...]


def first_kernel(coupling, n_col, keep, drive_ref, drive_own_ref, resist_ref, after_ref, *refs):
    pieces, refs = refs[:n_col], refs[n_col:]
    image_ref, spread_ref, right_ref, moment_ref = refs[0:4]
    kept = None
    if keep:
        kept_hbm = refs[4]
        vec_ref, acc_ref, kept_ref, sems = refs[5:]
        kept = (kept_ref, kept_hbm, sems)
    else:
        vec_ref, acc_ref = refs[4:]
    drive = drive_ref[...]
    scale = 1.0 / jnp.sqrt(jnp.sum(drive * drive, keepdims=True))
    vec_ref[...] = drive * scale
    product = couple(pieces, vec_ref, acc_ref, kept, right_ref, moment_ref)
    image = resist_ref[...] * (drive_own_ref[...] * scale) + coupling * product
    image_ref[...] = image
    spread_rows(spread_ref, image)
    if keep:
        for index in range(kept_ref.shape[0]):
            kept_copy(kept, index, out=True).wait()


def second_kernel(coupling, n_col, keep, drive_ref, image_ref, drive_own_ref, image_own_ref, resist_ref, after_ref, *refs):
    if keep:
        kept_hbm, refs = refs[0], refs[1:]
        vec_ref, acc_ref, kept_ref, sems = refs[4:]
        kept = (kept_ref, kept_hbm, sems)
        for index in range(kept_ref.shape[0]):
            kept_copy(kept, index, out=False).start()
    else:
        pieces, refs = refs[:n_col], refs[n_col:]
        vec_ref, acc_ref = refs[4:]
    basis_ref, basis_own_ref, stats_ref, known_ref = refs[0:4]
    drive = drive_ref[...]
    norm = jnp.sqrt(jnp.sum(drive * drive, keepdims=True))
    scale = 1.0 / norm
    basis_a = drive * scale
    image = image_ref[...]
    hessen_a = jnp.sum(image * basis_a, keepdims=True)
    rest = image - hessen_a * basis_a
    hessen_b = jnp.sqrt(jnp.sum(rest * rest, keepdims=True))
    inverse = 1.0 / hessen_b
    basis_b = rest * inverse
    vec_ref[...] = basis_b
    basis_ref[0:1, :] = basis_a
    basis_ref[1:2, :] = basis_b
    own_a = drive_own_ref[...] * scale
    own_b = (image_own_ref[...] - hessen_a * own_a) * inverse
    basis_own_ref[0:1, :] = own_a
    basis_own_ref[1:2, :] = own_b
    if keep:
        product = couple_kept(kept, vec_ref, acc_ref, n_col)
    else:
        product = couple(pieces, vec_ref, acc_ref)
    second = resist_ref[...] * own_b + coupling * product
    lane = iota((1, 128), 1)

    def three(a, b, c):
        return jnp.where(lane == 0, a, jnp.where(lane == 1, b, jnp.where(lane == 2, c, 0.0)))

    spread_rows(stats_ref, three(
        jnp.sum(second * own_a, keepdims=True),
        jnp.sum(second * own_b, keepdims=True),
        jnp.sum(second * second, keepdims=True),
    ))
    known_ref[...] = three(norm, hessen_a, hessen_b)


def group_kernel(owner_ref, points_ref, slot_ref, table_ref, left_ref, planes_ref, *, n_row):
    points = owner_ref.shape[1]
    chunk_count = left_ref.shape[0] // CHUNK
    owner = owner_ref[...]
    rows = max(8, n_row)
    marks = jnp.where(iota((rows, points), 0) == owner, 1.0, 0.0)
    tile = 256
    upper = jnp.where(iota((tile, tile), 0) <= iota((tile, tile), 1), 1.0, 0.0).astype(jnp.bfloat16)
    before = jnp.zeros((rows, 1), jnp.float32)
    ranks = []
    for piece in range(points // tile):
        part = dot(marks[:, piece * tile:(piece + 1) * tile].astype(jnp.bfloat16), upper)
        ranks.append(part + before - 1.0)
        before = before + part[:, tile - 1:tile]
    ranks = jnp.concatenate(ranks, axis=1)
    chunks = jnp.floor((before + (CHUNK - 1)) * (1.0 / CHUNK))
    start = jnp.zeros((1, 1), jnp.float32)
    starts = []
    for name in range(rows):
        starts.append(start)
        start = start + chunks[name:name + 1]
    starts = jnp.concatenate(starts, axis=0)
    slot = jnp.sum(marks * (ranks + starts * CHUNK), axis=0, keepdims=True).astype(jnp.int32)
    slot_ref[...] = slot
    lane = iota((rows, 128), 1)
    ended = jnp.sum(jnp.where(starts + chunks <= lane.astype(jnp.float32), 1.0, 0.0), axis=0, keepdims=True)
    block = jnp.minimum(ended, n_row - 1.0)
    place = iota((8, 128), 0)
    table_ref[...] = jnp.where(place == 0, block, start).astype(jnp.int32)
    high = jnp.where(iota((chunk_count, points), 0) == slot // CHUNK, 1.0, 0.0)
    low = jnp.where(iota((CHUNK, points), 0) == slot % CHUNK, 1.0, 0.0).astype(jnp.bfloat16)
    parts = split3(points_ref[...] - 0.5)
    spread = jnp.concatenate([high * part[k:k + 1] for k in range(3) for part in parts], axis=0).astype(jnp.bfloat16)
    placed = dot_nt(spread, low)
    planes = [placed[k * chunk_count:(k + 1) * chunk_count] for k in range(9)]
    x, y, z = (planes[3 * k] + planes[3 * k + 1] + planes[3 * k + 2] for k in range(3))
    sides = [-2.0 * x, -2.0 * y, -2.0 * z, jnp.ones_like(x), x * x + y * y + z * z + EPS_FIELD]
    sides = [split3(side) for side in sides]
    empty = jnp.zeros_like(x)
    for group, part in enumerate([0, 0, 1, 1, 0, 2]):
        for k in range(8):
            to = pl.ds((group * 8 + k) * chunk_count, chunk_count)
            planes_ref[to, :] = sides[k][part] if k < 5 else empty
    for chunk in range(chunk_count):
        left_ref[chunk * CHUNK:(chunk + 1) * CHUNK, :] = transposed(planes_ref[pl.ds(chunk, 48, stride=chunk_count), :])


def cube_halves(left, right):
    inverse = lax.rsqrt(dot(left, right))
    cube = inverse * inverse * inverse
    high = cube.astype(jnp.bfloat16)
    return high, (cube - high.astype(jnp.float32)).astype(jnp.bfloat16)


def weigh_kernel(group_ref, left_ref, right_ref, cubes_hbm, done_ref, cubes_ref, sems, *, n_row):
    width = right_ref.shape[1] // n_row
    done_ref[...] = jnp.zeros_like(done_ref)
    kept = (cubes_ref, cubes_hbm, sems)
    steps = (group_ref[1, 0] + GROUP - 1) // GROUP

    def step(k, carry):
        for part in range(GROUP):
            chunk = k * GROUP + part
            block_at = aligned(group_ref[0, chunk] * width, width)
            high, low = cube_halves(left_ref[aligned(chunk * CHUNK, CHUNK), :], right_ref[:, block_at])
            cubes_ref[chunk, 0:CHUNK] = high
            cubes_ref[chunk, CHUNK:2 * CHUNK] = low
            kept_copy(kept, chunk, out=True).start()
        return carry

    def finish(k, carry):
        for part in range(GROUP):
            kept_copy(kept, k * GROUP + part, out=True).wait()
        return carry

    lax.fori_loop(0, steps, step, 0)
    lax.fori_loop(0, steps, finish, 0)


def field_kernel(group_ref, length_ref, slot_ref, moment_ref, basis_ref, *refs, n_row, n_col, keep):
    chunk_count = refs[-1].shape[0] // 16 if not keep else refs[-3].shape[0] // 16
    steps = (group_ref[1, 0] + GROUP - 1) // GROUP
    if keep:
        cubes_hbm, out_ref, table_ref, sums_ref, cubes_ref, sems = refs
        kept = (cubes_ref, cubes_hbm, sems)

        def begin(k, carry):
            for part in range(GROUP):
                kept_copy(kept, k * GROUP + part, out=False).start()
            return carry

        lax.fori_loop(0, steps, begin, 0)
    else:
        left_ref, right_ref, out_ref, table_ref, sums_ref = refs
    segments = moment_ref.shape[1]
    width = segments // n_row
    seg_dev = width // n_col
    scale = 1.0 / math.sqrt(width)
    lane = iota((1, seg_dev), 1)
    sums_ref[...] = jnp.zeros_like(sums_ref)

    def table_step(block, carry):
        length = length_ref[block]
        for col in range(n_col):
            vec_at = aligned((col * n_row + block) * seg_dev, seg_dev)
            block_at = aligned((block * n_col + col) * seg_dev, seg_dev)
            both = moment_ref[:, block_at]
            active = jnp.where(lane + col * seg_dev < length, scale, 0.0)
            first = both * (basis_ref[0:1, vec_at] * active)
            second = both * (basis_ref[1:2, vec_at] * active)
            parts = jnp.concatenate([first, second], axis=0)
            high = parts.astype(jnp.bfloat16).astype(jnp.float32)
            table_ref[:, block_at] = jnp.concatenate([high, parts - high], axis=0).astype(jnp.bfloat16)
        return carry

    lax.fori_loop(0, n_row, table_step, 0, unroll=2)

    def step(k, carry):
        for part in range(GROUP):
            chunk = k * GROUP + part
            block_at = aligned(group_ref[0, chunk] * width, width)
            if keep:
                kept_copy(kept, chunk, out=False).wait()
                cubes = cubes_ref[chunk]
            else:
                high, low = cube_halves(left_ref[aligned(chunk * CHUNK, CHUNK), :], right_ref[:, block_at])
                cubes = jnp.concatenate([high, low], axis=0)
            both = dot_nt(cubes, table_ref[:, block_at])
            total = (both[0:CHUNK] + both[CHUNK:2 * CHUNK]).T
            sums_ref[pl.ds(chunk, 16, stride=chunk_count), :] = total[0:16] + total[16:32]
        return carry

    lax.fori_loop(0, steps, step, 0)
    sums = jnp.concatenate([sums_ref[0:6 * chunk_count], sums_ref[8 * chunk_count:14 * chunk_count]], axis=0)
    sums = jnp.concatenate(split3(sums), axis=1).astype(jnp.bfloat16)
    for tile in range(slot_ref.shape[1] // TILE):
        at = pl.ds(tile * TILE, TILE)
        slot = slot_ref[:, at]
        low = jnp.where(iota((CHUNK, TILE), 0) == slot % CHUNK, 1.0, 0.0).astype(jnp.bfloat16)
        high = jnp.where(iota((chunk_count, TILE), 0) == slot // CHUNK, 1.0, 0.0)
        found = dot(sums, jnp.concatenate([low, low, low], axis=0))
        for row in range(12):
            picked = found[row * chunk_count:(row + 1) * chunk_count] * high
            out_ref[row:row + 1, at] = jnp.sum(picked, axis=0, keepdims=True)


def final_kernel(stats_ref, known_ref, basis_own_ref, field_ref, points_ref, currents_ref, iron_ref):
    stats = jnp.sum(stats_ref[...], axis=0)
    known = known_ref[...]
    initial_norm, hessen_a, hessen_b = known[:, 0:1], known[:, 1:2], known[:, 2:3]
    hessen_c, hessen_d, normal_second = stats[:, 0:1], stats[:, 1:2], stats[:, 2:3]
    normal_first = hessen_a * hessen_a + hessen_b * hessen_b
    normal_cross = hessen_a * hessen_c + hessen_b * hessen_d
    target_first = initial_norm * hessen_a
    target_second = initial_norm * hessen_c
    determinant = normal_first * normal_second - normal_cross * normal_cross
    weight_first = (normal_second * target_first - normal_cross * target_second) / determinant
    weight_second = (normal_first * target_second - normal_cross * target_first) / determinant
    currents_ref[...] = weight_first * basis_own_ref[0:1, :] + weight_second * basis_own_ref[1:2, :]
    moments = weight_first * field_ref[0:6, :] + weight_second * field_ref[6:12, :]
    points = points_ref[...] - 0.5
    px, py, pz = points[0:1], points[1:2], points[2:3]
    iron_ref[0:1, :] = pz * moments[1:2] - py * moments[2:3] - moments[3:4]
    iron_ref[1:2, :] = px * moments[2:3] - pz * moments[0:1] - moments[4:5]
    iron_ref[2:3, :] = py * moments[0:1] - px * moments[1:2] - moments[5:6]


def shape(*sizes, dtype=jnp.float32):
    return jax.ShapeDtypeStruct(sizes, dtype)


def shards(drive, resist, centers, tangents, iron_points, owner, range_len):
    seg_dev = drive.shape[0]
    col_len = centers.shape[1]
    n_col = lax.axis_size("col")
    n_row = lax.axis_size("row")
    n_dev = n_col * n_row
    segments = seg_dev * n_dev
    width = n_col * seg_dev
    points_count = iron_points.shape[1]
    coupling = 0.5 / math.sqrt(segments)
    keep = seg_dev * segments * 4 <= KEEP_BYTES
    tiles = segments // TILE
    call = functools.partial(pl.pallas_call, compiler_params=pltpu.CompilerParams(vmem_limit_bytes=VMEM_LIMIT))
    scratch = [pltpu.VMEM((1, segments), jnp.float32), pltpu.VMEM((seg_dev, 128), jnp.float32)]
    if keep:
        scratch += [pltpu.VMEM((tiles, seg_dev, TILE), jnp.float32), pltpu.SemaphoreType.DMA((tiles,))]
    hbm = pl.BlockSpec(memory_space=pltpu.HBM)
    smem = pl.BlockSpec(memory_space=pltpu.SMEM)
    vmem = pl.BlockSpec(memory_space=pltpu.VMEM)

    def work(microseconds):
        return pl.CostEstimate(flops=int(microseconds * 1e9), bytes_accessed=0, transcendentals=0)

    def exchange(x):
        return lax.all_to_all(x, AXES, 0, 0, tiled=True)

    drive_own, resist_own, owners, points, spread, geometry = pl.pallas_call(
        entry_kernel,
        out_shape=(
            shape(1, seg_dev), shape(1, seg_dev), shape(1, points_count, dtype=jnp.int32), shape(3, points_count),
            shape(n_dev, 1, seg_dev), shape(6, col_len),
        ),
        in_specs=[hbm] * 6,
        scratch_shapes=[
            pltpu.VMEM((3, col_len), jnp.float32),
            pltpu.VMEM((3, col_len), jnp.float32),
            pltpu.SemaphoreType.DMA((6,)),
        ],
        compiler_params=pltpu.CompilerParams(vmem_limit_bytes=ENTRY_LIMIT),
        name="entry",
    )(drive[None, :], resist[None, :], centers, tangents, owner.reshape(1, points_count), iron_points)
    drive_all = exchange(spread).reshape(1, segments)
    pieces = [geometry] + [
        lax.ppermute(geometry, "col", [(k, (k + shift) % n_col) for k in range(n_col)]) for shift in range(1, n_col)
    ]

    chunk_count = points_count // CHUNK + n_row * (CHUNK - 1) // CHUNK
    chunk_count = -(-chunk_count // 8) * 8
    slot, group_table, left = call(
        functools.partial(group_kernel, n_row=n_row),
        out_shape=(
            shape(1, points_count, dtype=jnp.int32),
            shape(8, 128, dtype=jnp.int32),
            shape(chunk_count * CHUNK, 48, dtype=jnp.bfloat16),
        ),
        scratch_shapes=[pltpu.VMEM((48 * chunk_count, CHUNK), jnp.float32)],
        cost_estimate=work(3),
        name="group_points",
    )(owners, points)

    first = call(
        functools.partial(first_kernel, coupling, n_col, keep),
        out_shape=(
            shape(1, seg_dev), shape(n_dev, 1, seg_dev), shape(48, segments, dtype=jnp.bfloat16), shape(8, segments),
        ) + ((shape(tiles, seg_dev, TILE),) if keep else ()),
        out_specs=(vmem,) * 4 + ((hbm,) if keep else ()),
        scratch_shapes=scratch,
        cost_estimate=work(5),
        name="first_image",
    )(drive_all, drive_own, resist_own, group_table, *pieces)
    image_own, image_spread, right, moment = first[0:4]
    image_all = exchange(image_spread).reshape(1, segments)
    cube_shape = (chunk_count, 2 * CHUNK, width)
    cube_scratch = [pltpu.VMEM(cube_shape, jnp.bfloat16), pltpu.SemaphoreType.DMA((chunk_count,))]
    if keep:
        cubes, after = call(
            functools.partial(weigh_kernel, n_row=n_row),
            out_shape=(shape(*cube_shape, dtype=jnp.bfloat16), shape(8, 128)),
            in_specs=[smem, vmem, vmem],
            out_specs=(hbm, vmem),
            scratch_shapes=cube_scratch,
            cost_estimate=work(5),
            name="weigh",
        )(group_table, left, right)
    else:
        after = group_table
    basis, basis_own, stats, known = call(
        functools.partial(second_kernel, coupling, n_col, keep),
        out_shape=(shape(2, segments), shape(2, seg_dev), shape(n_dev, 1, 128), shape(1, 128)),
        in_specs=[vmem] * 6 + ([hbm] if keep else [vmem] * n_col),
        scratch_shapes=scratch,
        cost_estimate=work(2),
        name="second_image",
    )(drive_all, image_all, drive_own, image_own, resist_own, after, *(first[4:5] if keep else pieces))
    stats_all = exchange(stats)

    field = call(
        functools.partial(field_kernel, n_row=n_row, n_col=n_col, keep=keep),
        out_shape=shape(12, points_count),
        in_specs=[smem, smem, vmem, vmem, vmem] + ([hbm] if keep else [vmem, vmem]),
        scratch_shapes=[
            pltpu.VMEM((32, segments), jnp.bfloat16),
            pltpu.VMEM((16 * chunk_count, CHUNK), jnp.float32),
        ] + (cube_scratch if keep else []),
        cost_estimate=work(6),
        name="block_field",
    )(group_table, range_len, slot, moment, basis, *([cubes] if keep else [left, right]))
    currents, iron_field = call(
        final_kernel,
        out_shape=(shape(1, seg_dev), shape(3, points_count)),
        name="combine",
    )(stats_all, known, basis_own, field, points)
    return (currents[0], iron_field)


def solution(mesh):
    return jax.shard_map(
        shards,
        mesh=mesh,
        in_specs=(
            P(AXES),
            P(AXES),
            P(None, "col"),
            P(None, "col"),
            P(None, AXES),
            P(AXES, None),
            P(),
        ),
        out_specs=(P(AXES), P(None, AXES)),
        check_vma=False,
    )
```

```python
import functools
import math

import jax
import jax.numpy as jnp
from jax import lax
from jax.experimental import pallas as pl
from jax.experimental.pallas import tpu as pltpu
from jax.sharding import PartitionSpec as P

EPS_SEG = 0.0004
EPS_FIELD = 0.0025
AXES = ("col", "row")
CHUNK = 128
GROUP = 4
TILE = 512
KEEP_BYTES = 16 * 1024 * 1024
VMEM_LIMIT = 32 * 1024 * 1024
STREAM_LIMIT = 44 * 1024 * 1024
STREAM_BYTES = 20 * 1024 * 1024
ENTRY_LIMIT = 60 * 1024 * 1024


def split3(x):
    high = x.astype(jnp.bfloat16).astype(jnp.float32)
    rest = x - high
    middle = rest.astype(jnp.bfloat16).astype(jnp.float32)
    low = (rest - middle).astype(jnp.bfloat16).astype(jnp.float32)
    return high, middle, low


def left_parts(x):
    high, middle, low = split3(x)
    return jnp.concatenate([high, high, middle, middle, high, low], axis=0)


def right_parts(x):
    high, middle, low = split3(x)
    return jnp.concatenate([high, middle, high, middle, low, high], axis=0).astype(jnp.bfloat16)


def rows8(*rows):
    width = rows[0].shape[1]
    count = sum(r.shape[0] for r in rows)
    if count < 8:
        rows = rows + (jnp.zeros((8 - count, width), jnp.float32),)
    return jnp.concatenate(rows, axis=0)


def left_center(c, eps):
    square = jnp.sum(c * c, axis=0, keepdims=True)
    return rows8(-2.0 * c, jnp.ones_like(square), square + eps)


def right_center(c):
    square = jnp.sum(c * c, axis=0, keepdims=True)
    return rows8(c, square, jnp.ones_like(square))


def dot(a, b):
    return jnp.dot(a, b, preferred_element_type=jnp.float32)


def dot_nt(a, b):
    return lax.dot_general(a, b, (((1,), (1,)), ((), ())), preferred_element_type=jnp.float32)


def transposed(x):
    return x.T.astype(jnp.bfloat16)


def fold_lanes(x):
    total = x[:, 0:128]
    for piece in range(1, x.shape[1] // 128):
        total = total + x[:, piece * 128:(piece + 1) * 128]
    return total


def iota(shape, axis):
    return lax.broadcasted_iota(jnp.int32, shape, axis)


def aligned(start, size):
    return pl.ds(pl.multiple_of(start, size), size)


def piece_column(shift, n_col):
    return lax.rem(lax.axis_index("col") + n_col - shift, n_col)


def couple(pieces, vec_ref, acc_ref, kept=None, right_ref=None, moment_ref=None):
    seg_dev = acc_ref.shape[0]
    n_col = len(pieces)
    length = pieces[0].shape[1]
    own = pieces[0][:, aligned(lax.axis_index("row") * seg_dev, seg_dev)]
    lc = transposed(left_parts(left_center(own[0:3] - 0.5, EPS_SEG)))
    lt = transposed(left_parts(rows8(own[3:6])))
    acc_ref[...] = jnp.zeros_like(acc_ref)
    count = length // TILE
    for shift, piece in enumerate(pieces):
        col = piece_column(shift, n_col)

        def step(k, carry):
            geo = piece[:, aligned(k * TILE, TILE)]
            vec_at = pl.ds(pl.multiple_of(col * length + k * TILE, TILE), TILE)
            center, tangent = geo[0:3] - 0.5, geo[3:6]
            rc = right_parts(right_center(center))
            rt = right_parts(rows8(tangent))
            pair = dot(lt, rt) * lax.rsqrt(dot(lc, rc))
            if kept is not None:
                kept[0][shift * count + k] = pair
                kept_copy(kept, shift * count + k, out=True).start()
            if right_ref is not None:
                cross = jnp.concatenate([
                    tangent[1:2] * center[2:3] - tangent[2:3] * center[1:2],
                    tangent[2:3] * center[0:1] - tangent[0:1] * center[2:3],
                    tangent[0:1] * center[1:2] - tangent[1:2] * center[0:1],
                ], axis=0)
                both = rows8(tangent, cross)
                for part in range(TILE // seg_dev):
                    row = k * (TILE // seg_dev) + part
                    block_at = aligned((row * n_col + col) * seg_dev, seg_dev)
                    right_ref[:, block_at] = rc[:, part * seg_dev:(part + 1) * seg_dev]
                    moment_ref[:, block_at] = both[:, part * seg_dev:(part + 1) * seg_dev]
            acc_ref[...] += fold_lanes(pair * vec_ref[:, vec_at])
            return carry

        lax.fori_loop(0, count, step, 0, unroll=4)
    return jnp.sum(acc_ref[...].T, axis=0, keepdims=True)


def kept_copy(kept, index, out):
    local, remote, sems = kept
    if out:
        return pltpu.make_async_copy(local.at[index], remote.at[index], sems.at[index])
    return pltpu.make_async_copy(remote.at[index], local.at[index], sems.at[index])


def couple_kept(kept, vec_ref, acc_ref, n_col):
    acc_ref[...] = jnp.zeros_like(acc_ref)
    length = vec_ref.shape[1] // n_col
    count = length // TILE
    for shift in range(n_col):
        col = piece_column(shift, n_col)

        def step(k, carry):
            kept_copy(kept, shift * count + k, out=False).wait()
            vec_at = pl.ds(pl.multiple_of(col * length + k * TILE, TILE), TILE)
            acc_ref[...] += fold_lanes(kept[0][shift * count + k] * vec_ref[:, vec_at])
            return carry

        lax.fori_loop(0, count, step, 0, unroll=2)
    return jnp.sum(acc_ref[...].T, axis=0, keepdims=True)


def spread_rows(ref, row):
    for k in range(ref.shape[0]):
        ref[k] = row


def entry_kernel(drive_hbm, centers_hbm, tangents_hbm, spread_ref, geo_ref, drive_ref, centers, tangents, sems):
    pairs = ((drive_hbm, drive_ref), (centers_hbm, centers), (tangents_hbm, tangents))
    copies = [pltpu.make_async_copy(source, target, sems.at[k]) for k, (source, target) in enumerate(pairs)]
    for copy in copies:
        copy.start()
    for copy in copies:
        copy.wait()
    spread_rows(spread_ref, drive_ref[...])
    geo_ref[0:3] = centers[...]
    geo_ref[3:6] = tangents[...]


def first_kernel(coupling, n_col, keep, drive_ref, drive_own_ref, resist_ref, after_ref, *refs):
    pieces, refs = refs[:n_col], refs[n_col:]
    image_ref, spread_ref, right_ref, moment_ref = refs[0:4]
    kept = None
    if keep:
        kept_hbm = refs[4]
        vec_ref, acc_ref, kept_ref, sems = refs[5:]
        kept = (kept_ref, kept_hbm, sems)
    else:
        vec_ref, acc_ref = refs[4:]
    drive = drive_ref[...]
    scale = 1.0 / jnp.sqrt(jnp.sum(drive * drive, keepdims=True))
    vec_ref[...] = drive * scale
    product = couple(pieces, vec_ref, acc_ref, kept, right_ref, moment_ref)
    image = resist_ref[...] * (drive_own_ref[...] * scale) + coupling * product
    image_ref[...] = image
    spread_rows(spread_ref, image)
    if keep:
        for index in range(kept_ref.shape[0]):
            kept_copy(kept, index, out=True).wait()


def second_kernel(coupling, n_col, keep, drive_ref, image_ref, drive_own_ref, image_own_ref, resist_ref, after_ref, *refs):
    if keep:
        kept_hbm, refs = refs[0], refs[1:]
        vec_ref, acc_ref, kept_ref, sems = refs[4:]
        kept = (kept_ref, kept_hbm, sems)
        for index in range(kept_ref.shape[0]):
            kept_copy(kept, index, out=False).start()
    else:
        pieces, refs = refs[:n_col], refs[n_col:]
        vec_ref, acc_ref = refs[4:]
    basis_ref, basis_own_ref, stats_ref, known_ref = refs[0:4]
    drive = drive_ref[...]
    norm = jnp.sqrt(jnp.sum(drive * drive, keepdims=True))
    scale = 1.0 / norm
    basis_a = drive * scale
    image = image_ref[...]
    hessen_a = jnp.sum(image * basis_a, keepdims=True)
    rest = image - hessen_a * basis_a
    hessen_b = jnp.sqrt(jnp.sum(rest * rest, keepdims=True))
    inverse = 1.0 / hessen_b
    basis_b = rest * inverse
    vec_ref[...] = basis_b
    basis_ref[0:1, :] = basis_a
    basis_ref[1:2, :] = basis_b
    own_a = drive_own_ref[...] * scale
    own_b = (image_own_ref[...] - hessen_a * own_a) * inverse
    basis_own_ref[0:1, :] = own_a
    basis_own_ref[1:2, :] = own_b
    if keep:
        product = couple_kept(kept, vec_ref, acc_ref, n_col)
    else:
        product = couple(pieces, vec_ref, acc_ref)
    second = resist_ref[...] * own_b + coupling * product
    lane = iota((1, 128), 1)

    def three(a, b, c):
        return jnp.where(lane == 0, a, jnp.where(lane == 1, b, jnp.where(lane == 2, c, 0.0)))

    spread_rows(stats_ref, three(
        jnp.sum(second * own_a, keepdims=True),
        jnp.sum(second * own_b, keepdims=True),
        jnp.sum(second * second, keepdims=True),
    ))
    known_ref[...] = three(norm, hessen_a, hessen_b)


def group_kernel(owner_ref, points_ref, drive_in_ref, resist_in_ref, centers_in_ref, tangents_in_ref,
                 slot_ref, table_ref, left_ref, drive_ref, resist_ref, geo_ref, planes_ref, *, n_row):
    drive_ref[...] = drive_in_ref[...]
    resist_ref[...] = resist_in_ref[...]
    geo_ref[0:3] = centers_in_ref[...]
    geo_ref[3:6] = tangents_in_ref[...]
    points = owner_ref.shape[1]
    chunk_count = left_ref.shape[0] // CHUNK
    owner = owner_ref[...]
    rows = max(8, n_row)
    marks = jnp.where(iota((rows, points), 0) == owner, 1.0, 0.0)
    tile = 256
    upper = jnp.where(iota((tile, tile), 0) <= iota((tile, tile), 1), 1.0, 0.0).astype(jnp.bfloat16)
    before = jnp.zeros((rows, 1), jnp.float32)
    ranks = []
    for piece in range(points // tile):
        part = dot(marks[:, piece * tile:(piece + 1) * tile].astype(jnp.bfloat16), upper)
        ranks.append(part + before - 1.0)
        before = before + part[:, tile - 1:tile]
    ranks = jnp.concatenate(ranks, axis=1)
    chunks = jnp.floor((before + (CHUNK - 1)) * (1.0 / CHUNK))
    start = jnp.zeros((1, 1), jnp.float32)
    starts = []
    for name in range(rows):
        starts.append(start)
        start = start + chunks[name:name + 1]
    starts = jnp.concatenate(starts, axis=0)
    slot = jnp.sum(marks * (ranks + starts * CHUNK), axis=0, keepdims=True).astype(jnp.int32)
    slot_ref[...] = slot
    lane = iota((rows, 128), 1)
    ended = jnp.sum(jnp.where(starts + chunks <= lane.astype(jnp.float32), 1.0, 0.0), axis=0, keepdims=True)
    block = jnp.minimum(ended, n_row - 1.0)
    place = iota((8, 128), 0)
    table_ref[...] = jnp.where(place == 0, block, start).astype(jnp.int32)
    high = jnp.where(iota((chunk_count, points), 0) == slot // CHUNK, 1.0, 0.0)
    low = jnp.where(iota((CHUNK, points), 0) == slot % CHUNK, 1.0, 0.0).astype(jnp.bfloat16)
    parts = split3(points_ref[...] - 0.5)
    spread = jnp.concatenate([high * part[k:k + 1] for k in range(3) for part in parts], axis=0).astype(jnp.bfloat16)
    placed = dot_nt(spread, low)
    planes = [placed[k * chunk_count:(k + 1) * chunk_count] for k in range(9)]
    x, y, z = (planes[3 * k] + planes[3 * k + 1] + planes[3 * k + 2] for k in range(3))
    sides = [-2.0 * x, -2.0 * y, -2.0 * z, jnp.ones_like(x), x * x + y * y + z * z + EPS_FIELD]
    sides = [split3(side) for side in sides]
    empty = jnp.zeros_like(x)
    for group, part in enumerate([0, 0, 1, 1, 0, 2]):
        for k in range(8):
            to = pl.ds((group * 8 + k) * chunk_count, chunk_count)
            planes_ref[to, :] = sides[k][part] if k < 5 else empty
    for chunk in range(chunk_count):
        left_ref[chunk * CHUNK:(chunk + 1) * CHUNK, :] = transposed(planes_ref[pl.ds(chunk, 48, stride=chunk_count), :])


def cube_halves(left, right):
    inverse = lax.rsqrt(dot(left, right))
    cube = inverse * inverse * inverse
    high = cube.astype(jnp.bfloat16)
    return high, (cube - high.astype(jnp.float32)).astype(jnp.bfloat16)


def weigh_kernel(group_ref, left_ref, right_ref, cubes_hbm, done_ref, cubes_ref, sems, *, n_row):
    width = right_ref.shape[1] // n_row
    done_ref[...] = jnp.zeros_like(done_ref)
    kept = (cubes_ref, cubes_hbm, sems)
    steps = (group_ref[1, 0] + GROUP - 1) // GROUP

    def step(k, carry):
        for part in range(GROUP):
            chunk = k * GROUP + part
            block_at = aligned(group_ref[0, chunk] * width, width)
            high, low = cube_halves(left_ref[aligned(chunk * CHUNK, CHUNK), :], right_ref[:, block_at])
            cubes_ref[chunk, 0:CHUNK] = high
            cubes_ref[chunk, CHUNK:2 * CHUNK] = low
            kept_copy(kept, chunk, out=True).start()
        return carry

    def finish(k, carry):
        for part in range(GROUP):
            kept_copy(kept, k * GROUP + part, out=True).wait()
        return carry

    lax.fori_loop(0, steps, step, 0)
    lax.fori_loop(0, steps, finish, 0)


def field_kernel(group_ref, length_ref, slot_ref, moment_ref, basis_ref, *refs, n_row, n_col, keep):
    chunk_count = refs[-1].shape[0] // 16 if not keep else refs[-3].shape[0] // 16
    steps = (group_ref[1, 0] + GROUP - 1) // GROUP
    if keep:
        cubes_hbm, out_ref, table_ref, sums_ref, cubes_ref, sems = refs
        kept = (cubes_ref, cubes_hbm, sems)

        def begin(k, carry):
            for part in range(GROUP):
                kept_copy(kept, k * GROUP + part, out=False).start()
            return carry

        lax.fori_loop(0, steps, begin, 0)
    else:
        left_ref, right_ref, out_ref, table_ref, sums_ref = refs
    segments = moment_ref.shape[1]
    width = segments // n_row
    seg_dev = width // n_col
    scale = 1.0 / math.sqrt(width)
    lane = iota((1, seg_dev), 1)
    sums_ref[...] = jnp.zeros_like(sums_ref)

    def table_step(block, carry):
        length = length_ref[block]
        for col in range(n_col):
            vec_at = aligned((col * n_row + block) * seg_dev, seg_dev)
            block_at = aligned((block * n_col + col) * seg_dev, seg_dev)
            both = moment_ref[:, block_at]
            active = jnp.where(lane + col * seg_dev < length, scale, 0.0)
            first = both * (basis_ref[0:1, vec_at] * active)
            second = both * (basis_ref[1:2, vec_at] * active)
            parts = jnp.concatenate([first, second], axis=0)
            high = parts.astype(jnp.bfloat16).astype(jnp.float32)
            table_ref[:, block_at] = jnp.concatenate([high, parts - high], axis=0).astype(jnp.bfloat16)
        return carry

    lax.fori_loop(0, n_row, table_step, 0, unroll=2)

    def step(k, carry):
        for part in range(GROUP):
            chunk = k * GROUP + part
            block_at = aligned(group_ref[0, chunk] * width, width)
            if keep:
                kept_copy(kept, chunk, out=False).wait()
                cubes = cubes_ref[chunk]
            else:
                high, low = cube_halves(left_ref[aligned(chunk * CHUNK, CHUNK), :], right_ref[:, block_at])
                cubes = jnp.concatenate([high, low], axis=0)
            both = dot_nt(cubes, table_ref[:, block_at])
            total = (both[0:CHUNK] + both[CHUNK:2 * CHUNK]).T
            sums_ref[pl.ds(chunk, 16, stride=chunk_count), :] = total[0:16] + total[16:32]
        return carry

    lax.fori_loop(0, steps, step, 0)
    sums = jnp.concatenate([sums_ref[0:6 * chunk_count], sums_ref[8 * chunk_count:14 * chunk_count]], axis=0)
    sums = jnp.concatenate(split3(sums), axis=1).astype(jnp.bfloat16)
    for tile in range(slot_ref.shape[1] // TILE):
        at = pl.ds(tile * TILE, TILE)
        slot = slot_ref[:, at]
        low = jnp.where(iota((CHUNK, TILE), 0) == slot % CHUNK, 1.0, 0.0).astype(jnp.bfloat16)
        high = jnp.where(iota((chunk_count, TILE), 0) == slot // CHUNK, 1.0, 0.0)
        found = dot(sums, jnp.concatenate([low, low, low], axis=0))
        for row in range(12):
            picked = found[row * chunk_count:(row + 1) * chunk_count] * high
            out_ref[row:row + 1, at] = jnp.sum(picked, axis=0, keepdims=True)


def final_kernel(stats_ref, known_ref, basis_own_ref, field_ref, points_ref, currents_ref, iron_ref):
    stats = jnp.sum(stats_ref[...], axis=0)
    known = known_ref[...]
    initial_norm, hessen_a, hessen_b = known[:, 0:1], known[:, 1:2], known[:, 2:3]
    hessen_c, hessen_d, normal_second = stats[:, 0:1], stats[:, 1:2], stats[:, 2:3]
    normal_first = hessen_a * hessen_a + hessen_b * hessen_b
    normal_cross = hessen_a * hessen_c + hessen_b * hessen_d
    target_first = initial_norm * hessen_a
    target_second = initial_norm * hessen_c
    determinant = normal_first * normal_second - normal_cross * normal_cross
    weight_first = (normal_second * target_first - normal_cross * target_second) / determinant
    weight_second = (normal_first * target_second - normal_cross * target_first) / determinant
    currents_ref[...] = weight_first * basis_own_ref[0:1, :] + weight_second * basis_own_ref[1:2, :]
    moments = weight_first * field_ref[0:6, :] + weight_second * field_ref[6:12, :]
    points = points_ref[...] - 0.5
    px, py, pz = points[0:1], points[1:2], points[2:3]
    iron_ref[0:1, :] = pz * moments[1:2] - py * moments[2:3] - moments[3:4]
    iron_ref[1:2, :] = px * moments[2:3] - pz * moments[0:1] - moments[4:5]
    iron_ref[2:3, :] = py * moments[0:1] - px * moments[1:2] - moments[5:6]


def shape(*sizes, dtype=jnp.float32):
    return jax.ShapeDtypeStruct(sizes, dtype)


def shards(drive, resist, centers, tangents, iron_points, owner, range_len):
    seg_dev = drive.shape[0]
    col_len = centers.shape[1]
    n_col = lax.axis_size("col")
    n_row = lax.axis_size("row")
    n_dev = n_col * n_row
    segments = seg_dev * n_dev
    width = n_col * seg_dev
    points_count = iron_points.shape[1]
    coupling = 0.5 / math.sqrt(segments)
    keep = seg_dev * segments * 4 <= KEEP_BYTES
    tiles = segments // TILE
    call = functools.partial(pl.pallas_call, compiler_params=pltpu.CompilerParams(vmem_limit_bytes=VMEM_LIMIT))
    scratch = [pltpu.VMEM((1, segments), jnp.float32), pltpu.VMEM((seg_dev, 128), jnp.float32)]
    if keep:
        scratch += [pltpu.VMEM((tiles, seg_dev, TILE), jnp.float32), pltpu.SemaphoreType.DMA((tiles,))]
    hbm = pl.BlockSpec(memory_space=pltpu.HBM)
    smem = pl.BlockSpec(memory_space=pltpu.SMEM)
    vmem = pl.BlockSpec(memory_space=pltpu.VMEM)

    def work(microseconds):
        return pl.CostEstimate(flops=int(microseconds * 1e9), bytes_accessed=0, transcendentals=0)

    def roomy(row_bytes):
        return STREAM_BYTES // row_bytes

    def exchange(x):
        return lax.all_to_all(x, AXES, 0, 0, tiled=True)

    spread, geometry = pl.pallas_call(
        entry_kernel,
        out_shape=(shape(n_dev, 1, seg_dev), shape(6, col_len)),
        in_specs=[hbm] * 3,
        scratch_shapes=[
            pltpu.VMEM((1, seg_dev), jnp.float32),
            pltpu.VMEM((3, col_len), jnp.float32),
            pltpu.VMEM((3, col_len), jnp.float32),
            pltpu.SemaphoreType.DMA((3,)),
        ],
        compiler_params=pltpu.CompilerParams(vmem_limit_bytes=ENTRY_LIMIT),
        name="entry",
    )(drive[None, :], centers, tangents)
    drive_all = exchange(spread).reshape(1, segments)
    pieces = [
        lax.ppermute(geometry, "col", [(k, (k + shift) % n_col) for k in range(n_col)]) for shift in range(1, n_col)
    ]

    chunk_count = points_count // CHUNK + n_row * (CHUNK - 1) // CHUNK
    chunk_count = -(-chunk_count // 8) * 8
    slot, group_table, left, drive_own, resist_own, own_geometry = call(
        functools.partial(group_kernel, n_row=n_row),
        out_shape=(
            shape(1, points_count, dtype=jnp.int32),
            shape(8, 128, dtype=jnp.int32),
            shape(chunk_count * CHUNK, 48, dtype=jnp.bfloat16),
            shape(1, seg_dev),
            shape(1, seg_dev),
            shape(6, col_len),
        ),
        scratch_shapes=[pltpu.VMEM((48 * chunk_count, CHUNK), jnp.float32)],
        cost_estimate=work(3),
        name="group_points",
    )(owner.reshape(1, points_count), iron_points, drive[None, :], resist[None, :], centers, tangents)
    pieces = [own_geometry] + pieces

    stream = functools.partial(
        pl.pallas_call, compiler_params=pltpu.CompilerParams(vmem_limit_bytes=STREAM_LIMIT if keep else VMEM_LIMIT)
    )
    first = stream(
        functools.partial(first_kernel, coupling, n_col, keep),
        out_shape=(
            shape(1, seg_dev), shape(n_dev, 1, seg_dev), shape(48, segments, dtype=jnp.bfloat16), shape(8, segments),
        ) + ((shape(roomy(seg_dev * TILE * 4), seg_dev, TILE),) if keep else ()),
        out_specs=(vmem,) * 4 + ((hbm,) if keep else ()),
        scratch_shapes=scratch,
        cost_estimate=work(5),
        name="first_image",
    )(drive_all, drive_own, resist_own, group_table, *pieces)
    image_own, image_spread, right, moment = first[0:4]
    image_all = exchange(image_spread).reshape(1, segments)
    cube_shape = (chunk_count, 2 * CHUNK, width)
    cube_scratch = [pltpu.VMEM(cube_shape, jnp.bfloat16), pltpu.SemaphoreType.DMA((chunk_count,))]
    if keep:
        cubes, after = stream(
            functools.partial(weigh_kernel, n_row=n_row),
            out_shape=(shape(roomy(4 * CHUNK * width), *cube_shape[1:], dtype=jnp.bfloat16), shape(8, 128)),
            in_specs=[smem, vmem, vmem],
            out_specs=(hbm, vmem),
            scratch_shapes=cube_scratch,
            cost_estimate=work(5),
            name="weigh",
        )(group_table, left, right)
    else:
        after = group_table
    basis, basis_own, stats, known = stream(
        functools.partial(second_kernel, coupling, n_col, keep),
        out_shape=(shape(2, segments), shape(2, seg_dev), shape(n_dev, 1, 128), shape(1, 128)),
        in_specs=[vmem] * 6 + ([hbm] if keep else [vmem] * n_col),
        scratch_shapes=scratch,
        cost_estimate=work(2),
        name="second_image",
    )(drive_all, image_all, drive_own, image_own, resist_own, after, *(first[4:5] if keep else pieces))
    stats_all = exchange(stats)

    field = stream(
        functools.partial(field_kernel, n_row=n_row, n_col=n_col, keep=keep),
        out_shape=shape(12, points_count),
        in_specs=[smem, smem, vmem, vmem, vmem] + ([hbm] if keep else [vmem, vmem]),
        scratch_shapes=[
            pltpu.VMEM((32, segments), jnp.bfloat16),
            pltpu.VMEM((16 * chunk_count, CHUNK), jnp.float32),
        ] + (cube_scratch if keep else []),
        cost_estimate=work(6),
        name="block_field",
    )(group_table, range_len, slot, moment, basis, *([cubes] if keep else [left, right]))
    currents, iron_field = stream(
        final_kernel,
        out_shape=(shape(1, seg_dev), shape(3, points_count)),
        name="combine",
    )(stats_all, known, basis_own, field, iron_points)
    return (currents[0], iron_field)


def solution(mesh):
    return jax.shard_map(
        shards,
        mesh=mesh,
        in_specs=(
            P(AXES),
            P(AXES),
            P(None, "col"),
            P(None, "col"),
            P(None, AXES),
            P(AXES, None),
            P(),
        ),
        out_specs=(P(AXES), P(None, AXES)),
        check_vma=False,
    )
```

```python
import functools
import math

import jax
import jax.numpy as jnp
from jax import lax
from jax.experimental import pallas as pl
from jax.experimental.pallas import tpu as pltpu
from jax.sharding import PartitionSpec as P

EPS_SEG = 0.0004
EPS_FIELD = 0.0025
AXES = ("col", "row")
CHUNK = 128
GROUP = 4
TILE = 512
COLUMNS = 256
ROWS = 64
KEEP_BYTES = 16 * 1024 * 1024
VMEM_LIMIT = 32 * 1024 * 1024
STREAM_LIMIT = 44 * 1024 * 1024
STREAM_BYTES = 20 * 1024 * 1024
ENTRY_LIMIT = 60 * 1024 * 1024


def split3(x):
    high = x.astype(jnp.bfloat16).astype(jnp.float32)
    rest = x - high
    middle = rest.astype(jnp.bfloat16).astype(jnp.float32)
    low = (rest - middle).astype(jnp.bfloat16).astype(jnp.float32)
    return high, middle, low


def left_parts(x):
    high, middle, low = split3(x)
    return jnp.concatenate([high, high, middle, middle, high, low], axis=0)


def right_parts(x):
    high, middle, low = split3(x)
    return jnp.concatenate([high, middle, high, middle, low, high], axis=0).astype(jnp.bfloat16)


def rows8(*rows):
    width = rows[0].shape[1]
    count = sum(r.shape[0] for r in rows)
    if count < 8:
        rows = rows + (jnp.zeros((8 - count, width), jnp.float32),)
    return jnp.concatenate(rows, axis=0)


def left_center(c, eps):
    square = jnp.sum(c * c, axis=0, keepdims=True)
    return rows8(-2.0 * c, jnp.ones_like(square), square + eps)


def right_center(c):
    square = jnp.sum(c * c, axis=0, keepdims=True)
    return rows8(c, square, jnp.ones_like(square))


def dot(a, b):
    return jnp.dot(a, b, preferred_element_type=jnp.float32)


def dot_nt(a, b):
    return lax.dot_general(a, b, (((1,), (1,)), ((), ())), preferred_element_type=jnp.float32)


def transposed(x):
    return x.T.astype(jnp.bfloat16)


def fold_lanes(x):
    total = x[:, 0:128]
    for piece in range(1, x.shape[1] // 128):
        total = total + x[:, piece * 128:(piece + 1) * 128]
    return total


def iota(shape, axis):
    return lax.broadcasted_iota(jnp.int32, shape, axis)


def aligned(start, size):
    return pl.ds(pl.multiple_of(start, size), size)


def piece_column(shift, n_col):
    return lax.rem(lax.axis_index("col") + n_col - shift, n_col)


def own_sides(own_ref, left_ref):
    seg_dev = left_ref.shape[1]
    own = own_ref[:, aligned(lax.axis_index("row") * seg_dev, seg_dev)]
    left_ref[0] = transposed(left_parts(left_center(own[0:3] - 0.5, EPS_SEG)))
    left_ref[1] = transposed(left_parts(rows8(own[3:6])))


def couple_tile(left_ref, rc, rt, vec, acc_ref, kept_ref=None, index=0):
    for part in range(TILE // COLUMNS):
        columns = slice(part * COLUMNS, (part + 1) * COLUMNS)
        for row in range(0, acc_ref.shape[0], ROWS):
            rows = slice(row, row + ROWS)
            pair = dot(left_ref[1, rows], rt[:, columns]) * lax.rsqrt(dot(left_ref[0, rows], rc[:, columns]))
            if kept_ref is not None:
                kept_ref[index, rows, columns] = pair
            acc_ref[rows] += fold_lanes(pair * vec[:, columns])


def couple(pieces, vec_ref, acc_ref, left_ref, kept=None, right_ref=None, along_ref=None, moment_ref=None):
    seg_dev = acc_ref.shape[0]
    n_col = len(pieces)
    length = pieces[0].shape[1]
    own_sides(pieces[0], left_ref)
    acc_ref[...] = jnp.zeros_like(acc_ref)
    count = length // TILE
    for shift, piece in enumerate(pieces):
        col = piece_column(shift, n_col)
        keeps = kept is not None and (shift + 1) * count <= kept[0].shape[0]

        def step(k, carry):
            geo = piece[:, aligned(k * TILE, TILE)]
            vec_at = pl.ds(pl.multiple_of(col * length + k * TILE, TILE), TILE)
            center, tangent = geo[0:3] - 0.5, geo[3:6]
            rc = right_parts(right_center(center))
            rt = right_parts(rows8(tangent))
            index = shift * count + k
            couple_tile(left_ref, rc, rt, vec_ref[:, vec_at], acc_ref, kept[0] if keeps else None, index)
            if keeps:
                kept_copy(kept, index, out=True).start()
            if right_ref is not None:
                cross = jnp.concatenate([
                    tangent[1:2] * center[2:3] - tangent[2:3] * center[1:2],
                    tangent[2:3] * center[0:1] - tangent[0:1] * center[2:3],
                    tangent[0:1] * center[1:2] - tangent[1:2] * center[0:1],
                ], axis=0)
                both = rows8(tangent, cross)
                along_ref[:, vec_at] = rt
                for part in range(TILE // seg_dev):
                    row = k * (TILE // seg_dev) + part
                    block_at = aligned((row * n_col + col) * seg_dev, seg_dev)
                    right_ref[:, block_at] = rc[:, part * seg_dev:(part + 1) * seg_dev]
                    moment_ref[:, block_at] = both[:, part * seg_dev:(part + 1) * seg_dev]
            return carry

        lax.fori_loop(0, count, step, 0, unroll=4)
    return jnp.sum(acc_ref[...].T, axis=0, keepdims=True)


def couple_again(kept, own_ref, right_ref, along_ref, vec_ref, acc_ref, left_ref, n_col):
    own_sides(own_ref, left_ref)
    seg_dev = acc_ref.shape[0]
    acc_ref[...] = jnp.zeros_like(acc_ref)
    length = vec_ref.shape[1] // n_col
    count = length // TILE
    stored = kept[0].shape[0] // count
    for shift in list(range(stored, n_col)) + list(range(stored)):
        col = piece_column(shift, n_col)

        def step(k, carry):
            vec_at = pl.ds(pl.multiple_of(col * length + k * TILE, TILE), TILE)
            if shift < stored:
                kept_copy(kept, shift * count + k, out=False).wait()
                acc_ref[...] += fold_lanes(kept[0][shift * count + k] * vec_ref[:, vec_at])
            else:
                rc = jnp.concatenate([
                    right_ref[:, aligned(((k * (TILE // seg_dev) + part) * n_col + col) * seg_dev, seg_dev)]
                    for part in range(TILE // seg_dev)
                ], axis=1)
                couple_tile(left_ref, rc, along_ref[:, vec_at], vec_ref[:, vec_at], acc_ref)
            return carry

        lax.fori_loop(0, count, step, 0, unroll=4)
    return jnp.sum(acc_ref[...].T, axis=0, keepdims=True)


def kept_copy(kept, index, out):
    local, remote, sems = kept
    if out:
        return pltpu.make_async_copy(local.at[index], remote.at[index], sems.at[index])
    return pltpu.make_async_copy(remote.at[index], local.at[index], sems.at[index])


def spread_rows(ref, row):
    for k in range(ref.shape[0]):
        ref[k] = row


def entry_kernel(drive_hbm, centers_hbm, tangents_hbm, spread_ref, geo_ref, drive_ref, centers, tangents, sems):
    pairs = ((drive_hbm, drive_ref), (centers_hbm, centers), (tangents_hbm, tangents))
    copies = [pltpu.make_async_copy(source, target, sems.at[k]) for k, (source, target) in enumerate(pairs)]
    for copy in copies:
        copy.start()
    for copy in copies:
        copy.wait()
    spread_rows(spread_ref, drive_ref[...])
    geo_ref[0:3] = centers[...]
    geo_ref[3:6] = tangents[...]


def first_kernel(coupling, n_col, keep, drive_ref, drive_own_ref, resist_ref, after_ref, *refs):
    pieces, refs = refs[:n_col], refs[n_col:]
    image_ref, spread_ref, right_ref, along_ref, moment_ref = refs[0:5]
    kept = None
    if keep:
        kept_hbm = refs[5]
        vec_ref, acc_ref, left_ref, kept_ref, sems = refs[6:]
        kept = (kept_ref, kept_hbm, sems)
    else:
        vec_ref, acc_ref, left_ref = refs[5:]
    drive = drive_ref[...]
    scale = 1.0 / jnp.sqrt(jnp.sum(drive * drive, keepdims=True))
    vec_ref[...] = drive * scale
    product = couple(pieces, vec_ref, acc_ref, left_ref, kept, right_ref, along_ref, moment_ref)
    image = resist_ref[...] * (drive_own_ref[...] * scale) + coupling * product
    image_ref[...] = image
    spread_rows(spread_ref, image)
    if keep:
        for index in range(kept_ref.shape[0]):
            kept_copy(kept, index, out=True).wait()


def second_kernel(coupling, n_col, keep, drive_ref, image_ref, drive_own_ref, image_own_ref, resist_ref, after_ref, *refs):
    if keep:
        kept_hbm, own_ref, right_ref, along_ref = refs[0:4]
        refs = refs[4:]
        vec_ref, acc_ref, left_ref, kept_ref, sems = refs[4:]
        kept = (kept_ref, kept_hbm, sems)
        for index in range(kept_ref.shape[0]):
            kept_copy(kept, index, out=False).start()
    else:
        pieces, refs = refs[:n_col], refs[n_col:]
        vec_ref, acc_ref, left_ref = refs[4:]
    basis_ref, basis_own_ref, stats_ref, known_ref = refs[0:4]
    drive = drive_ref[...]
    norm = jnp.sqrt(jnp.sum(drive * drive, keepdims=True))
    scale = 1.0 / norm
    basis_a = drive * scale
    image = image_ref[...]
    hessen_a = jnp.sum(image * basis_a, keepdims=True)
    rest = image - hessen_a * basis_a
    hessen_b = jnp.sqrt(jnp.sum(rest * rest, keepdims=True))
    inverse = 1.0 / hessen_b
    basis_b = rest * inverse
    vec_ref[...] = basis_b
    basis_ref[0:1, :] = basis_a
    basis_ref[1:2, :] = basis_b
    own_a = drive_own_ref[...] * scale
    own_b = (image_own_ref[...] - hessen_a * own_a) * inverse
    basis_own_ref[0:1, :] = own_a
    basis_own_ref[1:2, :] = own_b
    if keep:
        product = couple_again(kept, own_ref, right_ref, along_ref, vec_ref, acc_ref, left_ref, n_col)
    else:
        product = couple(pieces, vec_ref, acc_ref, left_ref)
    second = resist_ref[...] * own_b + coupling * product
    lane = iota((1, 128), 1)

    def three(a, b, c):
        return jnp.where(lane == 0, a, jnp.where(lane == 1, b, jnp.where(lane == 2, c, 0.0)))

    spread_rows(stats_ref, three(
        jnp.sum(second * own_a, keepdims=True),
        jnp.sum(second * own_b, keepdims=True),
        jnp.sum(second * second, keepdims=True),
    ))
    known_ref[...] = three(norm, hessen_a, hessen_b)


def group_kernel(owner_ref, points_ref, drive_in_ref, resist_in_ref, centers_in_ref, tangents_in_ref,
                 slot_ref, table_ref, left_ref, drive_ref, resist_ref, geo_ref, planes_ref, *, n_row):
    drive_ref[...] = drive_in_ref[...]
    resist_ref[...] = resist_in_ref[...]
    geo_ref[0:3] = centers_in_ref[...]
    geo_ref[3:6] = tangents_in_ref[...]
    points = owner_ref.shape[1]
    chunk_count = left_ref.shape[0] // CHUNK
    owner = owner_ref[...]
    rows = max(8, n_row)
    marks = jnp.where(iota((rows, points), 0) == owner, 1.0, 0.0)
    tile = 256
    upper = jnp.where(iota((tile, tile), 0) <= iota((tile, tile), 1), 1.0, 0.0).astype(jnp.bfloat16)
    before = jnp.zeros((rows, 1), jnp.float32)
    ranks = []
    for piece in range(points // tile):
        part = dot(marks[:, piece * tile:(piece + 1) * tile].astype(jnp.bfloat16), upper)
        ranks.append(part + before - 1.0)
        before = before + part[:, tile - 1:tile]
    ranks = jnp.concatenate(ranks, axis=1)
    chunks = jnp.floor((before + (CHUNK - 1)) * (1.0 / CHUNK))
    start = jnp.zeros((1, 1), jnp.float32)
    starts = []
    for name in range(rows):
        starts.append(start)
        start = start + chunks[name:name + 1]
    starts = jnp.concatenate(starts, axis=0)
    slot = jnp.sum(marks * (ranks + starts * CHUNK), axis=0, keepdims=True).astype(jnp.int32)
    slot_ref[...] = slot
    lane = iota((rows, 128), 1)
    ended = jnp.sum(jnp.where(starts + chunks <= lane.astype(jnp.float32), 1.0, 0.0), axis=0, keepdims=True)
    block = jnp.minimum(ended, n_row - 1.0)
    place = iota((8, 128), 0)
    table_ref[...] = jnp.where(place == 0, block, start).astype(jnp.int32)
    high = jnp.where(iota((chunk_count, points), 0) == slot // CHUNK, 1.0, 0.0)
    low = jnp.where(iota((CHUNK, points), 0) == slot % CHUNK, 1.0, 0.0).astype(jnp.bfloat16)
    parts = split3(points_ref[...] - 0.5)
    spread = jnp.concatenate([high * part[k:k + 1] for k in range(3) for part in parts], axis=0).astype(jnp.bfloat16)
    placed = dot_nt(spread, low)
    planes = [placed[k * chunk_count:(k + 1) * chunk_count] for k in range(9)]
    x, y, z = (planes[3 * k] + planes[3 * k + 1] + planes[3 * k + 2] for k in range(3))
    sides = [-2.0 * x, -2.0 * y, -2.0 * z, jnp.ones_like(x), x * x + y * y + z * z + EPS_FIELD]
    sides = [split3(side) for side in sides]
    empty = jnp.zeros_like(x)
    for group, part in enumerate([0, 0, 1, 1, 0, 2]):
        for k in range(8):
            to = pl.ds((group * 8 + k) * chunk_count, chunk_count)
            planes_ref[to, :] = sides[k][part] if k < 5 else empty
    for chunk in range(chunk_count):
        left_ref[chunk * CHUNK:(chunk + 1) * CHUNK, :] = transposed(planes_ref[pl.ds(chunk, 48, stride=chunk_count), :])


def cube_halves(left, right):
    inverse = lax.rsqrt(dot(left, right))
    cube = inverse * inverse * inverse
    high = cube.astype(jnp.bfloat16)
    return high, (cube - high.astype(jnp.float32)).astype(jnp.bfloat16)


def weigh_kernel(group_ref, left_ref, right_ref, cubes_hbm, done_ref, cubes_ref, sems, *, n_row):
    width = right_ref.shape[1] // n_row
    done_ref[...] = jnp.zeros_like(done_ref)
    kept = (cubes_ref, cubes_hbm, sems)
    steps = (group_ref[1, 0] + GROUP - 1) // GROUP

    def step(k, carry):
        for part in range(GROUP):
            chunk = k * GROUP + part
            block_at = aligned(group_ref[0, chunk] * width, width)
            high, low = cube_halves(left_ref[aligned(chunk * CHUNK, CHUNK), :], right_ref[:, block_at])
            cubes_ref[chunk, 0:CHUNK] = high
            cubes_ref[chunk, CHUNK:2 * CHUNK] = low
            kept_copy(kept, chunk, out=True).start()
        return carry

    def finish(k, carry):
        for part in range(GROUP):
            kept_copy(kept, k * GROUP + part, out=True).wait()
        return carry

    lax.fori_loop(0, steps, step, 0)
    lax.fori_loop(0, steps, finish, 0)


def field_kernel(group_ref, length_ref, slot_ref, moment_ref, basis_ref, *refs, n_row, n_col, keep):
    chunk_count = refs[-1].shape[0] // 16 if not keep else refs[-3].shape[0] // 16
    steps = (group_ref[1, 0] + GROUP - 1) // GROUP
    if keep:
        cubes_hbm, out_ref, table_ref, sums_ref, cubes_ref, sems = refs
        kept = (cubes_ref, cubes_hbm, sems)

        def begin(k, carry):
            for part in range(GROUP):
                kept_copy(kept, k * GROUP + part, out=False).start()
            return carry

        lax.fori_loop(0, steps, begin, 0)
    else:
        left_ref, right_ref, out_ref, table_ref, sums_ref = refs
    segments = moment_ref.shape[1]
    width = segments // n_row
    seg_dev = width // n_col
    scale = 1.0 / math.sqrt(width)
    lane = iota((1, seg_dev), 1)
    sums_ref[...] = jnp.zeros_like(sums_ref)

    def table_step(block, carry):
        length = length_ref[block]
        for col in range(n_col):
            vec_at = aligned((col * n_row + block) * seg_dev, seg_dev)
            block_at = aligned((block * n_col + col) * seg_dev, seg_dev)
            both = moment_ref[:, block_at]
            active = jnp.where(lane + col * seg_dev < length, scale, 0.0)
            first = both * (basis_ref[0:1, vec_at] * active)
            second = both * (basis_ref[1:2, vec_at] * active)
            parts = jnp.concatenate([first, second], axis=0)
            high = parts.astype(jnp.bfloat16).astype(jnp.float32)
            table_ref[:, block_at] = jnp.concatenate([high, parts - high], axis=0).astype(jnp.bfloat16)
        return carry

    lax.fori_loop(0, n_row, table_step, 0, unroll=min(n_row, 8))

    def step(k, carry):
        for part in range(GROUP):
            chunk = k * GROUP + part
            block_at = aligned(group_ref[0, chunk] * width, width)
            if keep:
                kept_copy(kept, chunk, out=False).wait()
                cubes = cubes_ref[chunk]
            else:
                high, low = cube_halves(left_ref[aligned(chunk * CHUNK, CHUNK), :], right_ref[:, block_at])
                cubes = jnp.concatenate([high, low], axis=0)
            both = dot_nt(table_ref[:, block_at], cubes)
            total = both[:, 0:CHUNK] + both[:, CHUNK:2 * CHUNK]
            sums_ref[pl.ds(chunk, 16, stride=chunk_count), :] = total[0:16] + total[16:32]
        return carry

    lax.fori_loop(0, steps, step, 0)
    sums = jnp.concatenate([sums_ref[0:6 * chunk_count], sums_ref[8 * chunk_count:14 * chunk_count]], axis=0)
    sums = jnp.concatenate(split3(sums), axis=1).astype(jnp.bfloat16)
    for tile in range(slot_ref.shape[1] // TILE):
        at = pl.ds(tile * TILE, TILE)
        slot = slot_ref[:, at]
        low = jnp.where(iota((CHUNK, TILE), 0) == slot % CHUNK, 1.0, 0.0).astype(jnp.bfloat16)
        high = jnp.where(iota((chunk_count, TILE), 0) == slot // CHUNK, 1.0, 0.0)
        found = dot(sums, jnp.concatenate([low, low, low], axis=0))
        for row in range(12):
            picked = found[row * chunk_count:(row + 1) * chunk_count] * high
            out_ref[row:row + 1, at] = jnp.sum(picked, axis=0, keepdims=True)


def final_kernel(stats_ref, known_ref, basis_own_ref, field_ref, points_ref, currents_ref, iron_ref):
    stats = jnp.sum(stats_ref[...], axis=0)
    known = known_ref[...]
    initial_norm, hessen_a, hessen_b = known[:, 0:1], known[:, 1:2], known[:, 2:3]
    hessen_c, hessen_d, normal_second = stats[:, 0:1], stats[:, 1:2], stats[:, 2:3]
    normal_first = hessen_a * hessen_a + hessen_b * hessen_b
    normal_cross = hessen_a * hessen_c + hessen_b * hessen_d
    target_first = initial_norm * hessen_a
    target_second = initial_norm * hessen_c
    determinant = normal_first * normal_second - normal_cross * normal_cross
    weight_first = (normal_second * target_first - normal_cross * target_second) / determinant
    weight_second = (normal_first * target_second - normal_cross * target_first) / determinant
    currents_ref[...] = weight_first * basis_own_ref[0:1, :] + weight_second * basis_own_ref[1:2, :]
    moments = weight_first * field_ref[0:6, :] + weight_second * field_ref[6:12, :]
    points = points_ref[...] - 0.5
    px, py, pz = points[0:1], points[1:2], points[2:3]
    iron_ref[0:1, :] = pz * moments[1:2] - py * moments[2:3] - moments[3:4]
    iron_ref[1:2, :] = px * moments[2:3] - pz * moments[0:1] - moments[4:5]
    iron_ref[2:3, :] = py * moments[0:1] - px * moments[1:2] - moments[5:6]


def shape(*sizes, dtype=jnp.float32):
    return jax.ShapeDtypeStruct(sizes, dtype)


def shards(drive, resist, centers, tangents, iron_points, owner, range_len):
    seg_dev = drive.shape[0]
    col_len = centers.shape[1]
    n_col = lax.axis_size("col")
    n_row = lax.axis_size("row")
    n_dev = n_col * n_row
    segments = seg_dev * n_dev
    width = n_col * seg_dev
    points_count = iron_points.shape[1]
    coupling = 0.5 / math.sqrt(segments)
    keep = seg_dev * segments * 4 <= KEEP_BYTES
    call = functools.partial(pl.pallas_call, compiler_params=pltpu.CompilerParams(vmem_limit_bytes=VMEM_LIMIT))
    scratch = [
        pltpu.VMEM((1, segments), jnp.float32),
        pltpu.VMEM((seg_dev, 128), jnp.float32),
        pltpu.VMEM((2, seg_dev, 48), jnp.bfloat16),
    ]
    tiles = (n_col // 2) * (col_len // TILE)
    if keep:
        scratch += [pltpu.VMEM((tiles, seg_dev, TILE), jnp.float32), pltpu.SemaphoreType.DMA((tiles,))]
    hbm = pl.BlockSpec(memory_space=pltpu.HBM)
    smem = pl.BlockSpec(memory_space=pltpu.SMEM)
    vmem = pl.BlockSpec(memory_space=pltpu.VMEM)

    def work(microseconds):
        return pl.CostEstimate(flops=int(microseconds * 1e9), bytes_accessed=0, transcendentals=0)

    def roomy(row_bytes):
        return STREAM_BYTES // row_bytes

    def exchange(x):
        return lax.all_to_all(x, AXES, 0, 0, tiled=True)

    spread, geometry = pl.pallas_call(
        entry_kernel,
        out_shape=(shape(n_dev, 1, seg_dev), shape(6, col_len)),
        in_specs=[hbm] * 3,
        scratch_shapes=[
            pltpu.VMEM((1, seg_dev), jnp.float32),
            pltpu.VMEM((3, col_len), jnp.float32),
            pltpu.VMEM((3, col_len), jnp.float32),
            pltpu.SemaphoreType.DMA((3,)),
        ],
        compiler_params=pltpu.CompilerParams(vmem_limit_bytes=ENTRY_LIMIT),
        name="entry",
    )(drive[None, :], centers, tangents)
    drive_all = exchange(spread).reshape(1, segments)
    pieces = [
        lax.ppermute(geometry, "col", [(k, (k + shift) % n_col) for k in range(n_col)]) for shift in range(1, n_col)
    ]

    chunk_count = points_count // CHUNK + n_row * (CHUNK - 1) // CHUNK
    chunk_count = -(-chunk_count // 8) * 8
    slot, group_table, left, drive_own, resist_own, own_geometry = call(
        functools.partial(group_kernel, n_row=n_row),
        out_shape=(
            shape(1, points_count, dtype=jnp.int32),
            shape(8, 128, dtype=jnp.int32),
            shape(chunk_count * CHUNK, 48, dtype=jnp.bfloat16),
            shape(1, seg_dev),
            shape(1, seg_dev),
            shape(6, col_len),
        ),
        scratch_shapes=[pltpu.VMEM((48 * chunk_count, CHUNK), jnp.float32)],
        cost_estimate=work(3),
        name="group_points",
    )(owner.reshape(1, points_count), iron_points, drive[None, :], resist[None, :], centers, tangents)
    pieces = [own_geometry] + pieces

    stream = functools.partial(
        pl.pallas_call, compiler_params=pltpu.CompilerParams(vmem_limit_bytes=STREAM_LIMIT if keep else VMEM_LIMIT)
    )
    first = stream(
        functools.partial(first_kernel, coupling, n_col, keep),
        out_shape=(
            shape(1, seg_dev), shape(n_dev, 1, seg_dev), shape(48, segments, dtype=jnp.bfloat16),
            shape(48, segments, dtype=jnp.bfloat16), shape(8, segments),
        ) + ((shape(roomy(seg_dev * TILE * 4), seg_dev, TILE),) if keep else ()),
        out_specs=(vmem,) * 5 + ((hbm,) if keep else ()),
        scratch_shapes=scratch,
        cost_estimate=work(5),
        name="first_image",
    )(drive_all, drive_own, resist_own, group_table, *pieces)
    image_own, image_spread, right, along, moment = first[0:5]
    image_all = exchange(image_spread).reshape(1, segments)
    cube_shape = (chunk_count, 2 * CHUNK, width)
    cube_scratch = [pltpu.VMEM(cube_shape, jnp.bfloat16), pltpu.SemaphoreType.DMA((chunk_count,))]
    if keep:
        cubes, after = stream(
            functools.partial(weigh_kernel, n_row=n_row),
            out_shape=(shape(roomy(4 * CHUNK * width), *cube_shape[1:], dtype=jnp.bfloat16), shape(8, 128)),
            in_specs=[smem, vmem, vmem],
            out_specs=(hbm, vmem),
            scratch_shapes=cube_scratch,
            cost_estimate=work(5),
            name="weigh",
        )(group_table, left, right)
    else:
        after = group_table
    basis, basis_own, stats, known = stream(
        functools.partial(second_kernel, coupling, n_col, keep),
        out_shape=(shape(2, segments), shape(2, seg_dev), shape(n_dev, 1, 128), shape(1, 128)),
        in_specs=[vmem] * 6 + ([hbm] + [vmem] * 3 if keep else [vmem] * n_col),
        scratch_shapes=scratch,
        cost_estimate=work(2),
        name="second_image",
    )(drive_all, image_all, drive_own, image_own, resist_own, after, *([first[5], own_geometry, right, along] if keep else pieces))
    stats_all = exchange(stats)

    field = stream(
        functools.partial(field_kernel, n_row=n_row, n_col=n_col, keep=keep),
        out_shape=shape(12, points_count),
        in_specs=[smem, smem, vmem, vmem, vmem] + ([hbm] if keep else [vmem, vmem]),
        scratch_shapes=[
            pltpu.VMEM((32, segments), jnp.bfloat16),
            pltpu.VMEM((16 * chunk_count, CHUNK), jnp.float32),
        ] + (cube_scratch if keep else []),
        cost_estimate=work(6),
        name="block_field",
    )(group_table, range_len, slot, moment, basis, *([cubes] if keep else [left, right]))
    currents, iron_field = stream(
        final_kernel,
        out_shape=(shape(1, seg_dev), shape(3, points_count)),
        name="combine",
    )(stats_all, known, basis_own, field, iron_points)
    return (currents[0], iron_field)


def solution(mesh):
    return jax.shard_map(
        shards,
        mesh=mesh,
        in_specs=(
            P(AXES),
            P(AXES),
            P(None, "col"),
            P(None, "col"),
            P(None, AXES),
            P(AXES, None),
            P(),
        ),
        out_specs=(P(AXES), P(None, AXES)),
        check_vma=False,
    )
```

```python
import functools
import math

import jax
import jax.numpy as jnp
from jax import lax
from jax.experimental import pallas as pl
from jax.experimental.pallas import tpu as pltpu
from jax.sharding import PartitionSpec as P

EPS_SEG = 0.0004
EPS_FIELD = 0.0025
AXES = ("col", "row")
CHUNK = 128
GROUP = 4
TILE = 512
COLUMNS = 256
ROWS = 64
KEEP_BYTES = 16 * 1024 * 1024
VMEM_LIMIT = 32 * 1024 * 1024
STREAM_LIMIT = 44 * 1024 * 1024
STREAM_BYTES = 20 * 1024 * 1024
ENTRY_LIMIT = 60 * 1024 * 1024


def split3(x):
    high = x.astype(jnp.bfloat16).astype(jnp.float32)
    rest = x - high
    middle = rest.astype(jnp.bfloat16).astype(jnp.float32)
    low = (rest - middle).astype(jnp.bfloat16).astype(jnp.float32)
    return high, middle, low


def left_parts(x):
    high, middle, low = split3(x)
    return jnp.concatenate([high, high, middle, middle, high, low], axis=0)


def right_parts(x):
    high, middle, low = split3(x)
    return jnp.concatenate([high, middle, high, middle, low, high], axis=0).astype(jnp.bfloat16)


def rows8(*rows):
    width = rows[0].shape[1]
    count = sum(r.shape[0] for r in rows)
    if count < 8:
        rows = rows + (jnp.zeros((8 - count, width), jnp.float32),)
    return jnp.concatenate(rows, axis=0)


def left_center(c, eps):
    square = jnp.sum(c * c, axis=0, keepdims=True)
    return rows8(-2.0 * c, jnp.ones_like(square), square + eps)


def right_center(c):
    square = jnp.sum(c * c, axis=0, keepdims=True)
    return rows8(c, square, jnp.ones_like(square))


def dot(a, b):
    return jnp.dot(a, b, preferred_element_type=jnp.float32)


def dot_nt(a, b):
    return lax.dot_general(a, b, (((1,), (1,)), ((), ())), preferred_element_type=jnp.float32)


def transposed(x):
    return x.T.astype(jnp.bfloat16)


def iota(shape, axis):
    return lax.broadcasted_iota(jnp.int32, shape, axis)


def aligned(start, size):
    return pl.ds(pl.multiple_of(start, size), size)


def sides_kernel(*refs, n_col):
    pieces, (right_ref, moment_ref, left_ref, along_ref) = refs[:n_col], refs[n_col:]
    length = pieces[0].shape[1]
    seg_dev = left_ref.shape[0]
    own = pieces[0][:, aligned(lax.axis_index("row") * seg_dev, seg_dev)]
    left_ref[...] = transposed(left_parts(left_center(own[0:3] - 0.5, EPS_SEG)))
    tangent = rows8(own[3:6]).T
    for k in range(3):
        along_ref[k] = jnp.broadcast_to(tangent[:, k:k + 1], (seg_dev, 128))
    for shift, piece in enumerate(pieces):
        col = lax.rem(lax.axis_index("col") + n_col - shift, n_col)

        def step(k, carry):
            geo = piece[:, aligned(k * TILE, TILE)]
            to = pl.ds(pl.multiple_of(col * length + k * TILE, TILE), TILE)
            center, tangent = geo[0:3] - 0.5, geo[3:6]
            cross = jnp.concatenate([
                tangent[1:2] * center[2:3] - tangent[2:3] * center[1:2],
                tangent[2:3] * center[0:1] - tangent[0:1] * center[2:3],
                tangent[0:1] * center[1:2] - tangent[1:2] * center[0:1],
            ], axis=0)
            right_ref[:, to] = right_parts(right_center(center))
            moment_ref[:, to] = rows8(tangent, cross)
            return carry

        lax.fori_loop(0, length // TILE, step, 0, unroll=4)


def couple(right_ref, moment_ref, left_ref, along_ref, vec_ref, acc_ref):
    acc_ref[...] = jnp.zeros_like(acc_ref)

    def step(k, carry):
        at = aligned(k * TILE, TILE)
        turned = moment_ref[0:3, at] * vec_ref[:, at]
        right = right_ref[:, at]
        for first in range(0, TILE, COLUMNS):
            for row in range(0, acc_ref.shape[0], ROWS):
                rows = slice(row, row + ROWS)
                inverse = lax.rsqrt(dot(left_ref[rows], right[:, first:first + COLUMNS]))
                total = acc_ref[rows]
                for start in range(0, COLUMNS, 128):
                    lanes = slice(first + start, first + start + 128)
                    along = along_ref[0, rows] * turned[0:1, lanes]
                    along = along + along_ref[1, rows] * turned[1:2, lanes]
                    along = along + along_ref[2, rows] * turned[2:3, lanes]
                    total = total + along * inverse[:, start:start + 128]
                acc_ref[rows] = total
        return carry

    lax.fori_loop(0, vec_ref.shape[1] // TILE, step, 0, unroll=4)
    return jnp.sum(acc_ref[...].T, axis=0, keepdims=True)


def kept_copy(kept, index, out):
    local, remote, sems = kept
    if out:
        return pltpu.make_async_copy(local.at[index], remote.at[index], sems.at[index])
    return pltpu.make_async_copy(remote.at[index], local.at[index], sems.at[index])


def spread_rows(ref, row):
    for k in range(ref.shape[0]):
        ref[k] = row


def entry_kernel(drive_hbm, centers_hbm, tangents_hbm, spread_ref, geo_ref, drive_ref, centers, tangents, sems):
    pairs = ((drive_hbm, drive_ref), (centers_hbm, centers), (tangents_hbm, tangents))
    copies = [pltpu.make_async_copy(source, target, sems.at[k]) for k, (source, target) in enumerate(pairs)]
    for copy in copies:
        copy.start()
    for copy in copies:
        copy.wait()
    spread_rows(spread_ref, drive_ref[...])
    geo_ref[0:3] = centers[...]
    geo_ref[3:6] = tangents[...]


def first_kernel(coupling, drive_ref, drive_own_ref, resist_ref, after_ref, right_ref, moment_ref, left_ref, along_ref,
                 image_ref, spread_ref, vec_ref, acc_ref):
    drive = drive_ref[...]
    scale = 1.0 / jnp.sqrt(jnp.sum(drive * drive, keepdims=True))
    vec_ref[...] = drive * scale
    product = couple(right_ref, moment_ref, left_ref, along_ref, vec_ref, acc_ref)
    image = resist_ref[...] * (drive_own_ref[...] * scale) + coupling * product
    image_ref[...] = image
    spread_rows(spread_ref, image)


def second_kernel(coupling, drive_ref, image_ref, drive_own_ref, image_own_ref, resist_ref, after_ref,
                  right_ref, moment_ref, left_ref, along_ref,
                  basis_ref, basis_own_ref, stats_ref, known_ref, vec_ref, acc_ref):
    drive = drive_ref[...]
    norm = jnp.sqrt(jnp.sum(drive * drive, keepdims=True))
    scale = 1.0 / norm
    basis_a = drive * scale
    image = image_ref[...]
    hessen_a = jnp.sum(image * basis_a, keepdims=True)
    rest = image - hessen_a * basis_a
    hessen_b = jnp.sqrt(jnp.sum(rest * rest, keepdims=True))
    inverse = 1.0 / hessen_b
    basis_b = rest * inverse
    vec_ref[...] = basis_b
    basis_ref[0:1, :] = basis_a
    basis_ref[1:2, :] = basis_b
    own_a = drive_own_ref[...] * scale
    own_b = (image_own_ref[...] - hessen_a * own_a) * inverse
    basis_own_ref[0:1, :] = own_a
    basis_own_ref[1:2, :] = own_b
    product = couple(right_ref, moment_ref, left_ref, along_ref, vec_ref, acc_ref)
    second = resist_ref[...] * own_b + coupling * product
    lane = iota((1, 128), 1)

    def three(a, b, c):
        return jnp.where(lane == 0, a, jnp.where(lane == 1, b, jnp.where(lane == 2, c, 0.0)))

    spread_rows(stats_ref, three(
        jnp.sum(second * own_a, keepdims=True),
        jnp.sum(second * own_b, keepdims=True),
        jnp.sum(second * second, keepdims=True),
    ))
    known_ref[...] = three(norm, hessen_a, hessen_b)


def group_kernel(owner_ref, points_ref, drive_in_ref, resist_in_ref, centers_in_ref, tangents_in_ref,
                 slot_ref, table_ref, left_ref, drive_ref, resist_ref, geo_ref, planes_ref, *, n_row):
    drive_ref[...] = drive_in_ref[...]
    resist_ref[...] = resist_in_ref[...]
    geo_ref[0:3] = centers_in_ref[...]
    geo_ref[3:6] = tangents_in_ref[...]
    points = owner_ref.shape[1]
    chunk_count = left_ref.shape[0] // CHUNK
    owner = owner_ref[...]
    rows = max(8, n_row)
    marks = jnp.where(iota((rows, points), 0) == owner, 1.0, 0.0)
    tile = 256
    upper = jnp.where(iota((tile, tile), 0) <= iota((tile, tile), 1), 1.0, 0.0).astype(jnp.bfloat16)
    before = jnp.zeros((rows, 1), jnp.float32)
    ranks = []
    for piece in range(points // tile):
        part = dot(marks[:, piece * tile:(piece + 1) * tile].astype(jnp.bfloat16), upper)
        ranks.append(part + before - 1.0)
        before = before + part[:, tile - 1:tile]
    ranks = jnp.concatenate(ranks, axis=1)
    chunks = jnp.floor((before + (CHUNK - 1)) * (1.0 / CHUNK))
    start = jnp.zeros((1, 1), jnp.float32)
    starts = []
    for name in range(rows):
        starts.append(start)
        start = start + chunks[name:name + 1]
    starts = jnp.concatenate(starts, axis=0)
    slot = jnp.sum(marks * (ranks + starts * CHUNK), axis=0, keepdims=True).astype(jnp.int32)
    slot_ref[...] = slot
    lane = iota((rows, 128), 1)
    ended = jnp.sum(jnp.where(starts + chunks <= lane.astype(jnp.float32), 1.0, 0.0), axis=0, keepdims=True)
    block = jnp.minimum(ended, n_row - 1.0)
    place = iota((8, 128), 0)
    table_ref[...] = jnp.where(place == 0, block, start).astype(jnp.int32)
    high = jnp.where(iota((chunk_count, points), 0) == slot // CHUNK, 1.0, 0.0)
    low = jnp.where(iota((CHUNK, points), 0) == slot % CHUNK, 1.0, 0.0).astype(jnp.bfloat16)
    parts = split3(points_ref[...] - 0.5)
    spread = jnp.concatenate([high * part[k:k + 1] for k in range(3) for part in parts], axis=0).astype(jnp.bfloat16)
    placed = dot_nt(spread, low)
    planes = [placed[k * chunk_count:(k + 1) * chunk_count] for k in range(9)]
    x, y, z = (planes[3 * k] + planes[3 * k + 1] + planes[3 * k + 2] for k in range(3))
    sides = [-2.0 * x, -2.0 * y, -2.0 * z, jnp.ones_like(x), x * x + y * y + z * z + EPS_FIELD]
    sides = [split3(side) for side in sides]
    empty = jnp.zeros_like(x)
    for group, part in enumerate([0, 0, 1, 1, 0, 2]):
        for k in range(8):
            to = pl.ds((group * 8 + k) * chunk_count, chunk_count)
            planes_ref[to, :] = sides[k][part] if k < 5 else empty
    for chunk in range(chunk_count):
        left_ref[chunk * CHUNK:(chunk + 1) * CHUNK, :] = transposed(planes_ref[pl.ds(chunk, 48, stride=chunk_count), :])


def cube_halves(left, right):
    inverse = lax.rsqrt(dot(left, right))
    cube = inverse * inverse * inverse
    high = cube.astype(jnp.bfloat16)
    return high, (cube - high.astype(jnp.float32)).astype(jnp.bfloat16)


def block_part(block, col, n_row, seg_dev):
    return aligned((col * n_row + block) * seg_dev, seg_dev)


def chunk_steps(group_ref):
    return (group_ref[1, 0] + GROUP - 1) // GROUP


def weigh_kernel(group_ref, left_ref, right_ref, cubes_hbm, done_ref, cubes_ref, sems, *, n_row, n_col):
    seg_dev = right_ref.shape[1] // (n_row * n_col)
    done_ref[...] = jnp.zeros_like(done_ref)
    kept = (cubes_ref, cubes_hbm, sems)

    def step(k, carry):
        for part in range(GROUP):
            chunk = k * GROUP + part
            left = left_ref[aligned(chunk * CHUNK, CHUNK), :]
            for col in range(n_col):
                to = slice(col * seg_dev, (col + 1) * seg_dev)
                high, low = cube_halves(left, right_ref[:, block_part(group_ref[0, chunk], col, n_row, seg_dev)])
                cubes_ref[chunk, 0:CHUNK, to] = high
                cubes_ref[chunk, CHUNK:2 * CHUNK, to] = low
            kept_copy(kept, chunk, out=True).start()
        return carry

    def finish(k, carry):
        for part in range(GROUP):
            kept_copy(kept, k * GROUP + part, out=True).wait()
        return carry

    lax.fori_loop(0, chunk_steps(group_ref), step, 0)
    lax.fori_loop(0, chunk_steps(group_ref), finish, 0)


def field_kernel(group_ref, length_ref, slot_ref, moment_ref, basis_ref, *refs, n_row, n_col, keep):
    if keep:
        cubes_hbm, out_ref, table_ref, sums_ref, cubes_ref, sems = refs
        kept = (cubes_ref, cubes_hbm, sems)

        def begin(k, carry):
            for part in range(GROUP):
                kept_copy(kept, k * GROUP + part, out=False).start()
            return carry

        lax.fori_loop(0, chunk_steps(group_ref), begin, 0)
    else:
        left_ref, right_ref, out_ref, table_ref, sums_ref = refs
    chunk_count = sums_ref.shape[0] // 16
    seg_dev = moment_ref.shape[1] // (n_row * n_col)
    scale = 1.0 / math.sqrt(n_col * seg_dev)
    lane = iota((1, seg_dev), 1)
    sums_ref[...] = jnp.zeros_like(sums_ref)

    def table_step(block, carry):
        length = length_ref[block]
        for col in range(n_col):
            at = block_part(block, col, n_row, seg_dev)
            both = moment_ref[:, at]
            active = jnp.where(lane + col * seg_dev < length, scale, 0.0)
            first = both * (basis_ref[0:1, at] * active)
            second = both * (basis_ref[1:2, at] * active)
            parts = jnp.concatenate([first, second], axis=0)
            high = parts.astype(jnp.bfloat16).astype(jnp.float32)
            table_ref[:, at] = jnp.concatenate([high, parts - high], axis=0).astype(jnp.bfloat16)
        return carry

    lax.fori_loop(0, n_row, table_step, 0, unroll=min(n_row, 8))

    def block_row(ref, chunk):
        block = group_ref[0, chunk]
        return jnp.concatenate([ref[:, block_part(block, col, n_row, seg_dev)] for col in range(n_col)], axis=1)

    def cubes_of(chunk):
        return jnp.concatenate(cube_halves(left_ref[aligned(chunk * CHUNK, CHUNK), :], block_row(right_ref, chunk)), axis=0)

    def step(k, carry):
        for part in range(0, GROUP, 2):
            chunk = k * GROUP + part
            tables = jnp.concatenate([block_row(table_ref, chunk), block_row(table_ref, chunk + 1)], axis=0)
            if keep:
                kept_copy(kept, chunk, out=False).wait()
                kept_copy(kept, chunk + 1, out=False).wait()
                cubes = cubes_ref[pl.ds(chunk, 2)].reshape(4 * CHUNK, n_col * seg_dev)
            else:
                cubes = jnp.concatenate([cubes_of(chunk), cubes_of(chunk + 1)], axis=0)
            both = dot_nt(tables, cubes)
            for half in range(2):
                mine = both[32 * half:32 * half + 32, 2 * CHUNK * half:2 * CHUNK * (half + 1)]
                total = mine[:, 0:CHUNK] + mine[:, CHUNK:2 * CHUNK]
                sums_ref[pl.ds(chunk + half, 16, stride=chunk_count), :] = total[0:16] + total[16:32]
        return carry

    lax.fori_loop(0, chunk_steps(group_ref), step, 0)
    sums = jnp.concatenate([sums_ref[0:6 * chunk_count], sums_ref[8 * chunk_count:14 * chunk_count]], axis=0)
    sums = jnp.concatenate(split3(sums), axis=1).astype(jnp.bfloat16)
    for tile in range(slot_ref.shape[1] // TILE):
        at = pl.ds(tile * TILE, TILE)
        slot = slot_ref[:, at]
        low = jnp.where(iota((CHUNK, TILE), 0) == slot % CHUNK, 1.0, 0.0).astype(jnp.bfloat16)
        high = jnp.where(iota((chunk_count, TILE), 0) == slot // CHUNK, 1.0, 0.0)
        found = dot(sums, jnp.concatenate([low, low, low], axis=0))
        for row in range(12):
            picked = found[row * chunk_count:(row + 1) * chunk_count] * high
            out_ref[row:row + 1, at] = jnp.sum(picked, axis=0, keepdims=True)


def final_kernel(stats_ref, known_ref, basis_own_ref, field_ref, points_ref, currents_ref, iron_ref):
    stats = jnp.sum(stats_ref[...], axis=0)
    known = known_ref[...]
    initial_norm, hessen_a, hessen_b = known[:, 0:1], known[:, 1:2], known[:, 2:3]
    hessen_c, hessen_d, normal_second = stats[:, 0:1], stats[:, 1:2], stats[:, 2:3]
    normal_first = hessen_a * hessen_a + hessen_b * hessen_b
    normal_cross = hessen_a * hessen_c + hessen_b * hessen_d
    target_first = initial_norm * hessen_a
    target_second = initial_norm * hessen_c
    determinant = normal_first * normal_second - normal_cross * normal_cross
    weight_first = (normal_second * target_first - normal_cross * target_second) / determinant
    weight_second = (normal_first * target_second - normal_cross * target_first) / determinant
    currents_ref[...] = weight_first * basis_own_ref[0:1, :] + weight_second * basis_own_ref[1:2, :]
    moments = weight_first * field_ref[0:6, :] + weight_second * field_ref[6:12, :]
    points = points_ref[...] - 0.5
    px, py, pz = points[0:1], points[1:2], points[2:3]
    iron_ref[0:1, :] = pz * moments[1:2] - py * moments[2:3] - moments[3:4]
    iron_ref[1:2, :] = px * moments[2:3] - pz * moments[0:1] - moments[4:5]
    iron_ref[2:3, :] = py * moments[0:1] - px * moments[1:2] - moments[5:6]


def shape(*sizes, dtype=jnp.float32):
    return jax.ShapeDtypeStruct(sizes, dtype)


def shards(drive, resist, centers, tangents, iron_points, owner, range_len):
    seg_dev = drive.shape[0]
    col_len = centers.shape[1]
    n_col = lax.axis_size("col")
    n_row = lax.axis_size("row")
    n_dev = n_col * n_row
    segments = seg_dev * n_dev
    width = n_col * seg_dev
    points_count = iron_points.shape[1]
    coupling = 0.5 / math.sqrt(segments)
    call = functools.partial(pl.pallas_call, compiler_params=pltpu.CompilerParams(vmem_limit_bytes=VMEM_LIMIT))
    scratch = [pltpu.VMEM((1, segments), jnp.float32), pltpu.VMEM((seg_dev, 128), jnp.float32)]
    hbm = pl.BlockSpec(memory_space=pltpu.HBM)
    smem = pl.BlockSpec(memory_space=pltpu.SMEM)
    vmem = pl.BlockSpec(memory_space=pltpu.VMEM)

    def work(microseconds):
        return pl.CostEstimate(flops=int(microseconds * 1e9), bytes_accessed=0, transcendentals=0)

    def roomy(row_bytes):
        return STREAM_BYTES // row_bytes

    def exchange(x):
        return lax.all_to_all(x, AXES, 0, 0, tiled=True)

    spread, geometry = pl.pallas_call(
        entry_kernel,
        out_shape=(shape(n_dev, 1, seg_dev), shape(6, col_len)),
        in_specs=[hbm] * 3,
        scratch_shapes=[
            pltpu.VMEM((1, seg_dev), jnp.float32),
            pltpu.VMEM((3, col_len), jnp.float32),
            pltpu.VMEM((3, col_len), jnp.float32),
            pltpu.SemaphoreType.DMA((3,)),
        ],
        compiler_params=pltpu.CompilerParams(vmem_limit_bytes=ENTRY_LIMIT),
        name="entry",
    )(drive[None, :], centers, tangents)
    drive_all = exchange(spread).reshape(1, segments)
    pieces = [
        lax.ppermute(geometry, "col", [(k, (k + shift) % n_col) for k in range(n_col)]) for shift in range(1, n_col)
    ]

    chunk_count = points_count // CHUNK + n_row * (CHUNK - 1) // CHUNK
    chunk_count = -(-chunk_count // 8) * 8
    slot, group_table, left, drive_own, resist_own, own_geometry = call(
        functools.partial(group_kernel, n_row=n_row),
        out_shape=(
            shape(1, points_count, dtype=jnp.int32),
            shape(8, 128, dtype=jnp.int32),
            shape(chunk_count * CHUNK, 48, dtype=jnp.bfloat16),
            shape(1, seg_dev),
            shape(1, seg_dev),
            shape(6, col_len),
        ),
        scratch_shapes=[pltpu.VMEM((48 * chunk_count, CHUNK), jnp.float32)],
        cost_estimate=work(3),
        name="group_points",
    )(owner.reshape(1, points_count), iron_points, drive[None, :], resist[None, :], centers, tangents)
    pieces = [own_geometry] + pieces

    cube_shape = (chunk_count, 2 * CHUNK, width)
    keep = 2 * math.prod(cube_shape) <= KEEP_BYTES
    stream = functools.partial(
        pl.pallas_call, compiler_params=pltpu.CompilerParams(vmem_limit_bytes=STREAM_LIMIT if keep else VMEM_LIMIT)
    )
    sides = call(
        functools.partial(sides_kernel, n_col=n_col),
        out_shape=(
            shape(48, segments, dtype=jnp.bfloat16), shape(8, segments),
            shape(seg_dev, 48, dtype=jnp.bfloat16), shape(3, seg_dev, 128),
        ),
        cost_estimate=work(1),
        name="sides",
    )(*pieces)
    right, moment = sides[0:2]
    image_own, image_spread = call(
        functools.partial(first_kernel, coupling),
        out_shape=(shape(1, seg_dev), shape(n_dev, 1, seg_dev)),
        scratch_shapes=scratch,
        cost_estimate=work(3),
        name="first_image",
    )(drive_all, drive_own, resist_own, group_table, *sides)
    image_all = exchange(image_spread).reshape(1, segments)
    cube_scratch = [pltpu.VMEM(cube_shape, jnp.bfloat16), pltpu.SemaphoreType.DMA((chunk_count,))]
    if keep:
        cubes, after = stream(
            functools.partial(weigh_kernel, n_row=n_row, n_col=n_col),
            out_shape=(shape(roomy(4 * CHUNK * width), *cube_shape[1:], dtype=jnp.bfloat16), shape(8, 128)),
            in_specs=[smem, vmem, vmem],
            out_specs=(hbm, vmem),
            scratch_shapes=cube_scratch,
            cost_estimate=work(5),
            name="weigh",
        )(group_table, left, right)
    else:
        after = group_table
    basis, basis_own, stats, known = call(
        functools.partial(second_kernel, coupling),
        out_shape=(shape(2, segments), shape(2, seg_dev), shape(n_dev, 1, 128), shape(1, 128)),
        scratch_shapes=scratch,
        cost_estimate=work(3),
        name="second_image",
    )(drive_all, image_all, drive_own, image_own, resist_own, after, *sides)
    stats_all = exchange(stats)

    field = stream(
        functools.partial(field_kernel, n_row=n_row, n_col=n_col, keep=keep),
        out_shape=shape(12, points_count),
        in_specs=[smem, smem, vmem, vmem, vmem] + ([hbm] if keep else [vmem, vmem]),
        scratch_shapes=[
            pltpu.VMEM((32, segments), jnp.bfloat16),
            pltpu.VMEM((16 * chunk_count, CHUNK), jnp.float32),
        ] + (cube_scratch if keep else []),
        cost_estimate=work(6),
        name="block_field",
    )(group_table, range_len, slot, moment, basis, *([cubes] if keep else [left, right]))
    currents, iron_field = stream(
        final_kernel,
        out_shape=(shape(1, seg_dev), shape(3, points_count)),
        name="combine",
    )(stats_all, known, basis_own, field, iron_points)
    return (currents[0], iron_field)


def solution(mesh):
    return jax.shard_map(
        shards,
        mesh=mesh,
        in_specs=(
            P(AXES),
            P(AXES),
            P(None, "col"),
            P(None, "col"),
            P(None, AXES),
            P(AXES, None),
            P(),
        ),
        out_specs=(P(AXES), P(None, AXES)),
        check_vma=False,
    )
```

```python
import functools
import math

import jax
import jax.numpy as jnp
from jax import lax
from jax.experimental import pallas as pl
from jax.experimental.pallas import tpu as pltpu
from jax.sharding import PartitionSpec as P

EPS_SEG = 0.0004
EPS_FIELD = 0.0025
AXES = ("col", "row")
CHUNK = 128
GROUP = 4
TILE = 512
COLUMNS = 256
ROWS = 64
KEEP_BYTES = 16 * 1024 * 1024
VMEM_LIMIT = 32 * 1024 * 1024
STREAM_LIMIT = 44 * 1024 * 1024
STREAM_BYTES = 20 * 1024 * 1024
ENTRY_LIMIT = 60 * 1024 * 1024


def split3(x):
    high = x.astype(jnp.bfloat16).astype(jnp.float32)
    rest = x - high
    middle = rest.astype(jnp.bfloat16).astype(jnp.float32)
    low = (rest - middle).astype(jnp.bfloat16).astype(jnp.float32)
    return high, middle, low


def left_parts(x):
    high, middle, low = split3(x)
    return jnp.concatenate([high, high, middle, middle, high, low], axis=0)


def right_parts(x):
    high, middle, low = split3(x)
    return jnp.concatenate([high, middle, high, middle, low, high], axis=0).astype(jnp.bfloat16)


def rows8(*rows):
    width = rows[0].shape[1]
    count = sum(r.shape[0] for r in rows)
    if count < 8:
        rows = rows + (jnp.zeros((8 - count, width), jnp.float32),)
    return jnp.concatenate(rows, axis=0)


def left_center(c, eps):
    square = jnp.sum(c * c, axis=0, keepdims=True)
    return rows8(-2.0 * c, jnp.ones_like(square), square + eps)


def right_center(c):
    square = jnp.sum(c * c, axis=0, keepdims=True)
    return rows8(c, square, jnp.ones_like(square))


def dot(a, b):
    return jnp.dot(a, b, preferred_element_type=jnp.float32)


def dot_nt(a, b):
    return lax.dot_general(a, b, (((1,), (1,)), ((), ())), preferred_element_type=jnp.float32)


def transposed(x):
    return x.T.astype(jnp.bfloat16)


def iota(shape, axis):
    return lax.broadcasted_iota(jnp.int32, shape, axis)


def aligned(start, size):
    return pl.ds(pl.multiple_of(start, size), size)


def sides_kernel(*refs, n_col):
    pieces, (right_ref, moment_ref, left_ref, along_ref) = refs[:n_col], refs[n_col:]
    length = right_ref.shape[1] // n_col
    seg_dev = left_ref.shape[1]
    own_at = aligned(lax.axis_index("row") * seg_dev, seg_dev)
    tangent = rows8(pieces[0][3:6, own_at])
    left_ref[0] = transposed(left_parts(left_center(pieces[0][0:3, own_at] - 0.5, EPS_SEG)))
    left_ref[1] = transposed(left_parts(tangent))
    tangent = tangent.T
    for k in range(3):
        along_ref[k] = jnp.broadcast_to(tangent[:, k:k + 1], (seg_dev, 128))
    for shift, piece in enumerate(pieces):
        col = lax.rem(lax.axis_index("col") + n_col - shift, n_col)

        def step(k, carry):
            geo = piece[0:6, aligned(k * TILE, TILE)]
            to = pl.ds(pl.multiple_of(col * length + k * TILE, TILE), TILE)
            center, tangent = geo[0:3] - 0.5, geo[3:6]
            cross = jnp.concatenate([
                tangent[1:2] * center[2:3] - tangent[2:3] * center[1:2],
                tangent[2:3] * center[0:1] - tangent[0:1] * center[2:3],
                tangent[0:1] * center[1:2] - tangent[1:2] * center[0:1],
            ], axis=0)
            right_ref[:, to] = right_parts(right_center(center))
            moment_ref[:, to] = rows8(tangent, cross)
            return carry

        lax.fori_loop(0, length // TILE, step, 0, unroll=4)


def couple(right_ref, moment_ref, left_ref, along_ref, vec_ref, acc_ref):
    acc_ref[...] = jnp.zeros_like(acc_ref)

    def step(k, carry):
        at = aligned(k * TILE, TILE)
        turned = moment_ref[0:3, at] * vec_ref[:, at]
        right = right_ref[:, at]
        for first in range(0, TILE, COLUMNS):
            columns = slice(first, first + COLUMNS)
            by_product = first % (2 * COLUMNS) == 0
            if by_product:
                turned_parts = right_parts(rows8(turned[:, columns]))
            for row in range(0, acc_ref.shape[0], ROWS):
                rows = slice(row, row + ROWS)
                inverse = lax.rsqrt(dot(left_ref[0, rows], right[:, columns]))
                total = acc_ref[rows]
                if by_product:
                    pair = dot(left_ref[1, rows], turned_parts) * inverse
                    for start in range(0, COLUMNS, 128):
                        total = total + pair[:, start:start + 128]
                else:
                    for start in range(0, COLUMNS, 128):
                        lanes = slice(first + start, first + start + 128)
                        along = along_ref[0, rows] * turned[0:1, lanes]
                        along = along + along_ref[1, rows] * turned[1:2, lanes]
                        along = along + along_ref[2, rows] * turned[2:3, lanes]
                        total = total + along * inverse[:, start:start + 128]
                acc_ref[rows] = total
        return carry

    lax.fori_loop(0, vec_ref.shape[1] // TILE, step, 0, unroll=4)
    return jnp.sum(acc_ref[...].T, axis=0, keepdims=True)


def kept_copy(kept, index, out):
    local, remote, sems = kept
    if out:
        return pltpu.make_async_copy(local.at[index], remote.at[index], sems.at[index])
    return pltpu.make_async_copy(remote.at[index], local.at[index], sems.at[index])


def spread_rows(ref, row):
    for k in range(ref.shape[0]):
        ref[k] = row


def pack_kernel(centers_hbm, tangents_hbm, geo_ref, centers, tangents, sems):
    pairs = ((centers_hbm, centers), (tangents_hbm, tangents))
    copies = [pltpu.make_async_copy(source, target, sems.at[k]) for k, (source, target) in enumerate(pairs)]
    for copy in copies:
        copy.start()
    for copy in copies:
        copy.wait()
    geo_ref[0:3] = centers[...]
    geo_ref[3:6] = tangents[...]


def own_rows(bundle_ref, like_ref):
    seg_dev = like_ref.shape[1]
    return bundle_ref[10:11, 0:seg_dev], bundle_ref[10:11, seg_dev:2 * seg_dev]


def first_kernel(coupling, drive_ref, bundle_ref, after_ref, right_ref, moment_ref, left_ref, along_ref,
                 image_ref, spread_ref, vec_ref, acc_ref):
    drive = drive_ref[...]
    scale = 1.0 / jnp.sqrt(jnp.sum(drive * drive, keepdims=True))
    vec_ref[...] = drive * scale
    product = couple(right_ref, moment_ref, left_ref, along_ref, vec_ref, acc_ref)
    drive_own, resist_own = own_rows(bundle_ref, image_ref)
    image = resist_own * (drive_own * scale) + coupling * product
    image_ref[...] = image
    spread_rows(spread_ref, image)


def second_kernel(coupling, drive_ref, image_ref, image_own_ref, bundle_ref, after_ref,
                  right_ref, moment_ref, left_ref, along_ref,
                  basis_ref, basis_own_ref, stats_ref, known_ref, vec_ref, acc_ref):
    drive = drive_ref[...]
    norm = jnp.sqrt(jnp.sum(drive * drive, keepdims=True))
    scale = 1.0 / norm
    basis_a = drive * scale
    image = image_ref[...]
    hessen_a = jnp.sum(image * basis_a, keepdims=True)
    rest = image - hessen_a * basis_a
    hessen_b = jnp.sqrt(jnp.sum(rest * rest, keepdims=True))
    inverse = 1.0 / hessen_b
    basis_b = rest * inverse
    vec_ref[...] = basis_b
    basis_ref[0:1, :] = basis_a
    basis_ref[1:2, :] = basis_b
    drive_own, resist_own = own_rows(bundle_ref, image_own_ref)
    own_a = drive_own * scale
    own_b = (image_own_ref[...] - hessen_a * own_a) * inverse
    basis_own_ref[0:1, :] = own_a
    basis_own_ref[1:2, :] = own_b
    product = couple(right_ref, moment_ref, left_ref, along_ref, vec_ref, acc_ref)
    second = resist_own * own_b + coupling * product
    lane = iota((1, 128), 1)

    def three(a, b, c):
        return jnp.where(lane == 0, a, jnp.where(lane == 1, b, jnp.where(lane == 2, c, 0.0)))

    spread_rows(stats_ref, three(
        jnp.sum(second * own_a, keepdims=True),
        jnp.sum(second * own_b, keepdims=True),
        jnp.sum(second * second, keepdims=True),
    ))
    known_ref[...] = three(norm, hessen_a, hessen_b)


def group_kernel(bundle_ref, slot_ref, table_ref, left_ref, planes_ref, *, n_row):
    points = slot_ref.shape[1]
    chunk_count = left_ref.shape[0] // CHUNK
    owner = bundle_ref[9:10, 0:points].astype(jnp.int32)
    rows = max(8, n_row)
    marks = jnp.where(iota((rows, points), 0) == owner, 1.0, 0.0)
    tile = 256
    upper = jnp.where(iota((tile, tile), 0) <= iota((tile, tile), 1), 1.0, 0.0).astype(jnp.bfloat16)
    before = jnp.zeros((rows, 1), jnp.float32)
    ranks = []
    for piece in range(points // tile):
        part = dot(marks[:, piece * tile:(piece + 1) * tile].astype(jnp.bfloat16), upper)
        ranks.append(part + before - 1.0)
        before = before + part[:, tile - 1:tile]
    ranks = jnp.concatenate(ranks, axis=1)
    chunks = jnp.floor((before + (CHUNK - 1)) * (1.0 / CHUNK))
    start = jnp.zeros((1, 1), jnp.float32)
    starts = []
    for name in range(rows):
        starts.append(start)
        start = start + chunks[name:name + 1]
    starts = jnp.concatenate(starts, axis=0)
    slot = jnp.sum(marks * (ranks + starts * CHUNK), axis=0, keepdims=True).astype(jnp.int32)
    slot_ref[...] = slot
    lane = iota((rows, 128), 1)
    ended = jnp.sum(jnp.where(starts + chunks <= lane.astype(jnp.float32), 1.0, 0.0), axis=0, keepdims=True)
    block = jnp.minimum(ended, n_row - 1.0)
    place = iota((8, 128), 0)
    table_ref[...] = jnp.where(place == 0, block, start).astype(jnp.int32)
    high = jnp.where(iota((chunk_count, points), 0) == slot // CHUNK, 1.0, 0.0)
    low = jnp.where(iota((CHUNK, points), 0) == slot % CHUNK, 1.0, 0.0).astype(jnp.bfloat16)
    parts = split3(bundle_ref[6:9, 0:points] - 0.5)
    spread = jnp.concatenate([high * part[k:k + 1] for k in range(3) for part in parts], axis=0).astype(jnp.bfloat16)
    placed = dot_nt(spread, low)
    planes = [placed[k * chunk_count:(k + 1) * chunk_count] for k in range(9)]
    x, y, z = (planes[3 * k] + planes[3 * k + 1] + planes[3 * k + 2] for k in range(3))
    sides = [-2.0 * x, -2.0 * y, -2.0 * z, jnp.ones_like(x), x * x + y * y + z * z + EPS_FIELD]
    sides = [split3(side) for side in sides]
    empty = jnp.zeros_like(x)
    for group, part in enumerate([0, 0, 1, 1, 0, 2]):
        for k in range(8):
            to = pl.ds((group * 8 + k) * chunk_count, chunk_count)
            planes_ref[to, :] = sides[k][part] if k < 5 else empty
    for chunk in range(chunk_count):
        left_ref[chunk * CHUNK:(chunk + 1) * CHUNK, :] = transposed(planes_ref[pl.ds(chunk, 48, stride=chunk_count), :])


def cube_halves(left, right):
    inverse = lax.rsqrt(dot(left, right))
    cube = inverse * inverse * inverse
    high = cube.astype(jnp.bfloat16)
    return high, (cube - high.astype(jnp.float32)).astype(jnp.bfloat16)


def block_part(block, col, n_row, seg_dev):
    return aligned((col * n_row + block) * seg_dev, seg_dev)


def chunk_steps(group_ref):
    return (group_ref[1, 0] + GROUP - 1) // GROUP


def weigh_kernel(group_ref, left_ref, right_ref, cubes_hbm, done_ref, cubes_ref, sems, *, n_row, n_col):
    seg_dev = right_ref.shape[1] // (n_row * n_col)
    done_ref[...] = jnp.zeros_like(done_ref)
    kept = (cubes_ref, cubes_hbm, sems)

    def step(k, carry):
        for part in range(GROUP):
            chunk = k * GROUP + part
            left = left_ref[aligned(chunk * CHUNK, CHUNK), :]
            for col in range(n_col):
                to = slice(col * seg_dev, (col + 1) * seg_dev)
                high, low = cube_halves(left, right_ref[:, block_part(group_ref[0, chunk], col, n_row, seg_dev)])
                cubes_ref[chunk, 0:CHUNK, to] = high
                cubes_ref[chunk, CHUNK:2 * CHUNK, to] = low
            kept_copy(kept, chunk, out=True).start()
        return carry

    def finish(k, carry):
        for part in range(GROUP):
            kept_copy(kept, k * GROUP + part, out=True).wait()
        return carry

    lax.fori_loop(0, chunk_steps(group_ref), step, 0)
    lax.fori_loop(0, chunk_steps(group_ref), finish, 0)


def field_kernel(group_ref, length_ref, slot_ref, moment_ref, basis_ref, *refs, n_row, n_col, keep):
    if keep:
        cubes_hbm, out_ref, table_ref, sums_ref, cubes_ref, sems = refs
        kept = (cubes_ref, cubes_hbm, sems)

        def begin(k, carry):
            for part in range(GROUP):
                kept_copy(kept, k * GROUP + part, out=False).start()
            return carry

        lax.fori_loop(0, chunk_steps(group_ref), begin, 0)
    else:
        left_ref, right_ref, out_ref, table_ref, sums_ref = refs
    chunk_count = sums_ref.shape[0] // 16
    seg_dev = moment_ref.shape[1] // (n_row * n_col)
    scale = 1.0 / math.sqrt(n_col * seg_dev)
    lane = iota((1, seg_dev), 1)
    sums_ref[...] = jnp.zeros_like(sums_ref)

    def table_step(block, carry):
        length = length_ref[block]
        for col in range(n_col):
            at = block_part(block, col, n_row, seg_dev)
            both = moment_ref[:, at]
            active = jnp.where(lane + col * seg_dev < length, scale, 0.0)
            first = both * (basis_ref[0:1, at] * active)
            second = both * (basis_ref[1:2, at] * active)
            parts = jnp.concatenate([first, second], axis=0)
            high = parts.astype(jnp.bfloat16).astype(jnp.float32)
            table_ref[:, at] = jnp.concatenate([high, parts - high], axis=0).astype(jnp.bfloat16)
        return carry

    lax.fori_loop(0, n_row, table_step, 0, unroll=min(n_row, 8))

    def block_row(ref, chunk):
        block = group_ref[0, chunk]
        return jnp.concatenate([ref[:, block_part(block, col, n_row, seg_dev)] for col in range(n_col)], axis=1)

    def cubes_of(chunk):
        return jnp.concatenate(cube_halves(left_ref[aligned(chunk * CHUNK, CHUNK), :], block_row(right_ref, chunk)), axis=0)

    def step(k, carry):
        for part in range(0, GROUP, 2):
            chunk = k * GROUP + part
            tables = jnp.concatenate([block_row(table_ref, chunk), block_row(table_ref, chunk + 1)], axis=0)
            if keep:
                kept_copy(kept, chunk, out=False).wait()
                kept_copy(kept, chunk + 1, out=False).wait()
                cubes = cubes_ref[pl.ds(chunk, 2)].reshape(4 * CHUNK, n_col * seg_dev)
            else:
                cubes = jnp.concatenate([cubes_of(chunk), cubes_of(chunk + 1)], axis=0)
            both = dot_nt(tables, cubes)
            for half in range(2):
                mine = both[32 * half:32 * half + 32, 2 * CHUNK * half:2 * CHUNK * (half + 1)]
                total = mine[:, 0:CHUNK] + mine[:, CHUNK:2 * CHUNK]
                sums_ref[pl.ds(chunk + half, 16, stride=chunk_count), :] = total[0:16] + total[16:32]
        return carry

    lax.fori_loop(0, chunk_steps(group_ref), step, 0)
    sums = jnp.concatenate([sums_ref[0:6 * chunk_count], sums_ref[8 * chunk_count:14 * chunk_count]], axis=0)
    sums = jnp.concatenate(split3(sums), axis=1).astype(jnp.bfloat16)
    for tile in range(slot_ref.shape[1] // TILE):
        at = pl.ds(tile * TILE, TILE)
        slot = slot_ref[:, at]
        low = jnp.where(iota((CHUNK, TILE), 0) == slot % CHUNK, 1.0, 0.0).astype(jnp.bfloat16)
        high = jnp.where(iota((chunk_count, TILE), 0) == slot // CHUNK, 1.0, 0.0)
        found = dot(sums, jnp.concatenate([low, low, low], axis=0))
        for row in range(12):
            picked = found[row * chunk_count:(row + 1) * chunk_count] * high
            out_ref[row:row + 1, at] = jnp.sum(picked, axis=0, keepdims=True)


def final_kernel(stats_ref, known_ref, basis_own_ref, field_ref, bundle_ref, currents_ref, iron_ref):
    stats = jnp.sum(stats_ref[...], axis=0)
    known = known_ref[...]
    initial_norm, hessen_a, hessen_b = known[:, 0:1], known[:, 1:2], known[:, 2:3]
    hessen_c, hessen_d, normal_second = stats[:, 0:1], stats[:, 1:2], stats[:, 2:3]
    normal_first = hessen_a * hessen_a + hessen_b * hessen_b
    normal_cross = hessen_a * hessen_c + hessen_b * hessen_d
    target_first = initial_norm * hessen_a
    target_second = initial_norm * hessen_c
    determinant = normal_first * normal_second - normal_cross * normal_cross
    weight_first = (normal_second * target_first - normal_cross * target_second) / determinant
    weight_second = (normal_first * target_second - normal_cross * target_first) / determinant
    currents_ref[...] = weight_first * basis_own_ref[0:1, :] + weight_second * basis_own_ref[1:2, :]
    moments = weight_first * field_ref[0:6, :] + weight_second * field_ref[6:12, :]
    points = bundle_ref[6:9, 0:iron_ref.shape[1]] - 0.5
    px, py, pz = points[0:1], points[1:2], points[2:3]
    iron_ref[0:1, :] = pz * moments[1:2] - py * moments[2:3] - moments[3:4]
    iron_ref[1:2, :] = px * moments[2:3] - pz * moments[0:1] - moments[4:5]
    iron_ref[2:3, :] = py * moments[0:1] - px * moments[1:2] - moments[5:6]


def shape(*sizes, dtype=jnp.float32):
    return jax.ShapeDtypeStruct(sizes, dtype)


def shards(drive, resist, centers, tangents, iron_points, owner, range_len):
    seg_dev = drive.shape[0]
    col_len = centers.shape[1]
    n_col = lax.axis_size("col")
    n_row = lax.axis_size("row")
    n_dev = n_col * n_row
    segments = seg_dev * n_dev
    width = n_col * seg_dev
    points_count = iron_points.shape[1]
    coupling = 0.5 / math.sqrt(segments)
    call = functools.partial(pl.pallas_call, compiler_params=pltpu.CompilerParams(vmem_limit_bytes=VMEM_LIMIT))
    scratch = [pltpu.VMEM((1, segments), jnp.float32), pltpu.VMEM((seg_dev, 128), jnp.float32)]
    hbm = pl.BlockSpec(memory_space=pltpu.HBM)
    smem = pl.BlockSpec(memory_space=pltpu.SMEM)
    vmem = pl.BlockSpec(memory_space=pltpu.VMEM)

    def work(microseconds):
        return pl.CostEstimate(flops=int(microseconds * 1e9), bytes_accessed=0, transcendentals=0)

    def roomy(row_bytes):
        return STREAM_BYTES // row_bytes

    def exchange(x):
        return lax.all_to_all(x, AXES, 0, 0, tiled=True)

    drive_all = exchange(jnp.broadcast_to(drive[None, None, :], (n_dev, 1, seg_dev))).reshape(1, segments)
    geometry = pl.pallas_call(
        pack_kernel,
        out_shape=shape(6, col_len),
        in_specs=[hbm] * 2,
        scratch_shapes=[
            pltpu.VMEM((3, col_len), jnp.float32),
            pltpu.VMEM((3, col_len), jnp.float32),
            pltpu.SemaphoreType.DMA((2,)),
        ],
        compiler_params=pltpu.CompilerParams(vmem_limit_bytes=ENTRY_LIMIT),
        cost_estimate=work(8),
        name="pack",
    )(centers, tangents)
    longest = max(col_len, points_count, 2 * seg_dev)

    def wide(row):
        return jnp.pad(row, ((0, 0), (0, longest - row.shape[1])))

    bundle = jnp.concatenate([
        wide(centers), wide(tangents), wide(iron_points), wide(owner.reshape(1, points_count).astype(jnp.float32)),
        wide(jnp.concatenate([drive, resist])[None, :]),
    ], axis=0)
    pieces = [bundle] + [
        lax.ppermute(geometry, "col", [(k, (k + shift) % n_col) for k in range(n_col)]) for shift in range(1, n_col)
    ]

    chunk_count = points_count // CHUNK + n_row * (CHUNK - 1) // CHUNK
    chunk_count = -(-chunk_count // 8) * 8
    slot, group_table, left = call(
        functools.partial(group_kernel, n_row=n_row),
        out_shape=(
            shape(1, points_count, dtype=jnp.int32),
            shape(8, 128, dtype=jnp.int32),
            shape(chunk_count * CHUNK, 48, dtype=jnp.bfloat16),
        ),
        scratch_shapes=[pltpu.VMEM((48 * chunk_count, CHUNK), jnp.float32)],
        cost_estimate=work(3),
        name="group_points",
    )(bundle)

    cube_shape = (chunk_count, 2 * CHUNK, width)
    keep = 2 * math.prod(cube_shape) <= KEEP_BYTES
    stream = functools.partial(
        pl.pallas_call, compiler_params=pltpu.CompilerParams(vmem_limit_bytes=STREAM_LIMIT if keep else VMEM_LIMIT)
    )
    sides = call(
        functools.partial(sides_kernel, n_col=n_col),
        out_shape=(
            shape(48, segments, dtype=jnp.bfloat16), shape(8, segments),
            shape(2, seg_dev, 48, dtype=jnp.bfloat16), shape(3, seg_dev, 128),
        ),
        cost_estimate=work(1),
        name="sides",
    )(*pieces)
    right, moment = sides[0:2]
    image_own, image_spread = call(
        functools.partial(first_kernel, coupling),
        out_shape=(shape(1, seg_dev), shape(n_dev, 1, seg_dev)),
        scratch_shapes=scratch,
        cost_estimate=work(3),
        name="first_image",
    )(drive_all, bundle, group_table, *sides)
    image_all = exchange(image_spread).reshape(1, segments)
    cube_scratch = [pltpu.VMEM(cube_shape, jnp.bfloat16), pltpu.SemaphoreType.DMA((chunk_count,))]
    if keep:
        cubes, after = stream(
            functools.partial(weigh_kernel, n_row=n_row, n_col=n_col),
            out_shape=(shape(roomy(4 * CHUNK * width), *cube_shape[1:], dtype=jnp.bfloat16), shape(8, 128)),
            in_specs=[smem, vmem, vmem],
            out_specs=(hbm, vmem),
            scratch_shapes=cube_scratch,
            cost_estimate=work(5),
            name="weigh",
        )(group_table, left, right)
    else:
        after = group_table
    basis, basis_own, stats, known = call(
        functools.partial(second_kernel, coupling),
        out_shape=(shape(2, segments), shape(2, seg_dev), shape(n_dev, 1, 128), shape(1, 128)),
        scratch_shapes=scratch,
        cost_estimate=work(3),
        name="second_image",
    )(drive_all, image_all, image_own, bundle, after, *sides)
    stats_all = exchange(stats)

    field = stream(
        functools.partial(field_kernel, n_row=n_row, n_col=n_col, keep=keep),
        out_shape=shape(12, points_count),
        in_specs=[smem, smem, vmem, vmem, vmem] + ([hbm] if keep else [vmem, vmem]),
        scratch_shapes=[
            pltpu.VMEM((32, segments), jnp.bfloat16),
            pltpu.VMEM((16 * chunk_count, CHUNK), jnp.float32),
        ] + (cube_scratch if keep else []),
        cost_estimate=work(6),
        name="block_field",
    )(group_table, range_len, slot, moment, basis, *([cubes] if keep else [left, right]))
    currents, iron_field = stream(
        final_kernel,
        out_shape=(shape(1, seg_dev), shape(3, points_count)),
        name="combine",
    )(stats_all, known, basis_own, field, bundle)
    return (currents[0], iron_field)


def solution(mesh):
    return jax.shard_map(
        shards,
        mesh=mesh,
        in_specs=(
            P(AXES),
            P(AXES),
            P(None, "col"),
            P(None, "col"),
            P(None, AXES),
            P(AXES, None),
            P(),
        ),
        out_specs=(P(AXES), P(None, AXES)),
        check_vma=False,
    )
```

```python
import functools
import math

import jax
import jax.numpy as jnp
from jax import lax
from jax.experimental import pallas as pl
from jax.experimental.pallas import tpu as pltpu
from jax.sharding import PartitionSpec as P

EPS_SEG = 0.0004
EPS_FIELD = 0.0025
AXES = ("col", "row")
CHUNK = 128
GROUP = 4
TILE = 512
COLUMNS = 256
ROWS = 64
KEEP_BYTES = 16 * 1024 * 1024
VMEM_LIMIT = 32 * 1024 * 1024
STREAM_LIMIT = 44 * 1024 * 1024
STREAM_BYTES = 20 * 1024 * 1024
ENTRY_LIMIT = 60 * 1024 * 1024


def split3(x):
    high = x.astype(jnp.bfloat16).astype(jnp.float32)
    rest = x - high
    middle = rest.astype(jnp.bfloat16).astype(jnp.float32)
    low = (rest - middle).astype(jnp.bfloat16).astype(jnp.float32)
    return high, middle, low


def left_parts(x):
    high, middle, low = split3(x)
    return jnp.concatenate([high, high, middle, middle, high, low], axis=0)


def right_parts(x):
    high, middle, low = split3(x)
    return jnp.concatenate([high, middle, high, middle, low, high], axis=0).astype(jnp.bfloat16)


def rows8(*rows):
    width = rows[0].shape[1]
    count = sum(r.shape[0] for r in rows)
    if count < 8:
        rows = rows + (jnp.zeros((8 - count, width), jnp.float32),)
    return jnp.concatenate(rows, axis=0)


def left_center(c, eps):
    square = jnp.sum(c * c, axis=0, keepdims=True)
    return rows8(-2.0 * c, jnp.ones_like(square), square + eps)


def right_center(c):
    square = jnp.sum(c * c, axis=0, keepdims=True)
    return rows8(c, square, jnp.ones_like(square))


def dot(a, b):
    return jnp.dot(a, b, preferred_element_type=jnp.float32)


def dot_nt(a, b):
    return lax.dot_general(a, b, (((1,), (1,)), ((), ())), preferred_element_type=jnp.float32)


def transposed(x):
    return x.T.astype(jnp.bfloat16)


def iota(shape, axis):
    return lax.broadcasted_iota(jnp.int32, shape, axis)


def aligned(start, size):
    return pl.ds(pl.multiple_of(start, size), size)


def make_sides(gathered_ref, vec_ref, right_ref, moment_ref, left_ref, along_ref):
    seg_dev = left_ref.shape[1]
    own = gathered_ref[lax.axis_index("col") * lax.axis_size("row") + lax.axis_index("row")]
    tangent = rows8(own[3:6])
    left_ref[0] = transposed(left_parts(left_center(own[0:3] - 0.5, EPS_SEG)))
    left_ref[1] = transposed(left_parts(tangent))
    tangent = tangent.T
    for k in range(3):
        along_ref[k] = jnp.broadcast_to(tangent[:, k:k + 1], (seg_dev, 128))

    def step(k, carry):
        to = aligned(k * seg_dev, seg_dev)
        geo = gathered_ref[k]
        center, tangent = geo[0:3] - 0.5, geo[3:6]
        cross = jnp.concatenate([
            tangent[1:2] * center[2:3] - tangent[2:3] * center[1:2],
            tangent[2:3] * center[0:1] - tangent[0:1] * center[2:3],
            tangent[0:1] * center[1:2] - tangent[1:2] * center[0:1],
        ], axis=0)
        right_ref[:, to] = right_parts(right_center(center))
        moment_ref[:, to] = rows8(tangent, cross)
        vec_ref[:, to] = geo[6:7]
        return carry

    lax.fori_loop(0, gathered_ref.shape[0], step, 0, unroll=8)
    return own[6:7]


def couple(right_ref, moment_ref, left_ref, along_ref, vec_ref, acc_ref):
    acc_ref[...] = jnp.zeros_like(acc_ref)

    def step(k, carry):
        at = aligned(k * TILE, TILE)
        turned = moment_ref[0:3, at] * vec_ref[:, at]
        right = right_ref[:, at]
        for first in range(0, TILE, COLUMNS):
            columns = slice(first, first + COLUMNS)
            by_product = first % (2 * COLUMNS) == 0
            if by_product:
                turned_parts = right_parts(rows8(turned[:, columns]))
            for row in range(0, acc_ref.shape[0], ROWS):
                rows = slice(row, row + ROWS)
                inverse = lax.rsqrt(dot(left_ref[0, rows], right[:, columns]))
                total = acc_ref[rows]
                if by_product:
                    pair = dot(left_ref[1, rows], turned_parts) * inverse
                    for start in range(0, COLUMNS, 128):
                        total = total + pair[:, start:start + 128]
                else:
                    for start in range(0, COLUMNS, 128):
                        lanes = slice(first + start, first + start + 128)
                        along = along_ref[0, rows] * turned[0:1, lanes]
                        along = along + along_ref[1, rows] * turned[1:2, lanes]
                        along = along + along_ref[2, rows] * turned[2:3, lanes]
                        total = total + along * inverse[:, start:start + 128]
                acc_ref[rows] = total
        return carry

    lax.fori_loop(0, vec_ref.shape[1] // TILE, step, 0, unroll=4)
    return jnp.sum(acc_ref[...].T, axis=0, keepdims=True)


def kept_copy(kept, index, out):
    local, remote, sems = kept
    if out:
        return pltpu.make_async_copy(local.at[index], remote.at[index], sems.at[index])
    return pltpu.make_async_copy(remote.at[index], local.at[index], sems.at[index])


def spread_rows(ref, row):
    for k in range(ref.shape[0]):
        ref[k] = row


def pack_kernel(drive_hbm, centers_hbm, tangents_hbm, out_ref, drive, centers, tangents, sems):
    pairs = ((drive_hbm, drive), (centers_hbm, centers), (tangents_hbm, tangents))
    copies = [pltpu.make_async_copy(source, target, sems.at[k]) for k, (source, target) in enumerate(pairs)]
    for copy in copies:
        copy.start()
    for copy in copies:
        copy.wait()
    seg_dev = drive.shape[1]
    at = aligned(lax.axis_index("row") * seg_dev, seg_dev)
    spread_rows(out_ref, rows8(centers[:, at], tangents[:, at], drive[...]))


def own_rows(bundle_ref, like_ref):
    seg_dev = like_ref.shape[1]
    return bundle_ref[4:5, 0:seg_dev], bundle_ref[4:5, seg_dev:2 * seg_dev]


def first_kernel(coupling, gathered_ref, bundle_ref, after_ref,
                 image_ref, spread_ref, drive_ref, right_ref, moment_ref, left_ref, along_ref, acc_ref):
    drive_own = make_sides(gathered_ref, drive_ref, right_ref, moment_ref, left_ref, along_ref)
    drive = drive_ref[...]
    scale = 1.0 / jnp.sqrt(jnp.sum(drive * drive, keepdims=True))
    product = couple(right_ref, moment_ref, left_ref, along_ref, drive_ref, acc_ref)
    _, resist_own = own_rows(bundle_ref, image_ref)
    image = (resist_own * drive_own + coupling * product) * scale
    image_ref[...] = image
    spread_rows(spread_ref, image)


def second_kernel(coupling, drive_ref, image_ref, image_own_ref, bundle_ref, after_ref,
                  right_ref, moment_ref, left_ref, along_ref,
                  basis_ref, basis_own_ref, stats_ref, known_ref, vec_ref, acc_ref):
    drive = drive_ref[...]
    norm = jnp.sqrt(jnp.sum(drive * drive, keepdims=True))
    scale = 1.0 / norm
    basis_a = drive * scale
    image = image_ref[...]
    hessen_a = jnp.sum(image * basis_a, keepdims=True)
    rest = image - hessen_a * basis_a
    hessen_b = jnp.sqrt(jnp.sum(rest * rest, keepdims=True))
    inverse = 1.0 / hessen_b
    basis_b = rest * inverse
    vec_ref[...] = basis_b
    basis_ref[0:1, :] = basis_a
    basis_ref[1:2, :] = basis_b
    drive_own, resist_own = own_rows(bundle_ref, image_own_ref)
    own_a = drive_own * scale
    own_b = (image_own_ref[...] - hessen_a * own_a) * inverse
    basis_own_ref[0:1, :] = own_a
    basis_own_ref[1:2, :] = own_b
    product = couple(right_ref, moment_ref, left_ref, along_ref, vec_ref, acc_ref)
    second = resist_own * own_b + coupling * product
    lane = iota((1, 128), 1)

    def three(a, b, c):
        return jnp.where(lane == 0, a, jnp.where(lane == 1, b, jnp.where(lane == 2, c, 0.0)))

    spread_rows(stats_ref, three(
        jnp.sum(second * own_a, keepdims=True),
        jnp.sum(second * own_b, keepdims=True),
        jnp.sum(second * second, keepdims=True),
    ))
    known_ref[...] = three(norm, hessen_a, hessen_b)


def group_kernel(bundle_ref, slot_ref, table_ref, left_ref, planes_ref, *, n_row):
    points = slot_ref.shape[1]
    chunk_count = left_ref.shape[0] // CHUNK
    owner = bundle_ref[3:4, 0:points].astype(jnp.int32)
    rows = max(8, n_row)
    marks = jnp.where(iota((rows, points), 0) == owner, 1.0, 0.0)
    tile = 256
    upper = jnp.where(iota((tile, tile), 0) <= iota((tile, tile), 1), 1.0, 0.0).astype(jnp.bfloat16)
    before = jnp.zeros((rows, 1), jnp.float32)
    ranks = []
    for piece in range(points // tile):
        part = dot(marks[:, piece * tile:(piece + 1) * tile].astype(jnp.bfloat16), upper)
        ranks.append(part + before - 1.0)
        before = before + part[:, tile - 1:tile]
    ranks = jnp.concatenate(ranks, axis=1)
    chunks = jnp.floor((before + (CHUNK - 1)) * (1.0 / CHUNK))
    start = jnp.zeros((1, 1), jnp.float32)
    starts = []
    for name in range(rows):
        starts.append(start)
        start = start + chunks[name:name + 1]
    starts = jnp.concatenate(starts, axis=0)
    slot = jnp.sum(marks * (ranks + starts * CHUNK), axis=0, keepdims=True).astype(jnp.int32)
    slot_ref[...] = slot
    lane = iota((rows, 128), 1)
    ended = jnp.sum(jnp.where(starts + chunks <= lane.astype(jnp.float32), 1.0, 0.0), axis=0, keepdims=True)
    block = jnp.minimum(ended, n_row - 1.0)
    place = iota((8, 128), 0)
    table_ref[...] = jnp.where(place == 0, block, start).astype(jnp.int32)
    high = jnp.where(iota((chunk_count, points), 0) == slot // CHUNK, 1.0, 0.0)
    low = jnp.where(iota((CHUNK, points), 0) == slot % CHUNK, 1.0, 0.0).astype(jnp.bfloat16)
    parts = split3(bundle_ref[0:3, 0:points] - 0.5)
    spread = jnp.concatenate([high * part[k:k + 1] for k in range(3) for part in parts], axis=0).astype(jnp.bfloat16)
    placed = dot_nt(spread, low)
    planes = [placed[k * chunk_count:(k + 1) * chunk_count] for k in range(9)]
    x, y, z = (planes[3 * k] + planes[3 * k + 1] + planes[3 * k + 2] for k in range(3))
    sides = [-2.0 * x, -2.0 * y, -2.0 * z, jnp.ones_like(x), x * x + y * y + z * z + EPS_FIELD]
    sides = [split3(side) for side in sides]
    empty = jnp.zeros_like(x)
    for group, part in enumerate([0, 0, 1, 1, 0, 2]):
        for k in range(8):
            to = pl.ds((group * 8 + k) * chunk_count, chunk_count)
            planes_ref[to, :] = sides[k][part] if k < 5 else empty
    for chunk in range(chunk_count):
        left_ref[chunk * CHUNK:(chunk + 1) * CHUNK, :] = transposed(planes_ref[pl.ds(chunk, 48, stride=chunk_count), :])


def cube_halves(left, right):
    inverse = lax.rsqrt(dot(left, right))
    cube = inverse * inverse * inverse
    high = cube.astype(jnp.bfloat16)
    return high, (cube - high.astype(jnp.float32)).astype(jnp.bfloat16)


def block_part(block, col, n_row, seg_dev):
    return aligned((col * n_row + block) * seg_dev, seg_dev)


def chunk_steps(group_ref):
    return (group_ref[1, 0] + GROUP - 1) // GROUP


def weigh_kernel(group_ref, left_ref, right_ref, cubes_hbm, done_ref, cubes_ref, sems, *, n_row, n_col):
    seg_dev = right_ref.shape[1] // (n_row * n_col)
    done_ref[...] = jnp.zeros_like(done_ref)
    kept = (cubes_ref, cubes_hbm, sems)

    def step(k, carry):
        for part in range(GROUP):
            chunk = k * GROUP + part
            left = left_ref[aligned(chunk * CHUNK, CHUNK), :]
            for col in range(n_col):
                to = slice(col * seg_dev, (col + 1) * seg_dev)
                high, low = cube_halves(left, right_ref[:, block_part(group_ref[0, chunk], col, n_row, seg_dev)])
                cubes_ref[chunk, 0:CHUNK, to] = high
                cubes_ref[chunk, CHUNK:2 * CHUNK, to] = low
            kept_copy(kept, chunk, out=True).start()
        return carry

    def finish(k, carry):
        for part in range(GROUP):
            kept_copy(kept, k * GROUP + part, out=True).wait()
        return carry

    lax.fori_loop(0, chunk_steps(group_ref), step, 0)
    lax.fori_loop(0, chunk_steps(group_ref), finish, 0)


def field_kernel(group_ref, length_ref, slot_ref, moment_ref, basis_ref, *refs, n_row, n_col, keep):
    if keep:
        cubes_hbm, out_ref, table_ref, sums_ref, cubes_ref, sems = refs
        kept = (cubes_ref, cubes_hbm, sems)

        def begin(k, carry):
            for part in range(GROUP):
                kept_copy(kept, k * GROUP + part, out=False).start()
            return carry

        lax.fori_loop(0, chunk_steps(group_ref), begin, 0)
    else:
        left_ref, right_ref, out_ref, table_ref, sums_ref = refs
    chunk_count = sums_ref.shape[0] // 16
    seg_dev = moment_ref.shape[1] // (n_row * n_col)
    scale = 1.0 / math.sqrt(n_col * seg_dev)
    lane = iota((1, seg_dev), 1)
    sums_ref[...] = jnp.zeros_like(sums_ref)

    def table_step(block, carry):
        length = length_ref[block]
        for col in range(n_col):
            at = block_part(block, col, n_row, seg_dev)
            both = moment_ref[:, at]
            active = jnp.where(lane + col * seg_dev < length, scale, 0.0)
            first = both * (basis_ref[0:1, at] * active)
            second = both * (basis_ref[1:2, at] * active)
            parts = jnp.concatenate([first, second], axis=0)
            high = parts.astype(jnp.bfloat16).astype(jnp.float32)
            table_ref[:, at] = jnp.concatenate([high, parts - high], axis=0).astype(jnp.bfloat16)
        return carry

    lax.fori_loop(0, n_row, table_step, 0, unroll=min(n_row, 8))

    def block_row(ref, chunk):
        block = group_ref[0, chunk]
        return jnp.concatenate([ref[:, block_part(block, col, n_row, seg_dev)] for col in range(n_col)], axis=1)

    def cubes_of(chunk):
        return jnp.concatenate(cube_halves(left_ref[aligned(chunk * CHUNK, CHUNK), :], block_row(right_ref, chunk)), axis=0)

    def step(k, carry):
        for part in range(0, GROUP, 2):
            chunk = k * GROUP + part
            tables = jnp.concatenate([block_row(table_ref, chunk), block_row(table_ref, chunk + 1)], axis=0)
            if keep:
                kept_copy(kept, chunk, out=False).wait()
                kept_copy(kept, chunk + 1, out=False).wait()
                cubes = cubes_ref[pl.ds(chunk, 2)].reshape(4 * CHUNK, n_col * seg_dev)
            else:
                cubes = jnp.concatenate([cubes_of(chunk), cubes_of(chunk + 1)], axis=0)
            both = dot_nt(tables, cubes)
            for half in range(2):
                mine = both[32 * half:32 * half + 32, 2 * CHUNK * half:2 * CHUNK * (half + 1)]
                total = mine[:, 0:CHUNK] + mine[:, CHUNK:2 * CHUNK]
                sums_ref[pl.ds(chunk + half, 16, stride=chunk_count), :] = total[0:16] + total[16:32]
        return carry

    lax.fori_loop(0, chunk_steps(group_ref), step, 0)
    sums = jnp.concatenate([sums_ref[0:6 * chunk_count], sums_ref[8 * chunk_count:14 * chunk_count]], axis=0)
    sums = jnp.concatenate(split3(sums), axis=1).astype(jnp.bfloat16)
    for tile in range(slot_ref.shape[1] // TILE):
        at = pl.ds(tile * TILE, TILE)
        slot = slot_ref[:, at]
        low = jnp.where(iota((CHUNK, TILE), 0) == slot % CHUNK, 1.0, 0.0).astype(jnp.bfloat16)
        high = jnp.where(iota((chunk_count, TILE), 0) == slot // CHUNK, 1.0, 0.0)
        found = dot(sums, jnp.concatenate([low, low, low], axis=0))
        for row in range(12):
            picked = found[row * chunk_count:(row + 1) * chunk_count] * high
            out_ref[row:row + 1, at] = jnp.sum(picked, axis=0, keepdims=True)


def final_kernel(stats_ref, known_ref, basis_own_ref, field_ref, bundle_ref, currents_ref, iron_ref):
    stats = jnp.sum(stats_ref[...], axis=0)
    known = known_ref[...]
    initial_norm, hessen_a, hessen_b = known[:, 0:1], known[:, 1:2], known[:, 2:3]
    hessen_c, hessen_d, normal_second = stats[:, 0:1], stats[:, 1:2], stats[:, 2:3]
    normal_first = hessen_a * hessen_a + hessen_b * hessen_b
    normal_cross = hessen_a * hessen_c + hessen_b * hessen_d
    target_first = initial_norm * hessen_a
    target_second = initial_norm * hessen_c
    determinant = normal_first * normal_second - normal_cross * normal_cross
    weight_first = (normal_second * target_first - normal_cross * target_second) / determinant
    weight_second = (normal_first * target_second - normal_cross * target_first) / determinant
    currents_ref[...] = weight_first * basis_own_ref[0:1, :] + weight_second * basis_own_ref[1:2, :]
    moments = weight_first * field_ref[0:6, :] + weight_second * field_ref[6:12, :]
    points = bundle_ref[0:3, 0:iron_ref.shape[1]] - 0.5
    px, py, pz = points[0:1], points[1:2], points[2:3]
    iron_ref[0:1, :] = pz * moments[1:2] - py * moments[2:3] - moments[3:4]
    iron_ref[1:2, :] = px * moments[2:3] - pz * moments[0:1] - moments[4:5]
    iron_ref[2:3, :] = py * moments[0:1] - px * moments[1:2] - moments[5:6]


def shape(*sizes, dtype=jnp.float32):
    return jax.ShapeDtypeStruct(sizes, dtype)


def shards(drive, resist, centers, tangents, iron_points, owner, range_len):
    seg_dev = drive.shape[0]
    col_len = centers.shape[1]
    n_col = lax.axis_size("col")
    n_row = lax.axis_size("row")
    n_dev = n_col * n_row
    segments = seg_dev * n_dev
    width = n_col * seg_dev
    points_count = iron_points.shape[1]
    coupling = 0.5 / math.sqrt(segments)
    call = functools.partial(pl.pallas_call, compiler_params=pltpu.CompilerParams(vmem_limit_bytes=VMEM_LIMIT))
    scratch = [pltpu.VMEM((1, segments), jnp.float32), pltpu.VMEM((seg_dev, 128), jnp.float32)]
    hbm = pl.BlockSpec(memory_space=pltpu.HBM)
    smem = pl.BlockSpec(memory_space=pltpu.SMEM)
    vmem = pl.BlockSpec(memory_space=pltpu.VMEM)

    def work(microseconds):
        return pl.CostEstimate(flops=int(microseconds * 1e9), bytes_accessed=0, transcendentals=0)

    def roomy(row_bytes):
        return STREAM_BYTES // row_bytes

    def exchange(x):
        return lax.all_to_all(x, AXES, 0, 0, tiled=True)

    gathered = exchange(pl.pallas_call(
        pack_kernel,
        out_shape=shape(n_dev, 8, seg_dev),
        in_specs=[hbm] * 3,
        scratch_shapes=[
            pltpu.VMEM((1, seg_dev), jnp.float32),
            pltpu.VMEM((3, col_len), jnp.float32),
            pltpu.VMEM((3, col_len), jnp.float32),
            pltpu.SemaphoreType.DMA((3,)),
        ],
        compiler_params=pltpu.CompilerParams(vmem_limit_bytes=ENTRY_LIMIT),
        cost_estimate=work(1),
        name="pack",
    )(drive[None, :], centers, tangents))
    longest = max(points_count, 2 * seg_dev)

    def wide(row):
        return jnp.pad(row, ((0, 0), (0, longest - row.shape[1])))

    bundle = jnp.concatenate([
        wide(iron_points), wide(owner.reshape(1, points_count).astype(jnp.float32)),
        wide(jnp.concatenate([drive, resist])[None, :]),
    ], axis=0)
    chunk_count = points_count // CHUNK + n_row * (CHUNK - 1) // CHUNK
    chunk_count = -(-chunk_count // 8) * 8
    slot, group_table, left = call(
        functools.partial(group_kernel, n_row=n_row),
        out_shape=(
            shape(1, points_count, dtype=jnp.int32),
            shape(8, 128, dtype=jnp.int32),
            shape(chunk_count * CHUNK, 48, dtype=jnp.bfloat16),
        ),
        scratch_shapes=[pltpu.VMEM((48 * chunk_count, CHUNK), jnp.float32)],
        cost_estimate=work(3),
        name="group_points",
    )(bundle)

    cube_shape = (chunk_count, 2 * CHUNK, width)
    keep = 2 * math.prod(cube_shape) <= KEEP_BYTES
    stream = functools.partial(
        pl.pallas_call, compiler_params=pltpu.CompilerParams(vmem_limit_bytes=STREAM_LIMIT if keep else VMEM_LIMIT)
    )
    first = call(
        functools.partial(first_kernel, coupling),
        out_shape=(
            shape(1, seg_dev), shape(n_dev, 1, seg_dev), shape(1, segments),
            shape(48, segments, dtype=jnp.bfloat16), shape(8, segments),
            shape(2, seg_dev, 48, dtype=jnp.bfloat16), shape(3, seg_dev, 128),
        ),
        scratch_shapes=scratch[1:],
        cost_estimate=work(4),
        name="first_image",
    )(gathered, bundle, group_table)
    image_own, image_spread, drive_all = first[0:3]
    sides = first[3:]
    right, moment = sides[0:2]
    image_all = exchange(image_spread).reshape(1, segments)
    cube_scratch = [pltpu.VMEM(cube_shape, jnp.bfloat16), pltpu.SemaphoreType.DMA((chunk_count,))]
    if keep:
        cubes, after = stream(
            functools.partial(weigh_kernel, n_row=n_row, n_col=n_col),
            out_shape=(shape(roomy(4 * CHUNK * width), *cube_shape[1:], dtype=jnp.bfloat16), shape(8, 128)),
            in_specs=[smem, vmem, vmem],
            out_specs=(hbm, vmem),
            scratch_shapes=cube_scratch,
            cost_estimate=work(5),
            name="weigh",
        )(group_table, left, right)
    else:
        after = group_table
    basis, basis_own, stats, known = call(
        functools.partial(second_kernel, coupling),
        out_shape=(shape(2, segments), shape(2, seg_dev), shape(n_dev, 1, 128), shape(1, 128)),
        scratch_shapes=scratch,
        cost_estimate=work(3),
        name="second_image",
    )(drive_all, image_all, image_own, bundle, after, *sides)
    stats_all = exchange(stats)

    field = stream(
        functools.partial(field_kernel, n_row=n_row, n_col=n_col, keep=keep),
        out_shape=shape(12, points_count),
        in_specs=[smem, smem, vmem, vmem, vmem] + ([hbm] if keep else [vmem, vmem]),
        scratch_shapes=[
            pltpu.VMEM((32, segments), jnp.bfloat16),
            pltpu.VMEM((16 * chunk_count, CHUNK), jnp.float32),
        ] + (cube_scratch if keep else []),
        cost_estimate=work(6),
        name="block_field",
    )(group_table, range_len, slot, moment, basis, *([cubes] if keep else [left, right]))
    currents, iron_field = stream(
        final_kernel,
        out_shape=(shape(1, seg_dev), shape(3, points_count)),
        name="combine",
    )(stats_all, known, basis_own, field, bundle)
    return (currents[0], iron_field)


def solution(mesh):
    return jax.shard_map(
        shards,
        mesh=mesh,
        in_specs=(
            P(AXES),
            P(AXES),
            P(None, "col"),
            P(None, "col"),
            P(None, AXES),
            P(AXES, None),
            P(),
        ),
        out_specs=(P(AXES), P(None, AXES)),
        check_vma=False,
    )
```

```python
import functools
import math

import jax
import jax.numpy as jnp
from jax import lax
from jax.experimental import pallas as pl
from jax.experimental.pallas import tpu as pltpu
from jax.sharding import PartitionSpec as P

EPS_SEG = 0.0004
EPS_FIELD = 0.0025
AXES = ("col", "row")
CHUNK = 128
GROUP = 4
TILE = 512
COLUMNS = 256
ROWS = 64
KEEP_BYTES = 16 * 1024 * 1024
VMEM_LIMIT = 32 * 1024 * 1024
STREAM_LIMIT = 44 * 1024 * 1024
STREAM_BYTES = 20 * 1024 * 1024


def split3(x):
    high = x.astype(jnp.bfloat16).astype(jnp.float32)
    rest = x - high
    middle = rest.astype(jnp.bfloat16).astype(jnp.float32)
    low = (rest - middle).astype(jnp.bfloat16).astype(jnp.float32)
    return high, middle, low


def left_parts(x):
    high, middle, low = split3(x)
    return jnp.concatenate([high, high, middle, middle, high, low], axis=0)


def right_parts(x):
    high, middle, low = split3(x)
    return jnp.concatenate([high, middle, high, middle, low, high], axis=0).astype(jnp.bfloat16)


def rows8(*rows):
    width = rows[0].shape[1]
    count = sum(r.shape[0] for r in rows)
    if count < 8:
        rows = rows + (jnp.zeros((8 - count, width), jnp.float32),)
    return jnp.concatenate(rows, axis=0)


def left_center(c, eps):
    square = jnp.sum(c * c, axis=0, keepdims=True)
    return rows8(-2.0 * c, jnp.ones_like(square), square + eps)


def right_center(c):
    square = jnp.sum(c * c, axis=0, keepdims=True)
    return rows8(c, square, jnp.ones_like(square))


def dot(a, b):
    return jnp.dot(a, b, preferred_element_type=jnp.float32)


def dot_nt(a, b):
    return lax.dot_general(a, b, (((1,), (1,)), ((), ())), preferred_element_type=jnp.float32)


def transposed(x):
    return x.T.astype(jnp.bfloat16)


def iota(shape, axis):
    return lax.broadcasted_iota(jnp.int32, shape, axis)


def aligned(start, size):
    return pl.ds(pl.multiple_of(start, size), size)


def sides_kernel(joined_ref, other_ref, right_ref, moment_ref, left_ref, along_ref, *, offsets):
    n_col = len(offsets)
    half = n_col // 2
    length = right_ref.shape[1] // n_col
    seg_dev = left_ref.shape[1]
    own_at = aligned(lax.axis_index("row") * seg_dev, seg_dev)
    tangent = rows8(joined_ref[0, 3:6, own_at])
    left_ref[0] = transposed(left_parts(left_center(joined_ref[0, 0:3, own_at] - 0.5, EPS_SEG)))
    left_ref[1] = transposed(left_parts(tangent))
    tangent = tangent.T
    for k in range(3):
        along_ref[k] = jnp.broadcast_to(tangent[:, k:k + 1], (seg_dev, 128))
    for index, offset in enumerate(offsets):
        piece = joined_ref.at[index] if index < half else other_ref.at[index - half]
        col = jnp.bitwise_xor(lax.axis_index("col"), offset)

        def step(k, carry):
            geo = piece[:, aligned(k * TILE, TILE)]
            to = pl.ds(pl.multiple_of(col * length + k * TILE, TILE), TILE)
            center, tangent = geo[0:3] - 0.5, geo[3:6]
            cross = jnp.concatenate([
                tangent[1:2] * center[2:3] - tangent[2:3] * center[1:2],
                tangent[2:3] * center[0:1] - tangent[0:1] * center[2:3],
                tangent[0:1] * center[1:2] - tangent[1:2] * center[0:1],
            ], axis=0)
            right_ref[:, to] = right_parts(right_center(center))
            moment_ref[:, to] = rows8(tangent, cross)
            return carry

        lax.fori_loop(0, length // TILE, step, 0, unroll=4)


def couple(right_ref, moment_ref, left_ref, along_ref, vec_ref, acc_ref):
    acc_ref[...] = jnp.zeros_like(acc_ref)

    def step(k, carry):
        at = aligned(k * TILE, TILE)
        turned = moment_ref[0:3, at] * vec_ref[:, at]
        right = right_ref[:, at]
        for first in range(0, TILE, COLUMNS):
            columns = slice(first, first + COLUMNS)
            by_product = first % (2 * COLUMNS) == 0
            if by_product:
                turned_parts = right_parts(rows8(turned[:, columns]))
            for row in range(0, acc_ref.shape[0], ROWS):
                rows = slice(row, row + ROWS)
                inverse = lax.rsqrt(dot(left_ref[0, rows], right[:, columns]))
                total = acc_ref[rows]
                if by_product:
                    pair = dot(left_ref[1, rows], turned_parts) * inverse
                    for start in range(0, COLUMNS, 128):
                        total = total + pair[:, start:start + 128]
                else:
                    for start in range(0, COLUMNS, 128):
                        lanes = slice(first + start, first + start + 128)
                        along = along_ref[0, rows] * turned[0:1, lanes]
                        along = along + along_ref[1, rows] * turned[1:2, lanes]
                        along = along + along_ref[2, rows] * turned[2:3, lanes]
                        total = total + along * inverse[:, start:start + 128]
                acc_ref[rows] = total
        return carry

    lax.fori_loop(0, vec_ref.shape[1] // TILE, step, 0, unroll=4)
    return jnp.sum(acc_ref[...].T, axis=0, keepdims=True)


def kept_copy(kept, index, out):
    local, remote, sems = kept
    if out:
        return pltpu.make_async_copy(local.at[index], remote.at[index], sems.at[index])
    return pltpu.make_async_copy(remote.at[index], local.at[index], sems.at[index])


def spread_rows(ref, row):
    for k in range(ref.shape[0]):
        ref[k] = row


def join_kernel(*refs):
    out_ref = refs[-1]
    if len(refs) == 4:
        bundle_ref, centers_ref, tangents_ref = refs[0:3]
        out_ref[0] = bundle_ref[0:6, 0:out_ref.shape[2]]
        out_ref[1, 0:3] = centers_ref[...]
        out_ref[1, 3:6] = tangents_ref[...]
    else:
        held = refs[0].shape[0]
        out_ref[0:held] = refs[0][...]
        out_ref[held:2 * held] = refs[1][...]


def own_rows(bundle_ref, like_ref):
    seg_dev = like_ref.shape[1]
    return bundle_ref[10:11, 0:seg_dev], bundle_ref[10:11, seg_dev:2 * seg_dev]


def first_kernel(coupling, drive_ref, bundle_ref, after_ref, right_ref, moment_ref, left_ref, along_ref,
                 image_ref, spread_ref, vec_ref, acc_ref):
    drive = drive_ref[...]
    scale = 1.0 / jnp.sqrt(jnp.sum(drive * drive, keepdims=True))
    vec_ref[...] = drive * scale
    product = couple(right_ref, moment_ref, left_ref, along_ref, vec_ref, acc_ref)
    drive_own, resist_own = own_rows(bundle_ref, image_ref)
    image = resist_own * (drive_own * scale) + coupling * product
    image_ref[...] = image
    spread_rows(spread_ref, image)


def second_kernel(coupling, drive_ref, image_ref, image_own_ref, bundle_ref, after_ref,
                  right_ref, moment_ref, left_ref, along_ref,
                  basis_ref, basis_own_ref, stats_ref, known_ref, vec_ref, acc_ref):
    drive = drive_ref[...]
    norm = jnp.sqrt(jnp.sum(drive * drive, keepdims=True))
    scale = 1.0 / norm
    basis_a = drive * scale
    image = image_ref[...]
    hessen_a = jnp.sum(image * basis_a, keepdims=True)
    rest = image - hessen_a * basis_a
    hessen_b = jnp.sqrt(jnp.sum(rest * rest, keepdims=True))
    inverse = 1.0 / hessen_b
    basis_b = rest * inverse
    vec_ref[...] = basis_b
    basis_ref[0:1, :] = basis_a
    basis_ref[1:2, :] = basis_b
    drive_own, resist_own = own_rows(bundle_ref, image_own_ref)
    own_a = drive_own * scale
    own_b = (image_own_ref[...] - hessen_a * own_a) * inverse
    basis_own_ref[0:1, :] = own_a
    basis_own_ref[1:2, :] = own_b
    product = couple(right_ref, moment_ref, left_ref, along_ref, vec_ref, acc_ref)
    second = resist_own * own_b + coupling * product
    lane = iota((1, 128), 1)

    def three(a, b, c):
        return jnp.where(lane == 0, a, jnp.where(lane == 1, b, jnp.where(lane == 2, c, 0.0)))

    spread_rows(stats_ref, three(
        jnp.sum(second * own_a, keepdims=True),
        jnp.sum(second * own_b, keepdims=True),
        jnp.sum(second * second, keepdims=True),
    ))
    known_ref[...] = three(norm, hessen_a, hessen_b)


def group_kernel(bundle_ref, slot_ref, table_ref, left_ref, planes_ref, *, n_row):
    points = slot_ref.shape[1]
    chunk_count = left_ref.shape[0] // CHUNK
    owner = bundle_ref[9:10, 0:points].astype(jnp.int32)
    rows = max(8, n_row)
    marks = jnp.where(iota((rows, points), 0) == owner, 1.0, 0.0)
    tile = 256
    upper = jnp.where(iota((tile, tile), 0) <= iota((tile, tile), 1), 1.0, 0.0).astype(jnp.bfloat16)
    before = jnp.zeros((rows, 1), jnp.float32)
    ranks = []
    for piece in range(points // tile):
        part = dot(marks[:, piece * tile:(piece + 1) * tile].astype(jnp.bfloat16), upper)
        ranks.append(part + before - 1.0)
        before = before + part[:, tile - 1:tile]
    ranks = jnp.concatenate(ranks, axis=1)
    chunks = jnp.floor((before + (CHUNK - 1)) * (1.0 / CHUNK))
    start = jnp.zeros((1, 1), jnp.float32)
    starts = []
    for name in range(rows):
        starts.append(start)
        start = start + chunks[name:name + 1]
    starts = jnp.concatenate(starts, axis=0)
    slot = jnp.sum(marks * (ranks + starts * CHUNK), axis=0, keepdims=True).astype(jnp.int32)
    slot_ref[...] = slot
    lane = iota((rows, 128), 1)
    ended = jnp.sum(jnp.where(starts + chunks <= lane.astype(jnp.float32), 1.0, 0.0), axis=0, keepdims=True)
    block = jnp.minimum(ended, n_row - 1.0)
    place = iota((8, 128), 0)
    table_ref[...] = jnp.where(place == 0, block, start).astype(jnp.int32)
    high = jnp.where(iota((chunk_count, points), 0) == slot // CHUNK, 1.0, 0.0)
    low = jnp.where(iota((CHUNK, points), 0) == slot % CHUNK, 1.0, 0.0).astype(jnp.bfloat16)
    parts = split3(bundle_ref[6:9, 0:points] - 0.5)
    spread = jnp.concatenate([high * part[k:k + 1] for k in range(3) for part in parts], axis=0).astype(jnp.bfloat16)
    placed = dot_nt(spread, low)
    planes = [placed[k * chunk_count:(k + 1) * chunk_count] for k in range(9)]
    x, y, z = (planes[3 * k] + planes[3 * k + 1] + planes[3 * k + 2] for k in range(3))
    sides = [-2.0 * x, -2.0 * y, -2.0 * z, jnp.ones_like(x), x * x + y * y + z * z + EPS_FIELD]
    sides = [split3(side) for side in sides]
    empty = jnp.zeros_like(x)
    for group, part in enumerate([0, 0, 1, 1, 0, 2]):
        for k in range(8):
            to = pl.ds((group * 8 + k) * chunk_count, chunk_count)
            planes_ref[to, :] = sides[k][part] if k < 5 else empty
    for chunk in range(chunk_count):
        left_ref[chunk * CHUNK:(chunk + 1) * CHUNK, :] = transposed(planes_ref[pl.ds(chunk, 48, stride=chunk_count), :])


def cube_halves(left, right):
    inverse = lax.rsqrt(dot(left, right))
    cube = inverse * inverse * inverse
    high = cube.astype(jnp.bfloat16)
    return high, (cube - high.astype(jnp.float32)).astype(jnp.bfloat16)


def block_part(block, col, n_row, seg_dev):
    return aligned((col * n_row + block) * seg_dev, seg_dev)


def chunk_steps(group_ref):
    return (group_ref[1, 0] + GROUP - 1) // GROUP


def weigh_kernel(group_ref, left_ref, right_ref, cubes_hbm, done_ref, cubes_ref, sems, *, n_row, n_col):
    seg_dev = right_ref.shape[1] // (n_row * n_col)
    done_ref[...] = jnp.zeros_like(done_ref)
    kept = (cubes_ref, cubes_hbm, sems)

    def step(k, carry):
        for part in range(GROUP):
            chunk = k * GROUP + part
            left = left_ref[aligned(chunk * CHUNK, CHUNK), :]
            for col in range(n_col):
                to = slice(col * seg_dev, (col + 1) * seg_dev)
                high, low = cube_halves(left, right_ref[:, block_part(group_ref[0, chunk], col, n_row, seg_dev)])
                cubes_ref[chunk, 0:CHUNK, to] = high
                cubes_ref[chunk, CHUNK:2 * CHUNK, to] = low
            kept_copy(kept, chunk, out=True).start()
        return carry

    def finish(k, carry):
        for part in range(GROUP):
            kept_copy(kept, k * GROUP + part, out=True).wait()
        return carry

    lax.fori_loop(0, chunk_steps(group_ref), step, 0)
    lax.fori_loop(0, chunk_steps(group_ref), finish, 0)


def field_kernel(group_ref, length_ref, slot_ref, moment_ref, basis_ref, *refs, n_row, n_col, keep):
    if keep:
        cubes_hbm, out_ref, table_ref, sums_ref, cubes_ref, sems = refs
        kept = (cubes_ref, cubes_hbm, sems)

        def begin(k, carry):
            for part in range(GROUP):
                kept_copy(kept, k * GROUP + part, out=False).start()
            return carry

        lax.fori_loop(0, chunk_steps(group_ref), begin, 0)
    else:
        left_ref, right_ref, out_ref, table_ref, sums_ref = refs
    chunk_count = sums_ref.shape[0] // 16
    seg_dev = moment_ref.shape[1] // (n_row * n_col)
    scale = 1.0 / math.sqrt(n_col * seg_dev)
    lane = iota((1, seg_dev), 1)
    sums_ref[...] = jnp.zeros_like(sums_ref)

    def table_step(block, carry):
        length = length_ref[block]
        for col in range(n_col):
            at = block_part(block, col, n_row, seg_dev)
            both = moment_ref[:, at]
            active = jnp.where(lane + col * seg_dev < length, scale, 0.0)
            first = both * (basis_ref[0:1, at] * active)
            second = both * (basis_ref[1:2, at] * active)
            parts = jnp.concatenate([first, second], axis=0)
            high = parts.astype(jnp.bfloat16).astype(jnp.float32)
            table_ref[:, at] = jnp.concatenate([high, parts - high], axis=0).astype(jnp.bfloat16)
        return carry

    lax.fori_loop(0, n_row, table_step, 0, unroll=min(n_row, 8))

    def block_row(ref, chunk):
        block = group_ref[0, chunk]
        return jnp.concatenate([ref[:, block_part(block, col, n_row, seg_dev)] for col in range(n_col)], axis=1)

    def cubes_of(chunk):
        return jnp.concatenate(cube_halves(left_ref[aligned(chunk * CHUNK, CHUNK), :], block_row(right_ref, chunk)), axis=0)

    def step(k, carry):
        for part in range(0, GROUP, 2):
            chunk = k * GROUP + part
            tables = jnp.concatenate([block_row(table_ref, chunk), block_row(table_ref, chunk + 1)], axis=0)
            if keep:
                kept_copy(kept, chunk, out=False).wait()
                kept_copy(kept, chunk + 1, out=False).wait()
                cubes = cubes_ref[pl.ds(chunk, 2)].reshape(4 * CHUNK, n_col * seg_dev)
            else:
                cubes = jnp.concatenate([cubes_of(chunk), cubes_of(chunk + 1)], axis=0)
            both = dot_nt(tables, cubes)
            for half in range(2):
                mine = both[32 * half:32 * half + 32, 2 * CHUNK * half:2 * CHUNK * (half + 1)]
                total = mine[:, 0:CHUNK] + mine[:, CHUNK:2 * CHUNK]
                sums_ref[pl.ds(chunk + half, 16, stride=chunk_count), :] = total[0:16] + total[16:32]
        return carry

    lax.fori_loop(0, chunk_steps(group_ref), step, 0)
    sums = jnp.concatenate([sums_ref[0:6 * chunk_count], sums_ref[8 * chunk_count:14 * chunk_count]], axis=0)
    sums = jnp.concatenate(split3(sums), axis=1).astype(jnp.bfloat16)
    for tile in range(slot_ref.shape[1] // TILE):
        at = pl.ds(tile * TILE, TILE)
        slot = slot_ref[:, at]
        low = jnp.where(iota((CHUNK, TILE), 0) == slot % CHUNK, 1.0, 0.0).astype(jnp.bfloat16)
        high = jnp.where(iota((chunk_count, TILE), 0) == slot // CHUNK, 1.0, 0.0)
        found = dot(sums, jnp.concatenate([low, low, low], axis=0))
        for row in range(12):
            picked = found[row * chunk_count:(row + 1) * chunk_count] * high
            out_ref[row:row + 1, at] = jnp.sum(picked, axis=0, keepdims=True)


def final_kernel(stats_ref, known_ref, basis_own_ref, field_ref, bundle_ref, currents_ref, iron_ref):
    stats = jnp.sum(stats_ref[...], axis=0)
    known = known_ref[...]
    initial_norm, hessen_a, hessen_b = known[:, 0:1], known[:, 1:2], known[:, 2:3]
    hessen_c, hessen_d, normal_second = stats[:, 0:1], stats[:, 1:2], stats[:, 2:3]
    normal_first = hessen_a * hessen_a + hessen_b * hessen_b
    normal_cross = hessen_a * hessen_c + hessen_b * hessen_d
    target_first = initial_norm * hessen_a
    target_second = initial_norm * hessen_c
    determinant = normal_first * normal_second - normal_cross * normal_cross
    weight_first = (normal_second * target_first - normal_cross * target_second) / determinant
    weight_second = (normal_first * target_second - normal_cross * target_first) / determinant
    currents_ref[...] = weight_first * basis_own_ref[0:1, :] + weight_second * basis_own_ref[1:2, :]
    moments = weight_first * field_ref[0:6, :] + weight_second * field_ref[6:12, :]
    points = bundle_ref[6:9, 0:iron_ref.shape[1]] - 0.5
    px, py, pz = points[0:1], points[1:2], points[2:3]
    iron_ref[0:1, :] = pz * moments[1:2] - py * moments[2:3] - moments[3:4]
    iron_ref[1:2, :] = px * moments[2:3] - pz * moments[0:1] - moments[4:5]
    iron_ref[2:3, :] = py * moments[0:1] - px * moments[1:2] - moments[5:6]


def shape(*sizes, dtype=jnp.float32):
    return jax.ShapeDtypeStruct(sizes, dtype)


def shards(drive, resist, centers, tangents, iron_points, owner, range_len):
    seg_dev = drive.shape[0]
    col_len = centers.shape[1]
    n_col = lax.axis_size("col")
    n_row = lax.axis_size("row")
    n_dev = n_col * n_row
    segments = seg_dev * n_dev
    width = n_col * seg_dev
    points_count = iron_points.shape[1]
    coupling = 0.5 / math.sqrt(segments)
    call = functools.partial(pl.pallas_call, compiler_params=pltpu.CompilerParams(vmem_limit_bytes=VMEM_LIMIT))
    scratch = [pltpu.VMEM((1, segments), jnp.float32), pltpu.VMEM((seg_dev, 128), jnp.float32)]
    hbm = pl.BlockSpec(memory_space=pltpu.HBM)
    smem = pl.BlockSpec(memory_space=pltpu.SMEM)
    vmem = pl.BlockSpec(memory_space=pltpu.VMEM)

    def work(microseconds):
        return pl.CostEstimate(flops=int(microseconds * 1e9), bytes_accessed=0, transcendentals=0)

    def roomy(row_bytes):
        return STREAM_BYTES // row_bytes

    def exchange(x):
        return lax.all_to_all(x, AXES, 0, 0, tiled=True)

    drive_all = exchange(jnp.broadcast_to(drive[None, None, :], (n_dev, 1, seg_dev))).reshape(1, segments)
    longest = max(col_len, points_count, 2 * seg_dev)

    def wide(row):
        return jnp.pad(row, ((0, 0), (0, longest - row.shape[1])))

    bundle = jnp.concatenate([
        wide(centers), wide(tangents), wide(iron_points), wide(owner.reshape(1, points_count).astype(jnp.float32)),
        wide(jnp.concatenate([drive, resist])[None, :]),
    ], axis=0)

    def swap(x, bit):
        return lax.ppermute(x, "col", [(k, k ^ bit) for k in range(n_col)])

    bit = n_col // 2
    offsets = [0, bit]
    joined = call(
        join_kernel, out_shape=shape(2, 6, col_len), cost_estimate=work(1), name="join"
    )(bundle, swap(centers, bit), swap(tangents, bit))
    while bit > 1:
        bit //= 2
        other = swap(joined, bit)
        offsets = offsets + [offset ^ bit for offset in offsets]
        if bit > 1:
            joined = call(join_kernel, out_shape=shape(len(offsets), 6, col_len), name="join")(joined, other)

    chunk_count = points_count // CHUNK + n_row * (CHUNK - 1) // CHUNK
    chunk_count = -(-chunk_count // 8) * 8
    slot, group_table, left = call(
        functools.partial(group_kernel, n_row=n_row),
        out_shape=(
            shape(1, points_count, dtype=jnp.int32),
            shape(8, 128, dtype=jnp.int32),
            shape(chunk_count * CHUNK, 48, dtype=jnp.bfloat16),
        ),
        scratch_shapes=[pltpu.VMEM((48 * chunk_count, CHUNK), jnp.float32)],
        cost_estimate=work(3),
        name="group_points",
    )(bundle)

    cube_shape = (chunk_count, 2 * CHUNK, width)
    keep = 2 * math.prod(cube_shape) <= KEEP_BYTES
    stream = functools.partial(
        pl.pallas_call, compiler_params=pltpu.CompilerParams(vmem_limit_bytes=STREAM_LIMIT if keep else VMEM_LIMIT)
    )
    sides = call(
        functools.partial(sides_kernel, offsets=offsets),
        out_shape=(
            shape(48, segments, dtype=jnp.bfloat16), shape(8, segments),
            shape(2, seg_dev, 48, dtype=jnp.bfloat16), shape(3, seg_dev, 128),
        ),
        cost_estimate=work(1),
        name="sides",
    )(joined, other)
    right, moment = sides[0:2]
    image_own, image_spread = call(
        functools.partial(first_kernel, coupling),
        out_shape=(shape(1, seg_dev), shape(n_dev, 1, seg_dev)),
        scratch_shapes=scratch,
        cost_estimate=work(3),
        name="first_image",
    )(drive_all, bundle, group_table, *sides)
    image_all = exchange(image_spread).reshape(1, segments)
    cube_scratch = [pltpu.VMEM(cube_shape, jnp.bfloat16), pltpu.SemaphoreType.DMA((chunk_count,))]
    if keep:
        cubes, after = stream(
            functools.partial(weigh_kernel, n_row=n_row, n_col=n_col),
            out_shape=(shape(roomy(4 * CHUNK * width), *cube_shape[1:], dtype=jnp.bfloat16), shape(8, 128)),
            in_specs=[smem, vmem, vmem],
            out_specs=(hbm, vmem),
            scratch_shapes=cube_scratch,
            cost_estimate=work(5),
            name="weigh",
        )(group_table, left, right)
    else:
        after = group_table
    basis, basis_own, stats, known = call(
        functools.partial(second_kernel, coupling),
        out_shape=(shape(2, segments), shape(2, seg_dev), shape(n_dev, 1, 128), shape(1, 128)),
        scratch_shapes=scratch,
        cost_estimate=work(3),
        name="second_image",
    )(drive_all, image_all, image_own, bundle, after, *sides)
    stats_all = exchange(stats)

    field = stream(
        functools.partial(field_kernel, n_row=n_row, n_col=n_col, keep=keep),
        out_shape=shape(12, points_count),
        in_specs=[smem, smem, vmem, vmem, vmem] + ([hbm] if keep else [vmem, vmem]),
        scratch_shapes=[
            pltpu.VMEM((32, segments), jnp.bfloat16),
            pltpu.VMEM((16 * chunk_count, CHUNK), jnp.float32),
        ] + (cube_scratch if keep else []),
        cost_estimate=work(6),
        name="block_field",
    )(group_table, range_len, slot, moment, basis, *([cubes] if keep else [left, right]))
    currents, iron_field = stream(
        final_kernel,
        out_shape=(shape(1, seg_dev), shape(3, points_count)),
        name="combine",
    )(stats_all, known, basis_own, field, bundle)
    return (currents[0], iron_field)


def solution(mesh):
    return jax.shard_map(
        shards,
        mesh=mesh,
        in_specs=(
            P(AXES),
            P(AXES),
            P(None, "col"),
            P(None, "col"),
            P(None, AXES),
            P(AXES, None),
            P(),
        ),
        out_specs=(P(AXES), P(None, AXES)),
        check_vma=False,
    )
```

```python
import functools
import math

import jax
import jax.numpy as jnp
from jax import lax
from jax.experimental import pallas as pl
from jax.experimental.pallas import tpu as pltpu
from jax.sharding import PartitionSpec as P

EPS_SEG = 0.0004
EPS_FIELD = 0.0025
AXES = ("col", "row")
CHUNK = 128
GROUP = 4
TILE = 512
COLUMNS = 256
ROWS = 64
KEEP_BYTES = 16 * 1024 * 1024
VMEM_LIMIT = 32 * 1024 * 1024
STREAM_LIMIT = 44 * 1024 * 1024
ENTRY_LIMIT = 60 * 1024 * 1024
STREAM_BYTES = 20 * 1024 * 1024


def split3(x):
    high = x.astype(jnp.bfloat16).astype(jnp.float32)
    rest = x - high
    middle = rest.astype(jnp.bfloat16).astype(jnp.float32)
    low = (rest - middle).astype(jnp.bfloat16).astype(jnp.float32)
    return high, middle, low


def left_parts(x):
    high, middle, low = split3(x)
    return jnp.concatenate([high, high, middle, middle, high, low], axis=0)


def right_parts(x):
    high, middle, low = split3(x)
    return jnp.concatenate([high, middle, high, middle, low, high], axis=0).astype(jnp.bfloat16)


def rows8(*rows):
    width = rows[0].shape[1]
    count = sum(r.shape[0] for r in rows)
    if count < 8:
        rows = rows + (jnp.zeros((8 - count, width), jnp.float32),)
    return jnp.concatenate(rows, axis=0)


def left_center(c, eps):
    square = jnp.sum(c * c, axis=0, keepdims=True)
    return rows8(-2.0 * c, jnp.ones_like(square), square + eps)


def right_center(c):
    square = jnp.sum(c * c, axis=0, keepdims=True)
    return rows8(c, square, jnp.ones_like(square))


def dot(a, b):
    return jnp.dot(a, b, preferred_element_type=jnp.float32)


def dot_nt(a, b):
    return lax.dot_general(a, b, (((1,), (1,)), ((), ())), preferred_element_type=jnp.float32)


def transposed(x):
    return x.T.astype(jnp.bfloat16)


def iota(shape, axis):
    return lax.broadcasted_iota(jnp.int32, shape, axis)


def aligned(start, size):
    return pl.ds(pl.multiple_of(start, size), size)


def sides_kernel(joined_ref, other_ref, right_ref, moment_ref, left_ref, along_ref, *, offsets):
    n_col = len(offsets)
    half = n_col // 2
    length = right_ref.shape[1] // n_col
    seg_dev = left_ref.shape[1]
    own_at = aligned(lax.axis_index("row") * seg_dev, seg_dev)
    tangent = rows8(joined_ref[0, 3:6, own_at])
    left_ref[0] = transposed(left_parts(left_center(joined_ref[0, 0:3, own_at] - 0.5, EPS_SEG)))
    left_ref[1] = transposed(left_parts(tangent))
    tangent = tangent.T
    for k in range(3):
        along_ref[k] = jnp.broadcast_to(tangent[:, k:k + 1], (seg_dev, 128))
    for index, offset in enumerate(offsets):
        piece = joined_ref.at[index] if index < half else other_ref.at[index - half]
        col = jnp.bitwise_xor(lax.axis_index("col"), offset)

        def step(k, carry):
            geo = piece[:, aligned(k * TILE, TILE)]
            to = pl.ds(pl.multiple_of(col * length + k * TILE, TILE), TILE)
            center, tangent = geo[0:3] - 0.5, geo[3:6]
            cross = jnp.concatenate([
                tangent[1:2] * center[2:3] - tangent[2:3] * center[1:2],
                tangent[2:3] * center[0:1] - tangent[0:1] * center[2:3],
                tangent[0:1] * center[1:2] - tangent[1:2] * center[0:1],
            ], axis=0)
            right_ref[:, to] = right_parts(right_center(center))
            moment_ref[:, to] = rows8(tangent, cross)
            return carry

        lax.fori_loop(0, length // TILE, step, 0, unroll=4)


def couple(right_ref, moment_ref, left_ref, along_ref, vec_ref, acc_ref):
    acc_ref[...] = jnp.zeros_like(acc_ref)

    def step(k, carry):
        at = aligned(k * TILE, TILE)
        turned = moment_ref[0:3, at] * vec_ref[:, at]
        right = right_ref[:, at]
        for first in range(0, TILE, COLUMNS):
            columns = slice(first, first + COLUMNS)
            by_product = first % (2 * COLUMNS) == 0
            if by_product:
                turned_parts = right_parts(rows8(turned[:, columns]))
            for row in range(0, acc_ref.shape[0], ROWS):
                rows = slice(row, row + ROWS)
                inverse = lax.rsqrt(dot(left_ref[0, rows], right[:, columns]))
                total = acc_ref[rows]
                if by_product:
                    pair = dot(left_ref[1, rows], turned_parts) * inverse
                    for start in range(0, COLUMNS, 128):
                        total = total + pair[:, start:start + 128]
                else:
                    for start in range(0, COLUMNS, 128):
                        lanes = slice(first + start, first + start + 128)
                        along = along_ref[0, rows] * turned[0:1, lanes]
                        along = along + along_ref[1, rows] * turned[1:2, lanes]
                        along = along + along_ref[2, rows] * turned[2:3, lanes]
                        total = total + along * inverse[:, start:start + 128]
                acc_ref[rows] = total
        return carry

    lax.fori_loop(0, vec_ref.shape[1] // TILE, step, 0, unroll=4)
    return jnp.sum(acc_ref[...].T, axis=0, keepdims=True)


def kept_copy(kept, index, out):
    local, remote, sems = kept
    if out:
        return pltpu.make_async_copy(local.at[index], remote.at[index], sems.at[index])
    return pltpu.make_async_copy(remote.at[index], local.at[index], sems.at[index])


def spread_rows(ref, row):
    for k in range(ref.shape[0]):
        ref[k] = row


def spread_kernel(drive_hbm, out_ref, drive, sem):
    copy = pltpu.make_async_copy(drive_hbm, drive, sem)
    copy.start()
    copy.wait()
    spread_rows(out_ref, drive[...])


def join_kernel(*refs):
    out_ref = refs[-1]
    if len(refs) == 4:
        bundle_ref, centers_ref, tangents_ref = refs[0:3]
        out_ref[0] = bundle_ref[0:6, 0:out_ref.shape[2]]
        out_ref[1, 0:3] = centers_ref[...]
        out_ref[1, 3:6] = tangents_ref[...]
    else:
        held = refs[0].shape[0]
        out_ref[0:held] = refs[0][...]
        out_ref[held:2 * held] = refs[1][...]


def own_rows(bundle_ref, like_ref):
    seg_dev = like_ref.shape[1]
    return bundle_ref[10:11, 0:seg_dev], bundle_ref[10:11, seg_dev:2 * seg_dev]


def first_kernel(coupling, drive_ref, bundle_ref, after_ref, right_ref, moment_ref, left_ref, along_ref,
                 image_ref, spread_ref, vec_ref, acc_ref):
    drive = drive_ref[...]
    scale = 1.0 / jnp.sqrt(jnp.sum(drive * drive, keepdims=True))
    vec_ref[...] = drive * scale
    product = couple(right_ref, moment_ref, left_ref, along_ref, vec_ref, acc_ref)
    drive_own, resist_own = own_rows(bundle_ref, image_ref)
    image = resist_own * (drive_own * scale) + coupling * product
    image_ref[...] = image
    spread_rows(spread_ref, image)


def second_kernel(coupling, drive_ref, image_ref, image_own_ref, bundle_ref, after_ref,
                  right_ref, moment_ref, left_ref, along_ref,
                  basis_ref, basis_own_ref, stats_ref, known_ref, vec_ref, acc_ref):
    drive = drive_ref[...]
    norm = jnp.sqrt(jnp.sum(drive * drive, keepdims=True))
    scale = 1.0 / norm
    basis_a = drive * scale
    image = image_ref[...]
    hessen_a = jnp.sum(image * basis_a, keepdims=True)
    rest = image - hessen_a * basis_a
    hessen_b = jnp.sqrt(jnp.sum(rest * rest, keepdims=True))
    inverse = 1.0 / hessen_b
    basis_b = rest * inverse
    vec_ref[...] = basis_b
    basis_ref[0:1, :] = basis_a
    basis_ref[1:2, :] = basis_b
    drive_own, resist_own = own_rows(bundle_ref, image_own_ref)
    own_a = drive_own * scale
    own_b = (image_own_ref[...] - hessen_a * own_a) * inverse
    basis_own_ref[0:1, :] = own_a
    basis_own_ref[1:2, :] = own_b
    product = couple(right_ref, moment_ref, left_ref, along_ref, vec_ref, acc_ref)
    second = resist_own * own_b + coupling * product
    lane = iota((1, 128), 1)

    def three(a, b, c):
        return jnp.where(lane == 0, a, jnp.where(lane == 1, b, jnp.where(lane == 2, c, 0.0)))

    spread_rows(stats_ref, three(
        jnp.sum(second * own_a, keepdims=True),
        jnp.sum(second * own_b, keepdims=True),
        jnp.sum(second * second, keepdims=True),
    ))
    known_ref[...] = three(norm, hessen_a, hessen_b)


def group_kernel(bundle_ref, slot_ref, table_ref, left_ref, planes_ref, *, n_row):
    points = slot_ref.shape[1]
    chunk_count = left_ref.shape[0] // CHUNK
    owner = bundle_ref[9:10, 0:points].astype(jnp.int32)
    rows = max(8, n_row)
    marks = jnp.where(iota((rows, points), 0) == owner, 1.0, 0.0)
    tile = 256
    upper = jnp.where(iota((tile, tile), 0) <= iota((tile, tile), 1), 1.0, 0.0).astype(jnp.bfloat16)
    before = jnp.zeros((rows, 1), jnp.float32)
    ranks = []
    for piece in range(points // tile):
        part = dot(marks[:, piece * tile:(piece + 1) * tile].astype(jnp.bfloat16), upper)
        ranks.append(part + before - 1.0)
        before = before + part[:, tile - 1:tile]
    ranks = jnp.concatenate(ranks, axis=1)
    chunks = jnp.floor((before + (CHUNK - 1)) * (1.0 / CHUNK))
    start = jnp.zeros((1, 1), jnp.float32)
    starts = []
    for name in range(rows):
        starts.append(start)
        start = start + chunks[name:name + 1]
    starts = jnp.concatenate(starts, axis=0)
    slot = jnp.sum(marks * (ranks + starts * CHUNK), axis=0, keepdims=True).astype(jnp.int32)
    slot_ref[...] = slot
    lane = iota((rows, 128), 1)
    ended = jnp.sum(jnp.where(starts + chunks <= lane.astype(jnp.float32), 1.0, 0.0), axis=0, keepdims=True)
    block = jnp.minimum(ended, n_row - 1.0)
    place = iota((8, 128), 0)
    table_ref[...] = jnp.where(place == 0, block, start).astype(jnp.int32)
    high = jnp.where(iota((chunk_count, points), 0) == slot // CHUNK, 1.0, 0.0)
    low = jnp.where(iota((CHUNK, points), 0) == slot % CHUNK, 1.0, 0.0).astype(jnp.bfloat16)
    parts = split3(bundle_ref[6:9, 0:points] - 0.5)
    spread = jnp.concatenate([high * part[k:k + 1] for k in range(3) for part in parts], axis=0).astype(jnp.bfloat16)
    placed = dot_nt(spread, low)
    planes = [placed[k * chunk_count:(k + 1) * chunk_count] for k in range(9)]
    x, y, z = (planes[3 * k] + planes[3 * k + 1] + planes[3 * k + 2] for k in range(3))
    sides = [-2.0 * x, -2.0 * y, -2.0 * z, jnp.ones_like(x), x * x + y * y + z * z + EPS_FIELD]
    sides = [split3(side) for side in sides]
    empty = jnp.zeros_like(x)
    for group, part in enumerate([0, 0, 1, 1, 0, 2]):
        for k in range(8):
            to = pl.ds((group * 8 + k) * chunk_count, chunk_count)
            planes_ref[to, :] = sides[k][part] if k < 5 else empty
    for chunk in range(chunk_count):
        left_ref[chunk * CHUNK:(chunk + 1) * CHUNK, :] = transposed(planes_ref[pl.ds(chunk, 48, stride=chunk_count), :])


def cube_halves(left, right):
    inverse = lax.rsqrt(dot(left, right))
    cube = inverse * inverse * inverse
    high = cube.astype(jnp.bfloat16)
    return high, (cube - high.astype(jnp.float32)).astype(jnp.bfloat16)


def block_part(block, col, n_row, seg_dev):
    return aligned((col * n_row + block) * seg_dev, seg_dev)


def chunk_steps(group_ref):
    return (group_ref[1, 0] + GROUP - 1) // GROUP


def weigh_kernel(group_ref, left_ref, right_ref, cubes_hbm, done_ref, cubes_ref, sems, *, n_row, n_col):
    seg_dev = right_ref.shape[1] // (n_row * n_col)
    done_ref[...] = jnp.zeros_like(done_ref)
    kept = (cubes_ref, cubes_hbm, sems)

    def step(k, carry):
        for part in range(GROUP):
            chunk = k * GROUP + part
            left = left_ref[aligned(chunk * CHUNK, CHUNK), :]
            for col in range(n_col):
                to = slice(col * seg_dev, (col + 1) * seg_dev)
                high, low = cube_halves(left, right_ref[:, block_part(group_ref[0, chunk], col, n_row, seg_dev)])
                cubes_ref[chunk, 0:CHUNK, to] = high
                cubes_ref[chunk, CHUNK:2 * CHUNK, to] = low
            kept_copy(kept, chunk, out=True).start()
        return carry

    def finish(k, carry):
        for part in range(GROUP):
            kept_copy(kept, k * GROUP + part, out=True).wait()
        return carry

    lax.fori_loop(0, chunk_steps(group_ref), step, 0)
    lax.fori_loop(0, chunk_steps(group_ref), finish, 0)


def field_kernel(group_ref, length_ref, slot_ref, moment_ref, basis_ref, *refs, n_row, n_col, keep):
    if keep:
        cubes_hbm, out_ref, table_ref, sums_ref, cubes_ref, sems = refs
        kept = (cubes_ref, cubes_hbm, sems)

        def begin(k, carry):
            for part in range(GROUP):
                kept_copy(kept, k * GROUP + part, out=False).start()
            return carry

        lax.fori_loop(0, chunk_steps(group_ref), begin, 0)
    else:
        left_ref, right_ref, out_ref, table_ref, sums_ref = refs
    chunk_count = sums_ref.shape[0] // 16
    seg_dev = moment_ref.shape[1] // (n_row * n_col)
    scale = 1.0 / math.sqrt(n_col * seg_dev)
    lane = iota((1, seg_dev), 1)
    sums_ref[...] = jnp.zeros_like(sums_ref)

    def table_step(block, carry):
        length = length_ref[block]
        for col in range(n_col):
            at = block_part(block, col, n_row, seg_dev)
            both = moment_ref[:, at]
            active = jnp.where(lane + col * seg_dev < length, scale, 0.0)
            first = both * (basis_ref[0:1, at] * active)
            second = both * (basis_ref[1:2, at] * active)
            parts = jnp.concatenate([first, second], axis=0)
            high = parts.astype(jnp.bfloat16).astype(jnp.float32)
            table_ref[:, at] = jnp.concatenate([high, parts - high], axis=0).astype(jnp.bfloat16)
        return carry

    lax.fori_loop(0, n_row, table_step, 0, unroll=min(n_row, 8))

    def block_row(ref, chunk):
        block = group_ref[0, chunk]
        return jnp.concatenate([ref[:, block_part(block, col, n_row, seg_dev)] for col in range(n_col)], axis=1)

    def cubes_of(chunk):
        return jnp.concatenate(cube_halves(left_ref[aligned(chunk * CHUNK, CHUNK), :], block_row(right_ref, chunk)), axis=0)

    def step(k, carry):
        for part in range(0, GROUP, 2):
            chunk = k * GROUP + part
            tables = jnp.concatenate([block_row(table_ref, chunk), block_row(table_ref, chunk + 1)], axis=0)
            if keep:
                kept_copy(kept, chunk, out=False).wait()
                kept_copy(kept, chunk + 1, out=False).wait()
                cubes = cubes_ref[pl.ds(chunk, 2)].reshape(4 * CHUNK, n_col * seg_dev)
            else:
                cubes = jnp.concatenate([cubes_of(chunk), cubes_of(chunk + 1)], axis=0)
            both = dot_nt(tables, cubes)
            for half in range(2):
                mine = both[32 * half:32 * half + 32, 2 * CHUNK * half:2 * CHUNK * (half + 1)]
                total = mine[:, 0:CHUNK] + mine[:, CHUNK:2 * CHUNK]
                sums_ref[pl.ds(chunk + half, 16, stride=chunk_count), :] = total[0:16] + total[16:32]
        return carry

    lax.fori_loop(0, chunk_steps(group_ref), step, 0)
    sums = jnp.concatenate([sums_ref[0:6 * chunk_count], sums_ref[8 * chunk_count:14 * chunk_count]], axis=0)
    sums = jnp.concatenate(split3(sums), axis=1).astype(jnp.bfloat16)
    for tile in range(slot_ref.shape[1] // TILE):
        at = pl.ds(tile * TILE, TILE)
        slot = slot_ref[:, at]
        low = jnp.where(iota((CHUNK, TILE), 0) == slot % CHUNK, 1.0, 0.0).astype(jnp.bfloat16)
        high = jnp.where(iota((chunk_count, TILE), 0) == slot // CHUNK, 1.0, 0.0)
        found = dot(sums, jnp.concatenate([low, low, low], axis=0))
        for row in range(12):
            picked = found[row * chunk_count:(row + 1) * chunk_count] * high
            out_ref[row:row + 1, at] = jnp.sum(picked, axis=0, keepdims=True)


def final_kernel(stats_ref, known_ref, basis_own_ref, field_ref, bundle_ref, currents_ref, iron_ref):
    stats = jnp.sum(stats_ref[...], axis=0)
    known = known_ref[...]
    initial_norm, hessen_a, hessen_b = known[:, 0:1], known[:, 1:2], known[:, 2:3]
    hessen_c, hessen_d, normal_second = stats[:, 0:1], stats[:, 1:2], stats[:, 2:3]
    normal_first = hessen_a * hessen_a + hessen_b * hessen_b
    normal_cross = hessen_a * hessen_c + hessen_b * hessen_d
    target_first = initial_norm * hessen_a
    target_second = initial_norm * hessen_c
    determinant = normal_first * normal_second - normal_cross * normal_cross
    weight_first = (normal_second * target_first - normal_cross * target_second) / determinant
    weight_second = (normal_first * target_second - normal_cross * target_first) / determinant
    currents_ref[...] = weight_first * basis_own_ref[0:1, :] + weight_second * basis_own_ref[1:2, :]
    moments = weight_first * field_ref[0:6, :] + weight_second * field_ref[6:12, :]
    points = bundle_ref[6:9, 0:iron_ref.shape[1]] - 0.5
    px, py, pz = points[0:1], points[1:2], points[2:3]
    iron_ref[0:1, :] = pz * moments[1:2] - py * moments[2:3] - moments[3:4]
    iron_ref[1:2, :] = px * moments[2:3] - pz * moments[0:1] - moments[4:5]
    iron_ref[2:3, :] = py * moments[0:1] - px * moments[1:2] - moments[5:6]


def shape(*sizes, dtype=jnp.float32):
    return jax.ShapeDtypeStruct(sizes, dtype)


def shards(drive, resist, centers, tangents, iron_points, owner, range_len):
    seg_dev = drive.shape[0]
    col_len = centers.shape[1]
    n_col = lax.axis_size("col")
    n_row = lax.axis_size("row")
    n_dev = n_col * n_row
    segments = seg_dev * n_dev
    width = n_col * seg_dev
    points_count = iron_points.shape[1]
    coupling = 0.5 / math.sqrt(segments)
    call = functools.partial(pl.pallas_call, compiler_params=pltpu.CompilerParams(vmem_limit_bytes=VMEM_LIMIT))
    scratch = [pltpu.VMEM((1, segments), jnp.float32), pltpu.VMEM((seg_dev, 128), jnp.float32)]
    hbm = pl.BlockSpec(memory_space=pltpu.HBM)
    smem = pl.BlockSpec(memory_space=pltpu.SMEM)
    vmem = pl.BlockSpec(memory_space=pltpu.VMEM)

    def work(microseconds):
        return pl.CostEstimate(flops=int(microseconds * 1e9), bytes_accessed=0, transcendentals=0)

    def roomy(row_bytes):
        return STREAM_BYTES // row_bytes

    def exchange(x):
        return lax.all_to_all(x, AXES, 0, 0, tiled=True)

    drive_all = exchange(pl.pallas_call(
        spread_kernel,
        out_shape=shape(n_dev, 1, seg_dev),
        in_specs=[hbm],
        scratch_shapes=[pltpu.VMEM((1, seg_dev), jnp.float32), pltpu.SemaphoreType.DMA],
        compiler_params=pltpu.CompilerParams(vmem_limit_bytes=ENTRY_LIMIT),
        cost_estimate=work(8),
        name="spread",
    )(drive[None, :])).reshape(1, segments)
    longest = max(col_len, points_count, 2 * seg_dev)

    def wide(row):
        return jnp.pad(row, ((0, 0), (0, longest - row.shape[1])))

    bundle = jnp.concatenate([
        wide(centers), wide(tangents), wide(iron_points), wide(owner.reshape(1, points_count).astype(jnp.float32)),
        wide(jnp.concatenate([drive, resist])[None, :]),
    ], axis=0)

    def swap(x, bit):
        return lax.ppermute(x, "col", [(k, k ^ bit) for k in range(n_col)])

    bit = n_col // 2
    offsets = [0, bit]
    joined = call(
        join_kernel, out_shape=shape(2, 6, col_len), cost_estimate=work(1), name="join"
    )(bundle, swap(centers, bit), swap(tangents, bit))
    while bit > 1:
        bit //= 2
        other = swap(joined, bit)
        offsets = offsets + [offset ^ bit for offset in offsets]
        if bit > 1:
            joined = call(join_kernel, out_shape=shape(len(offsets), 6, col_len), name="join")(joined, other)

    chunk_count = points_count // CHUNK + n_row * (CHUNK - 1) // CHUNK
    chunk_count = -(-chunk_count // 8) * 8
    slot, group_table, left = call(
        functools.partial(group_kernel, n_row=n_row),
        out_shape=(
            shape(1, points_count, dtype=jnp.int32),
            shape(8, 128, dtype=jnp.int32),
            shape(chunk_count * CHUNK, 48, dtype=jnp.bfloat16),
        ),
        scratch_shapes=[pltpu.VMEM((48 * chunk_count, CHUNK), jnp.float32)],
        cost_estimate=work(3),
        name="group_points",
    )(bundle)

    cube_shape = (chunk_count, 2 * CHUNK, width)
    keep = 2 * math.prod(cube_shape) <= KEEP_BYTES
    stream = functools.partial(
        pl.pallas_call, compiler_params=pltpu.CompilerParams(vmem_limit_bytes=STREAM_LIMIT if keep else VMEM_LIMIT)
    )
    sides = call(
        functools.partial(sides_kernel, offsets=offsets),
        out_shape=(
            shape(48, segments, dtype=jnp.bfloat16), shape(8, segments),
            shape(2, seg_dev, 48, dtype=jnp.bfloat16), shape(3, seg_dev, 128),
        ),
        cost_estimate=work(1),
        name="sides",
    )(joined, other)
    right, moment = sides[0:2]
    image_own, image_spread = call(
        functools.partial(first_kernel, coupling),
        out_shape=(shape(1, seg_dev), shape(n_dev, 1, seg_dev)),
        scratch_shapes=scratch,
        cost_estimate=work(3),
        name="first_image",
    )(drive_all, bundle, group_table, *sides)
    image_all = exchange(image_spread).reshape(1, segments)
    cube_scratch = [pltpu.VMEM(cube_shape, jnp.bfloat16), pltpu.SemaphoreType.DMA((chunk_count,))]
    if keep:
        cubes, after = stream(
            functools.partial(weigh_kernel, n_row=n_row, n_col=n_col),
            out_shape=(shape(roomy(4 * CHUNK * width), *cube_shape[1:], dtype=jnp.bfloat16), shape(8, 128)),
            in_specs=[smem, vmem, vmem],
            out_specs=(hbm, vmem),
            scratch_shapes=cube_scratch,
            cost_estimate=work(5),
            name="weigh",
        )(group_table, left, right)
    else:
        after = group_table
    basis, basis_own, stats, known = call(
        functools.partial(second_kernel, coupling),
        out_shape=(shape(2, segments), shape(2, seg_dev), shape(n_dev, 1, 128), shape(1, 128)),
        scratch_shapes=scratch,
        cost_estimate=work(3),
        name="second_image",
    )(drive_all, image_all, image_own, bundle, after, *sides)
    stats_all = exchange(stats)

    field = stream(
        functools.partial(field_kernel, n_row=n_row, n_col=n_col, keep=keep),
        out_shape=shape(12, points_count),
        in_specs=[smem, smem, vmem, vmem, vmem] + ([hbm] if keep else [vmem, vmem]),
        scratch_shapes=[
            pltpu.VMEM((32, segments), jnp.bfloat16),
            pltpu.VMEM((16 * chunk_count, CHUNK), jnp.float32),
        ] + (cube_scratch if keep else []),
        cost_estimate=work(6),
        name="block_field",
    )(group_table, range_len, slot, moment, basis, *([cubes] if keep else [left, right]))
    currents, iron_field = stream(
        final_kernel,
        out_shape=(shape(1, seg_dev), shape(3, points_count)),
        name="combine",
    )(stats_all, known, basis_own, field, bundle)
    return (currents[0], iron_field)


def solution(mesh):
    return jax.shard_map(
        shards,
        mesh=mesh,
        in_specs=(
            P(AXES),
            P(AXES),
            P(None, "col"),
            P(None, "col"),
            P(None, AXES),
            P(AXES, None),
            P(),
        ),
        out_specs=(P(AXES), P(None, AXES)),
        check_vma=False,
    )
```

```python
import functools
import math

import jax
import jax.numpy as jnp
from jax import lax
from jax.experimental import pallas as pl
from jax.experimental.pallas import tpu as pltpu
from jax.sharding import PartitionSpec as P

EPS_SEG = 0.0004
EPS_FIELD = 0.0025
AXES = ("col", "row")
CHUNK = 128
GROUP = 4
TILE = 512
COLUMNS = 256
ROWS = 64
KEEP_BYTES = 16 * 1024 * 1024
VMEM_LIMIT = 32 * 1024 * 1024
STREAM_LIMIT = 44 * 1024 * 1024
ENTRY_LIMIT = 60 * 1024 * 1024
STREAM_BYTES = 20 * 1024 * 1024


def split3(x):
    high = x.astype(jnp.bfloat16).astype(jnp.float32)
    rest = x - high
    middle = rest.astype(jnp.bfloat16).astype(jnp.float32)
    low = (rest - middle).astype(jnp.bfloat16).astype(jnp.float32)
    return high, middle, low


def left_parts(x):
    high, middle, low = split3(x)
    return jnp.concatenate([high, high, middle, middle, high, low], axis=0)


def right_parts(x):
    high, middle, low = split3(x)
    return jnp.concatenate([high, middle, high, middle, low, high], axis=0).astype(jnp.bfloat16)


def rows8(*rows):
    width = rows[0].shape[1]
    count = sum(r.shape[0] for r in rows)
    if count < 8:
        rows = rows + (jnp.zeros((8 - count, width), jnp.float32),)
    return jnp.concatenate(rows, axis=0)


def left_center(c, eps):
    square = jnp.sum(c * c, axis=0, keepdims=True)
    return rows8(-2.0 * c, jnp.ones_like(square), square + eps)


def right_center(c):
    square = jnp.sum(c * c, axis=0, keepdims=True)
    return rows8(c, square, jnp.ones_like(square))


def dot(a, b):
    return jnp.dot(a, b, preferred_element_type=jnp.float32)


def dot_nt(a, b):
    return lax.dot_general(a, b, (((1,), (1,)), ((), ())), preferred_element_type=jnp.float32)


def transposed(x):
    return x.T.astype(jnp.bfloat16)


def iota(shape, axis):
    return lax.broadcasted_iota(jnp.int32, shape, axis)


def aligned(start, size):
    return pl.ds(pl.multiple_of(start, size), size)


def sides_kernel(*refs, n_col):
    pieces, (right_ref, moment_ref, left_ref, along_ref) = refs[:n_col], refs[n_col:]
    length = right_ref.shape[1] // n_col
    seg_dev = left_ref.shape[1]
    own_at = aligned(lax.axis_index("row") * seg_dev, seg_dev)
    tangent = rows8(pieces[0][3:6, own_at])
    left_ref[0] = transposed(left_parts(left_center(pieces[0][0:3, own_at] - 0.5, EPS_SEG)))
    left_ref[1] = transposed(left_parts(tangent))
    tangent = tangent.T
    for k in range(3):
        along_ref[k] = jnp.broadcast_to(tangent[:, k:k + 1], (seg_dev, 128))
    for offset, piece in enumerate(pieces):
        col = jnp.bitwise_xor(lax.axis_index("col"), offset)

        def step(k, carry):
            geo = piece[:, aligned(k * TILE, TILE)]
            to = pl.ds(pl.multiple_of(col * length + k * TILE, TILE), TILE)
            center, tangent = geo[0:3] - 0.5, geo[3:6]
            cross = jnp.concatenate([
                tangent[1:2] * center[2:3] - tangent[2:3] * center[1:2],
                tangent[2:3] * center[0:1] - tangent[0:1] * center[2:3],
                tangent[0:1] * center[1:2] - tangent[1:2] * center[0:1],
            ], axis=0)
            right_ref[:, to] = right_parts(right_center(center))
            moment_ref[:, to] = rows8(tangent, cross)
            return carry

        lax.fori_loop(0, length // TILE, step, 0, unroll=4)


def couple(right_ref, moment_ref, left_ref, along_ref, vec_ref, acc_ref):
    acc_ref[...] = jnp.zeros_like(acc_ref)

    def step(k, carry):
        at = aligned(k * TILE, TILE)
        turned = moment_ref[0:3, at] * vec_ref[:, at]
        right = right_ref[:, at]
        for first in range(0, TILE, COLUMNS):
            columns = slice(first, first + COLUMNS)
            by_product = first % (2 * COLUMNS) == 0
            if by_product:
                turned_parts = right_parts(rows8(turned[:, columns]))
            for row in range(0, acc_ref.shape[0], ROWS):
                rows = slice(row, row + ROWS)
                inverse = lax.rsqrt(dot(left_ref[0, rows], right[:, columns]))
                total = acc_ref[rows]
                if by_product:
                    pair = dot(left_ref[1, rows], turned_parts) * inverse
                    for start in range(0, COLUMNS, 128):
                        total = total + pair[:, start:start + 128]
                else:
                    for start in range(0, COLUMNS, 128):
                        lanes = slice(first + start, first + start + 128)
                        along = along_ref[0, rows] * turned[0:1, lanes]
                        along = along + along_ref[1, rows] * turned[1:2, lanes]
                        along = along + along_ref[2, rows] * turned[2:3, lanes]
                        total = total + along * inverse[:, start:start + 128]
                acc_ref[rows] = total
        return carry

    lax.fori_loop(0, vec_ref.shape[1] // TILE, step, 0, unroll=4)
    return jnp.sum(acc_ref[...].T, axis=0, keepdims=True)


def kept_copy(kept, index, out):
    local, remote, sems = kept
    if out:
        return pltpu.make_async_copy(local.at[index], remote.at[index], sems.at[index])
    return pltpu.make_async_copy(remote.at[index], local.at[index], sems.at[index])


def spread_rows(ref, row):
    for k in range(ref.shape[0]):
        ref[k] = row


def spread_kernel(drive_hbm, out_ref, drive, sem):
    copy = pltpu.make_async_copy(drive_hbm, drive, sem)
    copy.start()
    copy.wait()
    spread_rows(out_ref, drive[...])


def take_kernel(bundle_ref, out_ref):
    out_ref[...] = bundle_ref[0:6, 0:out_ref.shape[1]]


def own_rows(bundle_ref, like_ref):
    seg_dev = like_ref.shape[1]
    return bundle_ref[10:11, 0:seg_dev], bundle_ref[10:11, seg_dev:2 * seg_dev]


def first_kernel(coupling, drive_ref, bundle_ref, after_ref, right_ref, moment_ref, left_ref, along_ref,
                 image_ref, spread_ref, vec_ref, acc_ref):
    drive = drive_ref[...]
    scale = 1.0 / jnp.sqrt(jnp.sum(drive * drive, keepdims=True))
    vec_ref[...] = drive * scale
    product = couple(right_ref, moment_ref, left_ref, along_ref, vec_ref, acc_ref)
    drive_own, resist_own = own_rows(bundle_ref, image_ref)
    image = resist_own * (drive_own * scale) + coupling * product
    image_ref[...] = image
    spread_rows(spread_ref, image)


def second_kernel(coupling, drive_ref, image_ref, image_own_ref, bundle_ref, after_ref,
                  right_ref, moment_ref, left_ref, along_ref,
                  basis_ref, basis_own_ref, stats_ref, known_ref, vec_ref, acc_ref):
    drive = drive_ref[...]
    norm = jnp.sqrt(jnp.sum(drive * drive, keepdims=True))
    scale = 1.0 / norm
    basis_a = drive * scale
    image = image_ref[...]
    hessen_a = jnp.sum(image * basis_a, keepdims=True)
    rest = image - hessen_a * basis_a
    hessen_b = jnp.sqrt(jnp.sum(rest * rest, keepdims=True))
    inverse = 1.0 / hessen_b
    basis_b = rest * inverse
    vec_ref[...] = basis_b
    basis_ref[0:1, :] = basis_a
    basis_ref[1:2, :] = basis_b
    drive_own, resist_own = own_rows(bundle_ref, image_own_ref)
    own_a = drive_own * scale
    own_b = (image_own_ref[...] - hessen_a * own_a) * inverse
    basis_own_ref[0:1, :] = own_a
    basis_own_ref[1:2, :] = own_b
    product = couple(right_ref, moment_ref, left_ref, along_ref, vec_ref, acc_ref)
    second = resist_own * own_b + coupling * product
    lane = iota((1, 128), 1)

    def three(a, b, c):
        return jnp.where(lane == 0, a, jnp.where(lane == 1, b, jnp.where(lane == 2, c, 0.0)))

    spread_rows(stats_ref, three(
        jnp.sum(second * own_a, keepdims=True),
        jnp.sum(second * own_b, keepdims=True),
        jnp.sum(second * second, keepdims=True),
    ))
    known_ref[...] = three(norm, hessen_a, hessen_b)


def group_kernel(bundle_ref, slot_ref, table_ref, left_ref, planes_ref, *, n_row):
    points = slot_ref.shape[1]
    chunk_count = left_ref.shape[0] // CHUNK
    owner = bundle_ref[9:10, 0:points].astype(jnp.int32)
    rows = max(8, n_row)
    marks = jnp.where(iota((rows, points), 0) == owner, 1.0, 0.0)
    tile = 256
    upper = jnp.where(iota((tile, tile), 0) <= iota((tile, tile), 1), 1.0, 0.0).astype(jnp.bfloat16)
    before = jnp.zeros((rows, 1), jnp.float32)
    ranks = []
    for piece in range(points // tile):
        part = dot(marks[:, piece * tile:(piece + 1) * tile].astype(jnp.bfloat16), upper)
        ranks.append(part + before - 1.0)
        before = before + part[:, tile - 1:tile]
    ranks = jnp.concatenate(ranks, axis=1)
    chunks = jnp.floor((before + (CHUNK - 1)) * (1.0 / CHUNK))
    start = jnp.zeros((1, 1), jnp.float32)
    starts = []
    for name in range(rows):
        starts.append(start)
        start = start + chunks[name:name + 1]
    starts = jnp.concatenate(starts, axis=0)
    slot = jnp.sum(marks * (ranks + starts * CHUNK), axis=0, keepdims=True).astype(jnp.int32)
    slot_ref[...] = slot
    lane = iota((rows, 128), 1)
    ended = jnp.sum(jnp.where(starts + chunks <= lane.astype(jnp.float32), 1.0, 0.0), axis=0, keepdims=True)
    block = jnp.minimum(ended, n_row - 1.0)
    place = iota((8, 128), 0)
    table_ref[...] = jnp.where(place == 0, block, start).astype(jnp.int32)
    high = jnp.where(iota((chunk_count, points), 0) == slot // CHUNK, 1.0, 0.0)
    low = jnp.where(iota((CHUNK, points), 0) == slot % CHUNK, 1.0, 0.0).astype(jnp.bfloat16)
    parts = split3(bundle_ref[6:9, 0:points] - 0.5)
    spread = jnp.concatenate([high * part[k:k + 1] for k in range(3) for part in parts], axis=0).astype(jnp.bfloat16)
    placed = dot_nt(spread, low)
    planes = [placed[k * chunk_count:(k + 1) * chunk_count] for k in range(9)]
    x, y, z = (planes[3 * k] + planes[3 * k + 1] + planes[3 * k + 2] for k in range(3))
    sides = [-2.0 * x, -2.0 * y, -2.0 * z, jnp.ones_like(x), x * x + y * y + z * z + EPS_FIELD]
    sides = [split3(side) for side in sides]
    empty = jnp.zeros_like(x)
    for group, part in enumerate([0, 0, 1, 1, 0, 2]):
        for k in range(8):
            to = pl.ds((group * 8 + k) * chunk_count, chunk_count)
            planes_ref[to, :] = sides[k][part] if k < 5 else empty
    for chunk in range(chunk_count):
        left_ref[chunk * CHUNK:(chunk + 1) * CHUNK, :] = transposed(planes_ref[pl.ds(chunk, 48, stride=chunk_count), :])


def cube_halves(left, right):
    inverse = lax.rsqrt(dot(left, right))
    cube = inverse * inverse * inverse
    high = cube.astype(jnp.bfloat16)
    return high, (cube - high.astype(jnp.float32)).astype(jnp.bfloat16)


def block_part(block, col, n_row, seg_dev):
    return aligned((col * n_row + block) * seg_dev, seg_dev)


def chunk_steps(group_ref):
    return (group_ref[1, 0] + GROUP - 1) // GROUP


def weigh_kernel(group_ref, left_ref, right_ref, cubes_hbm, done_ref, cubes_ref, sems, *, n_row, n_col):
    seg_dev = right_ref.shape[1] // (n_row * n_col)
    done_ref[...] = jnp.zeros_like(done_ref)
    kept = (cubes_ref, cubes_hbm, sems)

    def step(k, carry):
        for part in range(GROUP):
            chunk = k * GROUP + part
            left = left_ref[aligned(chunk * CHUNK, CHUNK), :]
            for col in range(n_col):
                to = slice(col * seg_dev, (col + 1) * seg_dev)
                high, low = cube_halves(left, right_ref[:, block_part(group_ref[0, chunk], col, n_row, seg_dev)])
                cubes_ref[chunk, 0:CHUNK, to] = high
                cubes_ref[chunk, CHUNK:2 * CHUNK, to] = low
            kept_copy(kept, chunk, out=True).start()
        return carry

    def finish(k, carry):
        for part in range(GROUP):
            kept_copy(kept, k * GROUP + part, out=True).wait()
        return carry

    lax.fori_loop(0, chunk_steps(group_ref), step, 0)
    lax.fori_loop(0, chunk_steps(group_ref), finish, 0)


def field_kernel(group_ref, length_ref, slot_ref, moment_ref, basis_ref, *refs, n_row, n_col, keep):
    if keep:
        cubes_hbm, out_ref, table_ref, sums_ref, cubes_ref, sems = refs
        kept = (cubes_ref, cubes_hbm, sems)

        def begin(k, carry):
            for part in range(GROUP):
                kept_copy(kept, k * GROUP + part, out=False).start()
            return carry

        lax.fori_loop(0, chunk_steps(group_ref), begin, 0)
    else:
        left_ref, right_ref, out_ref, table_ref, sums_ref = refs
    chunk_count = sums_ref.shape[0] // 16
    seg_dev = moment_ref.shape[1] // (n_row * n_col)
    scale = 1.0 / math.sqrt(n_col * seg_dev)
    lane = iota((1, seg_dev), 1)
    sums_ref[...] = jnp.zeros_like(sums_ref)

    def table_step(block, carry):
        length = length_ref[block]
        for col in range(n_col):
            at = block_part(block, col, n_row, seg_dev)
            both = moment_ref[:, at]
            active = jnp.where(lane + col * seg_dev < length, scale, 0.0)
            first = both * (basis_ref[0:1, at] * active)
            second = both * (basis_ref[1:2, at] * active)
            parts = jnp.concatenate([first, second], axis=0)
            high = parts.astype(jnp.bfloat16).astype(jnp.float32)
            table_ref[:, at] = jnp.concatenate([high, parts - high], axis=0).astype(jnp.bfloat16)
        return carry

    lax.fori_loop(0, n_row, table_step, 0, unroll=min(n_row, 8))

    def block_row(ref, chunk):
        block = group_ref[0, chunk]
        return jnp.concatenate([ref[:, block_part(block, col, n_row, seg_dev)] for col in range(n_col)], axis=1)

    def cubes_of(chunk):
        return jnp.concatenate(cube_halves(left_ref[aligned(chunk * CHUNK, CHUNK), :], block_row(right_ref, chunk)), axis=0)

    def step(k, carry):
        for part in range(0, GROUP, 2):
            chunk = k * GROUP + part
            tables = jnp.concatenate([block_row(table_ref, chunk), block_row(table_ref, chunk + 1)], axis=0)
            if keep:
                kept_copy(kept, chunk, out=False).wait()
                kept_copy(kept, chunk + 1, out=False).wait()
                cubes = cubes_ref[pl.ds(chunk, 2)].reshape(4 * CHUNK, n_col * seg_dev)
            else:
                cubes = jnp.concatenate([cubes_of(chunk), cubes_of(chunk + 1)], axis=0)
            both = dot_nt(tables, cubes)
            for half in range(2):
                mine = both[32 * half:32 * half + 32, 2 * CHUNK * half:2 * CHUNK * (half + 1)]
                total = mine[:, 0:CHUNK] + mine[:, CHUNK:2 * CHUNK]
                sums_ref[pl.ds(chunk + half, 16, stride=chunk_count), :] = total[0:16] + total[16:32]
        return carry

    lax.fori_loop(0, chunk_steps(group_ref), step, 0)
    sums = jnp.concatenate([sums_ref[0:6 * chunk_count], sums_ref[8 * chunk_count:14 * chunk_count]], axis=0)
    sums = jnp.concatenate(split3(sums), axis=1).astype(jnp.bfloat16)
    for tile in range(slot_ref.shape[1] // TILE):
        at = pl.ds(tile * TILE, TILE)
        slot = slot_ref[:, at]
        low = jnp.where(iota((CHUNK, TILE), 0) == slot % CHUNK, 1.0, 0.0).astype(jnp.bfloat16)
        high = jnp.where(iota((chunk_count, TILE), 0) == slot // CHUNK, 1.0, 0.0)
        found = dot(sums, jnp.concatenate([low, low, low], axis=0))
        for row in range(12):
            picked = found[row * chunk_count:(row + 1) * chunk_count] * high
            out_ref[row:row + 1, at] = jnp.sum(picked, axis=0, keepdims=True)


def final_kernel(stats_ref, known_ref, basis_own_ref, field_ref, bundle_ref, currents_ref, iron_ref):
    stats = jnp.sum(stats_ref[...], axis=0)
    known = known_ref[...]
    initial_norm, hessen_a, hessen_b = known[:, 0:1], known[:, 1:2], known[:, 2:3]
    hessen_c, hessen_d, normal_second = stats[:, 0:1], stats[:, 1:2], stats[:, 2:3]
    normal_first = hessen_a * hessen_a + hessen_b * hessen_b
    normal_cross = hessen_a * hessen_c + hessen_b * hessen_d
    target_first = initial_norm * hessen_a
    target_second = initial_norm * hessen_c
    determinant = normal_first * normal_second - normal_cross * normal_cross
    weight_first = (normal_second * target_first - normal_cross * target_second) / determinant
    weight_second = (normal_first * target_second - normal_cross * target_first) / determinant
    currents_ref[...] = weight_first * basis_own_ref[0:1, :] + weight_second * basis_own_ref[1:2, :]
    moments = weight_first * field_ref[0:6, :] + weight_second * field_ref[6:12, :]
    points = bundle_ref[6:9, 0:iron_ref.shape[1]] - 0.5
    px, py, pz = points[0:1], points[1:2], points[2:3]
    iron_ref[0:1, :] = pz * moments[1:2] - py * moments[2:3] - moments[3:4]
    iron_ref[1:2, :] = px * moments[2:3] - pz * moments[0:1] - moments[4:5]
    iron_ref[2:3, :] = py * moments[0:1] - px * moments[1:2] - moments[5:6]


def shape(*sizes, dtype=jnp.float32):
    return jax.ShapeDtypeStruct(sizes, dtype)


def shards(drive, resist, centers, tangents, iron_points, owner, range_len):
    seg_dev = drive.shape[0]
    col_len = centers.shape[1]
    n_col = lax.axis_size("col")
    n_row = lax.axis_size("row")
    n_dev = n_col * n_row
    segments = seg_dev * n_dev
    width = n_col * seg_dev
    points_count = iron_points.shape[1]
    coupling = 0.5 / math.sqrt(segments)
    call = functools.partial(pl.pallas_call, compiler_params=pltpu.CompilerParams(vmem_limit_bytes=VMEM_LIMIT))
    scratch = [pltpu.VMEM((1, segments), jnp.float32), pltpu.VMEM((seg_dev, 128), jnp.float32)]
    hbm = pl.BlockSpec(memory_space=pltpu.HBM)
    smem = pl.BlockSpec(memory_space=pltpu.SMEM)
    vmem = pl.BlockSpec(memory_space=pltpu.VMEM)

    def work(microseconds):
        return pl.CostEstimate(flops=int(microseconds * 1e9), bytes_accessed=0, transcendentals=0)

    def roomy(row_bytes):
        return STREAM_BYTES // row_bytes

    def exchange(x):
        return lax.all_to_all(x, AXES, 0, 0, tiled=True)

    drive_all = exchange(pl.pallas_call(
        spread_kernel,
        out_shape=shape(n_dev, 1, seg_dev),
        in_specs=[hbm],
        scratch_shapes=[pltpu.VMEM((1, seg_dev), jnp.float32), pltpu.SemaphoreType.DMA],
        compiler_params=pltpu.CompilerParams(vmem_limit_bytes=ENTRY_LIMIT),
        cost_estimate=work(8),
        name="spread",
    )(drive[None, :])).reshape(1, segments)
    longest = max(col_len, points_count, 2 * seg_dev)

    def wide(row):
        return jnp.pad(row, ((0, 0), (0, longest - row.shape[1])))

    bundle = jnp.concatenate([
        wide(centers), wide(tangents), wide(iron_points), wide(owner.reshape(1, points_count).astype(jnp.float32)),
        wide(jnp.concatenate([drive, resist])[None, :]),
    ], axis=0)

    own_geometry = call(take_kernel, out_shape=shape(6, col_len), cost_estimate=work(1), name="take")(bundle)
    pieces = [own_geometry] + [
        lax.ppermute(own_geometry, "col", [(k, k ^ offset) for k in range(n_col)]) for offset in range(1, n_col)
    ]

    chunk_count = points_count // CHUNK + n_row * (CHUNK - 1) // CHUNK
    chunk_count = -(-chunk_count // 8) * 8
    slot, group_table, left = call(
        functools.partial(group_kernel, n_row=n_row),
        out_shape=(
            shape(1, points_count, dtype=jnp.int32),
            shape(8, 128, dtype=jnp.int32),
            shape(chunk_count * CHUNK, 48, dtype=jnp.bfloat16),
        ),
        scratch_shapes=[pltpu.VMEM((48 * chunk_count, CHUNK), jnp.float32)],
        cost_estimate=work(30),
        name="group_points",
    )(bundle)

    cube_shape = (chunk_count, 2 * CHUNK, width)
    keep = 2 * math.prod(cube_shape) <= KEEP_BYTES
    stream = functools.partial(
        pl.pallas_call, compiler_params=pltpu.CompilerParams(vmem_limit_bytes=STREAM_LIMIT if keep else VMEM_LIMIT)
    )
    sides = call(
        functools.partial(sides_kernel, n_col=n_col),
        out_shape=(
            shape(48, segments, dtype=jnp.bfloat16), shape(8, segments),
            shape(2, seg_dev, 48, dtype=jnp.bfloat16), shape(3, seg_dev, 128),
        ),
        cost_estimate=work(1),
        name="sides",
    )(*pieces)
    right, moment = sides[0:2]
    image_own, image_spread = call(
        functools.partial(first_kernel, coupling),
        out_shape=(shape(1, seg_dev), shape(n_dev, 1, seg_dev)),
        scratch_shapes=scratch,
        cost_estimate=work(3),
        name="first_image",
    )(drive_all, bundle, group_table, *sides)
    image_all = exchange(image_spread).reshape(1, segments)
    cube_scratch = [pltpu.VMEM(cube_shape, jnp.bfloat16), pltpu.SemaphoreType.DMA((chunk_count,))]
    if keep:
        cubes, after = stream(
            functools.partial(weigh_kernel, n_row=n_row, n_col=n_col),
            out_shape=(shape(roomy(4 * CHUNK * width), *cube_shape[1:], dtype=jnp.bfloat16), shape(8, 128)),
            in_specs=[smem, vmem, vmem],
            out_specs=(hbm, vmem),
            scratch_shapes=cube_scratch,
            cost_estimate=work(5),
            name="weigh",
        )(group_table, left, right)
    else:
        after = group_table
    basis, basis_own, stats, known = call(
        functools.partial(second_kernel, coupling),
        out_shape=(shape(2, segments), shape(2, seg_dev), shape(n_dev, 1, 128), shape(1, 128)),
        scratch_shapes=scratch,
        cost_estimate=work(3),
        name="second_image",
    )(drive_all, image_all, image_own, bundle, after, *sides)
    stats_all = exchange(stats)

    field = stream(
        functools.partial(field_kernel, n_row=n_row, n_col=n_col, keep=keep),
        out_shape=shape(12, points_count),
        in_specs=[smem, smem, vmem, vmem, vmem] + ([hbm] if keep else [vmem, vmem]),
        scratch_shapes=[
            pltpu.VMEM((32, segments), jnp.bfloat16),
            pltpu.VMEM((16 * chunk_count, CHUNK), jnp.float32),
        ] + (cube_scratch if keep else []),
        cost_estimate=work(6),
        name="block_field",
    )(group_table, range_len, slot, moment, basis, *([cubes] if keep else [left, right]))
    currents, iron_field = stream(
        final_kernel,
        out_shape=(shape(1, seg_dev), shape(3, points_count)),
        name="combine",
    )(stats_all, known, basis_own, field, bundle)
    return (currents[0], iron_field)


def solution(mesh):
    return jax.shard_map(
        shards,
        mesh=mesh,
        in_specs=(
            P(AXES),
            P(AXES),
            P(None, "col"),
            P(None, "col"),
            P(None, AXES),
            P(AXES, None),
            P(),
        ),
        out_specs=(P(AXES), P(None, AXES)),
        check_vma=False,
    )
```

```python
import functools
import math

import jax
import jax.numpy as jnp
from jax import lax
from jax.experimental import pallas as pl
from jax.experimental.pallas import tpu as pltpu
from jax.sharding import PartitionSpec as P

EPS_SEG = 0.0004
EPS_FIELD = 0.0025
AXES = ("col", "row")
CHUNK = 128
GROUP = 4
TILE = 512
COLUMNS = 256
ROWS = 64
KEEP_BYTES = 16 * 1024 * 1024
VMEM_LIMIT = 32 * 1024 * 1024
STREAM_LIMIT = 44 * 1024 * 1024
ENTRY_LIMIT = 60 * 1024 * 1024
STREAM_BYTES = 20 * 1024 * 1024


def split3(x):
    high = x.astype(jnp.bfloat16).astype(jnp.float32)
    rest = x - high
    middle = rest.astype(jnp.bfloat16).astype(jnp.float32)
    low = (rest - middle).astype(jnp.bfloat16).astype(jnp.float32)
    return high, middle, low


def left_parts(x):
    high, middle, low = split3(x)
    return jnp.concatenate([high, high, middle, middle, high, low], axis=0)


def right_parts(x):
    high, middle, low = split3(x)
    return jnp.concatenate([high, middle, high, middle, low, high], axis=0).astype(jnp.bfloat16)


def rows8(*rows):
    width = rows[0].shape[1]
    count = sum(r.shape[0] for r in rows)
    if count < 8:
        rows = rows + (jnp.zeros((8 - count, width), jnp.float32),)
    return jnp.concatenate(rows, axis=0)


def left_center(c, eps):
    square = jnp.sum(c * c, axis=0, keepdims=True)
    return rows8(-2.0 * c, jnp.ones_like(square), square + eps)


def right_center(c):
    square = jnp.sum(c * c, axis=0, keepdims=True)
    return rows8(c, square, jnp.ones_like(square))


def dot(a, b):
    return jnp.dot(a, b, preferred_element_type=jnp.float32)


def dot_nt(a, b):
    return lax.dot_general(a, b, (((1,), (1,)), ((), ())), preferred_element_type=jnp.float32)


def transposed(x):
    return x.T.astype(jnp.bfloat16)


def iota(shape, axis):
    return lax.broadcasted_iota(jnp.int32, shape, axis)


def aligned(start, size):
    return pl.ds(pl.multiple_of(start, size), size)


def sides_kernel(joined_ref, other_ref, right_ref, moment_ref, left_ref, along_ref, *, offsets):
    n_col = len(offsets)
    half = n_col // 2
    length = right_ref.shape[1] // n_col
    seg_dev = left_ref.shape[1]
    own_at = aligned(lax.axis_index("row") * seg_dev, seg_dev)
    tangent = rows8(joined_ref[0, 3:6, own_at])
    left_ref[0] = transposed(left_parts(left_center(joined_ref[0, 0:3, own_at] - 0.5, EPS_SEG)))
    left_ref[1] = transposed(left_parts(tangent))
    tangent = tangent.T
    for k in range(3):
        along_ref[k] = jnp.broadcast_to(tangent[:, k:k + 1], (seg_dev, 128))
    for index, offset in enumerate(offsets):
        piece = joined_ref.at[index] if index < half else other_ref.at[index - half]
        col = jnp.bitwise_xor(lax.axis_index("col"), offset)

        def step(k, carry):
            geo = piece[:, aligned(k * TILE, TILE)]
            to = pl.ds(pl.multiple_of(col * length + k * TILE, TILE), TILE)
            center, tangent = geo[0:3] - 0.5, geo[3:6]
            cross = jnp.concatenate([
                tangent[1:2] * center[2:3] - tangent[2:3] * center[1:2],
                tangent[2:3] * center[0:1] - tangent[0:1] * center[2:3],
                tangent[0:1] * center[1:2] - tangent[1:2] * center[0:1],
            ], axis=0)
            right_ref[:, to] = right_parts(right_center(center))
            moment_ref[:, to] = rows8(tangent, cross)
            return carry

        lax.fori_loop(0, length // TILE, step, 0, unroll=4)


def couple(right_ref, moment_ref, left_ref, along_ref, vec_ref, acc_ref):
    acc_ref[...] = jnp.zeros_like(acc_ref)

    def step(k, carry):
        at = aligned(k * TILE, TILE)
        turned = moment_ref[0:3, at] * vec_ref[:, at]
        right = right_ref[:, at]
        for first in range(0, TILE, COLUMNS):
            columns = slice(first, first + COLUMNS)
            by_product = first % (2 * COLUMNS) == 0
            if by_product:
                turned_parts = right_parts(rows8(turned[:, columns]))
            for row in range(0, acc_ref.shape[0], ROWS):
                rows = slice(row, row + ROWS)
                inverse = lax.rsqrt(dot(left_ref[0, rows], right[:, columns]))
                total = acc_ref[rows]
                if by_product:
                    pair = dot(left_ref[1, rows], turned_parts) * inverse
                    for start in range(0, COLUMNS, 128):
                        total = total + pair[:, start:start + 128]
                else:
                    for start in range(0, COLUMNS, 128):
                        lanes = slice(first + start, first + start + 128)
                        along = along_ref[0, rows] * turned[0:1, lanes]
                        along = along + along_ref[1, rows] * turned[1:2, lanes]
                        along = along + along_ref[2, rows] * turned[2:3, lanes]
                        total = total + along * inverse[:, start:start + 128]
                acc_ref[rows] = total
        return carry

    lax.fori_loop(0, vec_ref.shape[1] // TILE, step, 0, unroll=4)
    return jnp.sum(acc_ref[...].T, axis=0, keepdims=True)


def kept_copy(kept, index, out):
    local, remote, sems = kept
    if out:
        return pltpu.make_async_copy(local.at[index], remote.at[index], sems.at[index])
    return pltpu.make_async_copy(remote.at[index], local.at[index], sems.at[index])


def spread_rows(ref, row):
    for k in range(ref.shape[0]):
        ref[k] = row


def spread_kernel(drive_hbm, out_ref, drive, sem):
    copy = pltpu.make_async_copy(drive_hbm, drive, sem)
    copy.start()
    copy.wait()
    spread_rows(out_ref, drive[...])


def join_kernel(*refs):
    out_ref = refs[-1]
    if len(refs) == 4:
        bundle_ref, centers_ref, tangents_ref = refs[0:3]
        out_ref[0] = bundle_ref[0:6, 0:out_ref.shape[2]]
        out_ref[1, 0:3] = centers_ref[...]
        out_ref[1, 3:6] = tangents_ref[...]
    else:
        held = refs[0].shape[0]
        out_ref[0:held] = refs[0][...]
        out_ref[held:2 * held] = refs[1][...]


def own_rows(bundle_ref, like_ref):
    seg_dev = like_ref.shape[1]
    return bundle_ref[10:11, 0:seg_dev], bundle_ref[10:11, seg_dev:2 * seg_dev]


def first_kernel(coupling, drive_ref, bundle_ref, after_ref, right_ref, moment_ref, left_ref, along_ref,
                 image_ref, spread_ref, vec_ref, acc_ref):
    drive = drive_ref[...]
    scale = 1.0 / jnp.sqrt(jnp.sum(drive * drive, keepdims=True))
    vec_ref[...] = drive * scale
    product = couple(right_ref, moment_ref, left_ref, along_ref, vec_ref, acc_ref)
    drive_own, resist_own = own_rows(bundle_ref, image_ref)
    image = resist_own * (drive_own * scale) + coupling * product
    image_ref[...] = image
    spread_rows(spread_ref, image)


def second_kernel(coupling, drive_ref, image_ref, image_own_ref, bundle_ref, after_ref,
                  right_ref, moment_ref, left_ref, along_ref,
                  basis_ref, basis_own_ref, stats_ref, known_ref, vec_ref, acc_ref):
    drive = drive_ref[...]
    norm = jnp.sqrt(jnp.sum(drive * drive, keepdims=True))
    scale = 1.0 / norm
    basis_a = drive * scale
    image = image_ref[...]
    hessen_a = jnp.sum(image * basis_a, keepdims=True)
    rest = image - hessen_a * basis_a
    hessen_b = jnp.sqrt(jnp.sum(rest * rest, keepdims=True))
    inverse = 1.0 / hessen_b
    basis_b = rest * inverse
    vec_ref[...] = basis_b
    basis_ref[0:1, :] = basis_a
    basis_ref[1:2, :] = basis_b
    drive_own, resist_own = own_rows(bundle_ref, image_own_ref)
    own_a = drive_own * scale
    own_b = (image_own_ref[...] - hessen_a * own_a) * inverse
    basis_own_ref[0:1, :] = own_a
    basis_own_ref[1:2, :] = own_b
    product = couple(right_ref, moment_ref, left_ref, along_ref, vec_ref, acc_ref)
    second = resist_own * own_b + coupling * product
    lane = iota((1, 128), 1)

    def three(a, b, c):
        return jnp.where(lane == 0, a, jnp.where(lane == 1, b, jnp.where(lane == 2, c, 0.0)))

    spread_rows(stats_ref, three(
        jnp.sum(second * own_a, keepdims=True),
        jnp.sum(second * own_b, keepdims=True),
        jnp.sum(second * second, keepdims=True),
    ))
    known_ref[...] = three(norm, hessen_a, hessen_b)


def group_kernel(bundle_ref, slot_ref, table_ref, left_ref, planes_ref, *, n_row):
    points = slot_ref.shape[1]
    chunk_count = left_ref.shape[0] // CHUNK
    owner = bundle_ref[9:10, 0:points].astype(jnp.int32)
    rows = max(8, n_row)
    marks = jnp.where(iota((rows, points), 0) == owner, 1.0, 0.0)
    tile = 256
    upper = jnp.where(iota((tile, tile), 0) <= iota((tile, tile), 1), 1.0, 0.0).astype(jnp.bfloat16)
    before = jnp.zeros((rows, 1), jnp.float32)
    ranks = []
    for piece in range(points // tile):
        part = dot(marks[:, piece * tile:(piece + 1) * tile].astype(jnp.bfloat16), upper)
        ranks.append(part + before - 1.0)
        before = before + part[:, tile - 1:tile]
    ranks = jnp.concatenate(ranks, axis=1)
    chunks = jnp.floor((before + (CHUNK - 1)) * (1.0 / CHUNK))
    start = jnp.zeros((1, 1), jnp.float32)
    starts = []
    for name in range(rows):
        starts.append(start)
        start = start + chunks[name:name + 1]
    starts = jnp.concatenate(starts, axis=0)
    slot = jnp.sum(marks * (ranks + starts * CHUNK), axis=0, keepdims=True).astype(jnp.int32)
    slot_ref[...] = slot
    lane = iota((rows, 128), 1)
    ended = jnp.sum(jnp.where(starts + chunks <= lane.astype(jnp.float32), 1.0, 0.0), axis=0, keepdims=True)
    block = jnp.minimum(ended, n_row - 1.0)
    place = iota((8, 128), 0)
    table_ref[...] = jnp.where(place == 0, block, start).astype(jnp.int32)
    high = jnp.where(iota((chunk_count, points), 0) == slot // CHUNK, 1.0, 0.0)
    low = jnp.where(iota((CHUNK, points), 0) == slot % CHUNK, 1.0, 0.0).astype(jnp.bfloat16)
    parts = split3(bundle_ref[6:9, 0:points] - 0.5)
    spread = jnp.concatenate([high * part[k:k + 1] for k in range(3) for part in parts], axis=0).astype(jnp.bfloat16)
    placed = dot_nt(spread, low)
    planes = [placed[k * chunk_count:(k + 1) * chunk_count] for k in range(9)]
    x, y, z = (planes[3 * k] + planes[3 * k + 1] + planes[3 * k + 2] for k in range(3))
    sides = [-2.0 * x, -2.0 * y, -2.0 * z, jnp.ones_like(x), x * x + y * y + z * z + EPS_FIELD]
    sides = [split3(side) for side in sides]
    empty = jnp.zeros_like(x)
    for group, part in enumerate([0, 0, 1, 1, 0, 2]):
        for k in range(8):
            to = pl.ds((group * 8 + k) * chunk_count, chunk_count)
            planes_ref[to, :] = sides[k][part] if k < 5 else empty
    for chunk in range(chunk_count):
        left_ref[chunk * CHUNK:(chunk + 1) * CHUNK, :] = transposed(planes_ref[pl.ds(chunk, 48, stride=chunk_count), :])


def cube_halves(left, right):
    inverse = lax.rsqrt(dot(left, right))
    cube = inverse * inverse * inverse
    high = cube.astype(jnp.bfloat16)
    return high, (cube - high.astype(jnp.float32)).astype(jnp.bfloat16)


def block_part(block, col, n_row, seg_dev):
    return aligned((col * n_row + block) * seg_dev, seg_dev)


def chunk_steps(group_ref):
    return (group_ref[1, 0] + GROUP - 1) // GROUP


def weigh_kernel(group_ref, left_ref, right_ref, cubes_hbm, done_ref, cubes_ref, sems, *, n_row, n_col):
    seg_dev = right_ref.shape[1] // (n_row * n_col)
    done_ref[...] = jnp.zeros_like(done_ref)
    kept = (cubes_ref, cubes_hbm, sems)

    def step(k, carry):
        for part in range(GROUP):
            chunk = k * GROUP + part
            left = left_ref[aligned(chunk * CHUNK, CHUNK), :]
            for col in range(n_col):
                to = slice(col * seg_dev, (col + 1) * seg_dev)
                high, low = cube_halves(left, right_ref[:, block_part(group_ref[0, chunk], col, n_row, seg_dev)])
                cubes_ref[chunk, 0:CHUNK, to] = high
                cubes_ref[chunk, CHUNK:2 * CHUNK, to] = low
            kept_copy(kept, chunk, out=True).start()
        return carry

    def finish(k, carry):
        for part in range(GROUP):
            kept_copy(kept, k * GROUP + part, out=True).wait()
        return carry

    lax.fori_loop(0, chunk_steps(group_ref), step, 0)
    lax.fori_loop(0, chunk_steps(group_ref), finish, 0)


def field_kernel(group_ref, length_ref, slot_ref, moment_ref, basis_ref, *refs, n_row, n_col, keep):
    if keep:
        cubes_hbm, out_ref, table_ref, sums_ref, cubes_ref, sems = refs
        kept = (cubes_ref, cubes_hbm, sems)

        def begin(k, carry):
            for part in range(GROUP):
                kept_copy(kept, k * GROUP + part, out=False).start()
            return carry

        lax.fori_loop(0, chunk_steps(group_ref), begin, 0)
    else:
        left_ref, right_ref, out_ref, table_ref, sums_ref = refs
    chunk_count = sums_ref.shape[0] // 16
    seg_dev = moment_ref.shape[1] // (n_row * n_col)
    scale = 1.0 / math.sqrt(n_col * seg_dev)
    lane = iota((1, seg_dev), 1)
    sums_ref[...] = jnp.zeros_like(sums_ref)

    def table_step(block, carry):
        length = length_ref[block]
        for col in range(n_col):
            at = block_part(block, col, n_row, seg_dev)
            both = moment_ref[:, at]
            active = jnp.where(lane + col * seg_dev < length, scale, 0.0)
            first = both * (basis_ref[0:1, at] * active)
            second = both * (basis_ref[1:2, at] * active)
            parts = jnp.concatenate([first, second], axis=0)
            high = parts.astype(jnp.bfloat16).astype(jnp.float32)
            table_ref[:, at] = jnp.concatenate([high, parts - high], axis=0).astype(jnp.bfloat16)
        return carry

    lax.fori_loop(0, n_row, table_step, 0, unroll=min(n_row, 8))

    def block_row(ref, chunk):
        block = group_ref[0, chunk]
        return jnp.concatenate([ref[:, block_part(block, col, n_row, seg_dev)] for col in range(n_col)], axis=1)

    def cubes_of(chunk):
        return jnp.concatenate(cube_halves(left_ref[aligned(chunk * CHUNK, CHUNK), :], block_row(right_ref, chunk)), axis=0)

    def step(k, carry):
        for part in range(0, GROUP, 2):
            chunk = k * GROUP + part
            tables = jnp.concatenate([block_row(table_ref, chunk), block_row(table_ref, chunk + 1)], axis=0)
            if keep:
                kept_copy(kept, chunk, out=False).wait()
                kept_copy(kept, chunk + 1, out=False).wait()
                cubes = cubes_ref[pl.ds(chunk, 2)].reshape(4 * CHUNK, n_col * seg_dev)
            else:
                cubes = jnp.concatenate([cubes_of(chunk), cubes_of(chunk + 1)], axis=0)
            both = dot_nt(tables, cubes)
            for half in range(2):
                mine = both[32 * half:32 * half + 32, 2 * CHUNK * half:2 * CHUNK * (half + 1)]
                total = mine[:, 0:CHUNK] + mine[:, CHUNK:2 * CHUNK]
                sums_ref[pl.ds(chunk + half, 16, stride=chunk_count), :] = total[0:16] + total[16:32]
        return carry

    lax.fori_loop(0, chunk_steps(group_ref), step, 0)
    sums = jnp.concatenate([sums_ref[0:6 * chunk_count], sums_ref[8 * chunk_count:14 * chunk_count]], axis=0)
    sums = jnp.concatenate(split3(sums), axis=1).astype(jnp.bfloat16)
    for tile in range(slot_ref.shape[1] // TILE):
        at = pl.ds(tile * TILE, TILE)
        slot = slot_ref[:, at]
        low = jnp.where(iota((CHUNK, TILE), 0) == slot % CHUNK, 1.0, 0.0).astype(jnp.bfloat16)
        high = jnp.where(iota((chunk_count, TILE), 0) == slot // CHUNK, 1.0, 0.0)
        found = dot(sums, jnp.concatenate([low, low, low], axis=0))
        for row in range(12):
            picked = found[row * chunk_count:(row + 1) * chunk_count] * high
            out_ref[row:row + 1, at] = jnp.sum(picked, axis=0, keepdims=True)


def final_kernel(stats_ref, known_ref, basis_own_ref, field_ref, bundle_ref, currents_ref, iron_ref):
    stats = jnp.sum(stats_ref[...], axis=0)
    known = known_ref[...]
    initial_norm, hessen_a, hessen_b = known[:, 0:1], known[:, 1:2], known[:, 2:3]
    hessen_c, hessen_d, normal_second = stats[:, 0:1], stats[:, 1:2], stats[:, 2:3]
    normal_first = hessen_a * hessen_a + hessen_b * hessen_b
    normal_cross = hessen_a * hessen_c + hessen_b * hessen_d
    target_first = initial_norm * hessen_a
    target_second = initial_norm * hessen_c
    determinant = normal_first * normal_second - normal_cross * normal_cross
    weight_first = (normal_second * target_first - normal_cross * target_second) / determinant
    weight_second = (normal_first * target_second - normal_cross * target_first) / determinant
    currents_ref[...] = weight_first * basis_own_ref[0:1, :] + weight_second * basis_own_ref[1:2, :]
    moments = weight_first * field_ref[0:6, :] + weight_second * field_ref[6:12, :]
    points = bundle_ref[6:9, 0:iron_ref.shape[1]] - 0.5
    px, py, pz = points[0:1], points[1:2], points[2:3]
    iron_ref[0:1, :] = pz * moments[1:2] - py * moments[2:3] - moments[3:4]
    iron_ref[1:2, :] = px * moments[2:3] - pz * moments[0:1] - moments[4:5]
    iron_ref[2:3, :] = py * moments[0:1] - px * moments[1:2] - moments[5:6]


def shape(*sizes, dtype=jnp.float32):
    return jax.ShapeDtypeStruct(sizes, dtype)


def shards(drive, resist, centers, tangents, iron_points, owner, range_len):
    seg_dev = drive.shape[0]
    col_len = centers.shape[1]
    n_col = lax.axis_size("col")
    n_row = lax.axis_size("row")
    n_dev = n_col * n_row
    segments = seg_dev * n_dev
    width = n_col * seg_dev
    points_count = iron_points.shape[1]
    coupling = 0.5 / math.sqrt(segments)
    call = functools.partial(pl.pallas_call, compiler_params=pltpu.CompilerParams(vmem_limit_bytes=VMEM_LIMIT))
    scratch = [pltpu.VMEM((1, segments), jnp.float32), pltpu.VMEM((seg_dev, 128), jnp.float32)]
    hbm = pl.BlockSpec(memory_space=pltpu.HBM)
    smem = pl.BlockSpec(memory_space=pltpu.SMEM)
    vmem = pl.BlockSpec(memory_space=pltpu.VMEM)

    def work(microseconds):
        return pl.CostEstimate(flops=int(microseconds * 1e9), bytes_accessed=0, transcendentals=0)

    def roomy(row_bytes):
        return STREAM_BYTES // row_bytes

    def exchange(x):
        return lax.all_to_all(x, AXES, 0, 0, tiled=True)

    drive_all = exchange(pl.pallas_call(
        spread_kernel,
        out_shape=shape(n_dev, 1, seg_dev),
        in_specs=[hbm],
        scratch_shapes=[pltpu.VMEM((1, seg_dev), jnp.float32), pltpu.SemaphoreType.DMA],
        compiler_params=pltpu.CompilerParams(vmem_limit_bytes=ENTRY_LIMIT),
        cost_estimate=work(8),
        name="spread",
    )(drive[None, :])).reshape(1, segments)
    longest = max(col_len, points_count, 2 * seg_dev)

    def wide(row):
        return jnp.pad(row, ((0, 0), (0, longest - row.shape[1])))

    bundle = jnp.concatenate([
        wide(centers), wide(tangents), wide(iron_points), wide(owner.reshape(1, points_count).astype(jnp.float32)),
        wide(jnp.concatenate([drive, resist])[None, :]),
    ], axis=0)

    def swap(x, bit):
        return lax.ppermute(x, "col", [(k, k ^ bit) for k in range(n_col)])

    bit = 1
    offsets = [0, bit]
    joined = call(
        join_kernel, out_shape=shape(2, 6, col_len), cost_estimate=work(1), name="join"
    )(bundle, swap(centers, bit), swap(tangents, bit))
    while 2 * bit < n_col:
        bit *= 2
        other = swap(joined, bit)
        offsets = offsets + [offset ^ bit for offset in offsets]
        if 2 * bit < n_col:
            joined = call(join_kernel, out_shape=shape(len(offsets), 6, col_len), name="join")(joined, other)

    chunk_count = points_count // CHUNK + n_row * (CHUNK - 1) // CHUNK
    chunk_count = -(-chunk_count // 8) * 8
    slot, group_table, left = call(
        functools.partial(group_kernel, n_row=n_row),
        out_shape=(
            shape(1, points_count, dtype=jnp.int32),
            shape(8, 128, dtype=jnp.int32),
            shape(chunk_count * CHUNK, 48, dtype=jnp.bfloat16),
        ),
        scratch_shapes=[pltpu.VMEM((48 * chunk_count, CHUNK), jnp.float32)],
        cost_estimate=work(3),
        name="group_points",
    )(bundle)

    cube_shape = (chunk_count, 2 * CHUNK, width)
    keep = 2 * math.prod(cube_shape) <= KEEP_BYTES
    stream = functools.partial(
        pl.pallas_call, compiler_params=pltpu.CompilerParams(vmem_limit_bytes=STREAM_LIMIT if keep else VMEM_LIMIT)
    )
    sides = call(
        functools.partial(sides_kernel, offsets=offsets),
        out_shape=(
            shape(48, segments, dtype=jnp.bfloat16), shape(8, segments),
            shape(2, seg_dev, 48, dtype=jnp.bfloat16), shape(3, seg_dev, 128),
        ),
        cost_estimate=work(1),
        name="sides",
    )(joined, other)
    right, moment = sides[0:2]
    image_own, image_spread = call(
        functools.partial(first_kernel, coupling),
        out_shape=(shape(1, seg_dev), shape(n_dev, 1, seg_dev)),
        scratch_shapes=scratch,
        cost_estimate=work(3),
        name="first_image",
    )(drive_all, bundle, group_table, *sides)
    image_all = exchange(image_spread).reshape(1, segments)
    cube_scratch = [pltpu.VMEM(cube_shape, jnp.bfloat16), pltpu.SemaphoreType.DMA((chunk_count,))]
    if keep:
        cubes, after = stream(
            functools.partial(weigh_kernel, n_row=n_row, n_col=n_col),
            out_shape=(shape(roomy(4 * CHUNK * width), *cube_shape[1:], dtype=jnp.bfloat16), shape(8, 128)),
            in_specs=[smem, vmem, vmem],
            out_specs=(hbm, vmem),
            scratch_shapes=cube_scratch,
            cost_estimate=work(5),
            name="weigh",
        )(group_table, left, right)
    else:
        after = group_table
    basis, basis_own, stats, known = call(
        functools.partial(second_kernel, coupling),
        out_shape=(shape(2, segments), shape(2, seg_dev), shape(n_dev, 1, 128), shape(1, 128)),
        scratch_shapes=scratch,
        cost_estimate=work(3),
        name="second_image",
    )(drive_all, image_all, image_own, bundle, after, *sides)
    stats_all = exchange(stats)

    field = stream(
        functools.partial(field_kernel, n_row=n_row, n_col=n_col, keep=keep),
        out_shape=shape(12, points_count),
        in_specs=[smem, smem, vmem, vmem, vmem] + ([hbm] if keep else [vmem, vmem]),
        scratch_shapes=[
            pltpu.VMEM((32, segments), jnp.bfloat16),
            pltpu.VMEM((16 * chunk_count, CHUNK), jnp.float32),
        ] + (cube_scratch if keep else []),
        cost_estimate=work(6),
        name="block_field",
    )(group_table, range_len, slot, moment, basis, *([cubes] if keep else [left, right]))
    currents, iron_field = stream(
        final_kernel,
        out_shape=(shape(1, seg_dev), shape(3, points_count)),
        name="combine",
    )(stats_all, known, basis_own, field, bundle)
    return (currents[0], iron_field)


def solution(mesh):
    return jax.shard_map(
        shards,
        mesh=mesh,
        in_specs=(
            P(AXES),
            P(AXES),
            P(None, "col"),
            P(None, "col"),
            P(None, AXES),
            P(AXES, None),
            P(),
        ),
        out_specs=(P(AXES), P(None, AXES)),
        check_vma=False,
    )
```

```python
import functools
import math

import jax
import jax.numpy as jnp
from jax import lax
from jax.experimental import pallas as pl
from jax.experimental.pallas import tpu as pltpu
from jax.sharding import PartitionSpec as P

EPS_SEG = 0.0004
EPS_FIELD = 0.0025
AXES = ("col", "row")
CHUNK = 128
GROUP = 4
TILE = 512
COLUMNS = 256
ROWS = 64
KEEP_BYTES = 16 * 1024 * 1024
VMEM_LIMIT = 32 * 1024 * 1024
STREAM_LIMIT = 44 * 1024 * 1024
ENTRY_LIMIT = 60 * 1024 * 1024
STREAM_BYTES = 20 * 1024 * 1024


def split3(x):
    high = x.astype(jnp.bfloat16).astype(jnp.float32)
    rest = x - high
    middle = rest.astype(jnp.bfloat16).astype(jnp.float32)
    low = (rest - middle).astype(jnp.bfloat16).astype(jnp.float32)
    return high, middle, low


def left_parts(x):
    high, middle, low = split3(x)
    return jnp.concatenate([high, high, middle, middle, high, low], axis=0)


def right_parts(x):
    high, middle, low = split3(x)
    return jnp.concatenate([high, middle, high, middle, low, high], axis=0).astype(jnp.bfloat16)


def rows8(*rows):
    width = rows[0].shape[1]
    count = sum(r.shape[0] for r in rows)
    if count < 8:
        rows = rows + (jnp.zeros((8 - count, width), jnp.float32),)
    return jnp.concatenate(rows, axis=0)


def left_center(c, eps):
    square = jnp.sum(c * c, axis=0, keepdims=True)
    return rows8(-2.0 * c, jnp.ones_like(square), square + eps)


def right_center(c):
    square = jnp.sum(c * c, axis=0, keepdims=True)
    return rows8(c, square, jnp.ones_like(square))


def dot(a, b):
    return jnp.dot(a, b, preferred_element_type=jnp.float32)


def dot_nt(a, b):
    return lax.dot_general(a, b, (((1,), (1,)), ((), ())), preferred_element_type=jnp.float32)


def transposed(x):
    return x.T.astype(jnp.bfloat16)


def iota(shape, axis):
    return lax.broadcasted_iota(jnp.int32, shape, axis)


def aligned(start, size):
    return pl.ds(pl.multiple_of(start, size), size)


def sides_kernel(joined_ref, other_ref, right_ref, moment_ref, left_ref, along_ref, *, offsets):
    n_col = len(offsets)
    half = n_col // 2
    length = right_ref.shape[1] // n_col
    seg_dev = left_ref.shape[1]
    own_at = aligned(lax.axis_index("row") * seg_dev, seg_dev)
    tangent = rows8(joined_ref[0, 3:6, own_at])
    left_ref[0] = transposed(left_parts(left_center(joined_ref[0, 0:3, own_at] - 0.5, EPS_SEG)))
    left_ref[1] = transposed(left_parts(tangent))
    tangent = tangent.T
    for k in range(3):
        along_ref[k] = jnp.broadcast_to(tangent[:, k:k + 1], (seg_dev, 128))
    for index, offset in enumerate(offsets):
        piece = joined_ref.at[index] if index < half else other_ref.at[index - half]
        col = jnp.bitwise_xor(lax.axis_index("col"), offset)

        def step(k, carry):
            geo = piece[:, aligned(k * TILE, TILE)]
            to = pl.ds(pl.multiple_of(col * length + k * TILE, TILE), TILE)
            center, tangent = geo[0:3] - 0.5, geo[3:6]
            cross = jnp.concatenate([
                tangent[1:2] * center[2:3] - tangent[2:3] * center[1:2],
                tangent[2:3] * center[0:1] - tangent[0:1] * center[2:3],
                tangent[0:1] * center[1:2] - tangent[1:2] * center[0:1],
            ], axis=0)
            right_ref[:, to] = right_parts(right_center(center))
            moment_ref[:, to] = rows8(tangent, cross)
            return carry

        lax.fori_loop(0, length // TILE, step, 0, unroll=4)


def couple(right_ref, moment_ref, left_ref, along_ref, vec_ref, acc_ref):
    acc_ref[...] = jnp.zeros_like(acc_ref)

    def step(k, carry):
        at = aligned(k * TILE, TILE)
        turned = moment_ref[0:3, at] * vec_ref[:, at]
        right = right_ref[:, at]
        for first in range(0, TILE, COLUMNS):
            columns = slice(first, first + COLUMNS)
            by_product = first % (2 * COLUMNS) == 0
            if by_product:
                turned_parts = right_parts(rows8(turned[:, columns]))
            for row in range(0, acc_ref.shape[0], ROWS):
                rows = slice(row, row + ROWS)
                inverse = lax.rsqrt(dot(left_ref[0, rows], right[:, columns]))
                total = acc_ref[rows]
                if by_product:
                    pair = dot(left_ref[1, rows], turned_parts) * inverse
                    for start in range(0, COLUMNS, 128):
                        total = total + pair[:, start:start + 128]
                else:
                    for start in range(0, COLUMNS, 128):
                        lanes = slice(first + start, first + start + 128)
                        along = along_ref[0, rows] * turned[0:1, lanes]
                        along = along + along_ref[1, rows] * turned[1:2, lanes]
                        along = along + along_ref[2, rows] * turned[2:3, lanes]
                        total = total + along * inverse[:, start:start + 128]
                acc_ref[rows] = total
        return carry

    lax.fori_loop(0, vec_ref.shape[1] // TILE, step, 0, unroll=4)
    return jnp.sum(acc_ref[...].T, axis=0, keepdims=True)


def kept_copy(kept, index, out):
    local, remote, sems = kept
    if out:
        return pltpu.make_async_copy(local.at[index], remote.at[index], sems.at[index])
    return pltpu.make_async_copy(remote.at[index], local.at[index], sems.at[index])


def spread_rows(ref, row):
    for k in range(ref.shape[0]):
        ref[k] = row


def spread_kernel(drive_hbm, out_ref, drive, sem):
    copy = pltpu.make_async_copy(drive_hbm, drive, sem)
    copy.start()
    copy.wait()
    spread_rows(out_ref, drive[...])


def join_kernel(*refs):
    out_ref = refs[-1]
    if len(refs) == 5:
        bundle_ref, centers_ref, tangents_ref = refs[0:3]
        out_ref[0] = bundle_ref[0:6, 0:out_ref.shape[2]]
        out_ref[1, 0:3] = centers_ref[...]
        out_ref[1, 3:6] = tangents_ref[...]
    else:
        held = refs[0].shape[0]
        out_ref[0:held] = refs[0][...]
        out_ref[held:2 * held] = refs[1][...]


def own_rows(bundle_ref, like_ref):
    seg_dev = like_ref.shape[1]
    return bundle_ref[10:11, 0:seg_dev], bundle_ref[10:11, seg_dev:2 * seg_dev]


def first_kernel(coupling, drive_ref, bundle_ref, after_ref, right_ref, moment_ref, left_ref, along_ref,
                 image_ref, spread_ref, vec_ref, acc_ref):
    drive = drive_ref[...]
    scale = 1.0 / jnp.sqrt(jnp.sum(drive * drive, keepdims=True))
    vec_ref[...] = drive * scale
    product = couple(right_ref, moment_ref, left_ref, along_ref, vec_ref, acc_ref)
    drive_own, resist_own = own_rows(bundle_ref, image_ref)
    image = resist_own * (drive_own * scale) + coupling * product
    image_ref[...] = image
    spread_rows(spread_ref, image)


def second_kernel(coupling, drive_ref, image_ref, image_own_ref, bundle_ref, after_ref,
                  right_ref, moment_ref, left_ref, along_ref,
                  basis_ref, basis_own_ref, stats_ref, known_ref, vec_ref, acc_ref):
    drive = drive_ref[...]
    norm = jnp.sqrt(jnp.sum(drive * drive, keepdims=True))
    scale = 1.0 / norm
    basis_a = drive * scale
    image = image_ref[...]
    hessen_a = jnp.sum(image * basis_a, keepdims=True)
    rest = image - hessen_a * basis_a
    hessen_b = jnp.sqrt(jnp.sum(rest * rest, keepdims=True))
    inverse = 1.0 / hessen_b
    basis_b = rest * inverse
    vec_ref[...] = basis_b
    basis_ref[0:1, :] = basis_a
    basis_ref[1:2, :] = basis_b
    drive_own, resist_own = own_rows(bundle_ref, image_own_ref)
    own_a = drive_own * scale
    own_b = (image_own_ref[...] - hessen_a * own_a) * inverse
    basis_own_ref[0:1, :] = own_a
    basis_own_ref[1:2, :] = own_b
    product = couple(right_ref, moment_ref, left_ref, along_ref, vec_ref, acc_ref)
    second = resist_own * own_b + coupling * product
    lane = iota((1, 128), 1)

    def three(a, b, c):
        return jnp.where(lane == 0, a, jnp.where(lane == 1, b, jnp.where(lane == 2, c, 0.0)))

    spread_rows(stats_ref, three(
        jnp.sum(second * own_a, keepdims=True),
        jnp.sum(second * own_b, keepdims=True),
        jnp.sum(second * second, keepdims=True),
    ))
    known_ref[...] = three(norm, hessen_a, hessen_b)


def group_kernel(bundle_ref, slot_ref, table_ref, left_ref, planes_ref, *, n_row):
    points = slot_ref.shape[1]
    chunk_count = left_ref.shape[0] // CHUNK
    owner = bundle_ref[9:10, 0:points].astype(jnp.int32)
    rows = max(8, n_row)
    marks = jnp.where(iota((rows, points), 0) == owner, 1.0, 0.0)
    tile = 256
    upper = jnp.where(iota((tile, tile), 0) <= iota((tile, tile), 1), 1.0, 0.0).astype(jnp.bfloat16)
    before = jnp.zeros((rows, 1), jnp.float32)
    ranks = []
    for piece in range(points // tile):
        part = dot(marks[:, piece * tile:(piece + 1) * tile].astype(jnp.bfloat16), upper)
        ranks.append(part + before - 1.0)
        before = before + part[:, tile - 1:tile]
    ranks = jnp.concatenate(ranks, axis=1)
    chunks = jnp.floor((before + (CHUNK - 1)) * (1.0 / CHUNK))
    start = jnp.zeros((1, 1), jnp.float32)
    starts = []
    for name in range(rows):
        starts.append(start)
        start = start + chunks[name:name + 1]
    starts = jnp.concatenate(starts, axis=0)
    slot = jnp.sum(marks * (ranks + starts * CHUNK), axis=0, keepdims=True).astype(jnp.int32)
    slot_ref[...] = slot
    lane = iota((rows, 128), 1)
    ended = jnp.sum(jnp.where(starts + chunks <= lane.astype(jnp.float32), 1.0, 0.0), axis=0, keepdims=True)
    block = jnp.minimum(ended, n_row - 1.0)
    place = iota((8, 128), 0)
    table_ref[...] = jnp.where(place == 0, block, start).astype(jnp.int32)
    high = jnp.where(iota((chunk_count, points), 0) == slot // CHUNK, 1.0, 0.0)
    low = jnp.where(iota((CHUNK, points), 0) == slot % CHUNK, 1.0, 0.0).astype(jnp.bfloat16)
    parts = split3(bundle_ref[6:9, 0:points] - 0.5)
    spread = jnp.concatenate([high * part[k:k + 1] for k in range(3) for part in parts], axis=0).astype(jnp.bfloat16)
    placed = dot_nt(spread, low)
    planes = [placed[k * chunk_count:(k + 1) * chunk_count] for k in range(9)]
    x, y, z = (planes[3 * k] + planes[3 * k + 1] + planes[3 * k + 2] for k in range(3))
    sides = [-2.0 * x, -2.0 * y, -2.0 * z, jnp.ones_like(x), x * x + y * y + z * z + EPS_FIELD]
    sides = [split3(side) for side in sides]
    empty = jnp.zeros_like(x)
    for group, part in enumerate([0, 0, 1, 1, 0, 2]):
        for k in range(8):
            to = pl.ds((group * 8 + k) * chunk_count, chunk_count)
            planes_ref[to, :] = sides[k][part] if k < 5 else empty
    for chunk in range(chunk_count):
        left_ref[chunk * CHUNK:(chunk + 1) * CHUNK, :] = transposed(planes_ref[pl.ds(chunk, 48, stride=chunk_count), :])


def cube_halves(left, right):
    inverse = lax.rsqrt(dot(left, right))
    cube = inverse * inverse * inverse
    high = cube.astype(jnp.bfloat16)
    return high, (cube - high.astype(jnp.float32)).astype(jnp.bfloat16)


def block_part(block, col, n_row, seg_dev):
    return aligned((col * n_row + block) * seg_dev, seg_dev)


def chunk_steps(group_ref):
    return (group_ref[1, 0] + GROUP - 1) // GROUP


def weigh_kernel(group_ref, left_ref, right_ref, cubes_hbm, done_ref, cubes_ref, sems, *, n_row, n_col):
    seg_dev = right_ref.shape[1] // (n_row * n_col)
    done_ref[...] = jnp.zeros_like(done_ref)
    kept = (cubes_ref, cubes_hbm, sems)

    def step(k, carry):
        for part in range(GROUP):
            chunk = k * GROUP + part
            left = left_ref[aligned(chunk * CHUNK, CHUNK), :]
            for col in range(n_col):
                to = slice(col * seg_dev, (col + 1) * seg_dev)
                high, low = cube_halves(left, right_ref[:, block_part(group_ref[0, chunk], col, n_row, seg_dev)])
                cubes_ref[chunk, 0:CHUNK, to] = high
                cubes_ref[chunk, CHUNK:2 * CHUNK, to] = low
            kept_copy(kept, chunk, out=True).start()
        return carry

    def finish(k, carry):
        for part in range(GROUP):
            kept_copy(kept, k * GROUP + part, out=True).wait()
        return carry

    lax.fori_loop(0, chunk_steps(group_ref), step, 0)
    lax.fori_loop(0, chunk_steps(group_ref), finish, 0)


def field_kernel(group_ref, length_ref, slot_ref, moment_ref, basis_ref, *refs, n_row, n_col, keep):
    if keep:
        cubes_hbm, out_ref, table_ref, sums_ref, cubes_ref, sems = refs
        kept = (cubes_ref, cubes_hbm, sems)

        def begin(k, carry):
            for part in range(GROUP):
                kept_copy(kept, k * GROUP + part, out=False).start()
            return carry

        lax.fori_loop(0, chunk_steps(group_ref), begin, 0)
    else:
        left_ref, right_ref, out_ref, table_ref, sums_ref = refs
    chunk_count = sums_ref.shape[0] // 16
    seg_dev = moment_ref.shape[1] // (n_row * n_col)
    scale = 1.0 / math.sqrt(n_col * seg_dev)
    lane = iota((1, seg_dev), 1)
    sums_ref[...] = jnp.zeros_like(sums_ref)

    def table_step(block, carry):
        length = length_ref[block]
        for col in range(n_col):
            at = block_part(block, col, n_row, seg_dev)
            both = moment_ref[:, at]
            active = jnp.where(lane + col * seg_dev < length, scale, 0.0)
            first = both * (basis_ref[0:1, at] * active)
            second = both * (basis_ref[1:2, at] * active)
            parts = jnp.concatenate([first, second], axis=0)
            high = parts.astype(jnp.bfloat16).astype(jnp.float32)
            table_ref[:, at] = jnp.concatenate([high, parts - high], axis=0).astype(jnp.bfloat16)
        return carry

    lax.fori_loop(0, n_row, table_step, 0, unroll=min(n_row, 8))

    def block_row(ref, chunk):
        block = group_ref[0, chunk]
        return jnp.concatenate([ref[:, block_part(block, col, n_row, seg_dev)] for col in range(n_col)], axis=1)

    def cubes_of(chunk):
        return jnp.concatenate(cube_halves(left_ref[aligned(chunk * CHUNK, CHUNK), :], block_row(right_ref, chunk)), axis=0)

    def step(k, carry):
        for part in range(0, GROUP, 2):
            chunk = k * GROUP + part
            tables = jnp.concatenate([block_row(table_ref, chunk), block_row(table_ref, chunk + 1)], axis=0)
            if keep:
                kept_copy(kept, chunk, out=False).wait()
                kept_copy(kept, chunk + 1, out=False).wait()
                cubes = cubes_ref[pl.ds(chunk, 2)].reshape(4 * CHUNK, n_col * seg_dev)
            else:
                cubes = jnp.concatenate([cubes_of(chunk), cubes_of(chunk + 1)], axis=0)
            both = dot_nt(tables, cubes)
            for half in range(2):
                mine = both[32 * half:32 * half + 32, 2 * CHUNK * half:2 * CHUNK * (half + 1)]
                total = mine[:, 0:CHUNK] + mine[:, CHUNK:2 * CHUNK]
                sums_ref[pl.ds(chunk + half, 16, stride=chunk_count), :] = total[0:16] + total[16:32]
        return carry

    lax.fori_loop(0, chunk_steps(group_ref), step, 0)
    sums = jnp.concatenate([sums_ref[0:6 * chunk_count], sums_ref[8 * chunk_count:14 * chunk_count]], axis=0)
    sums = jnp.concatenate(split3(sums), axis=1).astype(jnp.bfloat16)
    for tile in range(slot_ref.shape[1] // TILE):
        at = pl.ds(tile * TILE, TILE)
        slot = slot_ref[:, at]
        low = jnp.where(iota((CHUNK, TILE), 0) == slot % CHUNK, 1.0, 0.0).astype(jnp.bfloat16)
        high = jnp.where(iota((chunk_count, TILE), 0) == slot // CHUNK, 1.0, 0.0)
        found = dot(sums, jnp.concatenate([low, low, low], axis=0))
        for row in range(12):
            picked = found[row * chunk_count:(row + 1) * chunk_count] * high
            out_ref[row:row + 1, at] = jnp.sum(picked, axis=0, keepdims=True)


def final_kernel(stats_ref, known_ref, basis_own_ref, field_ref, bundle_ref, currents_ref, iron_ref):
    stats = jnp.sum(stats_ref[...], axis=0)
    known = known_ref[...]
    initial_norm, hessen_a, hessen_b = known[:, 0:1], known[:, 1:2], known[:, 2:3]
    hessen_c, hessen_d, normal_second = stats[:, 0:1], stats[:, 1:2], stats[:, 2:3]
    normal_first = hessen_a * hessen_a + hessen_b * hessen_b
    normal_cross = hessen_a * hessen_c + hessen_b * hessen_d
    target_first = initial_norm * hessen_a
    target_second = initial_norm * hessen_c
    determinant = normal_first * normal_second - normal_cross * normal_cross
    weight_first = (normal_second * target_first - normal_cross * target_second) / determinant
    weight_second = (normal_first * target_second - normal_cross * target_first) / determinant
    currents_ref[...] = weight_first * basis_own_ref[0:1, :] + weight_second * basis_own_ref[1:2, :]
    moments = weight_first * field_ref[0:6, :] + weight_second * field_ref[6:12, :]
    points = bundle_ref[6:9, 0:iron_ref.shape[1]] - 0.5
    px, py, pz = points[0:1], points[1:2], points[2:3]
    iron_ref[0:1, :] = pz * moments[1:2] - py * moments[2:3] - moments[3:4]
    iron_ref[1:2, :] = px * moments[2:3] - pz * moments[0:1] - moments[4:5]
    iron_ref[2:3, :] = py * moments[0:1] - px * moments[1:2] - moments[5:6]


def shape(*sizes, dtype=jnp.float32):
    return jax.ShapeDtypeStruct(sizes, dtype)


def shards(drive, resist, centers, tangents, iron_points, owner, range_len):
    seg_dev = drive.shape[0]
    col_len = centers.shape[1]
    n_col = lax.axis_size("col")
    n_row = lax.axis_size("row")
    n_dev = n_col * n_row
    segments = seg_dev * n_dev
    width = n_col * seg_dev
    points_count = iron_points.shape[1]
    coupling = 0.5 / math.sqrt(segments)
    call = functools.partial(pl.pallas_call, compiler_params=pltpu.CompilerParams(vmem_limit_bytes=VMEM_LIMIT))
    scratch = [pltpu.VMEM((1, segments), jnp.float32), pltpu.VMEM((seg_dev, 128), jnp.float32)]
    hbm = pl.BlockSpec(memory_space=pltpu.HBM)
    smem = pl.BlockSpec(memory_space=pltpu.SMEM)
    vmem = pl.BlockSpec(memory_space=pltpu.VMEM)

    def work(microseconds):
        return pl.CostEstimate(flops=int(microseconds * 1e9), bytes_accessed=0, transcendentals=0)

    def roomy(row_bytes):
        return STREAM_BYTES // row_bytes

    def exchange(x):
        return lax.all_to_all(x, AXES, 0, 0, tiled=True)

    drive_all = exchange(pl.pallas_call(
        spread_kernel,
        out_shape=shape(n_dev, 1, seg_dev),
        in_specs=[hbm],
        scratch_shapes=[pltpu.VMEM((1, seg_dev), jnp.float32), pltpu.SemaphoreType.DMA],
        compiler_params=pltpu.CompilerParams(vmem_limit_bytes=ENTRY_LIMIT),
        cost_estimate=work(8),
        name="spread",
    )(drive[None, :])).reshape(1, segments)
    longest = max(col_len, points_count, 2 * seg_dev)

    def wide(row):
        return jnp.pad(row, ((0, 0), (0, longest - row.shape[1])))

    bundle = jnp.concatenate([
        wide(centers), wide(tangents), wide(iron_points), wide(owner.reshape(1, points_count).astype(jnp.float32)),
        wide(jnp.concatenate([drive, resist])[None, :]),
    ], axis=0)

    chunk_count = points_count // CHUNK + n_row * (CHUNK - 1) // CHUNK
    chunk_count = -(-chunk_count // 8) * 8
    slot, group_table, left = call(
        functools.partial(group_kernel, n_row=n_row),
        out_shape=(
            shape(1, points_count, dtype=jnp.int32),
            shape(8, 128, dtype=jnp.int32),
            shape(chunk_count * CHUNK, 48, dtype=jnp.bfloat16),
        ),
        scratch_shapes=[pltpu.VMEM((48 * chunk_count, CHUNK), jnp.float32)],
        cost_estimate=work(3),
        name="group_points",
    )(bundle)

    def swap(x, bit):
        return lax.ppermute(x, "col", [(k, k ^ bit) for k in range(n_col)])

    bit = n_col // 2
    offsets = [0, bit]
    joined = call(
        join_kernel, out_shape=shape(2, 6, col_len), cost_estimate=work(1), name="join"
    )(bundle, swap(centers, bit), swap(tangents, bit), group_table)
    while bit > 1:
        bit //= 2
        other = swap(joined, bit)
        offsets = offsets + [offset ^ bit for offset in offsets]
        if bit > 1:
            joined = call(join_kernel, out_shape=shape(len(offsets), 6, col_len), name="join")(joined, other)

    cube_shape = (chunk_count, 2 * CHUNK, width)
    keep = 2 * math.prod(cube_shape) <= KEEP_BYTES
    stream = functools.partial(
        pl.pallas_call, compiler_params=pltpu.CompilerParams(vmem_limit_bytes=STREAM_LIMIT if keep else VMEM_LIMIT)
    )
    sides = call(
        functools.partial(sides_kernel, offsets=offsets),
        out_shape=(
            shape(48, segments, dtype=jnp.bfloat16), shape(8, segments),
            shape(2, seg_dev, 48, dtype=jnp.bfloat16), shape(3, seg_dev, 128),
        ),
        cost_estimate=work(1),
        name="sides",
    )(joined, other)
    right, moment = sides[0:2]
    image_own, image_spread = call(
        functools.partial(first_kernel, coupling),
        out_shape=(shape(1, seg_dev), shape(n_dev, 1, seg_dev)),
        scratch_shapes=scratch,
        cost_estimate=work(3),
        name="first_image",
    )(drive_all, bundle, group_table, *sides)
    image_all = exchange(image_spread).reshape(1, segments)
    cube_scratch = [pltpu.VMEM(cube_shape, jnp.bfloat16), pltpu.SemaphoreType.DMA((chunk_count,))]
    if keep:
        cubes, after = stream(
            functools.partial(weigh_kernel, n_row=n_row, n_col=n_col),
            out_shape=(shape(roomy(4 * CHUNK * width), *cube_shape[1:], dtype=jnp.bfloat16), shape(8, 128)),
            in_specs=[smem, vmem, vmem],
            out_specs=(hbm, vmem),
            scratch_shapes=cube_scratch,
            cost_estimate=work(5),
            name="weigh",
        )(group_table, left, right)
    else:
        after = group_table
    basis, basis_own, stats, known = call(
        functools.partial(second_kernel, coupling),
        out_shape=(shape(2, segments), shape(2, seg_dev), shape(n_dev, 1, 128), shape(1, 128)),
        scratch_shapes=scratch,
        cost_estimate=work(3),
        name="second_image",
    )(drive_all, image_all, image_own, bundle, after, *sides)
    stats_all = exchange(stats)

    field = stream(
        functools.partial(field_kernel, n_row=n_row, n_col=n_col, keep=keep),
        out_shape=shape(12, points_count),
        in_specs=[smem, smem, vmem, vmem, vmem] + ([hbm] if keep else [vmem, vmem]),
        scratch_shapes=[
            pltpu.VMEM((32, segments), jnp.bfloat16),
            pltpu.VMEM((16 * chunk_count, CHUNK), jnp.float32),
        ] + (cube_scratch if keep else []),
        cost_estimate=work(6),
        name="block_field",
    )(group_table, range_len, slot, moment, basis, *([cubes] if keep else [left, right]))
    currents, iron_field = stream(
        final_kernel,
        out_shape=(shape(1, seg_dev), shape(3, points_count)),
        name="combine",
    )(stats_all, known, basis_own, field, bundle)
    return (currents[0], iron_field)


def solution(mesh):
    return jax.shard_map(
        shards,
        mesh=mesh,
        in_specs=(
            P(AXES),
            P(AXES),
            P(None, "col"),
            P(None, "col"),
            P(None, AXES),
            P(AXES, None),
            P(),
        ),
        out_specs=(P(AXES), P(None, AXES)),
        check_vma=False,
    )
```

```python
import functools
import math

import jax
import jax.numpy as jnp
from jax import lax
from jax.experimental import pallas as pl
from jax.experimental.pallas import tpu as pltpu
from jax.sharding import PartitionSpec as P

EPS_SEG = 0.0004
EPS_FIELD = 0.0025
AXES = ("col", "row")
CHUNK = 128
GROUP = 4
TILE = 512
COLUMNS = 256
ROWS = 64
KEEP_BYTES = 16 * 1024 * 1024
VMEM_LIMIT = 32 * 1024 * 1024
STREAM_LIMIT = 44 * 1024 * 1024
STREAM_BYTES = 20 * 1024 * 1024
ENTRY_LIMIT = 60 * 1024 * 1024


def split3(x):
    high = x.astype(jnp.bfloat16).astype(jnp.float32)
    rest = x - high
    middle = rest.astype(jnp.bfloat16).astype(jnp.float32)
    low = (rest - middle).astype(jnp.bfloat16).astype(jnp.float32)
    return high, middle, low


def left_parts(x):
    high, middle, low = split3(x)
    return jnp.concatenate([high, high, middle, middle, high, low], axis=0)


def right_parts(x):
    high, middle, low = split3(x)
    return jnp.concatenate([high, middle, high, middle, low, high], axis=0).astype(jnp.bfloat16)


def rows8(*rows):
    width = rows[0].shape[1]
    count = sum(r.shape[0] for r in rows)
    if count < 8:
        rows = rows + (jnp.zeros((8 - count, width), jnp.float32),)
    return jnp.concatenate(rows, axis=0)


def left_center(c, eps):
    square = jnp.sum(c * c, axis=0, keepdims=True)
    return rows8(-2.0 * c, jnp.ones_like(square), square + eps)


def right_center(c):
    square = jnp.sum(c * c, axis=0, keepdims=True)
    return rows8(c, square, jnp.ones_like(square))


def dot(a, b):
    return jnp.dot(a, b, preferred_element_type=jnp.float32)


def dot_nt(a, b):
    return lax.dot_general(a, b, (((1,), (1,)), ((), ())), preferred_element_type=jnp.float32)


def transposed(x):
    return x.T.astype(jnp.bfloat16)


def iota(shape, axis):
    return lax.broadcasted_iota(jnp.int32, shape, axis)


def aligned(start, size):
    return pl.ds(pl.multiple_of(start, size), size)


def sides_kernel(*refs, n_col):
    pieces, (right_ref, moment_ref, left_ref, along_ref) = refs[:n_col], refs[n_col:]
    length = right_ref.shape[1] // n_col
    seg_dev = left_ref.shape[1]
    own_at = aligned(lax.axis_index("row") * seg_dev, seg_dev)
    tangent = rows8(pieces[0][3:6, own_at])
    left_ref[0] = transposed(left_parts(left_center(pieces[0][0:3, own_at] - 0.5, EPS_SEG)))
    left_ref[1] = transposed(left_parts(tangent))
    tangent = tangent.T
    for k in range(3):
        along_ref[k] = jnp.broadcast_to(tangent[:, k:k + 1], (seg_dev, 128))
    for shift, piece in enumerate(pieces):
        col = lax.rem(lax.axis_index("col") + n_col - shift, n_col)

        def step(k, carry):
            geo = piece[0:6, aligned(k * TILE, TILE)]
            to = pl.ds(pl.multiple_of(col * length + k * TILE, TILE), TILE)
            center, tangent = geo[0:3] - 0.5, geo[3:6]
            cross = jnp.concatenate([
                tangent[1:2] * center[2:3] - tangent[2:3] * center[1:2],
                tangent[2:3] * center[0:1] - tangent[0:1] * center[2:3],
                tangent[0:1] * center[1:2] - tangent[1:2] * center[0:1],
            ], axis=0)
            right_ref[:, to] = right_parts(right_center(center))
            moment_ref[:, to] = rows8(tangent, cross)
            return carry

        lax.fori_loop(0, length // TILE, step, 0, unroll=4)


def couple(right_ref, moment_ref, left_ref, along_ref, vec_ref, acc_ref):
    acc_ref[...] = jnp.zeros_like(acc_ref)

    def step(k, carry):
        at = aligned(k * TILE, TILE)
        turned = moment_ref[0:3, at] * vec_ref[:, at]
        right = right_ref[:, at]
        for first in range(0, TILE, COLUMNS):
            columns = slice(first, first + COLUMNS)
            by_product = first % (2 * COLUMNS) == 0
            if by_product:
                turned_parts = right_parts(rows8(turned[:, columns]))
            for row in range(0, acc_ref.shape[0], ROWS):
                rows = slice(row, row + ROWS)
                inverse = lax.rsqrt(dot(left_ref[0, rows], right[:, columns]))
                total = acc_ref[rows]
                if by_product:
                    pair = dot(left_ref[1, rows], turned_parts) * inverse
                    for start in range(0, COLUMNS, 128):
                        total = total + pair[:, start:start + 128]
                else:
                    for start in range(0, COLUMNS, 128):
                        lanes = slice(first + start, first + start + 128)
                        along = along_ref[0, rows] * turned[0:1, lanes]
                        along = along + along_ref[1, rows] * turned[1:2, lanes]
                        along = along + along_ref[2, rows] * turned[2:3, lanes]
                        total = total + along * inverse[:, start:start + 128]
                acc_ref[rows] = total
        return carry

    lax.fori_loop(0, vec_ref.shape[1] // TILE, step, 0, unroll=4)
    return jnp.sum(acc_ref[...].T, axis=0, keepdims=True)


def part_bounds(n_col, seg_dev):
    width = n_col * seg_dev
    return ((0, width // 2), (width // 2, 3 * width // 4), (3 * width // 4, width))


def part_copy(kept, chunk, part, bounds, out):
    local, remote, sems = kept
    start, stop = bounds[part]
    here = local.at[chunk, :, start:stop]
    there = remote.at[chunk, :, start:stop]
    sem = sems.at[chunk * len(bounds) + part]
    return pltpu.make_async_copy(here, there, sem) if out else pltpu.make_async_copy(there, here, sem)


def for_parts(group_ref, length_ref, chunk, bounds, action, otherwise=None):
    used = chunk < group_ref[1, 0]
    length = length_ref[group_ref[0, chunk]]
    for part, (start, _) in enumerate(bounds):
        active = jnp.logical_and(used, start < length)
        pl.when(active)(functools.partial(action, part))
        if otherwise is not None:
            pl.when(jnp.logical_not(active))(functools.partial(otherwise, part))


def spread_rows(ref, row):
    for k in range(ref.shape[0]):
        ref[k] = row


def entry_kernel(drive_hbm, centers_hbm, tangents_hbm, spread_ref, geo_ref, drive, centers, tangents, sems):
    pairs = ((drive_hbm, drive), (centers_hbm, centers), (tangents_hbm, tangents))
    copies = [pltpu.make_async_copy(source, target, sems.at[k]) for k, (source, target) in enumerate(pairs)]
    for copy in copies:
        copy.start()
    for copy in copies:
        copy.wait()
    spread_rows(spread_ref, drive[...])
    geo_ref[0:3] = centers[...]
    geo_ref[3:6] = tangents[...]


def own_rows(bundle_ref, like_ref):
    seg_dev = like_ref.shape[1]
    return bundle_ref[10:11, 0:seg_dev], bundle_ref[10:11, seg_dev:2 * seg_dev]


def first_kernel(coupling, drive_ref, bundle_ref, after_ref, right_ref, moment_ref, left_ref, along_ref,
                 image_ref, spread_ref, vec_ref, acc_ref):
    drive = drive_ref[...]
    scale = 1.0 / jnp.sqrt(jnp.sum(drive * drive, keepdims=True))
    vec_ref[...] = drive * scale
    product = couple(right_ref, moment_ref, left_ref, along_ref, vec_ref, acc_ref)
    drive_own, resist_own = own_rows(bundle_ref, image_ref)
    image = resist_own * (drive_own * scale) + coupling * product
    image_ref[...] = image
    spread_rows(spread_ref, image)


def second_kernel(coupling, drive_ref, image_ref, image_own_ref, bundle_ref, after_ref,
                  right_ref, moment_ref, left_ref, along_ref,
                  basis_ref, basis_own_ref, stats_ref, known_ref, vec_ref, acc_ref):
    drive = drive_ref[...]
    norm = jnp.sqrt(jnp.sum(drive * drive, keepdims=True))
    scale = 1.0 / norm
    basis_a = drive * scale
    image = image_ref[...]
    hessen_a = jnp.sum(image * basis_a, keepdims=True)
    rest = image - hessen_a * basis_a
    hessen_b = jnp.sqrt(jnp.sum(rest * rest, keepdims=True))
    inverse = 1.0 / hessen_b
    basis_b = rest * inverse
    vec_ref[...] = basis_b
    basis_ref[0:1, :] = basis_a
    basis_ref[1:2, :] = basis_b
    drive_own, resist_own = own_rows(bundle_ref, image_own_ref)
    own_a = drive_own * scale
    own_b = (image_own_ref[...] - hessen_a * own_a) * inverse
    basis_own_ref[0:1, :] = own_a
    basis_own_ref[1:2, :] = own_b
    product = couple(right_ref, moment_ref, left_ref, along_ref, vec_ref, acc_ref)
    second = resist_own * own_b + coupling * product
    lane = iota((1, 128), 1)

    def three(a, b, c):
        return jnp.where(lane == 0, a, jnp.where(lane == 1, b, jnp.where(lane == 2, c, 0.0)))

    spread_rows(stats_ref, three(
        jnp.sum(second * own_a, keepdims=True),
        jnp.sum(second * own_b, keepdims=True),
        jnp.sum(second * second, keepdims=True),
    ))
    known_ref[...] = three(norm, hessen_a, hessen_b)


def group_kernel(bundle_ref, slot_ref, table_ref, left_ref, planes_ref, *, n_row):
    points = slot_ref.shape[1]
    chunk_count = left_ref.shape[0] // CHUNK
    owner = bundle_ref[9:10, 0:points].astype(jnp.int32)
    rows = max(8, n_row)
    marks = jnp.where(iota((rows, points), 0) == owner, 1.0, 0.0)
    tile = 256
    upper = jnp.where(iota((tile, tile), 0) <= iota((tile, tile), 1), 1.0, 0.0).astype(jnp.bfloat16)
    before = jnp.zeros((rows, 1), jnp.float32)
    ranks = []
    for piece in range(points // tile):
        part = dot(marks[:, piece * tile:(piece + 1) * tile].astype(jnp.bfloat16), upper)
        ranks.append(part + before - 1.0)
        before = before + part[:, tile - 1:tile]
    ranks = jnp.concatenate(ranks, axis=1)
    chunks = jnp.floor((before + (CHUNK - 1)) * (1.0 / CHUNK))
    start = jnp.zeros((1, 1), jnp.float32)
    starts = []
    for name in range(rows):
        starts.append(start)
        start = start + chunks[name:name + 1]
    starts = jnp.concatenate(starts, axis=0)
    slot = jnp.sum(marks * (ranks + starts * CHUNK), axis=0, keepdims=True).astype(jnp.int32)
    slot_ref[...] = slot
    lane = iota((rows, 128), 1)
    ended = jnp.sum(jnp.where(starts + chunks <= lane.astype(jnp.float32), 1.0, 0.0), axis=0, keepdims=True)
    block = jnp.minimum(ended, n_row - 1.0)
    place = iota((8, 128), 0)
    table_ref[...] = jnp.where(place == 0, block, start).astype(jnp.int32)
    high = jnp.where(iota((chunk_count, points), 0) == slot // CHUNK, 1.0, 0.0)
    low = jnp.where(iota((CHUNK, points), 0) == slot % CHUNK, 1.0, 0.0).astype(jnp.bfloat16)
    parts = split3(bundle_ref[6:9, 0:points] - 0.5)
    spread = jnp.concatenate([high * part[k:k + 1] for k in range(3) for part in parts], axis=0).astype(jnp.bfloat16)
    placed = dot_nt(spread, low)
    planes = [placed[k * chunk_count:(k + 1) * chunk_count] for k in range(9)]
    x, y, z = (planes[3 * k] + planes[3 * k + 1] + planes[3 * k + 2] for k in range(3))
    sides = [-2.0 * x, -2.0 * y, -2.0 * z, jnp.ones_like(x), x * x + y * y + z * z + EPS_FIELD]
    sides = [split3(side) for side in sides]
    empty = jnp.zeros_like(x)
    for group, part in enumerate([0, 0, 1, 1, 0, 2]):
        for k in range(8):
            to = pl.ds((group * 8 + k) * chunk_count, chunk_count)
            planes_ref[to, :] = sides[k][part] if k < 5 else empty
    for chunk in range(chunk_count):
        left_ref[chunk * CHUNK:(chunk + 1) * CHUNK, :] = transposed(planes_ref[pl.ds(chunk, 48, stride=chunk_count), :])


def cube_halves(left, right):
    inverse = lax.rsqrt(dot(left, right))
    cube = inverse * inverse * inverse
    high = cube.astype(jnp.bfloat16)
    return high, (cube - high.astype(jnp.float32)).astype(jnp.bfloat16)


def block_part(block, col, n_row, seg_dev):
    return aligned((col * n_row + block) * seg_dev, seg_dev)


def chunk_steps(group_ref):
    return (group_ref[1, 0] + GROUP - 1) // GROUP


def weigh_kernel(group_ref, length_ref, left_ref, right_ref, cubes_hbm, done_ref, cubes_ref, sems, *, n_row, n_col):
    seg_dev = right_ref.shape[1] // (n_row * n_col)
    done_ref[...] = jnp.zeros_like(done_ref)
    kept = (cubes_ref, cubes_hbm, sems)
    bounds = part_bounds(n_col, seg_dev)

    def step(k, carry):
        for part in range(GROUP):
            chunk = k * GROUP + part
            left = left_ref[aligned(chunk * CHUNK, CHUNK), :]
            for col in range(n_col):
                to = slice(col * seg_dev, (col + 1) * seg_dev)
                high, low = cube_halves(left, right_ref[:, block_part(group_ref[0, chunk], col, n_row, seg_dev)])
                cubes_ref[chunk, 0:CHUNK, to] = high
                cubes_ref[chunk, CHUNK:2 * CHUNK, to] = low
        for part in range(GROUP):
            chunk = k * GROUP + part
            for_parts(group_ref, length_ref, chunk, bounds,
                      lambda piece, chunk=chunk: part_copy(kept, chunk, piece, bounds, out=True).start())
        return carry

    def finish(chunk, carry):
        for_parts(group_ref, length_ref, chunk, bounds,
                  lambda piece: part_copy(kept, chunk, piece, bounds, out=True).wait())
        return carry

    lax.fori_loop(0, chunk_steps(group_ref), step, 0)
    lax.fori_loop(0, group_ref[1, 0], finish, 0)


def field_kernel(group_ref, length_ref, slot_ref, moment_ref, basis_ref, *refs, n_row, n_col, keep):
    if keep:
        cubes_hbm, out_ref, table_ref, sums_ref, cubes_ref, sems = refs
        kept = (cubes_ref, cubes_hbm, sems)

        bounds = part_bounds(n_col, moment_ref.shape[1] // (n_row * n_col))

        def clear(chunk, piece):
            start, stop = bounds[piece]
            cubes_ref[chunk, :, start:stop] = jnp.zeros((2 * CHUNK, stop - start), jnp.bfloat16)

        def begin(chunk, carry):
            for_parts(group_ref, length_ref, chunk, bounds,
                      lambda piece: part_copy(kept, chunk, piece, bounds, out=False).start(),
                      lambda piece: clear(chunk, piece))
            return carry

        def arrive(chunk):
            for_parts(group_ref, length_ref, chunk, bounds,
                      lambda piece: part_copy(kept, chunk, piece, bounds, out=False).wait())

        lax.fori_loop(0, chunk_steps(group_ref) * GROUP, begin, 0)
    else:
        left_ref, right_ref, out_ref, table_ref, sums_ref = refs
    chunk_count = sums_ref.shape[0] // 16
    seg_dev = moment_ref.shape[1] // (n_row * n_col)
    scale = 1.0 / math.sqrt(n_col * seg_dev)
    lane = iota((1, seg_dev), 1)
    sums_ref[...] = jnp.zeros_like(sums_ref)

    def table_step(block, carry):
        length = length_ref[block]
        for col in range(n_col):
            at = block_part(block, col, n_row, seg_dev)
            both = moment_ref[:, at]
            active = jnp.where(lane + col * seg_dev < length, scale, 0.0)
            first = both * (basis_ref[0:1, at] * active)
            second = both * (basis_ref[1:2, at] * active)
            parts = jnp.concatenate([first, second], axis=0)
            high = parts.astype(jnp.bfloat16).astype(jnp.float32)
            table_ref[:, at] = jnp.concatenate([high, parts - high], axis=0).astype(jnp.bfloat16)
        return carry

    lax.fori_loop(0, n_row, table_step, 0, unroll=min(n_row, 8))

    def block_row(ref, chunk):
        block = group_ref[0, chunk]
        return jnp.concatenate([ref[:, block_part(block, col, n_row, seg_dev)] for col in range(n_col)], axis=1)

    def cubes_of(chunk):
        return jnp.concatenate(cube_halves(left_ref[aligned(chunk * CHUNK, CHUNK), :], block_row(right_ref, chunk)), axis=0)

    def step(k, carry):
        if keep:
            for part in range(GROUP):
                arrive(k * GROUP + part)
        for part in range(0, GROUP, 2):
            chunk = k * GROUP + part
            tables = jnp.concatenate([block_row(table_ref, chunk), block_row(table_ref, chunk + 1)], axis=0)
            if keep:
                cubes = cubes_ref[pl.ds(chunk, 2)].reshape(4 * CHUNK, n_col * seg_dev)
            else:
                cubes = jnp.concatenate([cubes_of(chunk), cubes_of(chunk + 1)], axis=0)
            both = dot_nt(tables, cubes)
            for half in range(2):
                mine = both[32 * half:32 * half + 32, 2 * CHUNK * half:2 * CHUNK * (half + 1)]
                total = mine[:, 0:CHUNK] + mine[:, CHUNK:2 * CHUNK]
                sums_ref[pl.ds(chunk + half, 16, stride=chunk_count), :] = total[0:16] + total[16:32]
        return carry

    lax.fori_loop(0, chunk_steps(group_ref), step, 0)
    sums = jnp.concatenate([sums_ref[0:6 * chunk_count], sums_ref[8 * chunk_count:14 * chunk_count]], axis=0)
    sums = jnp.concatenate(split3(sums), axis=1).astype(jnp.bfloat16)
    for tile in range(slot_ref.shape[1] // TILE):
        at = pl.ds(tile * TILE, TILE)
        slot = slot_ref[:, at]
        low = jnp.where(iota((CHUNK, TILE), 0) == slot % CHUNK, 1.0, 0.0).astype(jnp.bfloat16)
        high = jnp.where(iota((chunk_count, TILE), 0) == slot // CHUNK, 1.0, 0.0)
        found = dot(sums, jnp.concatenate([low, low, low], axis=0))
        for row in range(12):
            picked = found[row * chunk_count:(row + 1) * chunk_count] * high
            out_ref[row:row + 1, at] = jnp.sum(picked, axis=0, keepdims=True)


def final_kernel(stats_ref, known_ref, basis_own_ref, field_ref, bundle_ref, currents_ref, iron_ref):
    stats = jnp.sum(stats_ref[...], axis=0)
    known = known_ref[...]
    initial_norm, hessen_a, hessen_b = known[:, 0:1], known[:, 1:2], known[:, 2:3]
    hessen_c, hessen_d, normal_second = stats[:, 0:1], stats[:, 1:2], stats[:, 2:3]
    normal_first = hessen_a * hessen_a + hessen_b * hessen_b
    normal_cross = hessen_a * hessen_c + hessen_b * hessen_d
    target_first = initial_norm * hessen_a
    target_second = initial_norm * hessen_c
    determinant = normal_first * normal_second - normal_cross * normal_cross
    weight_first = (normal_second * target_first - normal_cross * target_second) / determinant
    weight_second = (normal_first * target_second - normal_cross * target_first) / determinant
    currents_ref[...] = weight_first * basis_own_ref[0:1, :] + weight_second * basis_own_ref[1:2, :]
    moments = weight_first * field_ref[0:6, :] + weight_second * field_ref[6:12, :]
    points = bundle_ref[6:9, 0:iron_ref.shape[1]] - 0.5
    px, py, pz = points[0:1], points[1:2], points[2:3]
    iron_ref[0:1, :] = pz * moments[1:2] - py * moments[2:3] - moments[3:4]
    iron_ref[1:2, :] = px * moments[2:3] - pz * moments[0:1] - moments[4:5]
    iron_ref[2:3, :] = py * moments[0:1] - px * moments[1:2] - moments[5:6]


def shape(*sizes, dtype=jnp.float32):
    return jax.ShapeDtypeStruct(sizes, dtype)


def shards(drive, resist, centers, tangents, iron_points, owner, range_len):
    seg_dev = drive.shape[0]
    col_len = centers.shape[1]
    n_col = lax.axis_size("col")
    n_row = lax.axis_size("row")
    n_dev = n_col * n_row
    segments = seg_dev * n_dev
    width = n_col * seg_dev
    points_count = iron_points.shape[1]
    coupling = 0.5 / math.sqrt(segments)
    call = functools.partial(pl.pallas_call, compiler_params=pltpu.CompilerParams(vmem_limit_bytes=VMEM_LIMIT))
    scratch = [pltpu.VMEM((1, segments), jnp.float32), pltpu.VMEM((seg_dev, 128), jnp.float32)]
    hbm = pl.BlockSpec(memory_space=pltpu.HBM)
    smem = pl.BlockSpec(memory_space=pltpu.SMEM)
    vmem = pl.BlockSpec(memory_space=pltpu.VMEM)

    def work(microseconds):
        return pl.CostEstimate(flops=int(microseconds * 1e9), bytes_accessed=0, transcendentals=0)

    def roomy(row_bytes):
        return STREAM_BYTES // row_bytes

    def exchange(x):
        return lax.all_to_all(x, AXES, 0, 0, tiled=True)

    spread, geometry = pl.pallas_call(
        entry_kernel,
        out_shape=(shape(n_dev, 1, seg_dev), shape(6, col_len)),
        in_specs=[hbm] * 3,
        scratch_shapes=[
            pltpu.VMEM((1, seg_dev), jnp.float32),
            pltpu.VMEM((3, col_len), jnp.float32),
            pltpu.VMEM((3, col_len), jnp.float32),
            pltpu.SemaphoreType.DMA((3,)),
        ],
        compiler_params=pltpu.CompilerParams(vmem_limit_bytes=ENTRY_LIMIT),
        cost_estimate=work(8),
        name="entry",
    )(drive[None, :], centers, tangents)
    drive_all = exchange(spread).reshape(1, segments)
    longest = max(col_len, points_count, 2 * seg_dev)

    def wide(row):
        return jnp.pad(row, ((0, 0), (0, longest - row.shape[1])))

    bundle = jnp.concatenate([
        wide(centers), wide(tangents), wide(iron_points), wide(owner.reshape(1, points_count).astype(jnp.float32)),
        wide(jnp.concatenate([drive, resist])[None, :]),
    ], axis=0)
    pieces = [bundle] + [
        lax.ppermute(geometry, "col", [(k, (k + shift) % n_col) for k in range(n_col)]) for shift in range(1, n_col)
    ]

    chunk_count = points_count // CHUNK + n_row * (CHUNK - 1) // CHUNK
    chunk_count = -(-chunk_count // 8) * 8
    slot, group_table, left = call(
        functools.partial(group_kernel, n_row=n_row),
        out_shape=(
            shape(1, points_count, dtype=jnp.int32),
            shape(8, 128, dtype=jnp.int32),
            shape(chunk_count * CHUNK, 48, dtype=jnp.bfloat16),
        ),
        scratch_shapes=[pltpu.VMEM((48 * chunk_count, CHUNK), jnp.float32)],
        cost_estimate=work(3),
        name="group_points",
    )(bundle)

    cube_shape = (chunk_count, 2 * CHUNK, width)
    keep = 2 * math.prod(cube_shape) <= KEEP_BYTES
    stream = functools.partial(
        pl.pallas_call, compiler_params=pltpu.CompilerParams(vmem_limit_bytes=STREAM_LIMIT if keep else VMEM_LIMIT)
    )
    sides = call(
        functools.partial(sides_kernel, n_col=n_col),
        out_shape=(
            shape(48, segments, dtype=jnp.bfloat16), shape(8, segments),
            shape(2, seg_dev, 48, dtype=jnp.bfloat16), shape(3, seg_dev, 128),
        ),
        cost_estimate=work(1),
        name="sides",
    )(*pieces)
    right, moment = sides[0:2]
    image_own, image_spread = call(
        functools.partial(first_kernel, coupling),
        out_shape=(shape(1, seg_dev), shape(n_dev, 1, seg_dev)),
        scratch_shapes=scratch,
        cost_estimate=work(3),
        name="first_image",
    )(drive_all, bundle, group_table, *sides)
    image_all = exchange(image_spread).reshape(1, segments)
    cube_scratch = [pltpu.VMEM(cube_shape, jnp.bfloat16), pltpu.SemaphoreType.DMA((3 * chunk_count,))]
    if keep:
        cubes, after = stream(
            functools.partial(weigh_kernel, n_row=n_row, n_col=n_col),
            out_shape=(shape(roomy(4 * CHUNK * width), *cube_shape[1:], dtype=jnp.bfloat16), shape(8, 128)),
            in_specs=[smem, smem, vmem, vmem],
            out_specs=(hbm, vmem),
            scratch_shapes=cube_scratch,
            cost_estimate=work(5),
            name="weigh",
        )(group_table, range_len, left, right)
    else:
        after = group_table
    basis, basis_own, stats, known = call(
        functools.partial(second_kernel, coupling),
        out_shape=(shape(2, segments), shape(2, seg_dev), shape(n_dev, 1, 128), shape(1, 128)),
        scratch_shapes=scratch,
        cost_estimate=work(3),
        name="second_image",
    )(drive_all, image_all, image_own, bundle, after, *sides)
    stats_all = exchange(stats)

    field = stream(
        functools.partial(field_kernel, n_row=n_row, n_col=n_col, keep=keep),
        out_shape=shape(12, points_count),
        in_specs=[smem, smem, vmem, vmem, vmem] + ([hbm] if keep else [vmem, vmem]),
        scratch_shapes=[
            pltpu.VMEM((32, segments), jnp.bfloat16),
            pltpu.VMEM((16 * chunk_count, CHUNK), jnp.float32),
        ] + (cube_scratch if keep else []),
        cost_estimate=work(6),
        name="block_field",
    )(group_table, range_len, slot, moment, basis, *([cubes] if keep else [left, right]))
    currents, iron_field = stream(
        final_kernel,
        out_shape=(shape(1, seg_dev), shape(3, points_count)),
        name="combine",
    )(stats_all, known, basis_own, field, bundle)
    return (currents[0], iron_field)


def solution(mesh):
    return jax.shard_map(
        shards,
        mesh=mesh,
        in_specs=(
            P(AXES),
            P(AXES),
            P(None, "col"),
            P(None, "col"),
            P(None, AXES),
            P(AXES, None),
            P(),
        ),
        out_specs=(P(AXES), P(None, AXES)),
        check_vma=False,
    )
```

```python
import functools
import math

import jax
import jax.numpy as jnp
from jax import lax
from jax.experimental import pallas as pl
from jax.experimental.pallas import tpu as pltpu
from jax.sharding import PartitionSpec as P

EPS_SEG = 0.0004
EPS_FIELD = 0.0025
AXES = ("col", "row")
CHUNK = 128
GROUP = 4
TILE = 512
COLUMNS = 256
ROWS = 64
KEEP_BYTES = 16 * 1024 * 1024
VMEM_LIMIT = 32 * 1024 * 1024
STREAM_LIMIT = 44 * 1024 * 1024
STREAM_BYTES = 20 * 1024 * 1024
ENTRY_LIMIT = 60 * 1024 * 1024


def split3(x):
    high = x.astype(jnp.bfloat16).astype(jnp.float32)
    rest = x - high
    middle = rest.astype(jnp.bfloat16).astype(jnp.float32)
    low = (rest - middle).astype(jnp.bfloat16).astype(jnp.float32)
    return high, middle, low


def left_parts(x):
    high, middle, low = split3(x)
    return jnp.concatenate([high, high, middle, middle, high, low], axis=0)


def right_parts(x):
    high, middle, low = split3(x)
    return jnp.concatenate([high, middle, high, middle, low, high], axis=0).astype(jnp.bfloat16)


def rows8(*rows):
    width = rows[0].shape[1]
    count = sum(r.shape[0] for r in rows)
    if count < 8:
        rows = rows + (jnp.zeros((8 - count, width), jnp.float32),)
    return jnp.concatenate(rows, axis=0)


def left_center(c, eps):
    square = jnp.sum(c * c, axis=0, keepdims=True)
    return rows8(-2.0 * c, jnp.ones_like(square), square + eps)


def right_center(c):
    square = jnp.sum(c * c, axis=0, keepdims=True)
    return rows8(c, square, jnp.ones_like(square))


def dot(a, b):
    return jnp.dot(a, b, preferred_element_type=jnp.float32)


def dot_nt(a, b):
    return lax.dot_general(a, b, (((1,), (1,)), ((), ())), preferred_element_type=jnp.float32)


def transposed(x):
    return x.T.astype(jnp.bfloat16)


def iota(shape, axis):
    return lax.broadcasted_iota(jnp.int32, shape, axis)


def aligned(start, size):
    return pl.ds(pl.multiple_of(start, size), size)


def sides_kernel(*refs, n_col):
    pieces, (right_ref, moment_ref, left_ref, along_ref) = refs[:n_col], refs[n_col:]
    length = right_ref.shape[1] // n_col
    seg_dev = left_ref.shape[1]
    own_at = aligned(lax.axis_index("row") * seg_dev, seg_dev)
    tangent = rows8(pieces[0][3:6, own_at])
    left_ref[0] = transposed(left_parts(left_center(pieces[0][0:3, own_at] - 0.5, EPS_SEG)))
    left_ref[1] = transposed(left_parts(tangent))
    tangent = tangent.T
    for k in range(3):
        along_ref[k] = jnp.broadcast_to(tangent[:, k:k + 1], (seg_dev, 128))
    for shift, piece in enumerate(pieces):
        col = lax.rem(lax.axis_index("col") + n_col - shift, n_col)

        def step(k, carry):
            geo = piece[0:6, aligned(k * TILE, TILE)]
            to = pl.ds(pl.multiple_of(col * length + k * TILE, TILE), TILE)
            center, tangent = geo[0:3] - 0.5, geo[3:6]
            cross = jnp.concatenate([
                tangent[1:2] * center[2:3] - tangent[2:3] * center[1:2],
                tangent[2:3] * center[0:1] - tangent[0:1] * center[2:3],
                tangent[0:1] * center[1:2] - tangent[1:2] * center[0:1],
            ], axis=0)
            right_ref[:, to] = right_parts(right_center(center))
            moment_ref[:, to] = rows8(tangent, cross)
            return carry

        lax.fori_loop(0, length // TILE, step, 0, unroll=4)


def couple(right_ref, moment_ref, left_ref, along_ref, vec_ref, acc_ref):
    acc_ref[...] = jnp.zeros_like(acc_ref)

    def step(k, carry):
        at = aligned(k * TILE, TILE)
        turned = moment_ref[0:3, at] * vec_ref[:, at]
        right = right_ref[:, at]
        for first in range(0, TILE, COLUMNS):
            columns = slice(first, first + COLUMNS)
            by_product = first % (2 * COLUMNS) == 0
            if by_product:
                turned_parts = right_parts(rows8(turned[:, columns]))
            for row in range(0, acc_ref.shape[0], ROWS):
                rows = slice(row, row + ROWS)
                inverse = lax.rsqrt(dot(left_ref[0, rows], right[:, columns]))
                total = acc_ref[rows]
                if by_product:
                    pair = dot(left_ref[1, rows], turned_parts) * inverse
                    for start in range(0, COLUMNS, 128):
                        total = total + pair[:, start:start + 128]
                else:
                    for start in range(0, COLUMNS, 128):
                        lanes = slice(first + start, first + start + 128)
                        along = along_ref[0, rows] * turned[0:1, lanes]
                        along = along + along_ref[1, rows] * turned[1:2, lanes]
                        along = along + along_ref[2, rows] * turned[2:3, lanes]
                        total = total + along * inverse[:, start:start + 128]
                acc_ref[rows] = total
        return carry

    lax.fori_loop(0, vec_ref.shape[1] // TILE, step, 0, unroll=4)
    return jnp.sum(acc_ref[...].T, axis=0, keepdims=True)


def part_bounds(n_col, seg_dev):
    width = n_col * seg_dev
    return ((0, width // 2), (width // 2, 3 * width // 4), (3 * width // 4, width))


def part_copy(kept, chunk, part, bounds):
    local, remote, sems = kept
    start, stop = bounds[part]
    return pltpu.make_async_copy(
        remote.at[chunk, :, start:stop], local.at[chunk, :, start:stop], sems.at[chunk * len(bounds) + part]
    )


def for_parts(group_ref, length_ref, chunk, bounds, action, otherwise=None):
    used = chunk < group_ref[1, 0]
    length = length_ref[group_ref[0, chunk]]
    for part, (start, _) in enumerate(bounds):
        active = jnp.logical_and(used, start < length)
        pl.when(active)(functools.partial(action, part))
        if otherwise is not None:
            pl.when(jnp.logical_not(active))(functools.partial(otherwise, part))


def spread_rows(ref, row):
    for k in range(ref.shape[0]):
        ref[k] = row


def entry_kernel(drive_hbm, centers_hbm, tangents_hbm, spread_ref, geo_ref, drive, centers, tangents, sems):
    pairs = ((drive_hbm, drive), (centers_hbm, centers), (tangents_hbm, tangents))
    copies = [pltpu.make_async_copy(source, target, sems.at[k]) for k, (source, target) in enumerate(pairs)]
    for copy in copies:
        copy.start()
    for copy in copies:
        copy.wait()
    spread_rows(spread_ref, drive[...])
    geo_ref[0:3] = centers[...]
    geo_ref[3:6] = tangents[...]


def own_rows(bundle_ref, like_ref):
    seg_dev = like_ref.shape[1]
    return bundle_ref[10:11, 0:seg_dev], bundle_ref[10:11, seg_dev:2 * seg_dev]


def first_kernel(coupling, drive_ref, bundle_ref, after_ref, right_ref, moment_ref, left_ref, along_ref,
                 image_ref, spread_ref, vec_ref, acc_ref):
    drive = drive_ref[...]
    scale = 1.0 / jnp.sqrt(jnp.sum(drive * drive, keepdims=True))
    vec_ref[...] = drive * scale
    product = couple(right_ref, moment_ref, left_ref, along_ref, vec_ref, acc_ref)
    drive_own, resist_own = own_rows(bundle_ref, image_ref)
    image = resist_own * (drive_own * scale) + coupling * product
    image_ref[...] = image
    spread_rows(spread_ref, image)


def second_kernel(coupling, drive_ref, image_ref, image_own_ref, bundle_ref, after_ref,
                  right_ref, moment_ref, left_ref, along_ref,
                  basis_ref, basis_own_ref, stats_ref, known_ref, vec_ref, acc_ref):
    drive = drive_ref[...]
    norm = jnp.sqrt(jnp.sum(drive * drive, keepdims=True))
    scale = 1.0 / norm
    basis_a = drive * scale
    image = image_ref[...]
    hessen_a = jnp.sum(image * basis_a, keepdims=True)
    rest = image - hessen_a * basis_a
    hessen_b = jnp.sqrt(jnp.sum(rest * rest, keepdims=True))
    inverse = 1.0 / hessen_b
    basis_b = rest * inverse
    vec_ref[...] = basis_b
    basis_ref[0:1, :] = basis_a
    basis_ref[1:2, :] = basis_b
    drive_own, resist_own = own_rows(bundle_ref, image_own_ref)
    own_a = drive_own * scale
    own_b = (image_own_ref[...] - hessen_a * own_a) * inverse
    basis_own_ref[0:1, :] = own_a
    basis_own_ref[1:2, :] = own_b
    product = couple(right_ref, moment_ref, left_ref, along_ref, vec_ref, acc_ref)
    second = resist_own * own_b + coupling * product
    lane = iota((1, 128), 1)

    def three(a, b, c):
        return jnp.where(lane == 0, a, jnp.where(lane == 1, b, jnp.where(lane == 2, c, 0.0)))

    spread_rows(stats_ref, three(
        jnp.sum(second * own_a, keepdims=True),
        jnp.sum(second * own_b, keepdims=True),
        jnp.sum(second * second, keepdims=True),
    ))
    known_ref[...] = three(norm, hessen_a, hessen_b)


def group_kernel(bundle_ref, slot_ref, table_ref, left_ref, planes_ref, *, n_row):
    points = slot_ref.shape[1]
    chunk_count = left_ref.shape[0] // CHUNK
    owner = bundle_ref[9:10, 0:points].astype(jnp.int32)
    rows = max(8, n_row)
    marks = jnp.where(iota((rows, points), 0) == owner, 1.0, 0.0)
    tile = 256
    upper = jnp.where(iota((tile, tile), 0) <= iota((tile, tile), 1), 1.0, 0.0).astype(jnp.bfloat16)
    before = jnp.zeros((rows, 1), jnp.float32)
    ranks = []
    for piece in range(points // tile):
        part = dot(marks[:, piece * tile:(piece + 1) * tile].astype(jnp.bfloat16), upper)
        ranks.append(part + before - 1.0)
        before = before + part[:, tile - 1:tile]
    ranks = jnp.concatenate(ranks, axis=1)
    chunks = jnp.floor((before + (CHUNK - 1)) * (1.0 / CHUNK))
    start = jnp.zeros((1, 1), jnp.float32)
    starts = []
    for name in range(rows):
        starts.append(start)
        start = start + chunks[name:name + 1]
    starts = jnp.concatenate(starts, axis=0)
    slot = jnp.sum(marks * (ranks + starts * CHUNK), axis=0, keepdims=True).astype(jnp.int32)
    slot_ref[...] = slot
    lane = iota((rows, 128), 1)
    ended = jnp.sum(jnp.where(starts + chunks <= lane.astype(jnp.float32), 1.0, 0.0), axis=0, keepdims=True)
    block = jnp.minimum(ended, n_row - 1.0)
    place = iota((8, 128), 0)
    table_ref[...] = jnp.where(place == 0, block, start).astype(jnp.int32)
    high = jnp.where(iota((chunk_count, points), 0) == slot // CHUNK, 1.0, 0.0)
    low = jnp.where(iota((CHUNK, points), 0) == slot % CHUNK, 1.0, 0.0).astype(jnp.bfloat16)
    parts = split3(bundle_ref[6:9, 0:points] - 0.5)
    spread = jnp.concatenate([high * part[k:k + 1] for k in range(3) for part in parts], axis=0).astype(jnp.bfloat16)
    placed = dot_nt(spread, low)
    planes = [placed[k * chunk_count:(k + 1) * chunk_count] for k in range(9)]
    x, y, z = (planes[3 * k] + planes[3 * k + 1] + planes[3 * k + 2] for k in range(3))
    sides = [-2.0 * x, -2.0 * y, -2.0 * z, jnp.ones_like(x), x * x + y * y + z * z + EPS_FIELD]
    sides = [split3(side) for side in sides]
    empty = jnp.zeros_like(x)
    for group, part in enumerate([0, 0, 1, 1, 0, 2]):
        for k in range(8):
            to = pl.ds((group * 8 + k) * chunk_count, chunk_count)
            planes_ref[to, :] = sides[k][part] if k < 5 else empty
    for chunk in range(chunk_count):
        left_ref[chunk * CHUNK:(chunk + 1) * CHUNK, :] = transposed(planes_ref[pl.ds(chunk, 48, stride=chunk_count), :])


def cube_halves(left, right):
    inverse = lax.rsqrt(dot(left, right))
    cube = inverse * inverse * inverse
    high = cube.astype(jnp.bfloat16)
    return high, (cube - high.astype(jnp.float32)).astype(jnp.bfloat16)


def block_part(block, col, n_row, seg_dev):
    return aligned((col * n_row + block) * seg_dev, seg_dev)


def chunk_steps(group_ref):
    return (group_ref[1, 0] + GROUP - 1) // GROUP


def weigh_kernel(group_ref, left_ref, right_ref, cubes_hbm, done_ref, cubes_ref, sems, *, n_row, n_col):
    seg_dev = right_ref.shape[1] // (n_row * n_col)
    done_ref[...] = jnp.zeros_like(done_ref)

    def chunk_copy(chunk):
        return pltpu.make_async_copy(cubes_ref.at[chunk], cubes_hbm.at[chunk], sems.at[chunk])

    def step(k, carry):
        for part in range(GROUP):
            chunk = k * GROUP + part
            left = left_ref[aligned(chunk * CHUNK, CHUNK), :]
            for col in range(n_col):
                to = slice(col * seg_dev, (col + 1) * seg_dev)
                high, low = cube_halves(left, right_ref[:, block_part(group_ref[0, chunk], col, n_row, seg_dev)])
                cubes_ref[chunk, 0:CHUNK, to] = high
                cubes_ref[chunk, CHUNK:2 * CHUNK, to] = low
            chunk_copy(chunk).start()
        return carry

    def finish(k, carry):
        for part in range(GROUP):
            chunk_copy(k * GROUP + part).wait()
        return carry

    lax.fori_loop(0, chunk_steps(group_ref), step, 0)
    lax.fori_loop(0, chunk_steps(group_ref), finish, 0)


def field_kernel(group_ref, length_ref, slot_ref, moment_ref, basis_ref, *refs, n_row, n_col, keep):
    if keep:
        cubes_hbm, out_ref, table_ref, sums_ref, cubes_ref, sems = refs
        kept = (cubes_ref, cubes_hbm, sems)

        bounds = part_bounds(n_col, moment_ref.shape[1] // (n_row * n_col))

        def clear(chunk, piece):
            start, stop = bounds[piece]
            cubes_ref[chunk, :, start:stop] = jnp.zeros((2 * CHUNK, stop - start), jnp.bfloat16)

        def begin(chunk, carry):
            for_parts(group_ref, length_ref, chunk, bounds,
                      lambda piece: part_copy(kept, chunk, piece, bounds).start(),
                      lambda piece: clear(chunk, piece))
            return carry

        def arrive(chunk):
            for_parts(group_ref, length_ref, chunk, bounds,
                      lambda piece: part_copy(kept, chunk, piece, bounds).wait())

        lax.fori_loop(0, chunk_steps(group_ref) * GROUP, begin, 0)
    else:
        left_ref, right_ref, out_ref, table_ref, sums_ref = refs
    chunk_count = sums_ref.shape[0] // 16
    seg_dev = moment_ref.shape[1] // (n_row * n_col)
    scale = 1.0 / math.sqrt(n_col * seg_dev)
    lane = iota((1, seg_dev), 1)
    sums_ref[...] = jnp.zeros_like(sums_ref)

    def table_step(block, carry):
        length = length_ref[block]
        for col in range(n_col):
            at = block_part(block, col, n_row, seg_dev)
            both = moment_ref[:, at]
            active = jnp.where(lane + col * seg_dev < length, scale, 0.0)
            first = both * (basis_ref[0:1, at] * active)
            second = both * (basis_ref[1:2, at] * active)
            parts = jnp.concatenate([first, second], axis=0)
            high = parts.astype(jnp.bfloat16).astype(jnp.float32)
            table_ref[:, at] = jnp.concatenate([high, parts - high], axis=0).astype(jnp.bfloat16)
        return carry

    lax.fori_loop(0, n_row, table_step, 0, unroll=min(n_row, 8))

    def block_row(ref, chunk):
        block = group_ref[0, chunk]
        return jnp.concatenate([ref[:, block_part(block, col, n_row, seg_dev)] for col in range(n_col)], axis=1)

    def cubes_of(chunk):
        return jnp.concatenate(cube_halves(left_ref[aligned(chunk * CHUNK, CHUNK), :], block_row(right_ref, chunk)), axis=0)

    def step(k, carry):
        if keep:
            for part in range(GROUP):
                arrive(k * GROUP + part)
        for part in range(0, GROUP, 2):
            chunk = k * GROUP + part
            tables = jnp.concatenate([block_row(table_ref, chunk), block_row(table_ref, chunk + 1)], axis=0)
            if keep:
                cubes = cubes_ref[pl.ds(chunk, 2)].reshape(4 * CHUNK, n_col * seg_dev)
            else:
                cubes = jnp.concatenate([cubes_of(chunk), cubes_of(chunk + 1)], axis=0)
            both = dot_nt(tables, cubes)
            for half in range(2):
                mine = both[32 * half:32 * half + 32, 2 * CHUNK * half:2 * CHUNK * (half + 1)]
                total = mine[:, 0:CHUNK] + mine[:, CHUNK:2 * CHUNK]
                sums_ref[pl.ds(chunk + half, 16, stride=chunk_count), :] = total[0:16] + total[16:32]
        return carry

    lax.fori_loop(0, chunk_steps(group_ref), step, 0)
    sums = jnp.concatenate([sums_ref[0:6 * chunk_count], sums_ref[8 * chunk_count:14 * chunk_count]], axis=0)
    sums = jnp.concatenate(split3(sums), axis=1).astype(jnp.bfloat16)
    for tile in range(slot_ref.shape[1] // TILE):
        at = pl.ds(tile * TILE, TILE)
        slot = slot_ref[:, at]
        low = jnp.where(iota((CHUNK, TILE), 0) == slot % CHUNK, 1.0, 0.0).astype(jnp.bfloat16)
        high = jnp.where(iota((chunk_count, TILE), 0) == slot // CHUNK, 1.0, 0.0)
        found = dot(sums, jnp.concatenate([low, low, low], axis=0))
        for row in range(12):
            picked = found[row * chunk_count:(row + 1) * chunk_count] * high
            out_ref[row:row + 1, at] = jnp.sum(picked, axis=0, keepdims=True)


def final_kernel(stats_ref, known_ref, basis_own_ref, field_ref, bundle_ref, currents_ref, iron_ref):
    stats = jnp.sum(stats_ref[...], axis=0)
    known = known_ref[...]
    initial_norm, hessen_a, hessen_b = known[:, 0:1], known[:, 1:2], known[:, 2:3]
    hessen_c, hessen_d, normal_second = stats[:, 0:1], stats[:, 1:2], stats[:, 2:3]
    normal_first = hessen_a * hessen_a + hessen_b * hessen_b
    normal_cross = hessen_a * hessen_c + hessen_b * hessen_d
    target_first = initial_norm * hessen_a
    target_second = initial_norm * hessen_c
    determinant = normal_first * normal_second - normal_cross * normal_cross
    weight_first = (normal_second * target_first - normal_cross * target_second) / determinant
    weight_second = (normal_first * target_second - normal_cross * target_first) / determinant
    currents_ref[...] = weight_first * basis_own_ref[0:1, :] + weight_second * basis_own_ref[1:2, :]
    moments = weight_first * field_ref[0:6, :] + weight_second * field_ref[6:12, :]
    points = bundle_ref[6:9, 0:iron_ref.shape[1]] - 0.5
    px, py, pz = points[0:1], points[1:2], points[2:3]
    iron_ref[0:1, :] = pz * moments[1:2] - py * moments[2:3] - moments[3:4]
    iron_ref[1:2, :] = px * moments[2:3] - pz * moments[0:1] - moments[4:5]
    iron_ref[2:3, :] = py * moments[0:1] - px * moments[1:2] - moments[5:6]


def shape(*sizes, dtype=jnp.float32):
    return jax.ShapeDtypeStruct(sizes, dtype)


def shards(drive, resist, centers, tangents, iron_points, owner, range_len):
    seg_dev = drive.shape[0]
    col_len = centers.shape[1]
    n_col = lax.axis_size("col")
    n_row = lax.axis_size("row")
    n_dev = n_col * n_row
    segments = seg_dev * n_dev
    width = n_col * seg_dev
    points_count = iron_points.shape[1]
    coupling = 0.5 / math.sqrt(segments)
    call = functools.partial(pl.pallas_call, compiler_params=pltpu.CompilerParams(vmem_limit_bytes=VMEM_LIMIT))
    scratch = [pltpu.VMEM((1, segments), jnp.float32), pltpu.VMEM((seg_dev, 128), jnp.float32)]
    hbm = pl.BlockSpec(memory_space=pltpu.HBM)
    smem = pl.BlockSpec(memory_space=pltpu.SMEM)
    vmem = pl.BlockSpec(memory_space=pltpu.VMEM)

    def work(microseconds):
        return pl.CostEstimate(flops=int(microseconds * 1e9), bytes_accessed=0, transcendentals=0)

    def roomy(row_bytes):
        return STREAM_BYTES // row_bytes

    def exchange(x):
        return lax.all_to_all(x, AXES, 0, 0, tiled=True)

    spread, geometry = pl.pallas_call(
        entry_kernel,
        out_shape=(shape(n_dev, 1, seg_dev), shape(6, col_len)),
        in_specs=[hbm] * 3,
        scratch_shapes=[
            pltpu.VMEM((1, seg_dev), jnp.float32),
            pltpu.VMEM((3, col_len), jnp.float32),
            pltpu.VMEM((3, col_len), jnp.float32),
            pltpu.SemaphoreType.DMA((3,)),
        ],
        compiler_params=pltpu.CompilerParams(vmem_limit_bytes=ENTRY_LIMIT),
        cost_estimate=work(8),
        name="entry",
    )(drive[None, :], centers, tangents)
    drive_all = exchange(spread).reshape(1, segments)
    longest = max(col_len, points_count, 2 * seg_dev)

    def wide(row):
        return jnp.pad(row, ((0, 0), (0, longest - row.shape[1])))

    bundle = jnp.concatenate([
        wide(centers), wide(tangents), wide(iron_points), wide(owner.reshape(1, points_count).astype(jnp.float32)),
        wide(jnp.concatenate([drive, resist])[None, :]),
    ], axis=0)
    pieces = [bundle] + [
        lax.ppermute(geometry, "col", [(k, (k + shift) % n_col) for k in range(n_col)]) for shift in range(1, n_col)
    ]

    chunk_count = points_count // CHUNK + n_row * (CHUNK - 1) // CHUNK
    chunk_count = -(-chunk_count // 8) * 8
    slot, group_table, left = call(
        functools.partial(group_kernel, n_row=n_row),
        out_shape=(
            shape(1, points_count, dtype=jnp.int32),
            shape(8, 128, dtype=jnp.int32),
            shape(chunk_count * CHUNK, 48, dtype=jnp.bfloat16),
        ),
        scratch_shapes=[pltpu.VMEM((48 * chunk_count, CHUNK), jnp.float32)],
        cost_estimate=work(3),
        name="group_points",
    )(bundle)

    cube_shape = (chunk_count, 2 * CHUNK, width)
    keep = 2 * math.prod(cube_shape) <= KEEP_BYTES
    stream = functools.partial(
        pl.pallas_call, compiler_params=pltpu.CompilerParams(vmem_limit_bytes=STREAM_LIMIT if keep else VMEM_LIMIT)
    )
    sides = call(
        functools.partial(sides_kernel, n_col=n_col),
        out_shape=(
            shape(48, segments, dtype=jnp.bfloat16), shape(8, segments),
            shape(2, seg_dev, 48, dtype=jnp.bfloat16), shape(3, seg_dev, 128),
        ),
        cost_estimate=work(1),
        name="sides",
    )(*pieces)
    right, moment = sides[0:2]
    image_own, image_spread = call(
        functools.partial(first_kernel, coupling),
        out_shape=(shape(1, seg_dev), shape(n_dev, 1, seg_dev)),
        scratch_shapes=scratch,
        cost_estimate=work(3),
        name="first_image",
    )(drive_all, bundle, group_table, *sides)
    image_all = exchange(image_spread).reshape(1, segments)
    cube_scratch = [pltpu.VMEM(cube_shape, jnp.bfloat16), pltpu.SemaphoreType.DMA((3 * chunk_count,))]
    if keep:
        cubes, after = stream(
            functools.partial(weigh_kernel, n_row=n_row, n_col=n_col),
            out_shape=(shape(roomy(4 * CHUNK * width), *cube_shape[1:], dtype=jnp.bfloat16), shape(8, 128)),
            in_specs=[smem, vmem, vmem],
            out_specs=(hbm, vmem),
            scratch_shapes=cube_scratch,
            cost_estimate=work(5),
            name="weigh",
        )(group_table, left, right)
    else:
        after = group_table
    basis, basis_own, stats, known = call(
        functools.partial(second_kernel, coupling),
        out_shape=(shape(2, segments), shape(2, seg_dev), shape(n_dev, 1, 128), shape(1, 128)),
        scratch_shapes=scratch,
        cost_estimate=work(3),
        name="second_image",
    )(drive_all, image_all, image_own, bundle, after, *sides)
    stats_all = exchange(stats)

    field = stream(
        functools.partial(field_kernel, n_row=n_row, n_col=n_col, keep=keep),
        out_shape=shape(12, points_count),
        in_specs=[smem, smem, vmem, vmem, vmem] + ([hbm] if keep else [vmem, vmem]),
        scratch_shapes=[
            pltpu.VMEM((32, segments), jnp.bfloat16),
            pltpu.VMEM((16 * chunk_count, CHUNK), jnp.float32),
        ] + (cube_scratch if keep else []),
        cost_estimate=work(6),
        name="block_field",
    )(group_table, range_len, slot, moment, basis, *([cubes] if keep else [left, right]))
    currents, iron_field = stream(
        final_kernel,
        out_shape=(shape(1, seg_dev), shape(3, points_count)),
        name="combine",
    )(stats_all, known, basis_own, field, bundle)
    return (currents[0], iron_field)


def solution(mesh):
    return jax.shard_map(
        shards,
        mesh=mesh,
        in_specs=(
            P(AXES),
            P(AXES),
            P(None, "col"),
            P(None, "col"),
            P(None, AXES),
            P(AXES, None),
            P(),
        ),
        out_specs=(P(AXES), P(None, AXES)),
        check_vma=False,
    )
```

```python
import functools
import math

import jax
import jax.numpy as jnp
from jax import lax
from jax.experimental import pallas as pl
from jax.experimental.pallas import tpu as pltpu
from jax.sharding import PartitionSpec as P

EPS_SEG = 0.0004
EPS_FIELD = 0.0025
AXES = ("col", "row")
CHUNK = 128
GROUP = 4
EARLY = 8
TILE = 512
COLUMNS = 256
ROWS = 64
KEEP_BYTES = 16 * 1024 * 1024
VMEM_LIMIT = 32 * 1024 * 1024
STREAM_LIMIT = 44 * 1024 * 1024
STREAM_BYTES = 20 * 1024 * 1024
ENTRY_LIMIT = 60 * 1024 * 1024


def split3(x):
    high = x.astype(jnp.bfloat16).astype(jnp.float32)
    rest = x - high
    middle = rest.astype(jnp.bfloat16).astype(jnp.float32)
    low = (rest - middle).astype(jnp.bfloat16).astype(jnp.float32)
    return high, middle, low


def left_parts(x):
    high, middle, low = split3(x)
    return jnp.concatenate([high, high, middle, middle, high, low], axis=0)


def right_parts(x):
    high, middle, low = split3(x)
    return jnp.concatenate([high, middle, high, middle, low, high], axis=0).astype(jnp.bfloat16)


def rows8(*rows):
    width = rows[0].shape[1]
    count = sum(r.shape[0] for r in rows)
    if count < 8:
        rows = rows + (jnp.zeros((8 - count, width), jnp.float32),)
    return jnp.concatenate(rows, axis=0)


def left_center(c, eps):
    square = jnp.sum(c * c, axis=0, keepdims=True)
    return rows8(-2.0 * c, jnp.ones_like(square), square + eps)


def right_center(c):
    square = jnp.sum(c * c, axis=0, keepdims=True)
    return rows8(c, square, jnp.ones_like(square))


def dot(a, b):
    return jnp.dot(a, b, preferred_element_type=jnp.float32)


def dot_nt(a, b):
    return lax.dot_general(a, b, (((1,), (1,)), ((), ())), preferred_element_type=jnp.float32)


def transposed(x):
    return x.T.astype(jnp.bfloat16)


def iota(shape, axis):
    return lax.broadcasted_iota(jnp.int32, shape, axis)


def aligned(start, size):
    return pl.ds(pl.multiple_of(start, size), size)


def sides_kernel(*refs, n_col):
    pieces, (right_ref, moment_ref, left_ref, along_ref) = refs[:n_col], refs[n_col:]
    length = right_ref.shape[1] // n_col
    seg_dev = left_ref.shape[1]
    own_at = aligned(lax.axis_index("row") * seg_dev, seg_dev)
    tangent = rows8(pieces[0][3:6, own_at])
    left_ref[0] = transposed(left_parts(left_center(pieces[0][0:3, own_at] - 0.5, EPS_SEG)))
    left_ref[1] = transposed(left_parts(tangent))
    tangent = tangent.T
    for k in range(3):
        along_ref[k] = jnp.broadcast_to(tangent[:, k:k + 1], (seg_dev, 128))
    for shift, piece in enumerate(pieces):
        col = lax.rem(lax.axis_index("col") + n_col - shift, n_col)

        def step(k, carry):
            geo = piece[0:6, aligned(k * TILE, TILE)]
            to = pl.ds(pl.multiple_of(col * length + k * TILE, TILE), TILE)
            center, tangent = geo[0:3] - 0.5, geo[3:6]
            cross = jnp.concatenate([
                tangent[1:2] * center[2:3] - tangent[2:3] * center[1:2],
                tangent[2:3] * center[0:1] - tangent[0:1] * center[2:3],
                tangent[0:1] * center[1:2] - tangent[1:2] * center[0:1],
            ], axis=0)
            right_ref[:, to] = right_parts(right_center(center))
            moment_ref[:, to] = rows8(tangent, cross)
            return carry

        lax.fori_loop(0, length // TILE, step, 0, unroll=4)


def couple(right_ref, moment_ref, left_ref, along_ref, vec_ref, acc_ref):
    acc_ref[...] = jnp.zeros_like(acc_ref)

    def step(k, carry):
        at = aligned(k * TILE, TILE)
        turned = moment_ref[0:3, at] * vec_ref[:, at]
        right = right_ref[:, at]
        for first in range(0, TILE, COLUMNS):
            columns = slice(first, first + COLUMNS)
            by_product = first % (2 * COLUMNS) == 0
            if by_product:
                turned_parts = right_parts(rows8(turned[:, columns]))
            for row in range(0, acc_ref.shape[0], ROWS):
                rows = slice(row, row + ROWS)
                inverse = lax.rsqrt(dot(left_ref[0, rows], right[:, columns]))
                total = acc_ref[rows]
                if by_product:
                    pair = dot(left_ref[1, rows], turned_parts) * inverse
                    for start in range(0, COLUMNS, 128):
                        total = total + pair[:, start:start + 128]
                else:
                    for start in range(0, COLUMNS, 128):
                        lanes = slice(first + start, first + start + 128)
                        along = along_ref[0, rows] * turned[0:1, lanes]
                        along = along + along_ref[1, rows] * turned[1:2, lanes]
                        along = along + along_ref[2, rows] * turned[2:3, lanes]
                        total = total + along * inverse[:, start:start + 128]
                acc_ref[rows] = total
        return carry

    lax.fori_loop(0, vec_ref.shape[1] // TILE, step, 0, unroll=4)
    return jnp.sum(acc_ref[...].T, axis=0, keepdims=True)


def part_bounds(n_col, seg_dev):
    width = n_col * seg_dev
    return ((0, width // 2), (width // 2, 3 * width // 4), (3 * width // 4, width))


def part_copy(kept, chunk, part, bounds, remote, first):
    local, sems = kept
    start, stop = bounds[part]
    return pltpu.make_async_copy(
        remote.at[chunk - first, :, start:stop], local.at[chunk, :, start:stop], sems.at[chunk * len(bounds) + part]
    )


def for_parts(group_ref, length_ref, chunk, bounds, action, otherwise=None):
    used = chunk < group_ref[1, 0]
    length = length_ref[group_ref[0, chunk]]
    for part, (start, _) in enumerate(bounds):
        active = jnp.logical_and(used, start < length)
        pl.when(active)(functools.partial(action, part))
        if otherwise is not None:
            pl.when(jnp.logical_not(active))(functools.partial(otherwise, part))


def spread_rows(ref, row):
    for k in range(ref.shape[0]):
        ref[k] = row


def entry_kernel(drive_hbm, centers_hbm, tangents_hbm, spread_ref, geo_ref, drive, centers, tangents, sems):
    pairs = ((drive_hbm, drive), (centers_hbm, centers), (tangents_hbm, tangents))
    copies = [pltpu.make_async_copy(source, target, sems.at[k]) for k, (source, target) in enumerate(pairs)]
    for copy in copies:
        copy.start()
    for copy in copies:
        copy.wait()
    spread_rows(spread_ref, drive[...])
    geo_ref[0:3] = centers[...]
    geo_ref[3:6] = tangents[...]


def own_rows(bundle_ref, like_ref):
    seg_dev = like_ref.shape[1]
    return bundle_ref[10:11, 0:seg_dev], bundle_ref[10:11, seg_dev:2 * seg_dev]


def first_kernel(coupling, drive_ref, bundle_ref, after_ref, right_ref, moment_ref, left_ref, along_ref,
                 image_ref, spread_ref, vec_ref, acc_ref):
    drive = drive_ref[...]
    scale = 1.0 / jnp.sqrt(jnp.sum(drive * drive, keepdims=True))
    vec_ref[...] = drive * scale
    product = couple(right_ref, moment_ref, left_ref, along_ref, vec_ref, acc_ref)
    drive_own, resist_own = own_rows(bundle_ref, image_ref)
    image = resist_own * (drive_own * scale) + coupling * product
    image_ref[...] = image
    spread_rows(spread_ref, image)


def second_kernel(coupling, drive_ref, image_ref, image_own_ref, bundle_ref, after_ref,
                  right_ref, moment_ref, left_ref, along_ref,
                  basis_ref, basis_own_ref, stats_ref, known_ref, vec_ref, acc_ref):
    drive = drive_ref[...]
    norm = jnp.sqrt(jnp.sum(drive * drive, keepdims=True))
    scale = 1.0 / norm
    basis_a = drive * scale
    image = image_ref[...]
    hessen_a = jnp.sum(image * basis_a, keepdims=True)
    rest = image - hessen_a * basis_a
    hessen_b = jnp.sqrt(jnp.sum(rest * rest, keepdims=True))
    inverse = 1.0 / hessen_b
    basis_b = rest * inverse
    vec_ref[...] = basis_b
    basis_ref[0:1, :] = basis_a
    basis_ref[1:2, :] = basis_b
    drive_own, resist_own = own_rows(bundle_ref, image_own_ref)
    own_a = drive_own * scale
    own_b = (image_own_ref[...] - hessen_a * own_a) * inverse
    basis_own_ref[0:1, :] = own_a
    basis_own_ref[1:2, :] = own_b
    product = couple(right_ref, moment_ref, left_ref, along_ref, vec_ref, acc_ref)
    second = resist_own * own_b + coupling * product
    lane = iota((1, 128), 1)

    def three(a, b, c):
        return jnp.where(lane == 0, a, jnp.where(lane == 1, b, jnp.where(lane == 2, c, 0.0)))

    spread_rows(stats_ref, three(
        jnp.sum(second * own_a, keepdims=True),
        jnp.sum(second * own_b, keepdims=True),
        jnp.sum(second * second, keepdims=True),
    ))
    known_ref[...] = three(norm, hessen_a, hessen_b)


def group_kernel(bundle_ref, slot_ref, table_ref, left_ref, planes_ref, *, n_row):
    points = slot_ref.shape[1]
    chunk_count = left_ref.shape[0] // CHUNK
    owner = bundle_ref[9:10, 0:points].astype(jnp.int32)
    rows = max(8, n_row)
    marks = jnp.where(iota((rows, points), 0) == owner, 1.0, 0.0)
    tile = 256
    upper = jnp.where(iota((tile, tile), 0) <= iota((tile, tile), 1), 1.0, 0.0).astype(jnp.bfloat16)
    before = jnp.zeros((rows, 1), jnp.float32)
    ranks = []
    for piece in range(points // tile):
        part = dot(marks[:, piece * tile:(piece + 1) * tile].astype(jnp.bfloat16), upper)
        ranks.append(part + before - 1.0)
        before = before + part[:, tile - 1:tile]
    ranks = jnp.concatenate(ranks, axis=1)
    chunks = jnp.floor((before + (CHUNK - 1)) * (1.0 / CHUNK))
    start = jnp.zeros((1, 1), jnp.float32)
    starts = []
    for name in range(rows):
        starts.append(start)
        start = start + chunks[name:name + 1]
    starts = jnp.concatenate(starts, axis=0)
    slot = jnp.sum(marks * (ranks + starts * CHUNK), axis=0, keepdims=True).astype(jnp.int32)
    slot_ref[...] = slot
    lane = iota((rows, 128), 1)
    ended = jnp.sum(jnp.where(starts + chunks <= lane.astype(jnp.float32), 1.0, 0.0), axis=0, keepdims=True)
    block = jnp.minimum(ended, n_row - 1.0)
    place = iota((8, 128), 0)
    table_ref[...] = jnp.where(place == 0, block, start).astype(jnp.int32)
    high = jnp.where(iota((chunk_count, points), 0) == slot // CHUNK, 1.0, 0.0)
    low = jnp.where(iota((CHUNK, points), 0) == slot % CHUNK, 1.0, 0.0).astype(jnp.bfloat16)
    parts = split3(bundle_ref[6:9, 0:points] - 0.5)
    spread = jnp.concatenate([high * part[k:k + 1] for k in range(3) for part in parts], axis=0).astype(jnp.bfloat16)
    placed = dot_nt(spread, low)
    planes = [placed[k * chunk_count:(k + 1) * chunk_count] for k in range(9)]
    x, y, z = (planes[3 * k] + planes[3 * k + 1] + planes[3 * k + 2] for k in range(3))
    sides = [-2.0 * x, -2.0 * y, -2.0 * z, jnp.ones_like(x), x * x + y * y + z * z + EPS_FIELD]
    sides = [split3(side) for side in sides]
    empty = jnp.zeros_like(x)
    for group, part in enumerate([0, 0, 1, 1, 0, 2]):
        for k in range(8):
            to = pl.ds((group * 8 + k) * chunk_count, chunk_count)
            planes_ref[to, :] = sides[k][part] if k < 5 else empty
    for chunk in range(chunk_count):
        left_ref[chunk * CHUNK:(chunk + 1) * CHUNK, :] = transposed(planes_ref[pl.ds(chunk, 48, stride=chunk_count), :])


def cube_halves(left, right):
    inverse = lax.rsqrt(dot(left, right))
    cube = inverse * inverse * inverse
    high = cube.astype(jnp.bfloat16)
    return high, (cube - high.astype(jnp.float32)).astype(jnp.bfloat16)


def block_part(block, col, n_row, seg_dev):
    return aligned((col * n_row + block) * seg_dev, seg_dev)


def chunk_steps(group_ref):
    return (group_ref[1, 0] + GROUP - 1) // GROUP


def weigh_kernel(group_ref, left_ref, right_ref, cubes_hbm, done_ref, cubes_ref, sems, *, n_row, n_col, first, last):
    seg_dev = right_ref.shape[1] // (n_row * n_col)
    done_ref[...] = jnp.zeros_like(done_ref)
    stop = chunk_steps(group_ref) if last is None else last // GROUP

    def chunk_copy(place):
        return pltpu.make_async_copy(cubes_ref.at[place], cubes_hbm.at[place], sems.at[place])

    def step(k, carry):
        for part in range(GROUP):
            chunk = k * GROUP + part
            place = chunk - first
            left = left_ref[aligned(chunk * CHUNK, CHUNK), :]
            for col in range(n_col):
                to = slice(col * seg_dev, (col + 1) * seg_dev)
                high, low = cube_halves(left, right_ref[:, block_part(group_ref[0, chunk], col, n_row, seg_dev)])
                cubes_ref[place, 0:CHUNK, to] = high
                cubes_ref[place, CHUNK:2 * CHUNK, to] = low
            chunk_copy(place).start()
        return carry

    def finish(k, carry):
        for part in range(GROUP):
            chunk_copy(k * GROUP + part - first).wait()
        return carry

    lax.fori_loop(first // GROUP, stop, step, 0)
    lax.fori_loop(first // GROUP, stop, finish, 0)


def field_kernel(group_ref, length_ref, slot_ref, moment_ref, basis_ref, *refs, n_row, n_col, keep):
    if keep:
        early_hbm, late_hbm, out_ref, table_ref, sums_ref, cubes_ref, sems = refs
        kept = (cubes_ref, sems)

        bounds = part_bounds(n_col, moment_ref.shape[1] // (n_row * n_col))

        def clear(chunk, piece):
            start, stop = bounds[piece]
            cubes_ref[chunk, :, start:stop] = jnp.zeros((2 * CHUNK, stop - start), jnp.bfloat16)

        def begin(remote, first, chunk, carry):
            for_parts(group_ref, length_ref, chunk, bounds,
                      lambda piece: part_copy(kept, chunk, piece, bounds, remote, first).start(),
                      lambda piece: clear(chunk, piece))
            return carry

        def arrive(remote, first, chunk):
            for_parts(group_ref, length_ref, chunk, bounds,
                      lambda piece: part_copy(kept, chunk, piece, bounds, remote, first).wait())

        lax.fori_loop(0, EARLY, functools.partial(begin, early_hbm, 0), 0)
        lax.fori_loop(EARLY, chunk_steps(group_ref) * GROUP, functools.partial(begin, late_hbm, EARLY), 0)
    else:
        left_ref, right_ref, out_ref, table_ref, sums_ref = refs
    chunk_count = sums_ref.shape[0] // 16
    seg_dev = moment_ref.shape[1] // (n_row * n_col)
    scale = 1.0 / math.sqrt(n_col * seg_dev)
    lane = iota((1, seg_dev), 1)
    sums_ref[...] = jnp.zeros_like(sums_ref)

    def table_step(block, carry):
        length = length_ref[block]
        for col in range(n_col):
            at = block_part(block, col, n_row, seg_dev)
            both = moment_ref[:, at]
            active = jnp.where(lane + col * seg_dev < length, scale, 0.0)
            first = both * (basis_ref[0:1, at] * active)
            second = both * (basis_ref[1:2, at] * active)
            parts = jnp.concatenate([first, second], axis=0)
            high = parts.astype(jnp.bfloat16).astype(jnp.float32)
            table_ref[:, at] = jnp.concatenate([high, parts - high], axis=0).astype(jnp.bfloat16)
        return carry

    lax.fori_loop(0, n_row, table_step, 0, unroll=min(n_row, 8))

    def block_row(ref, chunk):
        block = group_ref[0, chunk]
        return jnp.concatenate([ref[:, block_part(block, col, n_row, seg_dev)] for col in range(n_col)], axis=1)

    def cubes_of(chunk):
        return jnp.concatenate(cube_halves(left_ref[aligned(chunk * CHUNK, CHUNK), :], block_row(right_ref, chunk)), axis=0)

    def step(source, k, carry):
        if keep:
            for part in range(GROUP):
                arrive(*source, k * GROUP + part)
        for part in range(0, GROUP, 2):
            chunk = k * GROUP + part
            tables = jnp.concatenate([block_row(table_ref, chunk), block_row(table_ref, chunk + 1)], axis=0)
            if keep:
                cubes = cubes_ref[pl.ds(chunk, 2)].reshape(4 * CHUNK, n_col * seg_dev)
            else:
                cubes = jnp.concatenate([cubes_of(chunk), cubes_of(chunk + 1)], axis=0)
            both = dot_nt(tables, cubes)
            for half in range(2):
                mine = both[32 * half:32 * half + 32, 2 * CHUNK * half:2 * CHUNK * (half + 1)]
                total = mine[:, 0:CHUNK] + mine[:, CHUNK:2 * CHUNK]
                sums_ref[pl.ds(chunk + half, 16, stride=chunk_count), :] = total[0:16] + total[16:32]
        return carry

    if keep:
        lax.fori_loop(0, EARLY // GROUP, functools.partial(step, (early_hbm, 0)), 0)
        lax.fori_loop(EARLY // GROUP, chunk_steps(group_ref), functools.partial(step, (late_hbm, EARLY)), 0)
    else:
        lax.fori_loop(0, chunk_steps(group_ref), functools.partial(step, None), 0)
    sums = jnp.concatenate([sums_ref[0:6 * chunk_count], sums_ref[8 * chunk_count:14 * chunk_count]], axis=0)
    sums = jnp.concatenate(split3(sums), axis=1).astype(jnp.bfloat16)
    for tile in range(slot_ref.shape[1] // TILE):
        at = pl.ds(tile * TILE, TILE)
        slot = slot_ref[:, at]
        low = jnp.where(iota((CHUNK, TILE), 0) == slot % CHUNK, 1.0, 0.0).astype(jnp.bfloat16)
        high = jnp.where(iota((chunk_count, TILE), 0) == slot // CHUNK, 1.0, 0.0)
        found = dot(sums, jnp.concatenate([low, low, low], axis=0))
        for row in range(12):
            picked = found[row * chunk_count:(row + 1) * chunk_count] * high
            out_ref[row:row + 1, at] = jnp.sum(picked, axis=0, keepdims=True)


def final_kernel(stats_ref, known_ref, basis_own_ref, field_ref, bundle_ref, currents_ref, iron_ref):
    stats = jnp.sum(stats_ref[...], axis=0)
    known = known_ref[...]
    initial_norm, hessen_a, hessen_b = known[:, 0:1], known[:, 1:2], known[:, 2:3]
    hessen_c, hessen_d, normal_second = stats[:, 0:1], stats[:, 1:2], stats[:, 2:3]
    normal_first = hessen_a * hessen_a + hessen_b * hessen_b
    normal_cross = hessen_a * hessen_c + hessen_b * hessen_d
    target_first = initial_norm * hessen_a
    target_second = initial_norm * hessen_c
    determinant = normal_first * normal_second - normal_cross * normal_cross
    weight_first = (normal_second * target_first - normal_cross * target_second) / determinant
    weight_second = (normal_first * target_second - normal_cross * target_first) / determinant
    currents_ref[...] = weight_first * basis_own_ref[0:1, :] + weight_second * basis_own_ref[1:2, :]
    moments = weight_first * field_ref[0:6, :] + weight_second * field_ref[6:12, :]
    points = bundle_ref[6:9, 0:iron_ref.shape[1]] - 0.5
    px, py, pz = points[0:1], points[1:2], points[2:3]
    iron_ref[0:1, :] = pz * moments[1:2] - py * moments[2:3] - moments[3:4]
    iron_ref[1:2, :] = px * moments[2:3] - pz * moments[0:1] - moments[4:5]
    iron_ref[2:3, :] = py * moments[0:1] - px * moments[1:2] - moments[5:6]


def shape(*sizes, dtype=jnp.float32):
    return jax.ShapeDtypeStruct(sizes, dtype)


def shards(drive, resist, centers, tangents, iron_points, owner, range_len):
    seg_dev = drive.shape[0]
    col_len = centers.shape[1]
    n_col = lax.axis_size("col")
    n_row = lax.axis_size("row")
    n_dev = n_col * n_row
    segments = seg_dev * n_dev
    width = n_col * seg_dev
    points_count = iron_points.shape[1]
    coupling = 0.5 / math.sqrt(segments)
    call = functools.partial(pl.pallas_call, compiler_params=pltpu.CompilerParams(vmem_limit_bytes=VMEM_LIMIT))
    scratch = [pltpu.VMEM((1, segments), jnp.float32), pltpu.VMEM((seg_dev, 128), jnp.float32)]
    hbm = pl.BlockSpec(memory_space=pltpu.HBM)
    smem = pl.BlockSpec(memory_space=pltpu.SMEM)
    vmem = pl.BlockSpec(memory_space=pltpu.VMEM)

    def work(microseconds):
        return pl.CostEstimate(flops=int(microseconds * 1e9), bytes_accessed=0, transcendentals=0)

    def roomy(row_bytes):
        return STREAM_BYTES // row_bytes

    def exchange(x):
        return lax.all_to_all(x, AXES, 0, 0, tiled=True)

    spread, geometry = pl.pallas_call(
        entry_kernel,
        out_shape=(shape(n_dev, 1, seg_dev), shape(6, col_len)),
        in_specs=[hbm] * 3,
        scratch_shapes=[
            pltpu.VMEM((1, seg_dev), jnp.float32),
            pltpu.VMEM((3, col_len), jnp.float32),
            pltpu.VMEM((3, col_len), jnp.float32),
            pltpu.SemaphoreType.DMA((3,)),
        ],
        compiler_params=pltpu.CompilerParams(vmem_limit_bytes=ENTRY_LIMIT),
        cost_estimate=work(8),
        name="entry",
    )(drive[None, :], centers, tangents)
    drive_all = exchange(spread).reshape(1, segments)
    longest = max(col_len, points_count, 2 * seg_dev)

    def wide(row):
        return jnp.pad(row, ((0, 0), (0, longest - row.shape[1])))

    bundle = jnp.concatenate([
        wide(centers), wide(tangents), wide(iron_points), wide(owner.reshape(1, points_count).astype(jnp.float32)),
        wide(jnp.concatenate([drive, resist])[None, :]),
    ], axis=0)
    pieces = [bundle] + [
        lax.ppermute(geometry, "col", [(k, (k + shift) % n_col) for k in range(n_col)]) for shift in range(1, n_col)
    ]

    chunk_count = points_count // CHUNK + n_row * (CHUNK - 1) // CHUNK
    chunk_count = -(-chunk_count // 8) * 8
    slot, group_table, left = call(
        functools.partial(group_kernel, n_row=n_row),
        out_shape=(
            shape(1, points_count, dtype=jnp.int32),
            shape(8, 128, dtype=jnp.int32),
            shape(chunk_count * CHUNK, 48, dtype=jnp.bfloat16),
        ),
        scratch_shapes=[pltpu.VMEM((48 * chunk_count, CHUNK), jnp.float32)],
        cost_estimate=work(3),
        name="group_points",
    )(bundle)

    cube_shape = (chunk_count, 2 * CHUNK, width)
    keep = 2 * math.prod(cube_shape) <= KEEP_BYTES
    stream = functools.partial(
        pl.pallas_call, compiler_params=pltpu.CompilerParams(vmem_limit_bytes=STREAM_LIMIT if keep else VMEM_LIMIT)
    )
    sides = call(
        functools.partial(sides_kernel, n_col=n_col),
        out_shape=(
            shape(48, segments, dtype=jnp.bfloat16), shape(8, segments),
            shape(2, seg_dev, 48, dtype=jnp.bfloat16), shape(3, seg_dev, 128),
        ),
        cost_estimate=work(1),
        name="sides",
    )(*pieces)
    right, moment = sides[0:2]
    def weigh(first, last, microseconds, name):
        count = (last or chunk_count) - first
        return stream(
            functools.partial(weigh_kernel, n_row=n_row, n_col=n_col, first=first, last=last),
            out_shape=(shape(roomy(4 * CHUNK * width), *cube_shape[1:], dtype=jnp.bfloat16), shape(8, 128)),
            in_specs=[smem, vmem, vmem],
            out_specs=(hbm, vmem),
            scratch_shapes=[pltpu.VMEM((count,) + cube_shape[1:], jnp.bfloat16), pltpu.SemaphoreType.DMA((count,))],
            cost_estimate=work(microseconds),
            name=name,
        )(group_table, left, right)

    if keep:
        early, before = weigh(0, EARLY, 2, "weigh_early")
    else:
        before = group_table
    image_own, image_spread = call(
        functools.partial(first_kernel, coupling),
        out_shape=(shape(1, seg_dev), shape(n_dev, 1, seg_dev)),
        scratch_shapes=scratch,
        cost_estimate=work(3),
        name="first_image",
    )(drive_all, bundle, before, *sides)
    image_all = exchange(image_spread).reshape(1, segments)
    cube_scratch = [pltpu.VMEM(cube_shape, jnp.bfloat16), pltpu.SemaphoreType.DMA((3 * chunk_count,))]
    if keep:
        late, after = weigh(EARLY, None, 4, "weigh_late")
    else:
        after = group_table
    basis, basis_own, stats, known = call(
        functools.partial(second_kernel, coupling),
        out_shape=(shape(2, segments), shape(2, seg_dev), shape(n_dev, 1, 128), shape(1, 128)),
        scratch_shapes=scratch,
        cost_estimate=work(3),
        name="second_image",
    )(drive_all, image_all, image_own, bundle, after, *sides)
    stats_all = exchange(stats)

    field = stream(
        functools.partial(field_kernel, n_row=n_row, n_col=n_col, keep=keep),
        out_shape=shape(12, points_count),
        in_specs=[smem, smem, vmem, vmem, vmem] + ([hbm, hbm] if keep else [vmem, vmem]),
        scratch_shapes=[
            pltpu.VMEM((32, segments), jnp.bfloat16),
            pltpu.VMEM((16 * chunk_count, CHUNK), jnp.float32),
        ] + (cube_scratch if keep else []),
        cost_estimate=work(6),
        name="block_field",
    )(group_table, range_len, slot, moment, basis, *([early, late] if keep else [left, right]))
    currents, iron_field = stream(
        final_kernel,
        out_shape=(shape(1, seg_dev), shape(3, points_count)),
        name="combine",
    )(stats_all, known, basis_own, field, bundle)
    return (currents[0], iron_field)


def solution(mesh):
    return jax.shard_map(
        shards,
        mesh=mesh,
        in_specs=(
            P(AXES),
            P(AXES),
            P(None, "col"),
            P(None, "col"),
            P(None, AXES),
            P(AXES, None),
            P(),
        ),
        out_specs=(P(AXES), P(None, AXES)),
        check_vma=False,
    )
```

```python
import functools
import math

import jax
import jax.numpy as jnp
from jax import lax
from jax.experimental import pallas as pl
from jax.experimental.pallas import tpu as pltpu
from jax.sharding import PartitionSpec as P

EPS_SEG = 0.0004
EPS_FIELD = 0.0025
AXES = ("col", "row")
CHUNK = 128
GROUP = 4
EARLY = 4
TILE = 512
COLUMNS = 256
ROWS = 64
KEEP_BYTES = 16 * 1024 * 1024
VMEM_LIMIT = 32 * 1024 * 1024
STREAM_LIMIT = 44 * 1024 * 1024
STREAM_BYTES = 20 * 1024 * 1024
ENTRY_LIMIT = 60 * 1024 * 1024


def split3(x):
    high = x.astype(jnp.bfloat16).astype(jnp.float32)
    rest = x - high
    middle = rest.astype(jnp.bfloat16).astype(jnp.float32)
    low = (rest - middle).astype(jnp.bfloat16).astype(jnp.float32)
    return high, middle, low


def left_parts(x):
    high, middle, low = split3(x)
    return jnp.concatenate([high, high, middle, middle, high, low], axis=0)


def right_parts(x):
    high, middle, low = split3(x)
    return jnp.concatenate([high, middle, high, middle, low, high], axis=0).astype(jnp.bfloat16)


def rows8(*rows):
    width = rows[0].shape[1]
    count = sum(r.shape[0] for r in rows)
    if count < 8:
        rows = rows + (jnp.zeros((8 - count, width), jnp.float32),)
    return jnp.concatenate(rows, axis=0)


def left_center(c, eps):
    square = jnp.sum(c * c, axis=0, keepdims=True)
    return rows8(-2.0 * c, jnp.ones_like(square), square + eps)


def right_center(c):
    square = jnp.sum(c * c, axis=0, keepdims=True)
    return rows8(c, square, jnp.ones_like(square))


def dot(a, b):
    return jnp.dot(a, b, preferred_element_type=jnp.float32)


def dot_nt(a, b):
    return lax.dot_general(a, b, (((1,), (1,)), ((), ())), preferred_element_type=jnp.float32)


def transposed(x):
    return x.T.astype(jnp.bfloat16)


def iota(shape, axis):
    return lax.broadcasted_iota(jnp.int32, shape, axis)


def aligned(start, size):
    return pl.ds(pl.multiple_of(start, size), size)


def sides_kernel(*refs, n_col):
    pieces, (right_ref, moment_ref, left_ref, along_ref) = refs[:n_col], refs[n_col:]
    length = right_ref.shape[1] // n_col
    seg_dev = left_ref.shape[1]
    own_at = aligned(lax.axis_index("row") * seg_dev, seg_dev)
    tangent = rows8(pieces[0][3:6, own_at])
    left_ref[0] = transposed(left_parts(left_center(pieces[0][0:3, own_at] - 0.5, EPS_SEG)))
    left_ref[1] = transposed(left_parts(tangent))
    tangent = tangent.T
    for k in range(3):
        along_ref[k] = jnp.broadcast_to(tangent[:, k:k + 1], (seg_dev, 128))
    for shift, piece in enumerate(pieces):
        col = lax.rem(lax.axis_index("col") + n_col - shift, n_col)

        def step(k, carry):
            geo = piece[0:6, aligned(k * TILE, TILE)]
            to = pl.ds(pl.multiple_of(col * length + k * TILE, TILE), TILE)
            center, tangent = geo[0:3] - 0.5, geo[3:6]
            cross = jnp.concatenate([
                tangent[1:2] * center[2:3] - tangent[2:3] * center[1:2],
                tangent[2:3] * center[0:1] - tangent[0:1] * center[2:3],
                tangent[0:1] * center[1:2] - tangent[1:2] * center[0:1],
            ], axis=0)
            right_ref[:, to] = right_parts(right_center(center))
            moment_ref[:, to] = rows8(tangent, cross)
            return carry

        lax.fori_loop(0, length // TILE, step, 0, unroll=4)


def couple(right_ref, moment_ref, left_ref, along_ref, vec_ref, acc_ref):
    acc_ref[...] = jnp.zeros_like(acc_ref)

    def step(k, carry):
        at = aligned(k * TILE, TILE)
        turned = moment_ref[0:3, at] * vec_ref[:, at]
        right = right_ref[:, at]
        for first in range(0, TILE, COLUMNS):
            columns = slice(first, first + COLUMNS)
            by_product = first % (2 * COLUMNS) == 0
            if by_product:
                turned_parts = right_parts(rows8(turned[:, columns]))
            for row in range(0, acc_ref.shape[0], ROWS):
                rows = slice(row, row + ROWS)
                inverse = lax.rsqrt(dot(left_ref[0, rows], right[:, columns]))
                total = acc_ref[rows]
                if by_product:
                    pair = dot(left_ref[1, rows], turned_parts) * inverse
                    for start in range(0, COLUMNS, 128):
                        total = total + pair[:, start:start + 128]
                else:
                    for start in range(0, COLUMNS, 128):
                        lanes = slice(first + start, first + start + 128)
                        along = along_ref[0, rows] * turned[0:1, lanes]
                        along = along + along_ref[1, rows] * turned[1:2, lanes]
                        along = along + along_ref[2, rows] * turned[2:3, lanes]
                        total = total + along * inverse[:, start:start + 128]
                acc_ref[rows] = total
        return carry

    lax.fori_loop(0, vec_ref.shape[1] // TILE, step, 0, unroll=4)
    return jnp.sum(acc_ref[...].T, axis=0, keepdims=True)


def part_bounds(n_col, seg_dev):
    width = n_col * seg_dev
    return ((0, width // 2), (width // 2, 3 * width // 4), (3 * width // 4, width))


def part_copy(kept, chunk, part, bounds, remote, first):
    local, sems = kept
    start, stop = bounds[part]
    return pltpu.make_async_copy(
        remote.at[chunk - first, :, start:stop], local.at[chunk, :, start:stop], sems.at[chunk * len(bounds) + part]
    )


def for_parts(group_ref, length_ref, chunk, bounds, action, otherwise=None):
    used = chunk < group_ref[1, 0]
    length = length_ref[group_ref[0, chunk]]
    for part, (start, _) in enumerate(bounds):
        active = jnp.logical_and(used, start < length)
        pl.when(active)(functools.partial(action, part))
        if otherwise is not None:
            pl.when(jnp.logical_not(active))(functools.partial(otherwise, part))


def spread_rows(ref, row):
    for k in range(ref.shape[0]):
        ref[k] = row


def entry_kernel(drive_hbm, centers_hbm, tangents_hbm, spread_ref, geo_ref, drive, centers, tangents, sems):
    pairs = ((drive_hbm, drive), (centers_hbm, centers), (tangents_hbm, tangents))
    copies = [pltpu.make_async_copy(source, target, sems.at[k]) for k, (source, target) in enumerate(pairs)]
    for copy in copies:
        copy.start()
    for copy in copies:
        copy.wait()
    spread_rows(spread_ref, drive[...])
    geo_ref[0:3] = centers[...]
    geo_ref[3:6] = tangents[...]


def own_rows(bundle_ref, like_ref):
    seg_dev = like_ref.shape[1]
    return bundle_ref[10:11, 0:seg_dev], bundle_ref[10:11, seg_dev:2 * seg_dev]


def first_kernel(coupling, drive_ref, bundle_ref, after_ref, right_ref, moment_ref, left_ref, along_ref,
                 image_ref, spread_ref, vec_ref, acc_ref):
    drive = drive_ref[...]
    scale = 1.0 / jnp.sqrt(jnp.sum(drive * drive, keepdims=True))
    vec_ref[...] = drive * scale
    product = couple(right_ref, moment_ref, left_ref, along_ref, vec_ref, acc_ref)
    drive_own, resist_own = own_rows(bundle_ref, image_ref)
    image = resist_own * (drive_own * scale) + coupling * product
    image_ref[...] = image
    spread_rows(spread_ref, image)


def second_kernel(coupling, drive_ref, image_ref, image_own_ref, bundle_ref, after_ref,
                  right_ref, moment_ref, left_ref, along_ref,
                  basis_ref, basis_own_ref, stats_ref, known_ref, vec_ref, acc_ref):
    drive = drive_ref[...]
    norm = jnp.sqrt(jnp.sum(drive * drive, keepdims=True))
    scale = 1.0 / norm
    basis_a = drive * scale
    image = image_ref[...]
    hessen_a = jnp.sum(image * basis_a, keepdims=True)
    rest = image - hessen_a * basis_a
    hessen_b = jnp.sqrt(jnp.sum(rest * rest, keepdims=True))
    inverse = 1.0 / hessen_b
    basis_b = rest * inverse
    vec_ref[...] = basis_b
    basis_ref[0:1, :] = basis_a
    basis_ref[1:2, :] = basis_b
    drive_own, resist_own = own_rows(bundle_ref, image_own_ref)
    own_a = drive_own * scale
    own_b = (image_own_ref[...] - hessen_a * own_a) * inverse
    basis_own_ref[0:1, :] = own_a
    basis_own_ref[1:2, :] = own_b
    product = couple(right_ref, moment_ref, left_ref, along_ref, vec_ref, acc_ref)
    second = resist_own * own_b + coupling * product
    lane = iota((1, 128), 1)

    def three(a, b, c):
        return jnp.where(lane == 0, a, jnp.where(lane == 1, b, jnp.where(lane == 2, c, 0.0)))

    spread_rows(stats_ref, three(
        jnp.sum(second * own_a, keepdims=True),
        jnp.sum(second * own_b, keepdims=True),
        jnp.sum(second * second, keepdims=True),
    ))
    known_ref[...] = three(norm, hessen_a, hessen_b)


def group_kernel(bundle_ref, slot_ref, table_ref, left_ref, planes_ref, *, n_row):
    points = slot_ref.shape[1]
    chunk_count = left_ref.shape[0] // CHUNK
    owner = bundle_ref[9:10, 0:points].astype(jnp.int32)
    rows = max(8, n_row)
    marks = jnp.where(iota((rows, points), 0) == owner, 1.0, 0.0)
    tile = 256
    upper = jnp.where(iota((tile, tile), 0) <= iota((tile, tile), 1), 1.0, 0.0).astype(jnp.bfloat16)
    before = jnp.zeros((rows, 1), jnp.float32)
    ranks = []
    for piece in range(points // tile):
        part = dot(marks[:, piece * tile:(piece + 1) * tile].astype(jnp.bfloat16), upper)
        ranks.append(part + before - 1.0)
        before = before + part[:, tile - 1:tile]
    ranks = jnp.concatenate(ranks, axis=1)
    chunks = jnp.floor((before + (CHUNK - 1)) * (1.0 / CHUNK))
    start = jnp.zeros((1, 1), jnp.float32)
    starts = []
    for name in range(rows):
        starts.append(start)
        start = start + chunks[name:name + 1]
    starts = jnp.concatenate(starts, axis=0)
    slot = jnp.sum(marks * (ranks + starts * CHUNK), axis=0, keepdims=True).astype(jnp.int32)
    slot_ref[...] = slot
    lane = iota((rows, 128), 1)
    ended = jnp.sum(jnp.where(starts + chunks <= lane.astype(jnp.float32), 1.0, 0.0), axis=0, keepdims=True)
    block = jnp.minimum(ended, n_row - 1.0)
    place = iota((8, 128), 0)
    table_ref[...] = jnp.where(place == 0, block, start).astype(jnp.int32)
    high = jnp.where(iota((chunk_count, points), 0) == slot // CHUNK, 1.0, 0.0)
    low = jnp.where(iota((CHUNK, points), 0) == slot % CHUNK, 1.0, 0.0).astype(jnp.bfloat16)
    parts = split3(bundle_ref[6:9, 0:points] - 0.5)
    spread = jnp.concatenate([high * part[k:k + 1] for k in range(3) for part in parts], axis=0).astype(jnp.bfloat16)
    placed = dot_nt(spread, low)
    planes = [placed[k * chunk_count:(k + 1) * chunk_count] for k in range(9)]
    x, y, z = (planes[3 * k] + planes[3 * k + 1] + planes[3 * k + 2] for k in range(3))
    sides = [-2.0 * x, -2.0 * y, -2.0 * z, jnp.ones_like(x), x * x + y * y + z * z + EPS_FIELD]
    sides = [split3(side) for side in sides]
    empty = jnp.zeros_like(x)
    for group, part in enumerate([0, 0, 1, 1, 0, 2]):
        for k in range(8):
            to = pl.ds((group * 8 + k) * chunk_count, chunk_count)
            planes_ref[to, :] = sides[k][part] if k < 5 else empty
    for chunk in range(chunk_count):
        left_ref[chunk * CHUNK:(chunk + 1) * CHUNK, :] = transposed(planes_ref[pl.ds(chunk, 48, stride=chunk_count), :])


def cube_halves(left, right):
    inverse = lax.rsqrt(dot(left, right))
    cube = inverse * inverse * inverse
    high = cube.astype(jnp.bfloat16)
    return high, (cube - high.astype(jnp.float32)).astype(jnp.bfloat16)


def block_part(block, col, n_row, seg_dev):
    return aligned((col * n_row + block) * seg_dev, seg_dev)


def chunk_steps(group_ref):
    return (group_ref[1, 0] + GROUP - 1) // GROUP


def weigh_kernel(group_ref, left_ref, right_ref, cubes_hbm, done_ref, cubes_ref, sems, *, n_row, n_col, first, last):
    seg_dev = right_ref.shape[1] // (n_row * n_col)
    done_ref[...] = jnp.zeros_like(done_ref)
    stop = chunk_steps(group_ref) if last is None else last // GROUP

    def chunk_copy(place):
        return pltpu.make_async_copy(cubes_ref.at[place], cubes_hbm.at[place], sems.at[place])

    def step(k, carry):
        for part in range(GROUP):
            chunk = k * GROUP + part
            place = chunk - first
            left = left_ref[aligned(chunk * CHUNK, CHUNK), :]
            for col in range(n_col):
                to = slice(col * seg_dev, (col + 1) * seg_dev)
                high, low = cube_halves(left, right_ref[:, block_part(group_ref[0, chunk], col, n_row, seg_dev)])
                cubes_ref[place, 0:CHUNK, to] = high
                cubes_ref[place, CHUNK:2 * CHUNK, to] = low
            chunk_copy(place).start()
        return carry

    def finish(k, carry):
        for part in range(GROUP):
            chunk_copy(k * GROUP + part - first).wait()
        return carry

    lax.fori_loop(first // GROUP, stop, step, 0)
    lax.fori_loop(first // GROUP, stop, finish, 0)


def field_kernel(group_ref, length_ref, slot_ref, moment_ref, basis_ref, *refs, n_row, n_col, keep):
    if keep:
        early_hbm, late_hbm, out_ref, table_ref, sums_ref, cubes_ref, sems = refs
        kept = (cubes_ref, sems)

        bounds = part_bounds(n_col, moment_ref.shape[1] // (n_row * n_col))

        def clear(chunk, piece):
            start, stop = bounds[piece]
            cubes_ref[chunk, :, start:stop] = jnp.zeros((2 * CHUNK, stop - start), jnp.bfloat16)

        def begin(remote, first, chunk, carry):
            for_parts(group_ref, length_ref, chunk, bounds,
                      lambda piece: part_copy(kept, chunk, piece, bounds, remote, first).start(),
                      lambda piece: clear(chunk, piece))
            return carry

        def arrive(remote, first, chunk):
            for_parts(group_ref, length_ref, chunk, bounds,
                      lambda piece: part_copy(kept, chunk, piece, bounds, remote, first).wait())

        lax.fori_loop(0, EARLY, functools.partial(begin, early_hbm, 0), 0)
        lax.fori_loop(EARLY, chunk_steps(group_ref) * GROUP, functools.partial(begin, late_hbm, EARLY), 0)
    else:
        left_ref, right_ref, out_ref, table_ref, sums_ref = refs
    chunk_count = sums_ref.shape[0] // 16
    seg_dev = moment_ref.shape[1] // (n_row * n_col)
    scale = 1.0 / math.sqrt(n_col * seg_dev)
    lane = iota((1, seg_dev), 1)
    sums_ref[...] = jnp.zeros_like(sums_ref)

    def table_step(block, carry):
        length = length_ref[block]
        for col in range(n_col):
            at = block_part(block, col, n_row, seg_dev)
            both = moment_ref[:, at]
            active = jnp.where(lane + col * seg_dev < length, scale, 0.0)
            first = both * (basis_ref[0:1, at] * active)
            second = both * (basis_ref[1:2, at] * active)
            parts = jnp.concatenate([first, second], axis=0)
            high = parts.astype(jnp.bfloat16).astype(jnp.float32)
            table_ref[:, at] = jnp.concatenate([high, parts - high], axis=0).astype(jnp.bfloat16)
        return carry

    lax.fori_loop(0, n_row, table_step, 0, unroll=min(n_row, 8))

    def block_row(ref, chunk):
        block = group_ref[0, chunk]
        return jnp.concatenate([ref[:, block_part(block, col, n_row, seg_dev)] for col in range(n_col)], axis=1)

    def cubes_of(chunk):
        return jnp.concatenate(cube_halves(left_ref[aligned(chunk * CHUNK, CHUNK), :], block_row(right_ref, chunk)), axis=0)

    def step(source, k, carry):
        if keep:
            for part in range(GROUP):
                arrive(*source, k * GROUP + part)
        for part in range(0, GROUP, 2):
            chunk = k * GROUP + part
            tables = jnp.concatenate([block_row(table_ref, chunk), block_row(table_ref, chunk + 1)], axis=0)
            if keep:
                cubes = cubes_ref[pl.ds(chunk, 2)].reshape(4 * CHUNK, n_col * seg_dev)
            else:
                cubes = jnp.concatenate([cubes_of(chunk), cubes_of(chunk + 1)], axis=0)
            both = dot_nt(tables, cubes)
            for half in range(2):
                mine = both[32 * half:32 * half + 32, 2 * CHUNK * half:2 * CHUNK * (half + 1)]
                total = mine[:, 0:CHUNK] + mine[:, CHUNK:2 * CHUNK]
                sums_ref[pl.ds(chunk + half, 16, stride=chunk_count), :] = total[0:16] + total[16:32]
        return carry

    if keep:
        lax.fori_loop(0, EARLY // GROUP, functools.partial(step, (early_hbm, 0)), 0)
        lax.fori_loop(EARLY // GROUP, chunk_steps(group_ref), functools.partial(step, (late_hbm, EARLY)), 0)
    else:
        lax.fori_loop(0, chunk_steps(group_ref), functools.partial(step, None), 0)
    sums = jnp.concatenate([sums_ref[0:6 * chunk_count], sums_ref[8 * chunk_count:14 * chunk_count]], axis=0)
    sums = jnp.concatenate(split3(sums), axis=1).astype(jnp.bfloat16)
    for tile in range(slot_ref.shape[1] // TILE):
        at = pl.ds(tile * TILE, TILE)
        slot = slot_ref[:, at]
        low = jnp.where(iota((CHUNK, TILE), 0) == slot % CHUNK, 1.0, 0.0).astype(jnp.bfloat16)
        high = jnp.where(iota((chunk_count, TILE), 0) == slot // CHUNK, 1.0, 0.0)
        found = dot(sums, jnp.concatenate([low, low, low], axis=0))
        for row in range(12):
            picked = found[row * chunk_count:(row + 1) * chunk_count] * high
            out_ref[row:row + 1, at] = jnp.sum(picked, axis=0, keepdims=True)


def final_kernel(stats_ref, known_ref, basis_own_ref, field_ref, bundle_ref, currents_ref, iron_ref):
    stats = jnp.sum(stats_ref[...], axis=0)
    known = known_ref[...]
    initial_norm, hessen_a, hessen_b = known[:, 0:1], known[:, 1:2], known[:, 2:3]
    hessen_c, hessen_d, normal_second = stats[:, 0:1], stats[:, 1:2], stats[:, 2:3]
    normal_first = hessen_a * hessen_a + hessen_b * hessen_b
    normal_cross = hessen_a * hessen_c + hessen_b * hessen_d
    target_first = initial_norm * hessen_a
    target_second = initial_norm * hessen_c
    determinant = normal_first * normal_second - normal_cross * normal_cross
    weight_first = (normal_second * target_first - normal_cross * target_second) / determinant
    weight_second = (normal_first * target_second - normal_cross * target_first) / determinant
    currents_ref[...] = weight_first * basis_own_ref[0:1, :] + weight_second * basis_own_ref[1:2, :]
    moments = weight_first * field_ref[0:6, :] + weight_second * field_ref[6:12, :]
    points = bundle_ref[6:9, 0:iron_ref.shape[1]] - 0.5
    px, py, pz = points[0:1], points[1:2], points[2:3]
    iron_ref[0:1, :] = pz * moments[1:2] - py * moments[2:3] - moments[3:4]
    iron_ref[1:2, :] = px * moments[2:3] - pz * moments[0:1] - moments[4:5]
    iron_ref[2:3, :] = py * moments[0:1] - px * moments[1:2] - moments[5:6]


def shape(*sizes, dtype=jnp.float32):
    return jax.ShapeDtypeStruct(sizes, dtype)


def shards(drive, resist, centers, tangents, iron_points, owner, range_len):
    seg_dev = drive.shape[0]
    col_len = centers.shape[1]
    n_col = lax.axis_size("col")
    n_row = lax.axis_size("row")
    n_dev = n_col * n_row
    segments = seg_dev * n_dev
    width = n_col * seg_dev
    points_count = iron_points.shape[1]
    coupling = 0.5 / math.sqrt(segments)
    call = functools.partial(pl.pallas_call, compiler_params=pltpu.CompilerParams(vmem_limit_bytes=VMEM_LIMIT))
    scratch = [pltpu.VMEM((1, segments), jnp.float32), pltpu.VMEM((seg_dev, 128), jnp.float32)]
    hbm = pl.BlockSpec(memory_space=pltpu.HBM)
    smem = pl.BlockSpec(memory_space=pltpu.SMEM)
    vmem = pl.BlockSpec(memory_space=pltpu.VMEM)

    def work(microseconds):
        return pl.CostEstimate(flops=int(microseconds * 1e9), bytes_accessed=0, transcendentals=0)

    def roomy(row_bytes):
        return STREAM_BYTES // row_bytes

    def exchange(x):
        return lax.all_to_all(x, AXES, 0, 0, tiled=True)

    spread, geometry = pl.pallas_call(
        entry_kernel,
        out_shape=(shape(n_dev, 1, seg_dev), shape(6, col_len)),
        in_specs=[hbm] * 3,
        scratch_shapes=[
            pltpu.VMEM((1, seg_dev), jnp.float32),
            pltpu.VMEM((3, col_len), jnp.float32),
            pltpu.VMEM((3, col_len), jnp.float32),
            pltpu.SemaphoreType.DMA((3,)),
        ],
        compiler_params=pltpu.CompilerParams(vmem_limit_bytes=ENTRY_LIMIT),
        cost_estimate=work(8),
        name="entry",
    )(drive[None, :], centers, tangents)
    drive_all = exchange(spread).reshape(1, segments)
    longest = max(col_len, points_count, 2 * seg_dev)

    def wide(row):
        return jnp.pad(row, ((0, 0), (0, longest - row.shape[1])))

    bundle = jnp.concatenate([
        wide(centers), wide(tangents), wide(iron_points), wide(owner.reshape(1, points_count).astype(jnp.float32)),
        wide(jnp.concatenate([drive, resist])[None, :]),
    ], axis=0)
    pieces = [bundle] + [
        lax.ppermute(geometry, "col", [(k, (k + shift) % n_col) for k in range(n_col)]) for shift in range(1, n_col)
    ]

    chunk_count = points_count // CHUNK + n_row * (CHUNK - 1) // CHUNK
    chunk_count = -(-chunk_count // 8) * 8
    slot, group_table, left = call(
        functools.partial(group_kernel, n_row=n_row),
        out_shape=(
            shape(1, points_count, dtype=jnp.int32),
            shape(8, 128, dtype=jnp.int32),
            shape(chunk_count * CHUNK, 48, dtype=jnp.bfloat16),
        ),
        scratch_shapes=[pltpu.VMEM((48 * chunk_count, CHUNK), jnp.float32)],
        cost_estimate=work(3),
        name="group_points",
    )(bundle)

    cube_shape = (chunk_count, 2 * CHUNK, width)
    keep = 2 * math.prod(cube_shape) <= KEEP_BYTES
    stream = functools.partial(
        pl.pallas_call, compiler_params=pltpu.CompilerParams(vmem_limit_bytes=STREAM_LIMIT if keep else VMEM_LIMIT)
    )
    sides = call(
        functools.partial(sides_kernel, n_col=n_col),
        out_shape=(
            shape(48, segments, dtype=jnp.bfloat16), shape(8, segments),
            shape(2, seg_dev, 48, dtype=jnp.bfloat16), shape(3, seg_dev, 128),
        ),
        cost_estimate=work(1),
        name="sides",
    )(*pieces)
    right, moment = sides[0:2]
    def weigh(first, last, microseconds, name):
        count = (last or chunk_count) - first
        return stream(
            functools.partial(weigh_kernel, n_row=n_row, n_col=n_col, first=first, last=last),
            out_shape=(shape(roomy(4 * CHUNK * width), *cube_shape[1:], dtype=jnp.bfloat16), shape(8, 128)),
            in_specs=[smem, vmem, vmem],
            out_specs=(hbm, vmem),
            scratch_shapes=[pltpu.VMEM((count,) + cube_shape[1:], jnp.bfloat16), pltpu.SemaphoreType.DMA((count,))],
            cost_estimate=work(microseconds),
            name=name,
        )(group_table, left, right)

    if keep:
        early, before = weigh(0, EARLY, 2, "weigh_early")
    else:
        before = group_table
    image_own, image_spread = call(
        functools.partial(first_kernel, coupling),
        out_shape=(shape(1, seg_dev), shape(n_dev, 1, seg_dev)),
        scratch_shapes=scratch,
        cost_estimate=work(3),
        name="first_image",
    )(drive_all, bundle, before, *sides)
    image_all = exchange(image_spread).reshape(1, segments)
    cube_scratch = [pltpu.VMEM(cube_shape, jnp.bfloat16), pltpu.SemaphoreType.DMA((3 * chunk_count,))]
    if keep:
        late, after = weigh(EARLY, None, 4, "weigh_late")
    else:
        after = group_table
    basis, basis_own, stats, known = call(
        functools.partial(second_kernel, coupling),
        out_shape=(shape(2, segments), shape(2, seg_dev), shape(n_dev, 1, 128), shape(1, 128)),
        scratch_shapes=scratch,
        cost_estimate=work(3),
        name="second_image",
    )(drive_all, image_all, image_own, bundle, after, *sides)
    stats_all = exchange(stats)

    field = stream(
        functools.partial(field_kernel, n_row=n_row, n_col=n_col, keep=keep),
        out_shape=shape(12, points_count),
        in_specs=[smem, smem, vmem, vmem, vmem] + ([hbm, hbm] if keep else [vmem, vmem]),
        scratch_shapes=[
            pltpu.VMEM((32, segments), jnp.bfloat16),
            pltpu.VMEM((16 * chunk_count, CHUNK), jnp.float32),
        ] + (cube_scratch if keep else []),
        cost_estimate=work(6),
        name="block_field",
    )(group_table, range_len, slot, moment, basis, *([early, late] if keep else [left, right]))
    currents, iron_field = stream(
        final_kernel,
        out_shape=(shape(1, seg_dev), shape(3, points_count)),
        name="combine",
    )(stats_all, known, basis_own, field, bundle)
    return (currents[0], iron_field)


def solution(mesh):
    return jax.shard_map(
        shards,
        mesh=mesh,
        in_specs=(
            P(AXES),
            P(AXES),
            P(None, "col"),
            P(None, "col"),
            P(None, AXES),
            P(AXES, None),
            P(),
        ),
        out_specs=(P(AXES), P(None, AXES)),
        check_vma=False,
    )
```

```python
import functools
import math

import jax
import jax.numpy as jnp
from jax import lax
from jax.experimental import pallas as pl
from jax.experimental.pallas import tpu as pltpu
from jax.sharding import PartitionSpec as P

EPS_SEG = 0.0004
EPS_FIELD = 0.0025
AXES = ("col", "row")
CHUNK = 128
GROUP = 4
EARLY = 8
TILE = 512
COLUMNS = 256
ROWS = 64
KEEP_BYTES = 16 * 1024 * 1024
VMEM_LIMIT = 32 * 1024 * 1024
STREAM_LIMIT = 44 * 1024 * 1024
STREAM_BYTES = 20 * 1024 * 1024
ENTRY_LIMIT = 60 * 1024 * 1024


def split3(x):
    high = x.astype(jnp.bfloat16).astype(jnp.float32)
    rest = x - high
    middle = rest.astype(jnp.bfloat16).astype(jnp.float32)
    low = (rest - middle).astype(jnp.bfloat16).astype(jnp.float32)
    return high, middle, low


def left_parts(x):
    high, middle, low = split3(x)
    return jnp.concatenate([high, high, middle, middle, high, low], axis=0)


def right_parts(x):
    high, middle, low = split3(x)
    return jnp.concatenate([high, middle, high, middle, low, high], axis=0).astype(jnp.bfloat16)


def rows8(*rows):
    width = rows[0].shape[1]
    count = sum(r.shape[0] for r in rows)
    if count < 8:
        rows = rows + (jnp.zeros((8 - count, width), jnp.float32),)
    return jnp.concatenate(rows, axis=0)


def left_center(c, eps):
    square = jnp.sum(c * c, axis=0, keepdims=True)
    return rows8(-2.0 * c, jnp.ones_like(square), square + eps)


def right_center(c):
    square = jnp.sum(c * c, axis=0, keepdims=True)
    return rows8(c, square, jnp.ones_like(square))


def dot(a, b):
    return jnp.dot(a, b, preferred_element_type=jnp.float32)


def dot_nt(a, b):
    return lax.dot_general(a, b, (((1,), (1,)), ((), ())), preferred_element_type=jnp.float32)


def transposed(x):
    return x.T.astype(jnp.bfloat16)


def iota(shape, axis):
    return lax.broadcasted_iota(jnp.int32, shape, axis)


def aligned(start, size):
    return pl.ds(pl.multiple_of(start, size), size)


def sides_kernel(*refs, n_col):
    pieces, (right_ref, moment_ref, left_ref, along_ref) = refs[:n_col], refs[n_col:]
    length = right_ref.shape[1] // n_col
    seg_dev = left_ref.shape[1]
    own_at = aligned(lax.axis_index("row") * seg_dev, seg_dev)
    tangent = rows8(pieces[0][3:6, own_at])
    left_ref[0] = transposed(left_parts(left_center(pieces[0][0:3, own_at] - 0.5, EPS_SEG)))
    left_ref[1] = transposed(left_parts(tangent))
    tangent = tangent.T
    for k in range(3):
        along_ref[k] = jnp.broadcast_to(tangent[:, k:k + 1], (seg_dev, 128))
    for shift, piece in enumerate(pieces):
        col = lax.rem(lax.axis_index("col") + n_col - shift, n_col)

        def step(k, carry):
            geo = piece[0:6, aligned(k * TILE, TILE)]
            to = pl.ds(pl.multiple_of(col * length + k * TILE, TILE), TILE)
            center, tangent = geo[0:3] - 0.5, geo[3:6]
            cross = jnp.concatenate([
                tangent[1:2] * center[2:3] - tangent[2:3] * center[1:2],
                tangent[2:3] * center[0:1] - tangent[0:1] * center[2:3],
                tangent[0:1] * center[1:2] - tangent[1:2] * center[0:1],
            ], axis=0)
            right_ref[:, to] = right_parts(right_center(center))
            moment_ref[:, to] = rows8(tangent, cross)
            return carry

        lax.fori_loop(0, length // TILE, step, 0, unroll=4)


def couple(right_ref, moment_ref, left_ref, along_ref, vec_ref, acc_ref):
    acc_ref[...] = jnp.zeros_like(acc_ref)

    def step(k, carry):
        at = aligned(k * TILE, TILE)
        turned = moment_ref[0:3, at] * vec_ref[:, at]
        right = right_ref[:, at]
        for first in range(0, TILE, COLUMNS):
            columns = slice(first, first + COLUMNS)
            by_product = first % (2 * COLUMNS) == 0
            if by_product:
                turned_parts = right_parts(rows8(turned[:, columns]))
            for row in range(0, acc_ref.shape[0], ROWS):
                rows = slice(row, row + ROWS)
                inverse = lax.rsqrt(dot(left_ref[0, rows], right[:, columns]))
                total = acc_ref[rows]
                if by_product:
                    pair = dot(left_ref[1, rows], turned_parts) * inverse
                    for start in range(0, COLUMNS, 128):
                        total = total + pair[:, start:start + 128]
                else:
                    for start in range(0, COLUMNS, 128):
                        lanes = slice(first + start, first + start + 128)
                        along = along_ref[0, rows] * turned[0:1, lanes]
                        along = along + along_ref[1, rows] * turned[1:2, lanes]
                        along = along + along_ref[2, rows] * turned[2:3, lanes]
                        total = total + along * inverse[:, start:start + 128]
                acc_ref[rows] = total
        return carry

    lax.fori_loop(0, vec_ref.shape[1] // TILE, step, 0, unroll=8)
    return jnp.sum(acc_ref[...].T, axis=0, keepdims=True)


def part_bounds(n_col, seg_dev):
    width = n_col * seg_dev
    return ((0, width // 2), (width // 2, 3 * width // 4), (3 * width // 4, width))


def part_copy(kept, chunk, part, bounds, remote, first):
    local, sems = kept
    start, stop = bounds[part]
    return pltpu.make_async_copy(
        remote.at[chunk - first, :, start:stop], local.at[chunk, :, start:stop], sems.at[chunk * len(bounds) + part]
    )


def for_parts(group_ref, length_ref, chunk, bounds, action, otherwise=None):
    used = chunk < group_ref[1, 0]
    length = length_ref[group_ref[0, chunk]]
    for part, (start, _) in enumerate(bounds):
        active = jnp.logical_and(used, start < length)
        pl.when(active)(functools.partial(action, part))
        if otherwise is not None:
            pl.when(jnp.logical_not(active))(functools.partial(otherwise, part))


def spread_rows(ref, row):
    for k in range(ref.shape[0]):
        ref[k] = row


def entry_kernel(drive_hbm, centers_hbm, tangents_hbm, spread_ref, geo_ref, drive, centers, tangents, sems):
    pairs = ((drive_hbm, drive), (centers_hbm, centers), (tangents_hbm, tangents))
    copies = [pltpu.make_async_copy(source, target, sems.at[k]) for k, (source, target) in enumerate(pairs)]
    for copy in copies:
        copy.start()
    for copy in copies:
        copy.wait()
    spread_rows(spread_ref, drive[...])
    geo_ref[0:3] = centers[...]
    geo_ref[3:6] = tangents[...]


def own_rows(bundle_ref, like_ref):
    seg_dev = like_ref.shape[1]
    return bundle_ref[10:11, 0:seg_dev], bundle_ref[10:11, seg_dev:2 * seg_dev]


def first_kernel(coupling, drive_ref, bundle_ref, after_ref, right_ref, moment_ref, left_ref, along_ref,
                 image_ref, spread_ref, vec_ref, acc_ref):
    drive = drive_ref[...]
    scale = 1.0 / jnp.sqrt(jnp.sum(drive * drive, keepdims=True))
    vec_ref[...] = drive * scale
    product = couple(right_ref, moment_ref, left_ref, along_ref, vec_ref, acc_ref)
    drive_own, resist_own = own_rows(bundle_ref, image_ref)
    image = resist_own * (drive_own * scale) + coupling * product
    image_ref[...] = image
    spread_rows(spread_ref, image)


def second_kernel(coupling, drive_ref, image_ref, image_own_ref, bundle_ref, after_ref,
                  right_ref, moment_ref, left_ref, along_ref,
                  basis_ref, basis_own_ref, stats_ref, known_ref, vec_ref, acc_ref):
    drive = drive_ref[...]
    norm = jnp.sqrt(jnp.sum(drive * drive, keepdims=True))
    scale = 1.0 / norm
    basis_a = drive * scale
    image = image_ref[...]
    hessen_a = jnp.sum(image * basis_a, keepdims=True)
    rest = image - hessen_a * basis_a
    hessen_b = jnp.sqrt(jnp.sum(rest * rest, keepdims=True))
    inverse = 1.0 / hessen_b
    basis_b = rest * inverse
    vec_ref[...] = basis_b
    basis_ref[0:1, :] = basis_a
    basis_ref[1:2, :] = basis_b
    drive_own, resist_own = own_rows(bundle_ref, image_own_ref)
    own_a = drive_own * scale
    own_b = (image_own_ref[...] - hessen_a * own_a) * inverse
    basis_own_ref[0:1, :] = own_a
    basis_own_ref[1:2, :] = own_b
    product = couple(right_ref, moment_ref, left_ref, along_ref, vec_ref, acc_ref)
    second = resist_own * own_b + coupling * product
    lane = iota((1, 128), 1)

    def three(a, b, c):
        return jnp.where(lane == 0, a, jnp.where(lane == 1, b, jnp.where(lane == 2, c, 0.0)))

    spread_rows(stats_ref, three(
        jnp.sum(second * own_a, keepdims=True),
        jnp.sum(second * own_b, keepdims=True),
        jnp.sum(second * second, keepdims=True),
    ))
    known_ref[...] = three(norm, hessen_a, hessen_b)


def group_kernel(bundle_ref, slot_ref, table_ref, left_ref, planes_ref, *, n_row):
    points = slot_ref.shape[1]
    chunk_count = left_ref.shape[0] // CHUNK
    owner = bundle_ref[9:10, 0:points].astype(jnp.int32)
    rows = max(8, n_row)
    marks = jnp.where(iota((rows, points), 0) == owner, 1.0, 0.0)
    tile = 256
    upper = jnp.where(iota((tile, tile), 0) <= iota((tile, tile), 1), 1.0, 0.0).astype(jnp.bfloat16)
    before = jnp.zeros((rows, 1), jnp.float32)
    ranks = []
    for piece in range(points // tile):
        part = dot(marks[:, piece * tile:(piece + 1) * tile].astype(jnp.bfloat16), upper)
        ranks.append(part + before - 1.0)
        before = before + part[:, tile - 1:tile]
    ranks = jnp.concatenate(ranks, axis=1)
    chunks = jnp.floor((before + (CHUNK - 1)) * (1.0 / CHUNK))
    start = jnp.zeros((1, 1), jnp.float32)
    starts = []
    for name in range(rows):
        starts.append(start)
        start = start + chunks[name:name + 1]
    starts = jnp.concatenate(starts, axis=0)
    slot = jnp.sum(marks * (ranks + starts * CHUNK), axis=0, keepdims=True).astype(jnp.int32)
    slot_ref[...] = slot
    lane = iota((rows, 128), 1)
    ended = jnp.sum(jnp.where(starts + chunks <= lane.astype(jnp.float32), 1.0, 0.0), axis=0, keepdims=True)
    block = jnp.minimum(ended, n_row - 1.0)
    place = iota((8, 128), 0)
    table_ref[...] = jnp.where(place == 0, block, start).astype(jnp.int32)
    high = jnp.where(iota((chunk_count, points), 0) == slot // CHUNK, 1.0, 0.0)
    low = jnp.where(iota((CHUNK, points), 0) == slot % CHUNK, 1.0, 0.0).astype(jnp.bfloat16)
    parts = split3(bundle_ref[6:9, 0:points] - 0.5)
    spread = jnp.concatenate([high * part[k:k + 1] for k in range(3) for part in parts], axis=0).astype(jnp.bfloat16)
    placed = dot_nt(spread, low)
    planes = [placed[k * chunk_count:(k + 1) * chunk_count] for k in range(9)]
    x, y, z = (planes[3 * k] + planes[3 * k + 1] + planes[3 * k + 2] for k in range(3))
    sides = [-2.0 * x, -2.0 * y, -2.0 * z, jnp.ones_like(x), x * x + y * y + z * z + EPS_FIELD]
    sides = [split3(side) for side in sides]
    empty = jnp.zeros_like(x)
    for group, part in enumerate([0, 0, 1, 1, 0, 2]):
        for k in range(8):
            to = pl.ds((group * 8 + k) * chunk_count, chunk_count)
            planes_ref[to, :] = sides[k][part] if k < 5 else empty
    for chunk in range(chunk_count):
        left_ref[chunk * CHUNK:(chunk + 1) * CHUNK, :] = transposed(planes_ref[pl.ds(chunk, 48, stride=chunk_count), :])


def cube_halves(left, right):
    inverse = lax.rsqrt(dot(left, right))
    cube = inverse * inverse * inverse
    high = cube.astype(jnp.bfloat16)
    return high, (cube - high.astype(jnp.float32)).astype(jnp.bfloat16)


def block_part(block, col, n_row, seg_dev):
    return aligned((col * n_row + block) * seg_dev, seg_dev)


def chunk_steps(group_ref):
    return (group_ref[1, 0] + GROUP - 1) // GROUP


def weigh_kernel(group_ref, left_ref, right_ref, cubes_hbm, done_ref, cubes_ref, sems, *, n_row, n_col, first, last):
    seg_dev = right_ref.shape[1] // (n_row * n_col)
    done_ref[...] = jnp.zeros_like(done_ref)
    stop = chunk_steps(group_ref) if last is None else last // GROUP

    def chunk_copy(place):
        return pltpu.make_async_copy(cubes_ref.at[place], cubes_hbm.at[place], sems.at[place])

    def step(k, carry):
        for part in range(GROUP):
            chunk = k * GROUP + part
            place = chunk - first
            left = left_ref[aligned(chunk * CHUNK, CHUNK), :]
            for col in range(n_col):
                to = slice(col * seg_dev, (col + 1) * seg_dev)
                high, low = cube_halves(left, right_ref[:, block_part(group_ref[0, chunk], col, n_row, seg_dev)])
                cubes_ref[place, 0:CHUNK, to] = high
                cubes_ref[place, CHUNK:2 * CHUNK, to] = low
            chunk_copy(place).start()
        return carry

    def finish(k, carry):
        for part in range(GROUP):
            chunk_copy(k * GROUP + part - first).wait()
        return carry

    lax.fori_loop(first // GROUP, stop, step, 0)
    lax.fori_loop(first // GROUP, stop, finish, 0)


def field_kernel(group_ref, length_ref, slot_ref, moment_ref, basis_ref, *refs, n_row, n_col, keep):
    if keep:
        early_hbm, late_hbm, out_ref, table_ref, sums_ref, cubes_ref, sems = refs
        kept = (cubes_ref, sems)

        bounds = part_bounds(n_col, moment_ref.shape[1] // (n_row * n_col))

        def clear(chunk, piece):
            start, stop = bounds[piece]
            cubes_ref[chunk, :, start:stop] = jnp.zeros((2 * CHUNK, stop - start), jnp.bfloat16)

        def begin(remote, first, chunk, carry):
            for_parts(group_ref, length_ref, chunk, bounds,
                      lambda piece: part_copy(kept, chunk, piece, bounds, remote, first).start(),
                      lambda piece: clear(chunk, piece))
            return carry

        def arrive(remote, first, chunk):
            for_parts(group_ref, length_ref, chunk, bounds,
                      lambda piece: part_copy(kept, chunk, piece, bounds, remote, first).wait())

        lax.fori_loop(0, EARLY, functools.partial(begin, early_hbm, 0), 0)
        lax.fori_loop(EARLY, chunk_steps(group_ref) * GROUP, functools.partial(begin, late_hbm, EARLY), 0)
    else:
        left_ref, right_ref, out_ref, table_ref, sums_ref = refs
    chunk_count = sums_ref.shape[0] // 16
    seg_dev = moment_ref.shape[1] // (n_row * n_col)
    scale = 1.0 / math.sqrt(n_col * seg_dev)
    lane = iota((1, seg_dev), 1)
    sums_ref[...] = jnp.zeros_like(sums_ref)

    def table_step(block, carry):
        length = length_ref[block]
        for col in range(n_col):
            at = block_part(block, col, n_row, seg_dev)
            both = moment_ref[:, at]
            active = jnp.where(lane + col * seg_dev < length, scale, 0.0)
            first = both * (basis_ref[0:1, at] * active)
            second = both * (basis_ref[1:2, at] * active)
            parts = jnp.concatenate([first, second], axis=0)
            high = parts.astype(jnp.bfloat16).astype(jnp.float32)
            table_ref[:, at] = jnp.concatenate([high, parts - high], axis=0).astype(jnp.bfloat16)
        return carry

    lax.fori_loop(0, n_row, table_step, 0, unroll=min(n_row, 8))

    def block_row(ref, chunk):
        block = group_ref[0, chunk]
        return jnp.concatenate([ref[:, block_part(block, col, n_row, seg_dev)] for col in range(n_col)], axis=1)

    def cubes_of(chunk):
        return jnp.concatenate(cube_halves(left_ref[aligned(chunk * CHUNK, CHUNK), :], block_row(right_ref, chunk)), axis=0)

    def step(source, k, carry):
        if keep:
            for part in range(GROUP):
                arrive(*source, k * GROUP + part)
        for part in range(0, GROUP, 2):
            chunk = k * GROUP + part
            tables = jnp.concatenate([block_row(table_ref, chunk), block_row(table_ref, chunk + 1)], axis=0)
            if keep:
                cubes = cubes_ref[pl.ds(chunk, 2)].reshape(4 * CHUNK, n_col * seg_dev)
            else:
                cubes = jnp.concatenate([cubes_of(chunk), cubes_of(chunk + 1)], axis=0)
            both = dot_nt(tables, cubes)
            for half in range(2):
                mine = both[32 * half:32 * half + 32, 2 * CHUNK * half:2 * CHUNK * (half + 1)]
                total = mine[:, 0:CHUNK] + mine[:, CHUNK:2 * CHUNK]
                sums_ref[pl.ds(chunk + half, 16, stride=chunk_count), :] = total[0:16] + total[16:32]
        return carry

    if keep:
        lax.fori_loop(0, EARLY // GROUP, functools.partial(step, (early_hbm, 0)), 0)
        lax.fori_loop(EARLY // GROUP, chunk_steps(group_ref), functools.partial(step, (late_hbm, EARLY)), 0)
    else:
        lax.fori_loop(0, chunk_steps(group_ref), functools.partial(step, None), 0)
    sums = jnp.concatenate([sums_ref[0:6 * chunk_count], sums_ref[8 * chunk_count:14 * chunk_count]], axis=0)
    sums = jnp.concatenate(split3(sums), axis=1).astype(jnp.bfloat16)
    for tile in range(slot_ref.shape[1] // TILE):
        at = pl.ds(tile * TILE, TILE)
        slot = slot_ref[:, at]
        low = jnp.where(iota((CHUNK, TILE), 0) == slot % CHUNK, 1.0, 0.0).astype(jnp.bfloat16)
        high = jnp.where(iota((chunk_count, TILE), 0) == slot // CHUNK, 1.0, 0.0)
        found = dot(sums, jnp.concatenate([low, low, low], axis=0))
        for row in range(12):
            picked = found[row * chunk_count:(row + 1) * chunk_count] * high
            out_ref[row:row + 1, at] = jnp.sum(picked, axis=0, keepdims=True)


def final_kernel(stats_ref, known_ref, basis_own_ref, field_ref, bundle_ref, currents_ref, iron_ref):
    stats = jnp.sum(stats_ref[...], axis=0)
    known = known_ref[...]
    initial_norm, hessen_a, hessen_b = known[:, 0:1], known[:, 1:2], known[:, 2:3]
    hessen_c, hessen_d, normal_second = stats[:, 0:1], stats[:, 1:2], stats[:, 2:3]
    normal_first = hessen_a * hessen_a + hessen_b * hessen_b
    normal_cross = hessen_a * hessen_c + hessen_b * hessen_d
    target_first = initial_norm * hessen_a
    target_second = initial_norm * hessen_c
    determinant = normal_first * normal_second - normal_cross * normal_cross
    weight_first = (normal_second * target_first - normal_cross * target_second) / determinant
    weight_second = (normal_first * target_second - normal_cross * target_first) / determinant
    currents_ref[...] = weight_first * basis_own_ref[0:1, :] + weight_second * basis_own_ref[1:2, :]
    moments = weight_first * field_ref[0:6, :] + weight_second * field_ref[6:12, :]
    points = bundle_ref[6:9, 0:iron_ref.shape[1]] - 0.5
    px, py, pz = points[0:1], points[1:2], points[2:3]
    iron_ref[0:1, :] = pz * moments[1:2] - py * moments[2:3] - moments[3:4]
    iron_ref[1:2, :] = px * moments[2:3] - pz * moments[0:1] - moments[4:5]
    iron_ref[2:3, :] = py * moments[0:1] - px * moments[1:2] - moments[5:6]


def shape(*sizes, dtype=jnp.float32):
    return jax.ShapeDtypeStruct(sizes, dtype)


def shards(drive, resist, centers, tangents, iron_points, owner, range_len):
    seg_dev = drive.shape[0]
    col_len = centers.shape[1]
    n_col = lax.axis_size("col")
    n_row = lax.axis_size("row")
    n_dev = n_col * n_row
    segments = seg_dev * n_dev
    width = n_col * seg_dev
    points_count = iron_points.shape[1]
    coupling = 0.5 / math.sqrt(segments)
    call = functools.partial(pl.pallas_call, compiler_params=pltpu.CompilerParams(vmem_limit_bytes=VMEM_LIMIT))
    scratch = [pltpu.VMEM((1, segments), jnp.float32), pltpu.VMEM((seg_dev, 128), jnp.float32)]
    hbm = pl.BlockSpec(memory_space=pltpu.HBM)
    smem = pl.BlockSpec(memory_space=pltpu.SMEM)
    vmem = pl.BlockSpec(memory_space=pltpu.VMEM)

    def work(microseconds):
        return pl.CostEstimate(flops=int(microseconds * 1e9), bytes_accessed=0, transcendentals=0)

    def roomy(row_bytes):
        return STREAM_BYTES // row_bytes

    def exchange(x):
        return lax.all_to_all(x, AXES, 0, 0, tiled=True)

    spread, geometry = pl.pallas_call(
        entry_kernel,
        out_shape=(shape(n_dev, 1, seg_dev), shape(6, col_len)),
        in_specs=[hbm] * 3,
        scratch_shapes=[
            pltpu.VMEM((1, seg_dev), jnp.float32),
            pltpu.VMEM((3, col_len), jnp.float32),
            pltpu.VMEM((3, col_len), jnp.float32),
            pltpu.SemaphoreType.DMA((3,)),
        ],
        compiler_params=pltpu.CompilerParams(vmem_limit_bytes=ENTRY_LIMIT),
        cost_estimate=work(8),
        name="entry",
    )(drive[None, :], centers, tangents)
    drive_all = exchange(spread).reshape(1, segments)
    longest = max(col_len, points_count, 2 * seg_dev)

    def wide(row):
        return jnp.pad(row, ((0, 0), (0, longest - row.shape[1])))

    bundle = jnp.concatenate([
        wide(centers), wide(tangents), wide(iron_points), wide(owner.reshape(1, points_count).astype(jnp.float32)),
        wide(jnp.concatenate([drive, resist])[None, :]),
    ], axis=0)
    pieces = [bundle] + [
        lax.ppermute(geometry, "col", [(k, (k + shift) % n_col) for k in range(n_col)]) for shift in range(1, n_col)
    ]

    chunk_count = points_count // CHUNK + n_row * (CHUNK - 1) // CHUNK
    chunk_count = -(-chunk_count // 8) * 8
    slot, group_table, left = call(
        functools.partial(group_kernel, n_row=n_row),
        out_shape=(
            shape(1, points_count, dtype=jnp.int32),
            shape(8, 128, dtype=jnp.int32),
            shape(chunk_count * CHUNK, 48, dtype=jnp.bfloat16),
        ),
        scratch_shapes=[pltpu.VMEM((48 * chunk_count, CHUNK), jnp.float32)],
        cost_estimate=work(3),
        name="group_points",
    )(bundle)

    cube_shape = (chunk_count, 2 * CHUNK, width)
    keep = 2 * math.prod(cube_shape) <= KEEP_BYTES
    stream = functools.partial(
        pl.pallas_call, compiler_params=pltpu.CompilerParams(vmem_limit_bytes=STREAM_LIMIT if keep else VMEM_LIMIT)
    )
    sides = call(
        functools.partial(sides_kernel, n_col=n_col),
        out_shape=(
            shape(48, segments, dtype=jnp.bfloat16), shape(8, segments),
            shape(2, seg_dev, 48, dtype=jnp.bfloat16), shape(3, seg_dev, 128),
        ),
        cost_estimate=work(1),
        name="sides",
    )(*pieces)
    right, moment = sides[0:2]
    def weigh(first, last, microseconds, name):
        count = (last or chunk_count) - first
        return stream(
            functools.partial(weigh_kernel, n_row=n_row, n_col=n_col, first=first, last=last),
            out_shape=(shape(roomy(4 * CHUNK * width), *cube_shape[1:], dtype=jnp.bfloat16), shape(8, 128)),
            in_specs=[smem, vmem, vmem],
            out_specs=(hbm, vmem),
            scratch_shapes=[pltpu.VMEM((count,) + cube_shape[1:], jnp.bfloat16), pltpu.SemaphoreType.DMA((count,))],
            cost_estimate=work(microseconds),
            name=name,
        )(group_table, left, right)

    if keep:
        early, before = weigh(0, EARLY, 2, "weigh_early")
    else:
        before = group_table
    image_own, image_spread = call(
        functools.partial(first_kernel, coupling),
        out_shape=(shape(1, seg_dev), shape(n_dev, 1, seg_dev)),
        scratch_shapes=scratch,
        cost_estimate=work(3),
        name="first_image",
    )(drive_all, bundle, before, *sides)
    image_all = exchange(image_spread).reshape(1, segments)
    cube_scratch = [pltpu.VMEM(cube_shape, jnp.bfloat16), pltpu.SemaphoreType.DMA((3 * chunk_count,))]
    if keep:
        late, after = weigh(EARLY, None, 4, "weigh_late")
    else:
        after = group_table
    basis, basis_own, stats, known = call(
        functools.partial(second_kernel, coupling),
        out_shape=(shape(2, segments), shape(2, seg_dev), shape(n_dev, 1, 128), shape(1, 128)),
        scratch_shapes=scratch,
        cost_estimate=work(3),
        name="second_image",
    )(drive_all, image_all, image_own, bundle, after, *sides)
    stats_all = exchange(stats)

    field = stream(
        functools.partial(field_kernel, n_row=n_row, n_col=n_col, keep=keep),
        out_shape=shape(12, points_count),
        in_specs=[smem, smem, vmem, vmem, vmem] + ([hbm, hbm] if keep else [vmem, vmem]),
        scratch_shapes=[
            pltpu.VMEM((32, segments), jnp.bfloat16),
            pltpu.VMEM((16 * chunk_count, CHUNK), jnp.float32),
        ] + (cube_scratch if keep else []),
        cost_estimate=work(6),
        name="block_field",
    )(group_table, range_len, slot, moment, basis, *([early, late] if keep else [left, right]))
    currents, iron_field = stream(
        final_kernel,
        out_shape=(shape(1, seg_dev), shape(3, points_count)),
        name="combine",
    )(stats_all, known, basis_own, field, bundle)
    return (currents[0], iron_field)


def solution(mesh):
    return jax.shard_map(
        shards,
        mesh=mesh,
        in_specs=(
            P(AXES),
            P(AXES),
            P(None, "col"),
            P(None, "col"),
            P(None, AXES),
            P(AXES, None),
            P(),
        ),
        out_specs=(P(AXES), P(None, AXES)),
        check_vma=False,
    )
```
